32 devices in a mesh: group: 2 (over y), lat: 8 (over z, x), lon: 2 (over core).
Axes of the slice: x: 2, y: 2, z: 4, core: 2. Of those that a mesh axis runs over, the one named last changes fastest.
Arguments:
- tracers: float32 [8, 32, 32, 1152], P('group', None, 'lat', 'lon'), parts along dimension 0, may hold values from -6 to 6
- courant_lat: float32 [64, 32, 1152], P('group', 'lat', 'lon'), parts along dimension 0, may hold values from -0.45 to 0.45
- courant_lon: float32 [64, 32, 1152], P('group', 'lat', 'lon'), parts along dimension 0, may hold values from -0.45 to 0.45
- surface_flux: float32 [8, 32, 1152], P('group', 'lat', 'lon'), parts along dimension 0, may hold values from -6 to 6
- mixing: float32 [32, 32], replicated, may hold values from -1 to 1
- decay_rate: float32 [4, 32], replicated, may hold values from 0.05 to 1
- owners: int32 [16, 2, 18, 1], P(('group', 'lat'), 'lon'), parts along dimension 0, may hold values from 0 to 7; in each aligned block of 18 rows (0 to 17, 18 to 35, ..., all dimensions but the last counted through in order) at most 5 rows name the same one
- polar_mask: int32 [64], P(('group', 'lat')), parts along dimension 0, may hold values 0 or 1
Outputs:
- tracers_out: float32 [8, 32, 32, 1152], P('group', None, 'lat', 'lon'), parts along dimension 0
- owner_energy: float32 [16, 2], P(('group', 'lat'), 'lon'), parts along dimension 0
The draws below stay inside these ranges and needn't reach their ends.
There are 2 independent parts, one for each index of `group`. The reference program is written for one: setup_inputs(seed, part) draws one part's arguments, and reference() takes and returns one part's arrays. A program takes and returns all parts, laid end to end along the dimension named above; an argument that names none is the same for every part. Nothing has to cross between parts.
Inputs may be any that keep to these rules, and one draw needn't show every extreme that they name: `owners`: the 18 blocks of one lat index and one lon index name one owner at most 5 times; in every draw some lat and lon index names one owner exactly 5 times.
All inputs are finite; a program needn't handle non-finite values. No bound on the sum of `polar_mask` on one device may be relied on, other than what follows from the above.
Results may differ from the reference program's by a relative error of at most 0.000073.
Values sent between devices are 32-bit elements; how exact they have to be, the bound alone decides.
No kernel may reach another device: no remote copies, remote signals or barrier semaphores. Data moves between devices by JAX's collectives and lax.ppermute only.
A program may use at most 128 MiB of HBM per device.

```python
import math
import jax
import jax.numpy as jnp
import numpy as np
from jax import lax

NLON = 1152
NTR = 4
LEV = 32
BLOCK = 128
ROWS_DEV = 4
NLAT = 32
NBLK = 18
CAP = 5
N_LAT = 8
N_LON = 2


def set_ends(result, rng, low, high):
    longest = result.shape.index(max(result.shape))
    spots = []
    for shift in (0, 1):
        where = [jax.random.randint(jax.random.fold_in(rng, axis), (), 0, length) for axis, length in enumerate(result.shape)]
        where[longest] = (where[longest] + shift) % result.shape[longest]
        spots.append(tuple(where))
    return result.at[spots[0]].set(low).at[spots[1]].set(high)


def steps_of(stream_key, shape, cuts, least, high):
    factor_of, own = 1.0, jax.random.fold_in(stream_key, 6)
    for dim, blocks in cuts:
        heights = jnp.exp(jax.random.uniform(jax.random.fold_in(own, dim), (blocks,), jnp.float32, least / len(cuts), high / len(cuts)))
        factor_of = factor_of * jnp.repeat(heights, shape[dim] // blocks).reshape([-1 if axis == dim else 1 for axis in range(len(shape))])
    return factor_of


def shared_out(own_key, own, number, rows, count, top, reach, lean):
    sequence = jax.random.permutation(own_key, count)
    crowded, usual = load_shares(count, rows * top, reach, lean, True), load_shares(count, rows * top, reach, lean, False)
    places = jnp.arange(count)

    def named(tallies, rotation):
        used = int((tallies > 0).sum())
        fixed = max(1, used // 4)
        passed = fixed + (places - fixed + rotation * (used - fixed)) % max(1, count - fixed)
        return jnp.zeros((count,), jnp.int32).at[sequence[jnp.where(places < fixed, places, passed)]].set(jnp.asarray(tallies, jnp.int32))

    tallies = jnp.where(number % 4 == 0, named(crowded, number // 4), named(usual, number - number // 4 - 1))
    mixed = jax.random.permutation(jax.random.fold_in(own, 3), count)
    donor, sink = mixed[0:count // 2 * 2:2], mixed[1:count // 2 * 2:2]
    margin = jnp.minimum(tallies[donor] - 1, reach - tallies[sink]) // 2
    margin = jnp.where((donor == sequence[0]) | (sink == sequence[0]) | (tallies[sink] == 0), 0, jnp.maximum(margin, 0))
    passed = jax.random.randint(jax.random.fold_in(own, 4), (count // 2,), 0, 1 << 20) % (margin + 1)
    tallies = tallies.at[donor].add(-passed).at[sink].add(passed)
    members = jnp.searchsorted(jnp.cumsum(tallies), jnp.arange(rows * top), side="right").astype(jnp.int32)
    listing = members.reshape(top, rows).T
    listing = listing[jax.random.permutation(jax.random.fold_in(own, 1), rows)]
    rotation = jax.random.randint(jax.random.fold_in(own, 2), (rows, 1), 0, top)
    return jnp.take_along_axis(listing, (jnp.arange(top)[None, :] + rotation) % top, axis=1)


def load_shares(amount, total, reach, lean, full):
    portions = [(1 << 20) // math.isqrt(grade ** lean) + 1 for grade in range(1, amount + 1)]
    largest = reach if full else min(reach, max(-(-total // amount), total * portions[0] // sum(portions)))
    least = 1 if total - largest >= amount - 1 else 0
    counts, rest = [largest] + [least] * (amount - 1), total - largest - least * (amount - 1)
    while rest > 0:
        free = [i for i in range(1, amount) if counts[i] < largest] or [i for i in range(1, amount) if counts[i] < reach]
        pool, budget = sum([portions[i] for i in free]), rest
        for i in free:
            more = min(reach - counts[i], max(1, budget * portions[i] // pool), rest)
            counts[i] = counts[i] + more
            rest = rest - more
    return np.array(counts)


def noise(rng, dims, deviation, reach, shards=(), kind=jnp.bfloat16):
    result = deviation * jax.random.normal(rng, dims, jnp.float32)
    if shards:
        result = result * steps_of(rng, dims, shards, -0.22, 0.18)
    return jnp.clip(result, -reach, reach).astype(kind)


def setup_inputs(seed: int = 0, part: int = 0) -> dict:
    seeds = jax.random.split(jax.random.key(seed), 9)
    part_keys = jax.random.split(jax.random.fold_in(seeds[8], part), 9)
    tracers = noise(part_keys[0], (NTR, LEV, NLAT, NLON), 1.0, 6.0, ((2, 8), (3, 2)), jnp.float32)
    courant_lat = jnp.clip(jax.random.uniform(part_keys[1], (LEV, NLAT, NLON), jnp.float32, -0.45, 0.45) * steps_of(part_keys[1], (LEV, NLAT, NLON), ((1, 8), (2, 2)), -0.4, 0.0), -0.45, 0.45)
    courant_lon = jnp.clip(jax.random.uniform(part_keys[2], (LEV, NLAT, NLON), jnp.float32, -0.45, 0.45) * steps_of(part_keys[2], (LEV, NLAT, NLON), ((1, 8), (2, 2)), -0.4, 0.0), -0.45, 0.45)
    surface_flux = noise(part_keys[3], (NTR, NLAT, NLON), 1.0, 6.0, ((1, 8), (2, 2)), jnp.float32)
    mixing = noise(seeds[4], (LEV, LEV), LEV ** -0.5, 1.0, (), jnp.float32)
    decay_rate = jnp.clip(jnp.exp(jax.random.uniform(seeds[5], (NTR, LEV), jnp.float32, math.log(0.05), math.log(1.0))), 0.05, 1.0)
    owners_keys = jax.random.split(jax.random.fold_in(part_keys[6], 1), N_LAT * N_LON * NBLK // NBLK)
    owners_turns = jax.random.permutation(jax.random.fold_in(part_keys[6], 3), N_LAT * N_LON * NBLK // NBLK)
    owners = jax.vmap(lambda own, number: shared_out(jax.random.fold_in(part_keys[6], 2), own, number, NBLK, N_LAT, 1, CAP, 2))(owners_keys, owners_turns).reshape((N_LAT, N_LON, NBLK, 1))
    polar_mask = set_ends((jax.random.randint(part_keys[7], (NLAT,), 0, 2) < 1).astype(jnp.int32), jax.random.fold_in(part_keys[7], 1), 0, 1)
    return dict(tracers=tracers, courant_lat=courant_lat, courant_lon=courant_lon, surface_flux=surface_flux, mixing=mixing, decay_rate=decay_rate, owners=owners, polar_mask=polar_mask)


def edges_along(padded, cell_count, along_dim):
    def window(offset):
        return lax.slice_in_dim(padded, offset, offset + cell_count + 1, axis=along_dim)
    return (7.0 / 12.0) * (window(2) + window(1)) - (1.0 / 12.0) * (window(3) + window(0))


def transport(tracers, lat_padded, lat_courant, lon_padded, lon_courant, first_row):
    band_rows = tracers.shape[2]
    sector = tracers.shape[3]
    lat_edges = edges_along(lat_padded, band_rows, 2)
    pole_mask = (first_row + jnp.arange(band_rows + 1) > 0).astype(jnp.float32)
    lat_flux = lat_courant[None] * lat_edges * pole_mask[:, None]
    lon_edges = edges_along(lon_padded, sector, 3)
    lon_flux = lon_courant[None] * lon_edges
    return tracers - (lat_flux[:, :, 1:] - lat_flux[:, :, :-1]) - (lon_flux[..., 1:] - lon_flux[..., :-1])


def reference(tracers, courant_lat, courant_lon, surface_flux, mixing, decay_rate, owners, polar_mask):
    lat_padded = jnp.pad(tracers, ((0, 0), (0, 0), (2, 2), (0, 0)))
    lat_courant = jnp.concatenate([courant_lat, jnp.zeros((LEV, 1, NLON), jnp.float32)], axis=1)
    lon_padded = jnp.concatenate([tracers[..., -2:], tracers, tracers[..., :2]], axis=3)
    lon_courant = jnp.concatenate([courant_lon, courant_lon[:, :, :1]], axis=2)
    advected = transport(tracers, lat_padded, lat_courant, lon_padded, lon_courant, 0)
    mixed_state = jnp.einsum("kl,tlyx->tkyx", mixing, advected, precision=lax.Precision.HIGHEST)
    mixed_state = mixed_state.at[:, LEV - 1].add(surface_flux)
    physics = mixed_state / (1.0 + decay_rate[:, :, None, None] * mixed_state * mixed_state)
    column_energy = jnp.sum((physics - advected) ** 2, axis=(0, 1))
    sector = NLON // N_LON
    block_energy = column_energy.reshape(N_LAT, ROWS_DEV, N_LON, sector).transpose(0, 2, 1, 3)
    block_energy = jnp.sum(block_energy.reshape(N_LAT, N_LON, NBLK, BLOCK), axis=3)
    onehot = (owners[..., 0][..., None] == jnp.arange(N_LAT)).astype(jnp.float32)
    owner_energy = jnp.einsum("aspo,asp->os", onehot, block_energy, precision=lax.Precision.HIGHEST) / (NBLK * BLOCK)
    latitude = (-0.5 + (jnp.arange(NLAT).astype(jnp.float32) + 0.5) / NLAT) * math.pi
    wavenumber = jnp.arange(NLON // 2 + 1)
    sine = jnp.sin(math.pi * wavenumber.astype(jnp.float32) / NLON)
    ratio_sq = (2.0 * jnp.cos(latitude)[:, None] / jnp.where(wavenumber == 0, 1.0, sine)[None]) ** 2
    damping = jnp.where(wavenumber[None] == 0, 1.0, jnp.minimum(1.0, ratio_sq))
    spectrum = jnp.fft.rfft(physics, axis=-1)
    filtered = jnp.fft.irfft(spectrum * damping, n=NLON, axis=-1).astype(physics.dtype)
    tracers_out = jnp.where(polar_mask[:, None] == 1, filtered, physics)
    return tracers_out, owner_energy
```

```python
import functools
import math

import jax
import jax.numpy as jnp
import numpy as np
from jax import lax
from jax.experimental import pallas as pl
from jax.experimental.pallas import tpu as pltpu
from jax.sharding import PartitionSpec as P

LANES = 128
BLOCK = 128
VMEM_BYTES = 24 * 1024 * 1024
NEAR = 7.0 / 12.0
FAR = 1.0 / 12.0
DOT_LAST = (((1,), (1,)), ((), ()))


def params():
    return pltpu.CompilerParams(vmem_limit_bytes=VMEM_BYTES)


def cost(flops, bytes_accessed):
    return pl.CostEstimate(flops=flops, bytes_accessed=bytes_accessed, transcendentals=0)


def split_high_low(value):
    high = value.astype(jnp.bfloat16)
    low = (value - high.astype(jnp.float32)).astype(jnp.bfloat16)
    return high, low


def split_table(table):
    high = table.astype(jnp.bfloat16.dtype)
    low = (table - high.astype(np.float64)).astype(jnp.bfloat16.dtype)
    return high, low


def spectral_tables(length):
    radix = length // LANES
    pairs = (radix - 1) // 2
    spot = np.arange(LANES)[:, None]
    number = np.arange(LANES)[None, :]
    is_cosine = number <= LANES // 2
    wave = np.where(is_cosine, number, number - LANES // 2)
    angle = 2.0 * np.pi * ((spot * wave) % LANES) / LANES
    first = np.where(is_cosine, np.cos(angle), np.sin(angle))
    others, numbers = [], [radix * wave[0]]
    weights = [np.where((wave[0] == 0) | (wave[0] == LANES // 2), 1.0, 2.0) / length]
    for residue in range(1, pairs + 1):
        whole = residue + radix * number
        angle = 2.0 * np.pi * ((spot * whole) % length) / length
        cosine, sine = np.cos(angle), np.sin(angle)
        others.append(np.block([[cosine, -sine], [sine, cosine]]))
        folded = np.minimum(whole[0], length - whole[0])
        numbers += [folded, folded]
        weights.append(np.full(2 * LANES, 2.0 / length))
    return first, np.concatenate(others, axis=0), np.concatenate(numbers), np.concatenate(weights)


def pack_rows(first, second):
    return jnp.concatenate([first, second], axis=1)


def second_half(packed, sector):
    skip, shift = sector // LANES, sector % LANES
    segments = [packed[:, LANES * i : LANES * (i + 1)] for i in range(packed.shape[1] // LANES)]
    if shift == 0:
        return jnp.concatenate(segments[skip:], axis=1)
    turned = [pltpu.roll(segment, LANES - shift, 1) for segment in segments[skip:]]
    lane = lax.broadcasted_iota(jnp.int32, turned[0].shape, 1)
    parts = [jnp.where(lane < LANES - shift, turned[i], turned[min(i + 1, len(turned) - 1)]) for i in range(len(turned))]
    return jnp.concatenate(parts, axis=1)


def pack_kernel(rows, levels, with_courant, *refs):
    if with_courant:
        tracer_ref, courant_ref, up_ref, down_ref = refs
    else:
        tracer_ref, up_ref, down_ref = refs
    up_ref[...] = pack_rows(tracer_ref[0, :, rows - 2, :], tracer_ref[0, :, rows - 1, :])
    down_ref[0:levels, :] = pack_rows(tracer_ref[0, :, 0, :], tracer_ref[0, :, 1, :])
    if with_courant:
        courant = courant_ref[:, 0, :]
        down_ref[levels : levels + levels // 2, :] = pack_rows(courant[: levels // 2], courant[levels // 2 :])


def base_kernel(rows, width, padded_ref, east_courant_ref, lat_courant_ref, base_ref):
    q = [padded_ref[0, r] for r in range(rows)]
    own_flux = [None] * (rows + 1)
    own_flux[0] = lat_courant_ref[0] * (NEAR * q[0] - FAR * q[1])
    own_flux[1] = lat_courant_ref[1] * (NEAR * (q[1] + q[0]) - FAR * q[2])
    own_flux[2] = lat_courant_ref[2] * (NEAR * (q[2] + q[1]) - FAR * (q[3] + q[0]))
    own_flux[3] = lat_courant_ref[3] * (NEAR * (q[3] + q[2]) - FAR * q[1])
    for r in range(rows):
        west, west2, east = pltpu.roll(q[r], 1, 1), pltpu.roll(q[r], 2, 1), pltpu.roll(q[r], width - 1, 1)
        flux = east_courant_ref[r] * (NEAR * (q[r] + west) - FAR * (east + west2))
        value = q[r] - (pltpu.roll(flux, width - 1, 1) - flux) + own_flux[r]
        if r + 1 < rows:
            value = value - own_flux[r + 1]
        base_ref[0, r] = value


def physics_kernel(rows, levels, sector, owner_count, *refs):
    if owner_count:
        owner_ref, refs = refs[0], refs[1:]
    (base_ref, padded_ref, low_ref, high_ref, courant_ref, top_ref, surface_ref, mixing_ref, decay_ref, energy_in_ref,
     physics_ref, energy_ref) = refs
    width = base_ref.shape[-1]
    low = low_ref[...]
    high = high_ref[0:levels, :]
    low_a, low_b = low[:, :width], second_half(low, sector)
    high_a, high_b = high[:, :width], second_half(high, sector)
    courant = [courant_ref[r] for r in range(rows)]
    south = courant[0] * (NEAR * low_b - FAR * low_a)
    south_in = courant[1] * (FAR * low_b)
    north_in = courant[3] * (FAR * high_a)
    north = top_ref[...] * (NEAR * (high_a + padded_ref[0, 3]) - FAR * (high_b + padded_ref[0, 2]))
    extra = [south + south_in, -south_in, north_in, -north_in - north]
    mix_high, mix_low = split_high_low(mixing_ref[...])
    mix = jnp.concatenate([mix_high, mix_high, mix_low, mix_low], axis=1)
    decay = decay_ref[0]
    level = lax.broadcasted_iota(jnp.int32, (levels, width), 0)
    lane = lax.broadcasted_iota(jnp.int32, (levels, width), 1)
    energies = []
    for r in range(rows):
        advected = base_ref[0, r] + extra[r]
        part_high, part_low = split_high_low(advected)
        stacked = jnp.concatenate([part_high, part_low, part_high, part_low], axis=0)
        mixed = jnp.dot(mix, stacked, preferred_element_type=jnp.float32)
        mixed = jnp.where(level == levels - 1, mixed + surface_ref[0, r : r + 1, :], mixed)
        physics = mixed / (1.0 + decay * mixed * mixed)
        physics_ref[r] = physics
        gap = jnp.where(lane < sector, physics - advected, 0.0)
        squared = gap * gap
        total = energy_in_ref[r]
        for k in range(levels // 8):
            total = total + squared[8 * k : 8 * k + 8]
        energies.append(total)
    if not owner_count:
        for r in range(rows):
            energy_ref[r] = energies[r]
        return
    spot = lax.broadcasted_iota(jnp.int32, (1, LANES), 1)
    result = jnp.zeros((1, LANES), jnp.float32)
    for owner in range(owner_count):
        chosen = jnp.zeros((8, LANES), jnp.float32)
        for r in range(rows):
            picked = jnp.where(owner_ref[r : r + 1, :] == owner, energies[r], 0.0)
            for k in range(width // LANES):
                chosen = chosen + picked[:, LANES * k : LANES * (k + 1)]
        summed = jnp.sum(jnp.sum(chosen, axis=0, keepdims=True), axis=1, keepdims=True)
        result = jnp.where(spot == owner, summed, result)
    energy_ref[...] = result


def filter_kernel(rows, levels, sector, radix, has_alias, *refs):
    mask_ref, own_ref, other_ref, table_high_ref, table_low_ref, first_high_ref, first_low_ref, scale_ref = refs[:8]
    out_ref, high_ref, low_ref, wave_ref = refs[8 + has_alias :]
    pairs = (radix - 1) // 2
    shift = sector % LANES
    own_segments = -(-sector // LANES)
    lane = lax.broadcasted_iota(jnp.int32, (levels, LANES), 1)
    cosine = lambda k, i: math.cos(2.0 * math.pi * ((k * i) % radix) / radix)
    sine = lambda k, i: math.sin(2.0 * math.pi * ((k * i) % radix) / radix)

    for r in range(rows):
        own = [own_ref[r, :, LANES * i : LANES * (i + 1)] for i in range(own_segments)]
        turned = [pltpu.roll(other_ref[r, :, LANES * i : LANES * (i + 1)], shift, 1) for i in range(own_segments)]
        joined = own[:-1] + [jnp.where(lane < shift, own[-1], turned[0])]
        joined += [jnp.where(lane < shift, turned[i], turned[i + 1]) for i in range(own_segments - 1)]
        plus = [joined[i] + joined[radix - i] for i in range(1, pairs + 1)]
        minus = [joined[radix - i] - joined[i] for i in range(1, pairs + 1)]
        waves = [sum(plus, joined[0])]
        for k in range(1, pairs + 1):
            waves.append(sum((cosine(k, i) * plus[i - 1] for i in range(1, pairs + 1)), joined[0]))
            waves.append(sum(sine(k, i) * minus[i - 1] for i in range(1, pairs + 1)))
        for i, wave in enumerate(waves):
            part_high, part_low = split_high_low(wave)
            high_ref[levels * r : levels * (r + 1), LANES * i : LANES * (i + 1)] = part_high
            low_ref[levels * r : levels * (r + 1), LANES * i : LANES * (i + 1)] = part_low

    def both_ways(begin, size, table_high, table_low):
        count = rows * levels

        def product(part_high, part_low, dims):
            stacked = jnp.concatenate([part_high, part_low], axis=0)
            main = lax.dot_general(stacked, table_high, dims, preferred_element_type=jnp.float32)
            rest = lax.dot_general(part_high, table_low, dims, preferred_element_type=jnp.float32)
            return main[:count] + (main[count:] + rest)

        spectrum = product(high_ref[:, begin : begin + size], low_ref[:, begin : begin + size], (((1,), (0,)), ((), ())))
        scaled = jnp.concatenate(
            [spectrum[levels * r : levels * (r + 1)] * scale_ref[r : r + 1, begin : begin + size] for r in range(rows)], axis=0
        )
        wave_ref[:, begin : begin + size] = product(*split_high_low(scaled), DOT_LAST)

    both_ways(0, LANES, first_high_ref[...], first_low_ref[...])
    for k in range(pairs):
        both_ways(
            LANES * (2 * k + 1), 2 * LANES,
            table_high_ref[2 * LANES * k : 2 * LANES * (k + 1), :], table_low_ref[2 * LANES * k : 2 * LANES * (k + 1), :],
        )

    for r in range(rows):
        waves = [wave_ref[levels * r : levels * (r + 1), LANES * i : LANES * (i + 1)] for i in range(radix)]
        filtered_row = mask_ref[r] == 1
        for n in range(own_segments):
            value = waves[0]
            for k in range(1, pairs + 1):
                value = value + cosine(k, n) * waves[2 * k - 1]
                if n:
                    value = value - sine(k, n) * waves[2 * k]
            begin = LANES * n
            size = min(LANES, sector - begin)
            value = jnp.where(filtered_row, value, own_ref[r, :, begin : begin + LANES])
            out_ref[0, :, r, begin : begin + size] = value[:, :size]


def vmem(shape, index=None):
    index = index or (0,) * len(shape)
    return pl.BlockSpec(shape, lambda i: index)


def on_device(tracers, courant_lat, courant_lon, surface_flux, mixing, decay_rate, owners, polar_mask):
    tracer_count, levels, rows, sector = tracers.shape
    assert rows == 4 and sector % 64 == 0 and lax.axis_size("lon") == 2
    f32 = jnp.float32
    lat_count, lat = lax.axis_size("lat"), lax.axis_index("lat")
    length = 2 * sector
    width = -(-sector // LANES) * LANES
    radix = length // LANES
    upward = [(i, i + 1) for i in range(lat_count - 1)]
    downward = [(i + 1, i) for i in range(lat_count - 1)]
    swap = [(0, 1), (1, 0)]

    from_south, from_north = [], []
    for t in range(tracer_count):
        with_courant = t == 0
        down_rows = levels + (levels // 2 if with_courant else 0)
        up, down = pl.pallas_call(
            functools.partial(pack_kernel, rows, levels, with_courant),
            grid=(1,),
            in_specs=[vmem((1, levels, rows, sector), (t, 0, 0, 0))]
            + ([vmem((levels, rows, sector))] if with_courant else []),
            out_specs=[vmem((levels, length)), vmem((down_rows, length))],
            out_shape=[jax.ShapeDtypeStruct((levels, length), f32), jax.ShapeDtypeStruct((down_rows, length), f32)],
            compiler_params=params(),
            cost_estimate=cost(0, 600_000),
            name="pack",
        )(tracers, *([courant_lat] if with_courant else []))
        from_south.append(lax.ppermute(up, "lat", upward))
        from_north.append(lax.ppermute(down, "lat", downward))

    by_row = jnp.transpose(tracers, (0, 2, 1, 3))
    lon_by_row = jnp.transpose(courant_lon, (1, 0, 2))
    lat_by_row = jnp.transpose(courant_lat, (1, 0, 2))
    ends = jnp.concatenate([by_row[..., -2:], by_row[..., :2]], axis=-1)
    lon_end = jnp.pad(lon_by_row[..., :1], ((0, 0), (0, 0), (0, 3)))
    sides = lax.ppermute(jnp.concatenate([ends, lon_end[None]], axis=0), "lon", swap)
    gap = width - sector - 4
    padded = jnp.concatenate(
        [by_row, sides[:tracer_count, ..., 2:], jnp.zeros((tracer_count, rows, levels, gap), f32), sides[:tracer_count, ..., :2]],
        axis=-1,
    )
    east_courant = jnp.concatenate(
        [lon_by_row, sides[tracer_count, ..., :1], jnp.zeros((rows, levels, width - sector - 1), f32)], axis=-1
    )
    not_pole = jnp.where((lat > 0) | (jnp.arange(rows) > 0), 1.0, 0.0)
    lat_courant = jnp.pad(lat_by_row * not_pole[:, None, None], ((0, 0), (0, 0), (0, width - sector)))
    base = pl.pallas_call(
        functools.partial(base_kernel, rows, width),
        grid=(tracer_count,),
        in_specs=[
            pl.BlockSpec((1, rows, levels, width), lambda t: (t, 0, 0, 0)),
            vmem((rows, levels, width)),
            vmem((rows, levels, width)),
        ],
        out_specs=pl.BlockSpec((1, rows, levels, width), lambda t: (t, 0, 0, 0)),
        out_shape=jax.ShapeDtypeStruct((tracer_count, rows, levels, width), f32),
        compiler_params=params(),
        cost_estimate=cost(0, 3_000_000),
        name="base",
    )(padded, east_courant, lat_courant)

    surface = jnp.pad(surface_flux, ((0, 0), (0, 0), (0, width - sector)))
    decay = decay_rate[:, :, None]
    block_count = rows * sector // BLOCK
    block_of = (np.arange(rows)[:, None] * sector + np.minimum(np.arange(width), sector - 1)[None]) // BLOCK
    owner_of = jnp.repeat(owners.reshape(block_count), BLOCK).reshape(rows, sector)
    owner_of = jnp.pad(owner_of, ((0, 0), (0, width - sector)))
    first, others, numbers, weights = spectral_tables(length)
    first_high, first_low = split_table(first)
    others_high, others_low = split_table(others)
    row_ids = (lat * rows + jnp.arange(rows)).astype(f32)
    latitude = (-0.5 + (row_ids + 0.5) / (lat_count * rows)) * math.pi
    inverse_sine = np.where(numbers == 0, 1.0, 1.0 / np.where(numbers == 0, 1.0, np.sin(np.pi * numbers / length)))
    ratio = 2.0 * jnp.cos(latitude)[:, None] * jnp.asarray(inverse_sine, f32)[None]
    damping = jnp.where(jnp.asarray(numbers == 0)[None], 1.0, jnp.minimum(1.0, ratio * ratio))
    scale = damping * jnp.asarray(weights, f32)[None]

    top_packed = from_north[0][levels:]
    top = jnp.concatenate([top_packed[:, :sector], top_packed[:, sector:]], axis=0)
    top = jnp.pad(top, ((0, 0), (0, width - sector)))

    energy = jnp.zeros((rows, 8, width), f32)
    own_parts, other_parts = [], []
    for t in range(tracer_count):
        last = t == tracer_count - 1
        energy_shape = (1, LANES) if last else (rows, 8, width)
        down_rows = from_north[t].shape[0]
        physics, energy = pl.pallas_call(
            functools.partial(physics_kernel, rows, levels, sector, lat_count if last else 0),
            grid=(1,),
            in_specs=([vmem((rows, width))] if last else [])
            + [
                vmem((1, rows, levels, width), (t, 0, 0, 0)),
                vmem((1, rows, levels, width), (t, 0, 0, 0)),
                vmem((levels, length)),
                vmem((down_rows, length)),
                vmem((rows, levels, width)),
                vmem((levels, width)),
                vmem((1, rows, width), (t, 0, 0)),
                vmem((levels, levels)),
                vmem((1, levels, 1), (t, 0, 0)),
                vmem((rows, 8, width)),
            ],
            out_specs=[vmem((rows, levels, width)), vmem(energy_shape)],
            out_shape=[jax.ShapeDtypeStruct((rows, levels, width), f32), jax.ShapeDtypeStruct(energy_shape, f32)],
            compiler_params=params(),
            cost_estimate=cost(50_000_000, 2_000_000),
            name="physics",
        )(
            *([owner_of] if last else []),
            base, padded, from_south[t], from_north[t], lat_courant, top, surface, mixing, decay, energy,
        )
        own_parts.append(physics)
        other_parts.append(lax.ppermute(physics, "lon", swap))

    out = None
    tables = (others_high, others_low, first_high, first_low)
    for t in range(tracer_count):
        has_alias = int(out is not None)
        out = pl.pallas_call(
            functools.partial(filter_kernel, rows, levels, sector, radix, has_alias),
            grid=(1,),
            in_specs=[
                pl.BlockSpec(memory_space=pltpu.SMEM),
                vmem((rows, levels, width)),
                vmem((rows, levels, width)),
                vmem(others_high.shape),
                vmem(others_low.shape),
                vmem(first_high.shape),
                vmem(first_low.shape),
                vmem((rows, length)),
            ]
            + [pl.BlockSpec(memory_space=pl.ANY)] * has_alias,
            out_specs=vmem((1, levels, rows, sector), (t, 0, 0, 0)),
            out_shape=jax.ShapeDtypeStruct(tracers.shape, f32),
            scratch_shapes=[
                pltpu.VMEM((rows * levels, length), jnp.bfloat16),
                pltpu.VMEM((rows * levels, length), jnp.bfloat16),
                pltpu.VMEM((rows * levels, length), f32),
            ],
            input_output_aliases={8: 0} if has_alias else {},
            compiler_params=params(),
            cost_estimate=cost(450_000_000, 3_000_000),
            name="filter",
        )(polar_mask, own_parts[t], other_parts[t], *(jnp.asarray(table) for table in tables), scale, *([out] if has_alias else []))

    step = 1
    while step < lat_count:
        energy = energy + lax.ppermute(energy, "lat", [(i, i ^ step) for i in range(lat_count)])
        step *= 2
    owner_energy = lax.dynamic_slice(energy, (0, lat), (1, 1)) / (block_count * BLOCK)
    return out, owner_energy


def solution(mesh):
    placed = (
        P("group", None, "lat", "lon"),
        P("group", "lat", "lon"),
        P("group", "lat", "lon"),
        P("group", "lat", "lon"),
        P(),
        P(),
        P(("group", "lat"), "lon", None, None),
        P(("group", "lat")),
    )
    return jax.shard_map(
        on_device,
        mesh=mesh,
        in_specs=placed,
        out_specs=(P("group", None, "lat", "lon"), P(("group", "lat"), "lon")),
        check_vma=False,
    )
```

```python
import functools
import math

import jax
import jax.numpy as jnp
import numpy as np
from jax import lax
from jax.experimental import pallas as pl
from jax.experimental.pallas import tpu as pltpu
from jax.sharding import PartitionSpec as P

LANES = 128
BLOCK = 128
VMEM_BYTES = 24 * 1024 * 1024
NEAR = 7.0 / 12.0
FAR = 1.0 / 12.0


def params():
    return pltpu.CompilerParams(vmem_limit_bytes=VMEM_BYTES)


def cost(flops, bytes_accessed):
    return pl.CostEstimate(flops=flops, bytes_accessed=bytes_accessed, transcendentals=0)


def split_high_low(value):
    high = value.astype(jnp.bfloat16)
    low = (value - high.astype(jnp.float32)).astype(jnp.bfloat16)
    return high, low


def split_table(table):
    high = table.astype(jnp.bfloat16.dtype)
    low = (table - high.astype(np.float64)).astype(jnp.bfloat16.dtype)
    return high, low


def spectral_tables(length):
    radix = length // LANES
    pairs = (radix - 1) // 2
    spot = np.arange(LANES)[:, None]
    number = np.arange(LANES)[None, :]
    is_cosine = number <= LANES // 2
    wave = np.where(is_cosine, number, number - LANES // 2)
    angle = 2.0 * np.pi * ((spot * wave) % LANES) / LANES
    first = np.where(is_cosine, np.cos(angle), np.sin(angle))
    others, numbers = [], [radix * wave[0]]
    weights = [np.where((wave[0] == 0) | (wave[0] == LANES // 2), 1.0, 2.0) / length]
    for residue in range(1, pairs + 1):
        whole = residue + radix * number
        angle = 2.0 * np.pi * ((spot * whole) % length) / length
        cosine, sine = np.cos(angle), np.sin(angle)
        others.append(np.block([[cosine, -sine], [sine, cosine]]))
        folded = np.minimum(whole[0], length - whole[0])
        numbers += [folded, folded]
        weights.append(np.full(2 * LANES, 2.0 / length))
    others += [table.T for table in others]
    return np.concatenate([first, first.T]), np.concatenate(others), np.concatenate(numbers), np.concatenate(weights)


def pack_rows(first, second):
    return jnp.concatenate([first, second], axis=1)


def second_half(packed, sector):
    skip, shift = sector // LANES, sector % LANES
    segments = [packed[:, LANES * i : LANES * (i + 1)] for i in range(packed.shape[1] // LANES)]
    if shift == 0:
        return jnp.concatenate(segments[skip:], axis=1)
    turned = [pltpu.roll(segment, LANES - shift, 1) for segment in segments[skip:]]
    lane = lax.broadcasted_iota(jnp.int32, turned[0].shape, 1)
    parts = [jnp.where(lane < LANES - shift, turned[i], turned[min(i + 1, len(turned) - 1)]) for i in range(len(turned))]
    return jnp.concatenate(parts, axis=1)


def pack_kernel(rows, levels, split, tracer_ref, courant_ref, *out_refs):
    up_refs, down_refs = out_refs[: len(split)], out_refs[len(split) :]
    for chunk, (begin, end) in enumerate(split):
        for t in range(begin, end):
            place = slice(levels * (t - begin), levels * (t - begin + 1))
            up_refs[chunk][place, :] = pack_rows(tracer_ref[t, :, rows - 2, :], tracer_ref[t, :, rows - 1, :])
            down_refs[chunk][place, :] = pack_rows(tracer_ref[t, :, 0, :], tracer_ref[t, :, 1, :])
    courant = courant_ref[:, 0, :]
    place = levels * (split[0][1] - split[0][0])
    down_refs[0][place : place + levels // 2, :] = pack_rows(courant[: levels // 2], courant[levels // 2 :])


def base_kernel(rows, width, padded_ref, east_courant_ref, lat_courant_ref, base_ref):
    q = [padded_ref[0, r] for r in range(rows)]
    own_flux = [None] * (rows + 1)
    own_flux[0] = lat_courant_ref[0] * (NEAR * q[0] - FAR * q[1])
    own_flux[1] = lat_courant_ref[1] * (NEAR * (q[1] + q[0]) - FAR * q[2])
    own_flux[2] = lat_courant_ref[2] * (NEAR * (q[2] + q[1]) - FAR * (q[3] + q[0]))
    own_flux[3] = lat_courant_ref[3] * (NEAR * (q[3] + q[2]) - FAR * q[1])
    for r in range(rows):
        west, west2, east = pltpu.roll(q[r], 1, 1), pltpu.roll(q[r], 2, 1), pltpu.roll(q[r], width - 1, 1)
        flux = east_courant_ref[r] * (NEAR * (q[r] + west) - FAR * (east + west2))
        value = q[r] - (pltpu.roll(flux, width - 1, 1) - flux) + own_flux[r]
        if r + 1 < rows:
            value = value - own_flux[r + 1]
        base_ref[0, r] = value


def physics_kernel(rows, levels, sector, owner_count, *refs):
    if owner_count:
        owner_ref, refs = refs[0], refs[1:]
    (base_ref, padded_ref, low_ref, high_ref, courant_ref, top_ref, surface_ref, mixing_ref, decay_ref, energy_in_ref,
     physics_ref, energy_ref) = refs
    width = base_ref.shape[-1]
    low = low_ref[...]
    high = high_ref[...]
    step = pl.program_id(0)
    low_a, low_b = low[:, :width], second_half(low, sector)
    high_a, high_b = high[:, :width], second_half(high, sector)
    courant = [courant_ref[r] for r in range(rows)]
    south = courant[0] * (NEAR * low_b - FAR * low_a)
    south_in = courant[1] * (FAR * low_b)
    north_in = courant[3] * (FAR * high_a)
    north = top_ref[...] * (NEAR * (high_a + padded_ref[0, 3]) - FAR * (high_b + padded_ref[0, 2]))
    extra = [south + south_in, -south_in, north_in, -north_in - north]
    mix_high, mix_low = split_high_low(mixing_ref[...])
    mix = jnp.concatenate([mix_high, mix_high, mix_low, mix_low], axis=1)
    decay = decay_ref[0]
    level = lax.broadcasted_iota(jnp.int32, (levels, width), 0)
    lane = lax.broadcasted_iota(jnp.int32, (levels, width), 1)
    energies = []
    for r in range(rows):
        advected = base_ref[0, r] + extra[r]
        part_high, part_low = split_high_low(advected)
        stacked = jnp.concatenate([part_high, part_low, part_high, part_low], axis=0)
        mixed = jnp.dot(mix, stacked, preferred_element_type=jnp.float32)
        mixed = jnp.where(level == levels - 1, mixed + surface_ref[0, r : r + 1, :], mixed)
        physics = mixed / (1.0 + decay * mixed * mixed)
        physics_ref[0, r] = physics
        gap = jnp.where(lane < sector, physics - advected, 0.0)
        squared = gap * gap
        total = energy_in_ref[r] if owner_count else jnp.where(step == 0, energy_in_ref[r], energy_ref[r])
        for k in range(levels // 8):
            total = total + squared[8 * k : 8 * k + 8]
        energies.append(total)
    if not owner_count:
        for r in range(rows):
            energy_ref[r] = energies[r]
        return
    for owner in range(owner_count):
        chosen = jnp.zeros((8, LANES), jnp.float32)
        for r in range(rows):
            picked = jnp.where(owner_ref[r : r + 1, :] == owner, energies[r], 0.0)
            for k in range(width // LANES):
                chosen = chosen + picked[:, LANES * k : LANES * (k + 1)]
        energy_ref[owner : owner + 1, :] = jnp.sum(chosen, axis=0, keepdims=True)


def filter_kernel(rows, levels, sector, radix, has_alias, *refs):
    mask_ref, own_ref, other_ref, table_high_ref, table_low_ref, first_high_ref, first_low_ref, scale_ref = refs[:8]
    out_ref, high_ref, low_ref, wave_ref = refs[8 + has_alias :]
    own_ref, other_ref = own_ref.at[0], other_ref.at[0]
    pairs = (radix - 1) // 2
    shift = sector % LANES
    own_segments = -(-sector // LANES)
    lane = lax.broadcasted_iota(jnp.int32, (levels, LANES), 1)
    cosine = lambda k, i: math.cos(2.0 * math.pi * ((k * i) % radix) / radix)
    sine = lambda k, i: math.sin(2.0 * math.pi * ((k * i) % radix) / radix)

    for r in range(rows):
        own = [own_ref[r, :, LANES * i : LANES * (i + 1)] for i in range(own_segments)]
        turned = [pltpu.roll(other_ref[r, :, LANES * i : LANES * (i + 1)], shift, 1) for i in range(own_segments)]
        joined = own[:-1] + [jnp.where(lane < shift, own[-1], turned[0])]
        joined += [jnp.where(lane < shift, turned[i], turned[i + 1]) for i in range(own_segments - 1)]
        plus = [joined[i] + joined[radix - i] for i in range(1, pairs + 1)]
        minus = [joined[radix - i] - joined[i] for i in range(1, pairs + 1)]
        waves = [sum(plus, joined[0])]
        for k in range(1, pairs + 1):
            waves.append(sum((cosine(k, i) * plus[i - 1] for i in range(1, pairs + 1)), joined[0]))
            waves.append(sum(sine(k, i) * minus[i - 1] for i in range(1, pairs + 1)))
        for i, wave in enumerate(waves):
            part_high, part_low = split_high_low(wave)
            high_ref[levels * r : levels * (r + 1), LANES * i : LANES * (i + 1)] = part_high
            low_ref[levels * r : levels * (r + 1), LANES * i : LANES * (i + 1)] = part_low

    def both_ways(begin, size, forward, inverse):
        count = rows * levels

        def product(part_high, part_low, table_high, table_low):
            stacked = jnp.concatenate([part_high, part_low], axis=0)
            main = jnp.dot(stacked, table_high, preferred_element_type=jnp.float32)
            rest = jnp.dot(part_high, table_low, preferred_element_type=jnp.float32)
            return main[:count] + (main[count:] + rest)

        spectrum = product(high_ref[:, begin : begin + size], low_ref[:, begin : begin + size], *forward)
        scaled = jnp.concatenate(
            [spectrum[levels * r : levels * (r + 1)] * scale_ref[r : r + 1, begin : begin + size] for r in range(rows)], axis=0
        )
        wave_ref[:, begin : begin + size] = product(*split_high_low(scaled), *inverse)

    def pair_of(high, low, begin, size):
        return high[begin : begin + size, :], low[begin : begin + size, :]

    both_ways(0, LANES, *(pair_of(first_high_ref, first_low_ref, LANES * i, LANES) for i in range(2)))
    for k in range(pairs):
        both_ways(
            LANES * (2 * k + 1), 2 * LANES,
            *(pair_of(table_high_ref, table_low_ref, 2 * LANES * (k + pairs * i), 2 * LANES) for i in range(2)),
        )

    for r in range(rows):
        waves = [wave_ref[levels * r : levels * (r + 1), LANES * i : LANES * (i + 1)] for i in range(radix)]
        filtered_row = mask_ref[r] == 1
        for n in range(own_segments):
            value = waves[0]
            for k in range(1, pairs + 1):
                value = value + cosine(k, n) * waves[2 * k - 1]
                if n:
                    value = value - sine(k, n) * waves[2 * k]
            begin = LANES * n
            size = min(LANES, sector - begin)
            value = jnp.where(filtered_row, value, own_ref[r, :, begin : begin + LANES])
            out_ref[0, :, r, begin : begin + size] = value[:, :size]


def vmem(shape, index=None):
    index = index or (0,) * len(shape)
    return pl.BlockSpec(shape, lambda i: index)


def on_device(tracers, courant_lat, courant_lon, surface_flux, mixing, decay_rate, owners, polar_mask):
    tracer_count, levels, rows, sector = tracers.shape
    assert rows == 4 and sector % 64 == 0 and lax.axis_size("lon") == 2
    f32 = jnp.float32
    lat_count, lat = lax.axis_size("lat"), lax.axis_index("lat")
    length = 2 * sector
    width = -(-sector // LANES) * LANES
    radix = length // LANES
    upward = [(i, i + 1) for i in range(lat_count - 1)]
    downward = [(i + 1, i) for i in range(lat_count - 1)]
    swap = [(0, 1), (1, 0)]

    split = [(0, tracer_count - 1), (tracer_count - 1, tracer_count)]
    up_rows = [levels * (end - begin) for begin, end in split]
    down_rows = [up_rows[0] + levels // 2] + up_rows[1:]
    packed_shapes = [(count, length) for count in up_rows + down_rows]
    packed = pl.pallas_call(
        functools.partial(pack_kernel, rows, levels, split),
        grid=(1,),
        in_specs=[vmem(tracers.shape), vmem(courant_lat.shape)],
        out_specs=[vmem(shape) for shape in packed_shapes],
        out_shape=[jax.ShapeDtypeStruct(shape, f32) for shape in packed_shapes],
        compiler_params=params(),
        cost_estimate=cost(0, 600_000),
        name="pack",
    )(tracers, courant_lat)
    up, down = packed[: len(split)], packed[len(split) :]
    from_south = [lax.ppermute(up[0], "lat", upward)]
    from_north = [lax.ppermute(down[0], "lat", downward)]
    tracers, courant_lat, courant_lon, up, down = lax.optimization_barrier((tracers, courant_lat, courant_lon, up, down))

    by_row = jnp.transpose(tracers, (0, 2, 1, 3))
    lon_by_row = jnp.transpose(courant_lon, (1, 0, 2))
    lat_by_row = jnp.transpose(courant_lat, (1, 0, 2))
    ends = jnp.concatenate([by_row[..., -2:], by_row[..., :2]], axis=-1)
    lon_end = jnp.pad(lon_by_row[..., :1], ((0, 0), (0, 0), (0, 3)))
    sides = lax.ppermute(jnp.concatenate([ends, lon_end[None]], axis=0), "lon", swap)
    gap = jnp.zeros((tracer_count, rows, levels, width - sector - 4), f32)
    padded = jnp.concatenate([by_row, sides[:tracer_count, ..., 2:], gap, sides[:tracer_count, ..., :2]], axis=-1)
    east_courant = jnp.concatenate(
        [lon_by_row, sides[tracer_count, ..., :1], jnp.zeros((rows, levels, width - sector - 1), f32)], axis=-1
    )
    not_pole = jnp.where((lat > 0) | (jnp.arange(rows) > 0), 1.0, 0.0)
    lat_courant = jnp.pad(lat_by_row * not_pole[:, None, None], ((0, 0), (0, 0), (0, width - sector)))
    base = pl.pallas_call(
        functools.partial(base_kernel, rows, width),
        grid=(tracer_count,),
        in_specs=[
            pl.BlockSpec((1, rows, levels, width), lambda t: (t, 0, 0, 0)),
            vmem((rows, levels, width)),
            vmem((rows, levels, width)),
        ],
        out_specs=pl.BlockSpec((1, rows, levels, width), lambda t: (t, 0, 0, 0)),
        out_shape=jax.ShapeDtypeStruct((tracer_count, rows, levels, width), f32),
        compiler_params=params(),
        cost_estimate=cost(0, 3_000_000),
        name="base",
    )(padded, east_courant, lat_courant)

    surface = jnp.pad(surface_flux, ((0, 0), (0, 0), (0, width - sector)))
    decay = decay_rate[:, :, None]
    block_count = rows * sector // BLOCK
    block_of = (np.arange(rows)[:, None] * sector + np.minimum(np.arange(width), sector - 1)[None]) // BLOCK
    owner_of = jnp.repeat(owners.reshape(block_count), BLOCK).reshape(rows, sector)
    owner_of = jnp.pad(owner_of, ((0, 0), (0, width - sector)))
    first, others, numbers, weights = spectral_tables(length)
    first_high, first_low = split_table(first)
    others_high, others_low = split_table(others)
    row_ids = (lat * rows + jnp.arange(rows)).astype(f32)
    latitude = (-0.5 + (row_ids + 0.5) / (lat_count * rows)) * math.pi
    inverse_sine = np.where(numbers == 0, 1.0, 1.0 / np.where(numbers == 0, 1.0, np.sin(np.pi * numbers / length)))
    ratio = 2.0 * jnp.cos(latitude)[:, None] * jnp.asarray(inverse_sine, f32)[None]
    damping = jnp.where(jnp.asarray(numbers == 0)[None], 1.0, jnp.minimum(1.0, ratio * ratio))
    scale = damping * jnp.asarray(weights, f32)[None]

    base, scale, surface, decay, owner_of, up, down = lax.optimization_barrier((base, scale, surface, decay, owner_of, up, down))
    from_south.append(lax.ppermute(up[1], "lat", upward))
    from_north.append(lax.ppermute(down[1], "lat", downward))
    top_packed = from_north[0][up_rows[0] :]
    top = jnp.concatenate([top_packed[:, :sector], top_packed[:, sector:]], axis=0)
    top = jnp.pad(top, ((0, 0), (0, width - sector)))

    energy = jnp.zeros((rows, 8, width), f32)
    out = None
    tables = (others_high, others_low, first_high, first_low)
    for chunk, (begin, end) in enumerate(split):
        last = chunk == len(split) - 1
        energy_shape = (lat_count, LANES) if last else (rows, 8, width)
        block = (1, rows, levels, width)
        physics, energy = pl.pallas_call(
            functools.partial(physics_kernel, rows, levels, sector, lat_count if last else 0),
            grid=(end - begin,),
            in_specs=([vmem((rows, width))] if last else [])
            + [
                pl.BlockSpec(block, lambda i, begin=begin: (begin + i, 0, 0, 0)),
                pl.BlockSpec(block, lambda i, begin=begin: (begin + i, 0, 0, 0)),
                pl.BlockSpec((levels, length), lambda i: (i, 0)),
                pl.BlockSpec((levels, length), lambda i: (i, 0)),
                vmem((rows, levels, width)),
                vmem((levels, width)),
                pl.BlockSpec((1, rows, width), lambda i, begin=begin: (begin + i, 0, 0)),
                vmem((levels, levels)),
                pl.BlockSpec((1, levels, 1), lambda i, begin=begin: (begin + i, 0, 0)),
                vmem((rows, 8, width)),
            ],
            out_specs=[pl.BlockSpec(block, lambda i: (i, 0, 0, 0)), vmem(energy_shape)],
            out_shape=[jax.ShapeDtypeStruct((end - begin,) + block[1:], f32), jax.ShapeDtypeStruct(energy_shape, f32)],
            compiler_params=params(),
            cost_estimate=cost(50_000_000, 2_000_000),
            name="physics",
        )(
            *([owner_of] if last else []),
            base, padded, from_south[chunk], from_north[chunk], lat_courant, top, surface, mixing, decay, energy,
        )
        other = lax.ppermute(physics, "lon", swap)
        if last:
            owner_parts = lax.all_to_all(energy, "lat", 0, 0, tiled=True)
        has_alias = int(out is not None)
        out = pl.pallas_call(
            functools.partial(filter_kernel, rows, levels, sector, radix, has_alias),
            grid=(end - begin,),
            in_specs=[
                pl.BlockSpec(memory_space=pltpu.SMEM),
                pl.BlockSpec(block, lambda i: (i, 0, 0, 0)),
                pl.BlockSpec(block, lambda i: (i, 0, 0, 0)),
            ]
            + [vmem(table.shape) for table in tables]
            + [vmem((rows, length))]
            + [pl.BlockSpec(memory_space=pl.ANY)] * has_alias,
            out_specs=pl.BlockSpec((1, levels, rows, sector), lambda i, begin=begin: (begin + i, 0, 0, 0)),
            out_shape=jax.ShapeDtypeStruct((tracer_count, levels, rows, sector), f32),
            scratch_shapes=[
                pltpu.VMEM((rows * levels, length), jnp.bfloat16),
                pltpu.VMEM((rows * levels, length), jnp.bfloat16),
                pltpu.VMEM((rows * levels, length), f32),
            ],
            input_output_aliases={8: 0} if has_alias else {},
            compiler_params=params(),
            cost_estimate=cost(450_000_000, 3_000_000),
            name="filter",
        )(polar_mask, physics, other, *(jnp.asarray(table) for table in tables), scale, *([out] if has_alias else []))
        if not last:
            energy, out = lax.optimization_barrier((energy, out))

    owner_energy = jnp.sum(owner_parts).reshape(1, 1) / (block_count * BLOCK)
    return out, owner_energy


def solution(mesh):
    placed = (
        P("group", None, "lat", "lon"),
        P("group", "lat", "lon"),
        P("group", "lat", "lon"),
        P("group", "lat", "lon"),
        P(),
        P(),
        P(("group", "lat"), "lon", None, None),
        P(("group", "lat")),
    )
    return jax.shard_map(
        on_device,
        mesh=mesh,
        in_specs=placed,
        out_specs=(P("group", None, "lat", "lon"), P(("group", "lat"), "lon")),
        check_vma=False,
    )
```

```python
import functools
import math

import jax
import jax.numpy as jnp
import numpy as np
from jax import lax
from jax.experimental import pallas as pl
from jax.experimental.pallas import tpu as pltpu
from jax.sharding import PartitionSpec as P

LANES = 128
BLOCK = 128
VMEM_BYTES = 12 * 1024 * 1024
NEAR = 7.0 / 12.0
FAR = 1.0 / 12.0


def params():
    return pltpu.CompilerParams(vmem_limit_bytes=VMEM_BYTES)


def cost(flops, bytes_accessed):
    return pl.CostEstimate(flops=flops, bytes_accessed=bytes_accessed, transcendentals=0)


def split_high_low(value):
    high = value.astype(jnp.bfloat16)
    low = (value - high.astype(jnp.float32)).astype(jnp.bfloat16)
    return high, low


def split_table(table):
    high = table.astype(jnp.bfloat16.dtype)
    low = (table - high.astype(np.float64)).astype(jnp.bfloat16.dtype)
    return high, low


def spectral_tables(length):
    radix = length // LANES
    pairs = (radix - 1) // 2
    spot = np.arange(LANES)[:, None]
    number = np.arange(LANES)[None, :]
    is_cosine = number <= LANES // 2
    wave = np.where(is_cosine, number, number - LANES // 2)
    angle = 2.0 * np.pi * ((spot * wave) % LANES) / LANES
    first = np.where(is_cosine, np.cos(angle), np.sin(angle))
    others, numbers = [], [radix * wave[0]]
    weights = [np.where((wave[0] == 0) | (wave[0] == LANES // 2), 1.0, 2.0) / length]
    for residue in range(1, pairs + 1):
        whole = residue + radix * number
        angle = 2.0 * np.pi * ((spot * whole) % length) / length
        cosine, sine = np.cos(angle), np.sin(angle)
        others.append(np.block([[cosine, -sine], [sine, cosine]]))
        folded = np.minimum(whole[0], length - whole[0])
        numbers += [folded, folded]
        weights.append(np.full(2 * LANES, 2.0 / length))
    others += [table.T for table in others]
    return np.concatenate([first, first.T]), np.concatenate(others), np.concatenate(numbers), np.concatenate(weights)


def pack_rows(first, second):
    return jnp.concatenate([first, second], axis=1)


def second_half(packed, sector):
    skip, shift = sector // LANES, sector % LANES
    segments = [packed[:, LANES * i : LANES * (i + 1)] for i in range(packed.shape[1] // LANES)]
    if shift == 0:
        return jnp.concatenate(segments[skip:], axis=1)
    turned = [pltpu.roll(segment, LANES - shift, 1) for segment in segments[skip:]]
    lane = lax.broadcasted_iota(jnp.int32, turned[0].shape, 1)
    parts = [jnp.where(lane < LANES - shift, turned[i], turned[min(i + 1, len(turned) - 1)]) for i in range(len(turned))]
    return jnp.concatenate(parts, axis=1)


def pack_kernel(tracer_count, rows, levels, tracer_hbm, courant_hbm, up_ref, down_ref, tracer_ref, courant_ref, sems):
    copies = [pltpu.make_async_copy(tracer_hbm.at[t], tracer_ref.at[t], sems.at[t]) for t in range(tracer_count)]
    copies.append(pltpu.make_async_copy(courant_hbm, courant_ref, sems.at[tracer_count]))
    for copy in copies:
        copy.start()
    for t in range(tracer_count):
        copies[t].wait()
        place = slice(levels * t, levels * (t + 1))
        up_ref[place, :] = pack_rows(tracer_ref[t, :, rows - 2, :], tracer_ref[t, :, rows - 1, :])
        down_ref[place, :] = pack_rows(tracer_ref[t, :, 0, :], tracer_ref[t, :, 1, :])
    copies[tracer_count].wait()
    courant = courant_ref[:, 0, :]
    down_ref[levels * tracer_count :, :] = pack_rows(courant[: levels // 2], courant[levels // 2 :])


def base_kernel(rows, width, padded_ref, east_courant_ref, lat_courant_ref, base_ref):
    q = [padded_ref[0, r] for r in range(rows)]
    own_flux = [None] * (rows + 1)
    own_flux[0] = lat_courant_ref[0] * (NEAR * q[0] - FAR * q[1])
    own_flux[1] = lat_courant_ref[1] * (NEAR * (q[1] + q[0]) - FAR * q[2])
    own_flux[2] = lat_courant_ref[2] * (NEAR * (q[2] + q[1]) - FAR * (q[3] + q[0]))
    own_flux[3] = lat_courant_ref[3] * (NEAR * (q[3] + q[2]) - FAR * q[1])
    for r in range(rows):
        west, west2, east = pltpu.roll(q[r], 1, 1), pltpu.roll(q[r], 2, 1), pltpu.roll(q[r], width - 1, 1)
        flux = east_courant_ref[r] * (NEAR * (q[r] + west) - FAR * (east + west2))
        value = q[r] - (pltpu.roll(flux, width - 1, 1) - flux) + own_flux[r]
        if r + 1 < rows:
            value = value - own_flux[r + 1]
        base_ref[0, r] = value


def physics_kernel(groups, rows, levels, sector, owner_count, *refs):
    (owner_ref, base_ref, padded_ref, low_ref, high_ref, courant_ref, surface_ref, mixing_ref, decay_ref) = refs[:9]
    physics_refs, energy_ref = refs[9:-1], refs[-1]
    width = base_ref.shape[-1]
    tracer_count = base_ref.shape[0]
    courant = [courant_ref[r] for r in range(rows)]
    top = high_ref[levels * tracer_count :, :]
    top = jnp.concatenate([top[:, :width], second_half(top, sector)], axis=0)
    mix_high, mix_low = split_high_low(mixing_ref[...])
    mix = jnp.concatenate([mix_high, mix_high, mix_low, mix_low], axis=1)
    level = lax.broadcasted_iota(jnp.int32, (levels, width), 0)
    lane = lax.broadcasted_iota(jnp.int32, (levels, width), 1)
    energies = [None] * rows
    for physics_ref, (begin, end) in zip(physics_refs, groups):
        for t in range(begin, end):
            low = low_ref[levels * t : levels * (t + 1), :]
            high = high_ref[levels * t : levels * (t + 1), :]
            low_a, low_b = low[:, :width], second_half(low, sector)
            high_a, high_b = high[:, :width], second_half(high, sector)
            south = courant[0] * (NEAR * low_b - FAR * low_a)
            south_in = courant[1] * (FAR * low_b)
            north_in = courant[3] * (FAR * high_a)
            north = top * (NEAR * (high_a + padded_ref[t, 3]) - FAR * (high_b + padded_ref[t, 2]))
            extra = [south + south_in, -south_in, north_in, -north_in - north]
            for r in range(rows):
                advected = base_ref[t, r] + extra[r]
                part_high, part_low = split_high_low(advected)
                stacked = jnp.concatenate([part_high, part_low, part_high, part_low], axis=0)
                mixed = jnp.dot(mix, stacked, preferred_element_type=jnp.float32)
                mixed = jnp.where(level == levels - 1, mixed + surface_ref[t, r : r + 1, :], mixed)
                physics = mixed / (1.0 + decay_ref[t] * mixed * mixed)
                physics_ref[t - begin, r] = physics
                gap = physics - advected
                squared = gap * gap
                total = squared[0:8]
                for k in range(1, levels // 8):
                    total = total + squared[8 * k : 8 * k + 8]
                energies[r] = total if energies[r] is None else energies[r] + total
    energies = [jnp.where(lane[0:8] < sector, energy, 0.0) for energy in energies]
    for owner in range(owner_count):
        chosen = jnp.zeros((8, LANES), jnp.float32)
        for r in range(rows):
            picked = jnp.where(owner_ref[r : r + 1, :] == owner, energies[r], 0.0)
            for k in range(width // LANES):
                chosen = chosen + picked[:, LANES * k : LANES * (k + 1)]
        energy_ref[owner : owner + 1, :] = jnp.sum(chosen, axis=0, keepdims=True)


def filter_kernel(rows, levels, sector, radix, has_alias, *refs):
    mask_ref, own_ref, other_ref, table_high_ref, table_low_ref, first_high_ref, first_low_ref, scale_ref = refs[:8]
    out_ref, high_ref, low_ref, wave_ref = refs[8 + has_alias :]
    step = pl.program_id(0)
    own_ref, other_ref = own_ref.at[step], other_ref.at[step]
    pairs = (radix - 1) // 2
    shift = sector % LANES
    own_segments = -(-sector // LANES)
    lane = lax.broadcasted_iota(jnp.int32, (levels, LANES), 1)
    cosine = lambda k, i: math.cos(2.0 * math.pi * ((k * i) % radix) / radix)
    sine = lambda k, i: math.sin(2.0 * math.pi * ((k * i) % radix) / radix)

    for r in range(rows):
        own = [own_ref[r, :, LANES * i : LANES * (i + 1)] for i in range(own_segments)]
        turned = [pltpu.roll(other_ref[r, :, LANES * i : LANES * (i + 1)], shift, 1) for i in range(own_segments)]
        joined = own[:-1] + [jnp.where(lane < shift, own[-1], turned[0])]
        joined += [jnp.where(lane < shift, turned[i], turned[i + 1]) for i in range(own_segments - 1)]
        plus = [joined[i] + joined[radix - i] for i in range(1, pairs + 1)]
        minus = [joined[radix - i] - joined[i] for i in range(1, pairs + 1)]
        waves = [sum(plus, joined[0])]
        for k in range(1, pairs + 1):
            waves.append(sum((cosine(k, i) * plus[i - 1] for i in range(1, pairs + 1)), joined[0]))
            waves.append(sum(sine(k, i) * minus[i - 1] for i in range(1, pairs + 1)))
        for i, wave in enumerate(waves):
            part_high, part_low = split_high_low(wave)
            high_ref[levels * r : levels * (r + 1), LANES * i : LANES * (i + 1)] = part_high
            low_ref[levels * r : levels * (r + 1), LANES * i : LANES * (i + 1)] = part_low

    def both_ways(begin, size, forward, inverse):
        count = rows * levels

        def product(part_high, part_low, table_high, table_low):
            stacked = jnp.concatenate([part_high, part_low], axis=0)
            main = jnp.dot(stacked, table_high, preferred_element_type=jnp.float32)
            rest = jnp.dot(part_high, table_low, preferred_element_type=jnp.float32)
            return main[:count] + (main[count:] + rest)

        spectrum = product(high_ref[:, begin : begin + size], low_ref[:, begin : begin + size], *forward)
        scaled = jnp.concatenate(
            [spectrum[levels * r : levels * (r + 1)] * scale_ref[r : r + 1, begin : begin + size] for r in range(rows)], axis=0
        )
        wave_ref[:, begin : begin + size] = product(*split_high_low(scaled), *inverse)

    def pair_of(high, low, begin, size):
        return high[begin : begin + size, :], low[begin : begin + size, :]

    both_ways(0, LANES, *(pair_of(first_high_ref, first_low_ref, LANES * i, LANES) for i in range(2)))
    for k in range(pairs):
        both_ways(
            LANES * (2 * k + 1), 2 * LANES,
            *(pair_of(table_high_ref, table_low_ref, 2 * LANES * (k + pairs * i), 2 * LANES) for i in range(2)),
        )

    for r in range(rows):
        waves = [wave_ref[levels * r : levels * (r + 1), LANES * i : LANES * (i + 1)] for i in range(radix)]
        filtered_row = mask_ref[r] == 1
        for n in range(own_segments):
            value = waves[0]
            for k in range(1, pairs + 1):
                value = value + cosine(k, n) * waves[2 * k - 1]
                if n:
                    value = value - sine(k, n) * waves[2 * k]
            begin = LANES * n
            size = min(LANES, sector - begin)
            value = jnp.where(filtered_row, value, own_ref[r, :, begin : begin + LANES])
            out_ref[0, :, r, begin : begin + size] = value[:, :size]


def vmem(shape, index=None):
    index = index or (0,) * len(shape)
    return pl.BlockSpec(shape, lambda i: index)


def on_device(tracers, courant_lat, courant_lon, surface_flux, mixing, decay_rate, owners, polar_mask):
    tracer_count, levels, rows, sector = tracers.shape
    assert rows == 4 and sector % 64 == 0 and lax.axis_size("lon") == 2
    f32 = jnp.float32
    lat_count, lat = lax.axis_size("lat"), lax.axis_index("lat")
    length = 2 * sector
    width = -(-sector // LANES) * LANES
    radix = length // LANES
    upward = [(i, i + 1) for i in range(lat_count - 1)]
    downward = [(i + 1, i) for i in range(lat_count - 1)]
    swap = [(0, 1), (1, 0)]

    whole = pl.BlockSpec(memory_space=pltpu.VMEM)
    in_hbm = pl.BlockSpec(memory_space=pltpu.HBM)
    up_shape = (levels * tracer_count, length)
    down_shape = (levels * tracer_count + levels // 2, length)
    up, down = pl.pallas_call(
        functools.partial(pack_kernel, tracer_count, rows, levels),
        in_specs=[in_hbm, in_hbm],
        out_specs=[whole, whole],
        out_shape=[jax.ShapeDtypeStruct(up_shape, f32), jax.ShapeDtypeStruct(down_shape, f32)],
        scratch_shapes=[
            pltpu.VMEM(tracers.shape, f32),
            pltpu.VMEM(courant_lat.shape, f32),
            pltpu.SemaphoreType.DMA((tracer_count + 1,)),
        ],
        compiler_params=params(),
        cost_estimate=cost(0, 600_000),
        name="pack",
    )(tracers, courant_lat)
    from_south = lax.ppermute(up, "lat", upward)
    from_north = lax.ppermute(down, "lat", downward)
    tracers, courant_lat, courant_lon, up, down = lax.optimization_barrier((tracers, courant_lat, courant_lon, up, down))

    by_row = jnp.transpose(tracers, (0, 2, 1, 3))
    lon_by_row = jnp.transpose(courant_lon, (1, 0, 2))
    lat_by_row = jnp.transpose(courant_lat, (1, 0, 2))
    ends = jnp.concatenate([by_row[..., -2:], by_row[..., :2]], axis=-1)
    lon_end = jnp.pad(lon_by_row[..., :1], ((0, 0), (0, 0), (0, 3)))
    sides = lax.ppermute(jnp.concatenate([ends, lon_end[None]], axis=0), "lon", swap)
    gap = jnp.zeros((tracer_count, rows, levels, width - sector - 4), f32)
    padded = jnp.concatenate([by_row, sides[:tracer_count, ..., 2:], gap, sides[:tracer_count, ..., :2]], axis=-1)
    east_courant = jnp.concatenate(
        [lon_by_row, sides[tracer_count, ..., :1], jnp.zeros((rows, levels, width - sector - 1), f32)], axis=-1
    )
    not_pole = jnp.where((lat > 0) | (jnp.arange(rows) > 0), 1.0, 0.0)
    lat_courant = jnp.pad(lat_by_row * not_pole[:, None, None], ((0, 0), (0, 0), (0, width - sector)))
    base = pl.pallas_call(
        functools.partial(base_kernel, rows, width),
        grid=(tracer_count,),
        in_specs=[
            pl.BlockSpec((1, rows, levels, width), lambda t: (t, 0, 0, 0)),
            vmem((rows, levels, width)),
            vmem((rows, levels, width)),
        ],
        out_specs=pl.BlockSpec((1, rows, levels, width), lambda t: (t, 0, 0, 0)),
        out_shape=jax.ShapeDtypeStruct((tracer_count, rows, levels, width), f32),
        compiler_params=params(),
        cost_estimate=cost(0, 3_000_000),
        name="base",
    )(padded, east_courant, lat_courant)

    surface = jnp.pad(surface_flux, ((0, 0), (0, 0), (0, width - sector)))
    decay = decay_rate[:, :, None]
    block_count = rows * sector // BLOCK
    block_of = (np.arange(rows)[:, None] * sector + np.minimum(np.arange(width), sector - 1)[None]) // BLOCK
    owner_of = jnp.repeat(owners.reshape(block_count), BLOCK).reshape(rows, sector)
    owner_of = jnp.pad(owner_of, ((0, 0), (0, width - sector)))
    first, others, numbers, weights = spectral_tables(length)
    first_high, first_low = split_table(first)
    others_high, others_low = split_table(others)
    row_ids = (lat * rows + jnp.arange(rows)).astype(f32)
    latitude = (-0.5 + (row_ids + 0.5) / (lat_count * rows)) * math.pi
    inverse_sine = np.where(numbers == 0, 1.0, 1.0 / np.where(numbers == 0, 1.0, np.sin(np.pi * numbers / length)))
    ratio = 2.0 * jnp.cos(latitude)[:, None] * jnp.asarray(inverse_sine, f32)[None]
    damping = jnp.where(jnp.asarray(numbers == 0)[None], 1.0, jnp.minimum(1.0, ratio * ratio))
    scale = damping * jnp.asarray(weights, f32)[None]

    groups = [(0, 1), (1, 2), (2, tracer_count)]
    physics_shapes = [(end - begin, rows, levels, width) for begin, end in groups]
    *physics, energy = pl.pallas_call(
        functools.partial(physics_kernel, groups, rows, levels, sector, lat_count),
        in_specs=[whole] * 9,
        out_specs=[whole] * (len(groups) + 1),
        out_shape=[jax.ShapeDtypeStruct(shape, f32) for shape in physics_shapes + [(lat_count, LANES)]],
        compiler_params=params(),
        cost_estimate=cost(50_000_000, 4_000_000),
        name="physics",
    )(owner_of, base, padded, from_south, from_north, lat_courant, surface, mixing, decay)
    other = [lax.ppermute(part, "lon", swap) for part in physics]

    out = None
    tables = [jnp.asarray(table) for table in (others_high, others_low, first_high, first_low)]
    distance = 1
    for chunk in range(max(len(groups), lat_count.bit_length() - 1)):
        if distance < lat_count:
            received = lax.ppermute(energy, "lat", [(i, i ^ distance) for i in range(lat_count)])
            distance *= 2
        else:
            received = None
        if chunk < len(groups):
            begin, end = groups[chunk]
            has_alias = int(out is not None)
            out = pl.pallas_call(
                functools.partial(filter_kernel, rows, levels, sector, radix, has_alias),
                grid=(end - begin,),
                in_specs=[pl.BlockSpec(memory_space=pltpu.SMEM)]
                + [whole] * (3 + len(tables))
                + [pl.BlockSpec(memory_space=pl.ANY)] * has_alias,
                out_specs=pl.BlockSpec((1, levels, rows, sector), lambda i, begin=begin: (begin + i, 0, 0, 0)),
                out_shape=jax.ShapeDtypeStruct((tracer_count, levels, rows, sector), f32),
                scratch_shapes=[
                    pltpu.VMEM((rows * levels, length), jnp.bfloat16),
                    pltpu.VMEM((rows * levels, length), jnp.bfloat16),
                    pltpu.VMEM((rows * levels, length), f32),
                ],
                input_output_aliases={8: 0} if has_alias else {},
                compiler_params=params(),
                cost_estimate=cost(450_000_000, 3_000_000),
                name="filter",
            )(polar_mask, physics[chunk], other[chunk], *tables, scale, *([out] if has_alias else []))
        if received is not None:
            received, out = lax.optimization_barrier((received, out))
            energy = energy + received
        if chunk + 1 < len(groups):
            energy, physics[chunk + 1] = lax.optimization_barrier((energy, physics[chunk + 1]))

    owner_energy = jnp.sum(lax.dynamic_slice_in_dim(energy, lat, 1, 0)).reshape(1, 1) / (block_count * BLOCK)
    return out, owner_energy


def solution(mesh):
    placed = (
        P("group", None, "lat", "lon"),
        P("group", "lat", "lon"),
        P("group", "lat", "lon"),
        P("group", "lat", "lon"),
        P(),
        P(),
        P(("group", "lat"), "lon", None, None),
        P(("group", "lat")),
    )
    return jax.shard_map(
        on_device,
        mesh=mesh,
        in_specs=placed,
        out_specs=(P("group", None, "lat", "lon"), P(("group", "lat"), "lon")),
        check_vma=False,
    )
```

```python
import functools
import math

import jax
import jax.numpy as jnp
import numpy as np
from jax import lax
from jax.experimental import pallas as pl
from jax.experimental.pallas import tpu as pltpu
from jax.sharding import PartitionSpec as P

LANES = 128
BLOCK = 128
VMEM_BYTES = 6 * 1024 * 1024
PACK_VMEM_BYTES = 60 * 1024 * 1024
NEAR = 7.0 / 12.0
FAR = 1.0 / 12.0


def params(limit=VMEM_BYTES):
    return pltpu.CompilerParams(vmem_limit_bytes=limit)


def cost(flops, bytes_accessed):
    return pl.CostEstimate(flops=flops, bytes_accessed=bytes_accessed, transcendentals=0)


def split_high_low(value):
    high = value.astype(jnp.bfloat16)
    low = (value - high.astype(jnp.float32)).astype(jnp.bfloat16)
    return high, low


def stacked_table(table):
    high = table.astype(jnp.bfloat16.dtype)
    low = (table - high.astype(np.float64)).astype(jnp.bfloat16.dtype)
    return np.concatenate([high, high, low])


def spectral_tables(length):
    radix = length // LANES
    pairs = (radix - 1) // 2
    spot = np.arange(LANES)[:, None]
    number = np.arange(LANES)[None, :]
    is_cosine = number <= LANES // 2
    wave = np.where(is_cosine, number, number - LANES // 2)
    angle = 2.0 * np.pi * ((spot * wave) % LANES) / LANES
    first = np.where(is_cosine, np.cos(angle), np.sin(angle))
    others, numbers = [], [radix * wave[0]]
    weights = [np.where((wave[0] == 0) | (wave[0] == LANES // 2), 1.0, 2.0) / length]
    for residue in range(1, pairs + 1):
        whole = residue + radix * number
        angle = 2.0 * np.pi * ((spot * whole) % length) / length
        cosine, sine = np.cos(angle), np.sin(angle)
        others.append(np.block([[cosine, -sine], [sine, cosine]]))
        folded = np.minimum(whole[0], length - whole[0])
        numbers += [folded, folded]
        weights.append(np.full(2 * LANES, 2.0 / length))
    others += [table.T for table in others]
    first = np.concatenate([stacked_table(first), stacked_table(first.T)])
    return first, np.concatenate([stacked_table(table) for table in others]), np.concatenate(numbers), np.concatenate(weights)


def pack_rows(first, second):
    return jnp.concatenate([first, second], axis=1)


def second_half(packed, sector):
    skip, shift = sector // LANES, sector % LANES
    segments = [packed[:, LANES * i : LANES * (i + 1)] for i in range(packed.shape[1] // LANES)]
    if shift == 0:
        return jnp.concatenate(segments[skip:], axis=1)
    turned = [pltpu.roll(segment, LANES - shift, 1) for segment in segments[skip:]]
    lane = lax.broadcasted_iota(jnp.int32, turned[0].shape, 1)
    parts = [jnp.where(lane < LANES - shift, turned[i], turned[min(i + 1, len(turned) - 1)]) for i in range(len(turned))]
    return jnp.concatenate(parts, axis=1)


def pack_kernel(tracer_count, rows, levels, tracer_hbm, courant_hbm, up_ref, down_ref, tracer_ref, courant_ref, sems):
    copies = [pltpu.make_async_copy(tracer_hbm.at[t], tracer_ref.at[t], sems.at[t]) for t in range(tracer_count)]
    copies.append(pltpu.make_async_copy(courant_hbm, courant_ref, sems.at[tracer_count]))
    for copy in copies:
        copy.start()
    for t in range(tracer_count):
        copies[t].wait()
        place = slice(levels * t, levels * (t + 1))
        up_ref[place, :] = pack_rows(tracer_ref[t, :, rows - 2, :], tracer_ref[t, :, rows - 1, :])
        down_ref[place, :] = pack_rows(tracer_ref[t, :, 0, :], tracer_ref[t, :, 1, :])
    copies[tracer_count].wait()
    courant = courant_ref[:, 0, :]
    down_ref[levels * tracer_count :, :] = pack_rows(courant[: levels // 2], courant[levels // 2 :])


def base_kernel(rows, width, padded_ref, east_courant_ref, lat_courant_ref, base_ref):
    q = [padded_ref[0, r] for r in range(rows)]
    own_flux = [None] * (rows + 1)
    own_flux[0] = lat_courant_ref[0] * (NEAR * q[0] - FAR * q[1])
    own_flux[1] = lat_courant_ref[1] * (NEAR * (q[1] + q[0]) - FAR * q[2])
    own_flux[2] = lat_courant_ref[2] * (NEAR * (q[2] + q[1]) - FAR * (q[3] + q[0]))
    own_flux[3] = lat_courant_ref[3] * (NEAR * (q[3] + q[2]) - FAR * q[1])
    for r in range(rows):
        west, west2, east = pltpu.roll(q[r], 1, 1), pltpu.roll(q[r], 2, 1), pltpu.roll(q[r], width - 1, 1)
        flux = east_courant_ref[r] * (NEAR * (q[r] + west) - FAR * (east + west2))
        value = q[r] - (pltpu.roll(flux, width - 1, 1) - flux) + own_flux[r]
        if r + 1 < rows:
            value = value - own_flux[r + 1]
        base_ref[0, r] = value


def physics_kernel(groups, rows, levels, sector, owner_count, *refs):
    (owner_ref, base_ref, padded_ref, low_ref, high_ref, courant_ref, surface_ref, mixing_ref, decay_ref) = refs[:9]
    physics_refs, energy_ref = refs[9:-1], refs[-1]
    width = base_ref.shape[-1]
    tracer_count = base_ref.shape[0]
    courant = [courant_ref[r] for r in range(rows)]
    top = high_ref[levels * tracer_count :, :]
    top = jnp.concatenate([top[:, :width], second_half(top, sector)], axis=0)
    mix_high, mix_low = split_high_low(mixing_ref[...])
    mix = jnp.concatenate([mix_high, mix_high, mix_low, mix_low], axis=1)
    level = lax.broadcasted_iota(jnp.int32, (levels, width), 0)
    lane = lax.broadcasted_iota(jnp.int32, (levels, width), 1)
    energies = [None] * rows
    for physics_ref, (begin, end) in zip(physics_refs, groups):
        for t in range(begin, end):
            low = low_ref[levels * t : levels * (t + 1), :]
            high = high_ref[levels * t : levels * (t + 1), :]
            low_a, low_b = low[:, :width], second_half(low, sector)
            high_a, high_b = high[:, :width], second_half(high, sector)
            south = courant[0] * (NEAR * low_b - FAR * low_a)
            south_in = courant[1] * (FAR * low_b)
            north_in = courant[3] * (FAR * high_a)
            north = top * (NEAR * (high_a + padded_ref[t, 3]) - FAR * (high_b + padded_ref[t, 2]))
            extra = [south + south_in, -south_in, north_in, -north_in - north]
            for r in range(rows):
                advected = base_ref[t, r] + extra[r]
                part_high, part_low = split_high_low(advected)
                stacked = jnp.concatenate([part_high, part_low, part_high, part_low], axis=0)
                mixed = jnp.dot(mix, stacked, preferred_element_type=jnp.float32)
                mixed = jnp.where(level == levels - 1, mixed + surface_ref[t, r : r + 1, :], mixed)
                physics = mixed / (1.0 + decay_ref[t] * mixed * mixed)
                physics_ref[t - begin, r] = physics
                gap = physics - advected
                squared = gap * gap
                total = squared[0:8]
                for k in range(1, levels // 8):
                    total = total + squared[8 * k : 8 * k + 8]
                energies[r] = total if energies[r] is None else energies[r] + total
    energies = [jnp.where(lane[0:8] < sector, energy, 0.0) for energy in energies]
    spot = lax.broadcasted_iota(jnp.int32, (1, LANES), 1)
    result = jnp.zeros((1, LANES), jnp.float32)
    for owner in range(owner_count):
        chosen = jnp.zeros((8, LANES), jnp.float32)
        for r in range(rows):
            picked = jnp.where(owner_ref[r : r + 1, :] == owner, energies[r], 0.0)
            for k in range(width // LANES):
                chosen = chosen + picked[:, LANES * k : LANES * (k + 1)]
        total = jnp.sum(jnp.sum(chosen, axis=0, keepdims=True), axis=1, keepdims=True)
        result = jnp.where(spot == owner, total, result)
    energy_ref[...] = result


def filter_kernel(rows, levels, sector, radix, has_alias, *refs):
    mask_ref, own_ref, other_ref, table_ref, first_ref, scale_ref = refs[:6]
    out_ref, stack_ref, wave_ref = refs[6 + has_alias :]
    step = pl.program_id(0)
    own_ref, other_ref = own_ref.at[step], other_ref.at[step]
    pairs = (radix - 1) // 2
    shift = sector % LANES
    own_segments = -(-sector // LANES)
    lane = lax.broadcasted_iota(jnp.int32, (levels, LANES), 1)
    cosine = lambda k, i: math.cos(2.0 * math.pi * ((k * i) % radix) / radix)
    sine = lambda k, i: math.sin(2.0 * math.pi * ((k * i) % radix) / radix)

    def store_stack(r, begin, size, wave):
        part_high, part_low = split_high_low(wave)
        place = slice(levels * r, levels * (r + 1))
        for i, part in enumerate((part_high, part_low, part_high)):
            stack_ref[place, begin + size * i : begin + size * i + LANES] = part

    for r in range(rows):
        own = [own_ref[r, :, LANES * i : LANES * (i + 1)] for i in range(own_segments)]
        turned = [pltpu.roll(other_ref[r, :, LANES * i : LANES * (i + 1)], shift, 1) for i in range(own_segments)]
        joined = own[:-1] + [jnp.where(lane < shift, own[-1], turned[0])]
        joined += [jnp.where(lane < shift, turned[i], turned[i + 1]) for i in range(own_segments - 1)]
        plus = [joined[i] + joined[radix - i] for i in range(1, pairs + 1)]
        minus = [joined[radix - i] - joined[i] for i in range(1, pairs + 1)]
        store_stack(r, 0, LANES, sum(plus, joined[0]))
        for k in range(1, pairs + 1):
            begin = 3 * LANES * (2 * k - 1)
            real = sum((cosine(k, i) * plus[i - 1] for i in range(1, pairs + 1)), joined[0])
            imaginary = sine(k, 1) * minus[0]
            for i in range(2, pairs + 1):
                imaginary = imaginary + sine(k, i) * minus[i - 1]
            store_stack(r, begin, 2 * LANES, real)
            store_stack(r, begin + LANES, 2 * LANES, imaginary)

    def both_ways(begin, size, forward, inverse):
        spectrum = jnp.dot(stack_ref[:, 3 * begin : 3 * (begin + size)], forward, preferred_element_type=jnp.float32)
        scaled = jnp.concatenate(
            [spectrum[levels * r : levels * (r + 1)] * scale_ref[r : r + 1, begin : begin + size] for r in range(rows)], axis=0
        )
        part_high, part_low = split_high_low(scaled)
        stacked = jnp.concatenate([part_high, part_low, part_high], axis=1)
        wave_ref[:, begin : begin + size] = jnp.dot(stacked, inverse, preferred_element_type=jnp.float32)

    both_ways(0, LANES, first_ref[: 3 * LANES, :], first_ref[3 * LANES :, :])
    for k in range(pairs):
        tables = [table_ref[6 * LANES * (k + pairs * i) : 6 * LANES * (k + pairs * i + 1), :] for i in range(2)]
        both_ways(LANES * (2 * k + 1), 2 * LANES, *tables)

    for r in range(rows):
        waves = [wave_ref[levels * r : levels * (r + 1), LANES * i : LANES * (i + 1)] for i in range(radix)]
        filtered_row = mask_ref[r] == 1
        for n in range(own_segments):
            value = waves[0]
            for k in range(1, pairs + 1):
                value = value + (cosine(k, n) * waves[2 * k - 1] if n else waves[2 * k - 1])
                if n:
                    value = value - sine(k, n) * waves[2 * k]
            begin = LANES * n
            size = min(LANES, sector - begin)
            value = jnp.where(filtered_row, value, own_ref[r, :, begin : begin + LANES])
            out_ref[0, :, r, begin : begin + size] = value[:, :size]


def vmem(shape, index=None):
    index = index or (0,) * len(shape)
    return pl.BlockSpec(shape, lambda i: index)


def on_device(tracers, courant_lat, courant_lon, surface_flux, mixing, decay_rate, owners, polar_mask):
    tracer_count, levels, rows, sector = tracers.shape
    assert rows == 4 and sector % 64 == 0 and lax.axis_size("lon") == 2
    f32 = jnp.float32
    lat_count, lat = lax.axis_size("lat"), lax.axis_index("lat")
    length = 2 * sector
    width = -(-sector // LANES) * LANES
    radix = length // LANES
    upward = [(i, i + 1) for i in range(lat_count - 1)]
    downward = [(i + 1, i) for i in range(lat_count - 1)]
    swap = [(0, 1), (1, 0)]

    whole = pl.BlockSpec(memory_space=pltpu.VMEM)
    in_hbm = pl.BlockSpec(memory_space=pltpu.HBM)
    up_shape = (levels * tracer_count, length)
    down_shape = (levels * tracer_count + levels // 2, length)
    up, down = pl.pallas_call(
        functools.partial(pack_kernel, tracer_count, rows, levels),
        in_specs=[in_hbm, in_hbm],
        out_specs=[whole, whole],
        out_shape=[jax.ShapeDtypeStruct(up_shape, f32), jax.ShapeDtypeStruct(down_shape, f32)],
        scratch_shapes=[
            pltpu.VMEM(tracers.shape, f32),
            pltpu.VMEM(courant_lat.shape, f32),
            pltpu.SemaphoreType.DMA((tracer_count + 1,)),
        ],
        compiler_params=params(PACK_VMEM_BYTES),
        cost_estimate=cost(0, 600_000),
        name="pack",
    )(tracers, courant_lat)
    from_south = lax.ppermute(up, "lat", upward)
    from_north = lax.ppermute(down, "lat", downward)
    tracers, courant_lat, courant_lon, up, down = lax.optimization_barrier((tracers, courant_lat, courant_lon, up, down))

    by_row = jnp.transpose(tracers, (0, 2, 1, 3))
    lon_by_row = jnp.transpose(courant_lon, (1, 0, 2))
    lat_by_row = jnp.transpose(courant_lat, (1, 0, 2))
    ends = jnp.concatenate([by_row[..., -2:], by_row[..., :2]], axis=-1)
    lon_end = jnp.pad(lon_by_row[..., :1], ((0, 0), (0, 0), (0, 3)))
    sides = lax.ppermute(jnp.concatenate([ends, lon_end[None]], axis=0), "lon", swap)
    gap = jnp.zeros((tracer_count, rows, levels, width - sector - 4), f32)
    padded = jnp.concatenate([by_row, sides[:tracer_count, ..., 2:], gap, sides[:tracer_count, ..., :2]], axis=-1)
    east_courant = jnp.concatenate(
        [lon_by_row, sides[tracer_count, ..., :1], jnp.zeros((rows, levels, width - sector - 1), f32)], axis=-1
    )
    not_pole = jnp.where((lat > 0) | (jnp.arange(rows) > 0), 1.0, 0.0)
    lat_courant = jnp.pad(lat_by_row * not_pole[:, None, None], ((0, 0), (0, 0), (0, width - sector)))
    base = pl.pallas_call(
        functools.partial(base_kernel, rows, width),
        grid=(tracer_count,),
        in_specs=[
            pl.BlockSpec((1, rows, levels, width), lambda t: (t, 0, 0, 0)),
            vmem((rows, levels, width)),
            vmem((rows, levels, width)),
        ],
        out_specs=pl.BlockSpec((1, rows, levels, width), lambda t: (t, 0, 0, 0)),
        out_shape=jax.ShapeDtypeStruct((tracer_count, rows, levels, width), f32),
        compiler_params=params(),
        cost_estimate=cost(0, 3_000_000),
        name="base",
    )(padded, east_courant, lat_courant)

    surface = jnp.pad(surface_flux, ((0, 0), (0, 0), (0, width - sector)))
    decay = decay_rate[:, :, None]
    block_count = rows * sector // BLOCK
    block_of = (np.arange(rows)[:, None] * sector + np.minimum(np.arange(width), sector - 1)[None]) // BLOCK
    owner_of = jnp.repeat(owners.reshape(block_count), BLOCK).reshape(rows, sector)
    owner_of = jnp.pad(owner_of, ((0, 0), (0, width - sector)))
    first, others, numbers, weights = spectral_tables(length)
    row_ids = (lat * rows + jnp.arange(rows)).astype(f32)
    latitude = (-0.5 + (row_ids + 0.5) / (lat_count * rows)) * math.pi
    inverse_sine = np.where(numbers == 0, 1.0, 1.0 / np.where(numbers == 0, 1.0, np.sin(np.pi * numbers / length)))
    ratio = 2.0 * jnp.cos(latitude)[:, None] * jnp.asarray(inverse_sine, f32)[None]
    damping = jnp.where(jnp.asarray(numbers == 0)[None], 1.0, jnp.minimum(1.0, ratio * ratio))
    scale = damping * jnp.asarray(weights, f32)[None]

    base, scale, owner_of, surface, decay = lax.optimization_barrier((base, scale, owner_of, surface, decay))
    groups = [(0, 1), (1, 2), (2, tracer_count)]
    physics_shapes = [(end - begin, rows, levels, width) for begin, end in groups]
    *physics, energy = pl.pallas_call(
        functools.partial(physics_kernel, groups, rows, levels, sector, lat_count),
        in_specs=[whole] * 9,
        out_specs=[whole] * (len(groups) + 1),
        out_shape=[jax.ShapeDtypeStruct(shape, f32) for shape in physics_shapes + [(1, LANES)]],
        compiler_params=params(),
        cost_estimate=cost(50_000_000, 4_000_000),
        name="physics",
    )(owner_of, base, padded, from_south, from_north, lat_courant, surface, mixing, decay)
    other = [lax.ppermute(part, "lon", swap) for part in physics]

    out = None
    tables = [jnp.asarray(table) for table in (others, first)]
    distance = 1
    for chunk in range(max(len(groups), lat_count.bit_length() - 1)):
        if distance < lat_count:
            received = lax.ppermute(energy, "lat", [(i, i ^ distance) for i in range(lat_count)])
            distance *= 2
        else:
            received = None
        if chunk < len(groups):
            begin, end = groups[chunk]
            has_alias = int(out is not None)
            out = pl.pallas_call(
                functools.partial(filter_kernel, rows, levels, sector, radix, has_alias),
                grid=(end - begin,),
                in_specs=[pl.BlockSpec(memory_space=pltpu.SMEM)]
                + [whole] * (3 + len(tables))
                + [pl.BlockSpec(memory_space=pl.ANY)] * has_alias,
                out_specs=pl.BlockSpec((1, levels, rows, sector), lambda i, begin=begin: (begin + i, 0, 0, 0)),
                out_shape=jax.ShapeDtypeStruct((tracer_count, levels, rows, sector), f32),
                scratch_shapes=[
                    pltpu.VMEM((rows * levels, 3 * length), jnp.bfloat16),
                    pltpu.VMEM((rows * levels, length), f32),
                ],
                input_output_aliases={6: 0} if has_alias else {},
                compiler_params=params(),
                cost_estimate=cost(450_000_000, 3_000_000),
                name="filter",
            )(polar_mask, physics[chunk], other[chunk], *tables, scale, *([out] if has_alias else []))
        if received is not None:
            received, out = lax.optimization_barrier((received, out))
            energy = energy + received
        if chunk + 1 < len(groups):
            energy, physics[chunk + 1] = lax.optimization_barrier((energy, physics[chunk + 1]))

    owner_energy = lax.dynamic_slice(energy, (0, lat), (1, 1)) / (block_count * BLOCK)
    return out, owner_energy


def solution(mesh):
    placed = (
        P("group", None, "lat", "lon"),
        P("group", "lat", "lon"),
        P("group", "lat", "lon"),
        P("group", "lat", "lon"),
        P(),
        P(),
        P(("group", "lat"), "lon", None, None),
        P(("group", "lat")),
    )
    return jax.shard_map(
        on_device,
        mesh=mesh,
        in_specs=placed,
        out_specs=(P("group", None, "lat", "lon"), P(("group", "lat"), "lon")),
        check_vma=False,
    )
```

```python
import functools
import math

import jax
import jax.numpy as jnp
import numpy as np
from jax import lax
from jax.experimental import pallas as pl
from jax.experimental.pallas import tpu as pltpu
from jax.sharding import PartitionSpec as P

LANES = 128
BLOCK = 128
VMEM_BYTES = 6 * 1024 * 1024
RESULT_PIECES = 4
NEAR = 7.0 / 12.0
FAR = 1.0 / 12.0


def params():
    return pltpu.CompilerParams(vmem_limit_bytes=VMEM_BYTES)


def cost(flops, bytes_accessed):
    return pl.CostEstimate(flops=flops, bytes_accessed=bytes_accessed, transcendentals=0)


def split_high_low(value):
    high = value.astype(jnp.bfloat16)
    low = (value - high.astype(jnp.float32)).astype(jnp.bfloat16)
    return high, low


def split_table(table):
    high = table.astype(jnp.bfloat16.dtype)
    return high, (table - high.astype(np.float64)).astype(jnp.bfloat16.dtype)


def spectral_tables(length):
    radix = length // LANES
    pairs = (radix - 1) // 2
    spot = np.arange(LANES)[:, None]
    number = np.arange(LANES)[None, :]
    is_cosine = number <= LANES // 2
    wave = np.where(is_cosine, number, number - LANES // 2)
    angle = 2.0 * np.pi * ((spot * wave) % LANES) / LANES
    first = np.where(is_cosine, np.cos(angle), np.sin(angle))
    others, numbers = [], [radix * wave[0]]
    weights = [np.where((wave[0] == 0) | (wave[0] == LANES // 2), 1.0, 2.0) / length]
    for residue in range(1, pairs + 1):
        whole = residue + radix * number
        angle = 2.0 * np.pi * ((spot * whole) % length) / length
        cosine, sine = np.cos(angle), np.sin(angle)
        others.append(np.block([[cosine, -sine], [sine, cosine]]))
        folded = np.minimum(whole[0], length - whole[0])
        numbers += [folded, folded]
        weights.append(np.full(2 * LANES, 2.0 / length))
    others += [table.T for table in others]
    return np.concatenate([first, first.T]), np.concatenate(others), np.concatenate(numbers), np.concatenate(weights)


def pack_rows(first, second):
    return jnp.concatenate([first, second], axis=1)


def second_half(packed, sector):
    skip, shift = sector // LANES, sector % LANES
    segments = [packed[:, LANES * i : LANES * (i + 1)] for i in range(packed.shape[1] // LANES)]
    if shift == 0:
        return jnp.concatenate(segments[skip:], axis=1)
    turned = [pltpu.roll(segment, LANES - shift, 1) for segment in segments[skip:]]
    lane = lax.broadcasted_iota(jnp.int32, turned[0].shape, 1)
    parts = [jnp.where(lane < LANES - shift, turned[i], turned[min(i + 1, len(turned) - 1)]) for i in range(len(turned))]
    return jnp.concatenate(parts, axis=1)


def pack_kernel(split, rows, levels, tracer_hbm, courant_hbm, *refs):
    up_refs, down_refs = refs[: len(split)], refs[len(split) : 2 * len(split)]
    tracer_ref, courant_ref, sems = refs[2 * len(split) :]
    tracer_count = tracer_ref.shape[0]
    copies = [pltpu.make_async_copy(courant_hbm, courant_ref, sems.at[tracer_count])]
    copies += [pltpu.make_async_copy(tracer_hbm.at[t], tracer_ref.at[t], sems.at[t]) for t in range(tracer_count)]
    for copy in copies:
        copy.start()
    copies[0].wait()
    courant = courant_ref[:, 0, :]
    place = levels * (split[0][1] - split[0][0])
    down_refs[0][place : place + levels // 2, :] = pack_rows(courant[: levels // 2], courant[levels // 2 :])
    for (begin, end), up_ref, down_ref in zip(split, up_refs, down_refs):
        for t in range(begin, end):
            copies[t + 1].wait()
            place = slice(levels * (t - begin), levels * (t - begin + 1))
            up_ref[place, :] = pack_rows(tracer_ref[t, :, rows - 2, :], tracer_ref[t, :, rows - 1, :])
            down_ref[place, :] = pack_rows(tracer_ref[t, :, 0, :], tracer_ref[t, :, 1, :])


def base_kernel(rows, width, padded_ref, east_courant_ref, lat_courant_ref, base_ref, north_ref):
    q = [padded_ref[0, r] for r in range(rows)]
    north_ref[0] = NEAR * q[3] - FAR * q[2]
    own_flux = [None] * (rows + 1)
    own_flux[0] = lat_courant_ref[0] * (NEAR * q[0] - FAR * q[1])
    own_flux[1] = lat_courant_ref[1] * (NEAR * (q[1] + q[0]) - FAR * q[2])
    own_flux[2] = lat_courant_ref[2] * (NEAR * (q[2] + q[1]) - FAR * (q[3] + q[0]))
    own_flux[3] = lat_courant_ref[3] * (NEAR * (q[3] + q[2]) - FAR * q[1])
    for r in range(rows):
        west, west2, east = pltpu.roll(q[r], 1, 1), pltpu.roll(q[r], 2, 1), pltpu.roll(q[r], width - 1, 1)
        flux = east_courant_ref[r] * (NEAR * (q[r] + west) - FAR * (east + west2))
        value = q[r] - (pltpu.roll(flux, width - 1, 1) - flux) + own_flux[r]
        if r + 1 < rows:
            value = value - own_flux[r + 1]
        base_ref[0, r] = value


def physics_kernel(begin, levels, sector, owner_count, *refs):
    base_ref, north_ref, low_ref, high_ref, top_ref, courant_ref, surface_ref, mixing_ref, decay_ref, owner_ref, energy_in_ref = refs[:11]
    physics_ref, energy_ref = refs[11:]
    rows, width = base_ref.shape[1], base_ref.shape[-1]
    count = physics_ref.shape[0]
    courant = [courant_ref[r] for r in range(rows)]
    top = top_ref[top_ref.shape[0] - levels // 2 :, :]
    top = jnp.concatenate([top[:, :width], second_half(top, sector)], axis=0)
    mix_high, mix_low = split_high_low(mixing_ref[...])
    mix = jnp.concatenate([mix_high, mix_high, mix_low, mix_low], axis=1)
    level = lax.broadcasted_iota(jnp.int32, (8, width), 0)
    lane = lax.broadcasted_iota(jnp.int32, (8, width), 1)
    energies = [energy_in_ref[r] for r in range(rows)]
    for i in range(count):
        t = begin + i
        low = low_ref[levels * i : levels * (i + 1), :]
        high = high_ref[levels * i : levels * (i + 1), :]
        low_a, low_b = low[:, :width], second_half(low, sector)
        high_a, high_b = high[:, :width], second_half(high, sector)
        south = courant[0] * (NEAR * low_b - FAR * low_a)
        south_in = courant[1] * (FAR * low_b)
        north_in = courant[3] * (FAR * high_a)
        north = top * (NEAR * high_a - FAR * high_b + north_ref[t])
        extra = [south + south_in, -south_in, north_in, -north_in - north]
        for r in range(rows):
            advected = base_ref[t, r] + extra[r]
            part_high, part_low = split_high_low(advected)
            stacked = jnp.concatenate([part_high, part_low, part_high, part_low], axis=0)
            mixed = jnp.dot(mix, stacked, preferred_element_type=jnp.float32)
            surface = jnp.where(level == 7, surface_ref[t, r : r + 1, :], 0.0)
            mixed = jnp.concatenate([mixed[: levels - 8], mixed[levels - 8 :] + surface], axis=0)
            physics = mixed / (1.0 + decay_ref[t] * mixed * mixed)
            physics_ref[i, r] = physics
            gap = physics - advected
            squared = gap * gap
            for k in range(levels // 8):
                energies[r] = energies[r] + squared[8 * k : 8 * k + 8]
    if not owner_count:
        for r in range(rows):
            energy_ref[r] = energies[r]
        return
    energies = [jnp.where(lane < sector, energy, 0.0) for energy in energies]
    spot = lax.broadcasted_iota(jnp.int32, (1, LANES), 1)
    result = jnp.zeros((1, LANES), jnp.float32)
    for owner in range(owner_count):
        chosen = jnp.zeros((8, LANES), jnp.float32)
        for r in range(rows):
            picked = jnp.where(owner_ref[r : r + 1, :] == owner, energies[r], 0.0)
            for k in range(width // LANES):
                chosen = chosen + picked[:, LANES * k : LANES * (k + 1)]
        total = jnp.sum(jnp.sum(chosen, axis=0, keepdims=True), axis=1, keepdims=True)
        result = jnp.where(spot == owner, total, result)
    energy_ref[...] = result


def filter_kernel(first_tracer, chosen, radix, has_alias, *refs):
    out_hbm, stack_ref, wave_ref, result_ref, sems = refs[8 + has_alias :]
    levels = out_hbm.shape[1]
    piece = levels // RESULT_PIECES
    copies = []
    for place, i in enumerate(chosen):
        filter_tracer(radix, refs[0], refs[1].at[i], refs[2].at[i], *refs[3:8], result_ref.at[place], stack_ref, wave_ref)
        for part in range(RESULT_PIECES):
            span = pl.ds(piece * part, piece)
            copies.append(
                pltpu.make_async_copy(result_ref.at[place, span], out_hbm.at[first_tracer + i, span], sems.at[place, part])
            )
            copies[-1].start()
    for copy in copies:
        copy.wait()


def filter_tracer(
    radix, mask_ref, own_ref, other_ref, table_high_ref, table_low_ref, first_high_ref, first_low_ref, scale_ref, out_ref,
    stack_ref, wave_ref,
):
    levels, rows, sector = out_ref.shape
    pairs = (radix - 1) // 2
    shift = sector % LANES
    own_segments = -(-sector // LANES)
    lane = lax.broadcasted_iota(jnp.int32, (levels, LANES), 1)
    cosine = lambda k, i: math.cos(2.0 * math.pi * ((k * i) % radix) / radix)
    sine = lambda k, i: math.sin(2.0 * math.pi * ((k * i) % radix) / radix)

    def store_stack(r, begin, size, wave):
        part_high, part_low = split_high_low(wave)
        place = slice(levels * r, levels * (r + 1))
        for i, part in enumerate((part_high, part_low, part_high)):
            stack_ref[place, begin + size * i : begin + size * i + LANES] = part

    for r in range(rows):
        own = [own_ref[r, :, LANES * i : LANES * (i + 1)] for i in range(own_segments)]
        turned = [pltpu.roll(other_ref[r, :, LANES * i : LANES * (i + 1)], shift, 1) for i in range(own_segments)]
        joined = own[:-1] + [jnp.where(lane < shift, own[-1], turned[0])]
        joined += [jnp.where(lane < shift, turned[i], turned[i + 1]) for i in range(own_segments - 1)]
        plus = [joined[i] + joined[radix - i] for i in range(1, pairs + 1)]
        minus = [joined[radix - i] - joined[i] for i in range(1, pairs + 1)]
        store_stack(r, 0, LANES, sum(plus, joined[0]))
        for k in range(1, pairs + 1):
            begin = 3 * LANES * (2 * k - 1)
            real = sum((cosine(k, i) * plus[i - 1] for i in range(1, pairs + 1)), joined[0])
            imaginary = sine(k, 1) * minus[0]
            for i in range(2, pairs + 1):
                imaginary = imaginary + sine(k, i) * minus[i - 1]
            store_stack(r, begin, 2 * LANES, real)
            store_stack(r, begin + LANES, 2 * LANES, imaginary)

    def both_ways(begin, size, forward, inverse):
        spectrum = jnp.dot(stack_ref[:, 3 * begin : 3 * (begin + size)], forward, preferred_element_type=jnp.float32)
        scaled = jnp.concatenate(
            [spectrum[levels * r : levels * (r + 1)] * scale_ref[r : r + 1, begin : begin + size] for r in range(rows)], axis=0
        )
        part_high, part_low = split_high_low(scaled)
        stacked = jnp.concatenate([part_high, part_low, part_high], axis=1)
        wave_ref[:, begin : begin + size] = jnp.dot(stacked, inverse, preferred_element_type=jnp.float32)

    def table_of(high, low, begin, size):
        part_high = high[begin : begin + size, :]
        return jnp.concatenate([part_high, part_high, low[begin : begin + size, :]], axis=0)

    both_ways(0, LANES, *(table_of(first_high_ref, first_low_ref, LANES * i, LANES) for i in range(2)))
    for k in range(pairs):
        tables = (table_of(table_high_ref, table_low_ref, 2 * LANES * (k + pairs * i), 2 * LANES) for i in range(2))
        both_ways(LANES * (2 * k + 1), 2 * LANES, *tables)

    for r in range(rows):
        waves = [wave_ref[levels * r : levels * (r + 1), LANES * i : LANES * (i + 1)] for i in range(radix)]
        filtered_row = mask_ref[r] == 1
        for n in range(own_segments):
            value = waves[0]
            for k in range(1, pairs + 1):
                value = value + (cosine(k, n) * waves[2 * k - 1] if n else waves[2 * k - 1])
                if n:
                    value = value - sine(k, n) * waves[2 * k]
            begin = LANES * n
            size = min(LANES, sector - begin)
            value = jnp.where(filtered_row, value, own_ref[r, :, begin : begin + LANES])
            out_ref[:, r, begin : begin + size] = value[:, :size]


def vmem(shape, index=None):
    index = index or (0,) * len(shape)
    return pl.BlockSpec(shape, lambda i: index)


def on_device(tracers, courant_lat, courant_lon, surface_flux, mixing, decay_rate, owners, polar_mask):
    tracer_count, levels, rows, sector = tracers.shape
    assert rows == 4 and sector % 64 == 0 and lax.axis_size("lon") == 2
    f32 = jnp.float32
    lat_count, lat = lax.axis_size("lat"), lax.axis_index("lat")
    length = 2 * sector
    width = -(-sector // LANES) * LANES
    radix = length // LANES
    upward = [(i, i + 1) for i in range(lat_count - 1)]
    downward = [(i + 1, i) for i in range(lat_count - 1)]
    swap = [(0, 1), (1, 0)]

    whole = pl.BlockSpec(memory_space=pltpu.VMEM)
    in_hbm = pl.BlockSpec(memory_space=pltpu.HBM)
    split = [(0, tracer_count // 2), (tracer_count // 2, tracer_count)]
    up_rows = [levels * (end - begin) for begin, end in split]
    packed_shapes = [(count, length) for count in up_rows + [up_rows[0] + levels // 2] + up_rows[1:]]
    packed = pl.pallas_call(
        functools.partial(pack_kernel, split, rows, levels),
        in_specs=[in_hbm, in_hbm],
        out_specs=[whole] * len(packed_shapes),
        out_shape=[jax.ShapeDtypeStruct(shape, f32) for shape in packed_shapes],
        scratch_shapes=[
            pltpu.VMEM(tracers.shape, f32),
            pltpu.VMEM(courant_lat.shape, f32),
            pltpu.SemaphoreType.DMA((tracer_count + 1,)),
        ],
        compiler_params=params(),
        cost_estimate=cost(0, 600_000),
        name="pack",
    )(*(pltpu.with_memory_space_constraint(array, pltpu.HBM) for array in (tracers, courant_lat)))
    up, down = packed[: len(split)], packed[len(split) :]
    from_north = [lax.ppermute(down[0], "lat", downward)]
    from_south = [lax.ppermute(up[0], "lat", upward)]
    tracers, courant_lat, courant_lon, up, down = lax.optimization_barrier((tracers, courant_lat, courant_lon, up, down))

    by_row = jnp.transpose(tracers, (0, 2, 1, 3))
    lon_by_row = jnp.transpose(courant_lon, (1, 0, 2))
    lat_by_row = jnp.transpose(courant_lat, (1, 0, 2))
    ends = jnp.concatenate([by_row[..., -2:], by_row[..., :2]], axis=-1)
    lon_end = jnp.pad(lon_by_row[..., :1], ((0, 0), (0, 0), (0, 3)))
    sides = lax.ppermute(jnp.concatenate([ends, lon_end[None]], axis=0), "lon", swap)
    gap = jnp.zeros((tracer_count, rows, levels, width - sector - 4), f32)
    padded = jnp.concatenate([by_row, sides[:tracer_count, ..., 2:], gap, sides[:tracer_count, ..., :2]], axis=-1)
    east_courant = jnp.concatenate(
        [lon_by_row, sides[tracer_count, ..., :1], jnp.zeros((rows, levels, width - sector - 1), f32)], axis=-1
    )
    not_pole = jnp.where((lat > 0) | (jnp.arange(rows) > 0), 1.0, 0.0)
    lat_courant = jnp.pad(lat_by_row * not_pole[:, None, None], ((0, 0), (0, 0), (0, width - sector)))
    base, north = pl.pallas_call(
        functools.partial(base_kernel, rows, width),
        grid=(tracer_count,),
        in_specs=[
            pl.BlockSpec((1, rows, levels, width), lambda t: (t, 0, 0, 0)),
            vmem((rows, levels, width)),
            vmem((rows, levels, width)),
        ],
        out_specs=[
            pl.BlockSpec((1, rows, levels, width), lambda t: (t, 0, 0, 0)),
            pl.BlockSpec((1, levels, width), lambda t: (t, 0, 0)),
        ],
        out_shape=[
            jax.ShapeDtypeStruct((tracer_count, rows, levels, width), f32),
            jax.ShapeDtypeStruct((tracer_count, levels, width), f32),
        ],
        compiler_params=params(),
        cost_estimate=cost(0, 3_000_000),
        name="base",
    )(padded, east_courant, lat_courant)

    surface = jnp.pad(surface_flux, ((0, 0), (0, 0), (0, width - sector)))
    decay = decay_rate[:, :, None]
    block_count = rows * sector // BLOCK
    block_of = (np.arange(rows)[:, None] * sector + np.minimum(np.arange(width), sector - 1)[None]) // BLOCK
    owner_of = jnp.repeat(owners.reshape(block_count), BLOCK).reshape(rows, sector)
    owner_of = jnp.pad(owner_of, ((0, 0), (0, width - sector)))
    first, others, numbers, weights = spectral_tables(length)
    row_ids = (lat * rows + jnp.arange(rows)).astype(f32)
    latitude = (-0.5 + (row_ids + 0.5) / (lat_count * rows)) * math.pi
    inverse_sine = np.where(numbers == 0, 1.0, 1.0 / np.where(numbers == 0, 1.0, np.sin(np.pi * numbers / length)))
    ratio = 2.0 * jnp.cos(latitude)[:, None] * jnp.asarray(inverse_sine, f32)[None]
    damping = jnp.where(jnp.asarray(numbers == 0)[None], 1.0, jnp.minimum(1.0, ratio * ratio))
    scale = damping * jnp.asarray(weights, f32)[None]

    base, scale, owner_of, surface, decay, up, down = lax.optimization_barrier((base, scale, owner_of, surface, decay, up, down))
    from_north.append(lax.ppermute(down[1], "lat", downward))
    from_south.append(lax.ppermute(up[1], "lat", upward))

    tables = [jnp.asarray(part) for table in (others, first) for part in split_table(table)]
    physics, other = [], []

    def run_physics(chunk, energy):
        begin, end = split[chunk]
        last = chunk == len(split) - 1
        shapes = [(end - begin, rows, levels, width), (1, LANES) if last else energy.shape]
        result, energy = pl.pallas_call(
            functools.partial(physics_kernel, begin, levels, sector, lat_count if last else 0),
            in_specs=[whole] * 11,
            out_specs=[whole] * 2,
            out_shape=[jax.ShapeDtypeStruct(shape, f32) for shape in shapes],
            compiler_params=params(),
            cost_estimate=cost(0, 0),
            name="physics",
        )(base, north, from_south[chunk], from_north[chunk], from_north[0], lat_courant, surface, mixing, decay, owner_of, energy)
        physics.append(result)
        other.append(lax.ppermute(result, "lon", swap))
        return energy

    def run_filter(chunk, chosen, out):
        has_alias = int(out is not None)
        return pl.pallas_call(
            functools.partial(filter_kernel, split[chunk][0], chosen, radix, has_alias),
            in_specs=[pl.BlockSpec(memory_space=pltpu.SMEM)]
            + [whole] * (3 + len(tables))
            + [pl.BlockSpec(memory_space=pl.ANY)] * has_alias,
            out_specs=in_hbm,
            out_shape=jax.ShapeDtypeStruct((tracer_count, levels, rows, sector), f32),
            scratch_shapes=[
                pltpu.VMEM((rows * levels, 3 * length), jnp.bfloat16),
                pltpu.VMEM((rows * levels, length), f32),
                pltpu.VMEM((len(chosen), levels, rows, sector), f32),
                pltpu.SemaphoreType.DMA((len(chosen), RESULT_PIECES)),
            ],
            input_output_aliases={8: 0} if has_alias else {},
            compiler_params=params(),
            cost_estimate=cost(0, 0),
            name="filter",
        )(polar_mask, physics[chunk], other[chunk], *tables, scale, *([out] if has_alias else []))

    energy = run_physics(0, jnp.zeros((rows, 8, width), f32))
    out = run_filter(0, range(split[0][1] - split[0][0]), None)
    energy, out = lax.optimization_barrier((energy, out))
    energy = run_physics(1, energy)

    left = list(range(split[1][1] - split[1][0]))
    distance = 1
    while distance < lat_count:
        received = lax.ppermute(energy, "lat", [(i, i ^ distance) for i in range(lat_count)])
        distance *= 2
        if left:
            out = run_filter(1, left[:1], out)
            left = left[1:]
            received, out = lax.optimization_barrier((received, out))
        energy = energy + received
        energy, out = lax.optimization_barrier((energy, out))
    if left:
        out = run_filter(1, left, out)

    owner_energy = lax.dynamic_slice(energy, (0, lat), (1, 1)) / (block_count * BLOCK)
    return out, owner_energy


def solution(mesh):
    placed = (
        P("group", None, "lat", "lon"),
        P("group", "lat", "lon"),
        P("group", "lat", "lon"),
        P("group", "lat", "lon"),
        P(),
        P(),
        P(("group", "lat"), "lon", None, None),
        P(("group", "lat")),
    )
    return jax.shard_map(
        on_device,
        mesh=mesh,
        in_specs=placed,
        out_specs=(P("group", None, "lat", "lon"), P(("group", "lat"), "lon")),
        check_vma=False,
    )
```

```python
import functools
import math

import jax
import jax.numpy as jnp
import numpy as np
from jax import lax
from jax.experimental import pallas as pl
from jax.experimental.pallas import tpu as pltpu
from jax.sharding import PartitionSpec as P

LANES = 128
BLOCK = 128
VMEM_BYTES = 6 * 1024 * 1024
RESULT_PIECES = 4
NEAR = 7.0 / 12.0
FAR = 1.0 / 12.0


def params():
    return pltpu.CompilerParams(vmem_limit_bytes=VMEM_BYTES)


def cost(flops, bytes_accessed):
    return pl.CostEstimate(flops=flops, bytes_accessed=bytes_accessed, transcendentals=0)


def split_high_low(value):
    high = value.astype(jnp.bfloat16)
    low = (value - high.astype(jnp.float32)).astype(jnp.bfloat16)
    return high, low


def split_table(table):
    high = table.astype(jnp.bfloat16.dtype)
    return high, (table - high.astype(np.float64)).astype(jnp.bfloat16.dtype)


def spectral_tables(length):
    radix = length // LANES
    pairs = (radix - 1) // 2
    spot = np.arange(LANES)[:, None]
    number = np.arange(LANES)[None, :]
    is_cosine = number <= LANES // 2
    wave = np.where(is_cosine, number, number - LANES // 2)
    angle = 2.0 * np.pi * ((spot * wave) % LANES) / LANES
    first = np.where(is_cosine, np.cos(angle), np.sin(angle))
    others, numbers = [], [radix * wave[0]]
    weights = [np.where((wave[0] == 0) | (wave[0] == LANES // 2), 1.0, 2.0) / length]
    for residue in range(1, pairs + 1):
        whole = residue + radix * number
        angle = 2.0 * np.pi * ((spot * whole) % length) / length
        cosine, sine = np.cos(angle), np.sin(angle)
        others.append(np.block([[cosine, -sine], [sine, cosine]]))
        folded = np.minimum(whole[0], length - whole[0])
        numbers += [folded, folded]
        weights.append(np.full(2 * LANES, 2.0 / length))
    others += [table.T for table in others]
    return np.concatenate([first, first.T]), np.concatenate(others), np.concatenate(numbers), np.concatenate(weights)


def pack_rows(first, second):
    return jnp.concatenate([first, second], axis=1)


def second_half(packed, sector):
    skip, shift = sector // LANES, sector % LANES
    segments = [packed[:, LANES * i : LANES * (i + 1)] for i in range(packed.shape[1] // LANES)]
    if shift == 0:
        return jnp.concatenate(segments[skip:], axis=1)
    turned = [pltpu.roll(segment, LANES - shift, 1) for segment in segments[skip:]]
    lane = lax.broadcasted_iota(jnp.int32, turned[0].shape, 1)
    parts = [jnp.where(lane < LANES - shift, turned[i], turned[min(i + 1, len(turned) - 1)]) for i in range(len(turned))]
    return jnp.concatenate(parts, axis=1)


def pack_kernel(rows, levels, tracer_hbm, courant_hbm, up_ref, down_ref, tracer_ref, courant_ref, sems):
    tracer_count = tracer_ref.shape[0]
    copies = [pltpu.make_async_copy(tracer_hbm.at[t], tracer_ref.at[t], sems.at[t]) for t in range(tracer_count)]
    copies.append(pltpu.make_async_copy(courant_hbm, courant_ref, sems.at[tracer_count]))
    for copy in copies:
        copy.start()
    for t in range(tracer_count):
        copies[t].wait()
        place = slice(levels * t, levels * (t + 1))
        up_ref[place, :] = pack_rows(tracer_ref[t, :, rows - 2, :], tracer_ref[t, :, rows - 1, :])
        down_ref[place, :] = pack_rows(tracer_ref[t, :, 0, :], tracer_ref[t, :, 1, :])
    copies[tracer_count].wait()
    courant = courant_ref[:, 0, :]
    down_ref[levels * tracer_count :, :] = pack_rows(courant[: levels // 2], courant[levels // 2 :])


def base_kernel(rows, width, padded_ref, east_courant_ref, lat_courant_ref, base_ref, north_ref):
    q = [padded_ref[0, r] for r in range(rows)]
    north_ref[0] = NEAR * q[3] - FAR * q[2]
    own_flux = [None] * (rows + 1)
    own_flux[0] = lat_courant_ref[0] * (NEAR * q[0] - FAR * q[1])
    own_flux[1] = lat_courant_ref[1] * (NEAR * (q[1] + q[0]) - FAR * q[2])
    own_flux[2] = lat_courant_ref[2] * (NEAR * (q[2] + q[1]) - FAR * (q[3] + q[0]))
    own_flux[3] = lat_courant_ref[3] * (NEAR * (q[3] + q[2]) - FAR * q[1])
    for r in range(rows):
        west, west2, east = pltpu.roll(q[r], 1, 1), pltpu.roll(q[r], 2, 1), pltpu.roll(q[r], width - 1, 1)
        flux = east_courant_ref[r] * (NEAR * (q[r] + west) - FAR * (east + west2))
        value = q[r] - (pltpu.roll(flux, width - 1, 1) - flux) + own_flux[r]
        if r + 1 < rows:
            value = value - own_flux[r + 1]
        base_ref[0, r] = value


def physics_kernel(levels, sector, owner_count, first_ref, *refs):
    base_ref, north_ref, low_ref, high_ref, courant_ref, surface_ref, mixing_ref, decay_ref, owner_ref, energy_in_ref = refs[:10]
    physics_refs, energy_ref = refs[10:-1], refs[-1]
    rows, width = base_ref.shape[1], base_ref.shape[-1]
    courant = [courant_ref[r] for r in range(rows)]
    top = high_ref[high_ref.shape[0] - levels // 2 :, :]
    top = jnp.concatenate([top[:, :width], second_half(top, sector)], axis=0)
    mix_high, mix_low = split_high_low(mixing_ref[...])
    mix = jnp.concatenate([mix_high, mix_high, mix_low, mix_low], axis=1)
    level = lax.broadcasted_iota(jnp.int32, (8, width), 0)
    lane = lax.broadcasted_iota(jnp.int32, (8, width), 1)
    energies = [energy_in_ref[r] for r in range(rows)]
    for i, physics_ref in enumerate(physics_refs):
        t = first_ref[0] + i
        place = pl.ds(pl.multiple_of(levels * t, levels), levels)
        low, high = low_ref[place, :], high_ref[place, :]
        low_a, low_b = low[:, :width], second_half(low, sector)
        high_a, high_b = high[:, :width], second_half(high, sector)
        south = courant[0] * (NEAR * low_b - FAR * low_a)
        south_in = courant[1] * (FAR * low_b)
        north_in = courant[3] * (FAR * high_a)
        north = top * (NEAR * high_a - FAR * high_b + north_ref[t])
        extra = [south + south_in, -south_in, north_in, -north_in - north]
        for r in range(rows):
            advected = base_ref[t, r] + extra[r]
            part_high, part_low = split_high_low(advected)
            stacked = jnp.concatenate([part_high, part_low, part_high, part_low], axis=0)
            mixed = jnp.dot(mix, stacked, preferred_element_type=jnp.float32)
            surface = jnp.where(level == 7, surface_ref[t, r : r + 1, :], 0.0)
            mixed = jnp.concatenate([mixed[: levels - 8], mixed[levels - 8 :] + surface], axis=0)
            physics = mixed / (1.0 + decay_ref[t] * mixed * mixed)
            physics_ref[r] = physics
            gap = physics - advected
            squared = gap * gap
            for k in range(levels // 8):
                energies[r] = energies[r] + squared[8 * k : 8 * k + 8]
    if not owner_count:
        for r in range(rows):
            energy_ref[r] = energies[r]
        return
    energies = [jnp.where(lane < sector, energy, 0.0) for energy in energies]
    spot = lax.broadcasted_iota(jnp.int32, (1, LANES), 1)
    result = jnp.zeros((1, LANES), jnp.float32)
    for owner in range(owner_count):
        chosen = jnp.zeros((8, LANES), jnp.float32)
        for r in range(rows):
            picked = jnp.where(owner_ref[r : r + 1, :] == owner, energies[r], 0.0)
            for k in range(width // LANES):
                chosen = chosen + picked[:, LANES * k : LANES * (k + 1)]
        total = jnp.sum(jnp.sum(chosen, axis=0, keepdims=True), axis=1, keepdims=True)
        result = jnp.where(spot == owner, total, result)
    energy_ref[...] = result


def send_result(result_ref, out_hbm, tracer, sems):
    piece = result_ref.shape[0] // RESULT_PIECES
    copies = []
    for part in range(RESULT_PIECES):
        span = pl.ds(piece * part, piece)
        copies.append(pltpu.make_async_copy(result_ref.at[span], out_hbm.at[tracer, span], sems.at[part]))
        copies[-1].start()
    return copies


def filter_kernel(radix, place, first_ref, *refs):
    inputs, refs = refs[:8], refs[8:]
    copies = []
    if place:
        before_ref, result_ref, back_ref, out_hbm, stack_ref, wave_ref, sems = refs
        copies = send_result(before_ref, out_hbm, first_ref[0] + place - 1, sems)
    else:
        result_ref, back_ref, stack_ref, wave_ref = refs
    filter_tracer(radix, *inputs, result_ref, back_ref, stack_ref, wave_ref)
    for copy in copies:
        copy.wait()


def finish_kernel(place, keep_ref, first_ref, *refs):
    before_ref, received_refs = refs[0], refs[1 : 2 + place]
    out_hbm, result_ref, sems = refs[3 + place :]
    levels, rows, sector = before_ref.shape
    copies = send_result(before_ref, out_hbm, keep_ref[0] + place, sems.at[place + 1])
    for i, received_ref in enumerate(received_refs):
        for r in range(rows):
            result_ref[i, :, r, :] = received_ref[r, :, :sector]
        copies += send_result(result_ref.at[i], out_hbm, first_ref[0] + i, sems.at[i])
    for copy in copies:
        copy.wait()


def filter_tracer(
    radix, mask_ref, own_ref, other_ref, table_high_ref, table_low_ref, first_high_ref, first_low_ref, scale_ref, out_ref, back_ref,
    stack_ref, wave_ref,
):
    levels, rows, sector = out_ref.shape
    pairs = (radix - 1) // 2
    shift = sector % LANES
    own_segments = -(-sector // LANES)
    lane = lax.broadcasted_iota(jnp.int32, (levels, LANES), 1)
    cosine = lambda k, i: math.cos(2.0 * math.pi * ((k * i) % radix) / radix)
    sine = lambda k, i: math.sin(2.0 * math.pi * ((k * i) % radix) / radix)

    def store_stack(r, begin, size, wave):
        part_high, part_low = split_high_low(wave)
        place = slice(levels * r, levels * (r + 1))
        for i, part in enumerate((part_high, part_low, part_high)):
            stack_ref[place, begin + size * i : begin + size * i + LANES] = part

    for r in range(rows):
        own = [own_ref[r, :, LANES * i : LANES * (i + 1)] for i in range(own_segments)]
        turned = [pltpu.roll(other_ref[r, :, LANES * i : LANES * (i + 1)], shift, 1) for i in range(own_segments)]
        joined = own[:-1] + [jnp.where(lane < shift, own[-1], turned[0])]
        joined += [jnp.where(lane < shift, turned[i], turned[i + 1]) for i in range(own_segments - 1)]
        plus = [joined[i] + joined[radix - i] for i in range(1, pairs + 1)]
        minus = [joined[radix - i] - joined[i] for i in range(1, pairs + 1)]
        store_stack(r, 0, LANES, sum(plus, joined[0]))
        for k in range(1, pairs + 1):
            begin = 3 * LANES * (2 * k - 1)
            real = sum((cosine(k, i) * plus[i - 1] for i in range(1, pairs + 1)), joined[0])
            imaginary = sine(k, 1) * minus[0]
            for i in range(2, pairs + 1):
                imaginary = imaginary + sine(k, i) * minus[i - 1]
            store_stack(r, begin, 2 * LANES, real)
            store_stack(r, begin + LANES, 2 * LANES, imaginary)

    def both_ways(begin, size, forward, inverse):
        spectrum = jnp.dot(stack_ref[:, 3 * begin : 3 * (begin + size)], forward, preferred_element_type=jnp.float32)
        scaled = jnp.concatenate(
            [spectrum[levels * r : levels * (r + 1)] * scale_ref[r : r + 1, begin : begin + size] for r in range(rows)], axis=0
        )
        part_high, part_low = split_high_low(scaled)
        stacked = jnp.concatenate([part_high, part_low, part_high], axis=1)
        wave_ref[:, begin : begin + size] = jnp.dot(stacked, inverse, preferred_element_type=jnp.float32)

    def table_of(high, low, begin, size):
        part_high = high[begin : begin + size, :]
        return jnp.concatenate([part_high, part_high, low[begin : begin + size, :]], axis=0)

    both_ways(0, LANES, *(table_of(first_high_ref, first_low_ref, LANES * i, LANES) for i in range(2)))
    for k in range(pairs):
        tables = (table_of(table_high_ref, table_low_ref, 2 * LANES * (k + pairs * i), 2 * LANES) for i in range(2))
        both_ways(LANES * (2 * k + 1), 2 * LANES, *tables)

    for r in range(rows):
        waves = [wave_ref[levels * r : levels * (r + 1), LANES * i : LANES * (i + 1)] for i in range(radix)]
        results = [None] * radix
        results[0] = sum((waves[2 * k - 1] for k in range(1, pairs + 1)), waves[0])
        for n in range(1, pairs + 1):
            even = sum((cosine(k, n) * waves[2 * k - 1] for k in range(1, pairs + 1)), waves[0])
            odd = sine(1, n) * waves[2]
            for k in range(2, pairs + 1):
                odd = odd + sine(k, n) * waves[2 * k]
            results[n], results[radix - n] = even - odd, even + odd
        filtered_row = mask_ref[r] == 1
        turned = [pltpu.roll(result, LANES - shift, 1) for result in results[own_segments - 1 :]]
        for n in range(own_segments):
            begin = LANES * n
            size = min(LANES, sector - begin)
            value = jnp.where(filtered_row, results[n], own_ref[r, :, begin : begin + LANES])
            out_ref[:, r, begin : begin + size] = value[:, :size]
            value = jnp.where(lane < LANES - shift, turned[n], turned[min(n + 1, own_segments - 1)])
            back_ref[r, :, begin : begin + LANES] = jnp.where(filtered_row, value, other_ref[r, :, begin : begin + LANES])


def vmem(shape, index=None):
    index = index or (0,) * len(shape)
    return pl.BlockSpec(shape, lambda i: index)


def on_device(tracers, courant_lat, courant_lon, surface_flux, mixing, decay_rate, owners, polar_mask):
    tracer_count, levels, rows, sector = tracers.shape
    assert rows == 4 and sector % 64 == 0 and lax.axis_size("lon") == 2
    f32 = jnp.float32
    lat_count, lat = lax.axis_size("lat"), lax.axis_index("lat")
    length = 2 * sector
    width = -(-sector // LANES) * LANES
    radix = length // LANES
    upward = [(i, i + 1) for i in range(lat_count - 1)]
    downward = [(i + 1, i) for i in range(lat_count - 1)]
    swap = [(0, 1), (1, 0)]

    whole = pl.BlockSpec(memory_space=pltpu.VMEM)
    in_hbm = pl.BlockSpec(memory_space=pltpu.HBM)
    scalars = pl.BlockSpec(memory_space=pltpu.SMEM)
    up, down = pl.pallas_call(
        functools.partial(pack_kernel, rows, levels),
        in_specs=[in_hbm, in_hbm],
        out_specs=[whole, whole],
        out_shape=[
            jax.ShapeDtypeStruct((levels * tracer_count, length), f32),
            jax.ShapeDtypeStruct((levels * tracer_count + levels // 2, length), f32),
        ],
        scratch_shapes=[
            pltpu.VMEM(tracers.shape, f32),
            pltpu.VMEM(courant_lat.shape, f32),
            pltpu.SemaphoreType.DMA((tracer_count + 1,)),
        ],
        compiler_params=params(),
        cost_estimate=cost(0, 600_000),
        name="pack",
    )(*(pltpu.with_memory_space_constraint(array, pltpu.HBM) for array in (tracers, courant_lat)))
    from_north = lax.ppermute(down, "lat", downward)
    from_south = lax.ppermute(up, "lat", upward)
    tracers, courant_lat, courant_lon, up, down = lax.optimization_barrier((tracers, courant_lat, courant_lon, up, down))

    by_row = jnp.transpose(tracers, (0, 2, 1, 3))
    lon_by_row = jnp.transpose(courant_lon, (1, 0, 2))
    lat_by_row = jnp.transpose(courant_lat, (1, 0, 2))
    ends = jnp.concatenate([by_row[..., -2:], by_row[..., :2]], axis=-1)
    lon_end = jnp.pad(lon_by_row[..., :1], ((0, 0), (0, 0), (0, 3)))
    sides = lax.ppermute(jnp.concatenate([ends, lon_end[None]], axis=0), "lon", swap)
    gap = jnp.zeros((tracer_count, rows, levels, width - sector - 4), f32)
    padded = jnp.concatenate([by_row, sides[:tracer_count, ..., 2:], gap, sides[:tracer_count, ..., :2]], axis=-1)
    east_courant = jnp.concatenate(
        [lon_by_row, sides[tracer_count, ..., :1], jnp.zeros((rows, levels, width - sector - 1), f32)], axis=-1
    )
    not_pole = jnp.where((lat > 0) | (jnp.arange(rows) > 0), 1.0, 0.0)
    lat_courant = jnp.pad(lat_by_row * not_pole[:, None, None], ((0, 0), (0, 0), (0, width - sector)))
    base, north = pl.pallas_call(
        functools.partial(base_kernel, rows, width),
        grid=(tracer_count,),
        in_specs=[
            pl.BlockSpec((1, rows, levels, width), lambda t: (t, 0, 0, 0)),
            vmem((rows, levels, width)),
            vmem((rows, levels, width)),
        ],
        out_specs=[
            pl.BlockSpec((1, rows, levels, width), lambda t: (t, 0, 0, 0)),
            pl.BlockSpec((1, levels, width), lambda t: (t, 0, 0)),
        ],
        out_shape=[
            jax.ShapeDtypeStruct((tracer_count, rows, levels, width), f32),
            jax.ShapeDtypeStruct((tracer_count, levels, width), f32),
        ],
        compiler_params=params(),
        cost_estimate=cost(0, 3_000_000),
        name="base",
    )(padded, east_courant, lat_courant)

    surface = jnp.pad(surface_flux, ((0, 0), (0, 0), (0, width - sector)))
    decay = decay_rate[:, :, None]
    block_count = rows * sector // BLOCK
    block_of = (np.arange(rows)[:, None] * sector + np.minimum(np.arange(width), sector - 1)[None]) // BLOCK
    owner_of = jnp.repeat(owners.reshape(block_count), BLOCK).reshape(rows, sector)
    owner_of = jnp.pad(owner_of, ((0, 0), (0, width - sector)))
    first, others, numbers, weights = spectral_tables(length)
    row_ids = (lat * rows + jnp.arange(rows)).astype(f32)
    latitude = (-0.5 + (row_ids + 0.5) / (lat_count * rows)) * math.pi
    inverse_sine = np.where(numbers == 0, 1.0, 1.0 / np.where(numbers == 0, 1.0, np.sin(np.pi * numbers / length)))
    ratio = 2.0 * jnp.cos(latitude)[:, None] * jnp.asarray(inverse_sine, f32)[None]
    damping = jnp.where(jnp.asarray(numbers == 0)[None], 1.0, jnp.minimum(1.0, ratio * ratio))
    scale = damping * jnp.asarray(weights, f32)[None]

    base, scale, owner_of, surface, decay = lax.optimization_barrier((base, scale, owner_of, surface, decay))

    half = tracer_count // 2
    keep = (half * lax.axis_index("lon")).reshape(1)
    give = half - keep
    sector_shape = jax.ShapeDtypeStruct((rows, levels, width), f32)
    result_shape = jax.ShapeDtypeStruct((levels, rows, sector), f32)
    out_shape = jax.ShapeDtypeStruct((tracer_count, levels, rows, sector), f32)

    def run_physics(first, energy, last):
        energy_shape = (1, LANES) if last else energy.shape
        *results, energy = pl.pallas_call(
            functools.partial(physics_kernel, levels, sector, lat_count if last else 0),
            in_specs=[scalars] + [whole] * 10,
            out_specs=[whole] * (half + 1),
            out_shape=[sector_shape] * half + [jax.ShapeDtypeStruct(energy_shape, f32)],
            compiler_params=params(),
            cost_estimate=cost(50_000_000, 2_000_000),
            name="physics",
        )(first, base, north, from_south, from_north, lat_courant, surface, mixing, decay, owner_of, energy)
        return results, energy

    given, energy = run_physics(give, jnp.zeros((rows, 8, width), f32), False)
    other = [lax.ppermute(part, "lon", swap) for part in given]
    kept, energy = run_physics(keep, energy, True)

    tables = [jnp.asarray(part) for table in (others, first) for part in split_table(table)]
    distances = [1 << i for i in range(lat_count.bit_length() - 1)]

    def send_energy(energy):
        distance = distances.pop(0)
        return lax.ppermute(energy, "lat", [(i, i ^ distance) for i in range(lat_count)])

    result, received = None, []
    for i in range(half):
        coming = send_energy(energy)
        outputs = [result_shape, sector_shape] + ([out_shape] if i else [])
        outputs = pl.pallas_call(
            functools.partial(filter_kernel, radix, i),
            in_specs=[scalars, scalars] + [whole] * (7 + min(i, 1)),
            out_specs=[whole, whole] + ([in_hbm] if i else []),
            out_shape=outputs,
            scratch_shapes=[
                pltpu.VMEM((rows * levels, 3 * length), jnp.bfloat16),
                pltpu.VMEM((rows * levels, length), f32),
            ]
            + ([pltpu.SemaphoreType.DMA((RESULT_PIECES,))] if i else []),
            compiler_params=params(),
            cost_estimate=cost(2_000_000_000, 6_000_000),
            name="filter",
        )(keep, polar_mask, kept[i], other[i], *tables, scale, *([result] if i else []))
        result, back = outputs[:2]
        coming, result = lax.optimization_barrier((coming, result))
        energy = energy + coming
        energy, back = lax.optimization_barrier((energy, back))
        received.append(lax.ppermute(back, "lon", swap))
        if i + 1 < half:
            energy, kept[i + 1] = lax.optimization_barrier((energy, kept[i + 1]))
        out = outputs[-1]
    coming = send_energy(energy)
    out = pl.pallas_call(
        functools.partial(finish_kernel, half - 1),
        in_specs=[scalars, scalars] + [whole] * (1 + half) + [in_hbm],
        out_specs=in_hbm,
        out_shape=out_shape,
        scratch_shapes=[
            pltpu.VMEM((half,) + result_shape.shape, f32),
            pltpu.SemaphoreType.DMA((half + 1, RESULT_PIECES)),
        ],
        input_output_aliases={3 + half: 0},
        compiler_params=params(),
        cost_estimate=cost(0, 3_000_000),
        name="finish",
    )(keep, give, result, *received, out)
    coming, out = lax.optimization_barrier((coming, out))
    energy = energy + coming
    while distances:
        energy = energy + send_energy(energy)

    owner_energy = lax.dynamic_slice(energy, (0, lat), (1, 1)) / (block_count * BLOCK)
    return out, owner_energy


def solution(mesh):
    placed = (
        P("group", None, "lat", "lon"),
        P("group", "lat", "lon"),
        P("group", "lat", "lon"),
        P("group", "lat", "lon"),
        P(),
        P(),
        P(("group", "lat"), "lon", None, None),
        P(("group", "lat")),
    )
    return jax.shard_map(
        on_device,
        mesh=mesh,
        in_specs=placed,
        out_specs=(P("group", None, "lat", "lon"), P(("group", "lat"), "lon")),
        check_vma=False,
    )
```

```python
import functools
import math

import jax
import jax.numpy as jnp
import numpy as np
from jax import lax
from jax.experimental import pallas as pl
from jax.experimental.pallas import tpu as pltpu
from jax.sharding import PartitionSpec as P

LANES = 128
BLOCK = 128
VMEM_BYTES = 6 * 1024 * 1024
RESULT_PIECES = 4
NEAR = 7.0 / 12.0
FAR = 1.0 / 12.0


def params():
    return pltpu.CompilerParams(vmem_limit_bytes=VMEM_BYTES)


def cost(flops, bytes_accessed):
    return pl.CostEstimate(flops=flops, bytes_accessed=bytes_accessed, transcendentals=0)


def split_high_low(value):
    high = value.astype(jnp.bfloat16)
    low = (value - high.astype(jnp.float32)).astype(jnp.bfloat16)
    return high, low


def split_table(table):
    high = table.astype(jnp.bfloat16.dtype)
    return high, (table - high.astype(np.float64)).astype(jnp.bfloat16.dtype)


def spectral_tables(length):
    radix = length // LANES
    pairs = (radix - 1) // 2
    spot = np.arange(LANES)[:, None]
    number = np.arange(LANES)[None, :]
    is_cosine = number <= LANES // 2
    wave = np.where(is_cosine, number, number - LANES // 2)
    angle = 2.0 * np.pi * ((spot * wave) % LANES) / LANES
    first = np.where(is_cosine, np.cos(angle), np.sin(angle))
    others, numbers = [], [radix * wave[0]]
    weights = [np.where((wave[0] == 0) | (wave[0] == LANES // 2), 1.0, 2.0) / length]
    for residue in range(1, pairs + 1):
        whole = residue + radix * number
        angle = 2.0 * np.pi * ((spot * whole) % length) / length
        cosine, sine = np.cos(angle), np.sin(angle)
        others.append(np.block([[cosine, -sine], [sine, cosine]]))
        folded = np.minimum(whole[0], length - whole[0])
        numbers += [folded, folded]
        weights.append(np.full(2 * LANES, 2.0 / length))
    forward = np.concatenate(others), first
    inverse = np.concatenate([table.T for table in others]), first.T
    return forward, inverse, np.concatenate(numbers), np.concatenate(weights)


def pack_rows(first, second):
    return jnp.concatenate([first, second], axis=1)


def second_half(packed, sector):
    skip, shift = sector // LANES, sector % LANES
    segments = [packed[:, LANES * i : LANES * (i + 1)] for i in range(packed.shape[1] // LANES)]
    if shift == 0:
        return jnp.concatenate(segments[skip:], axis=1)
    turned = [pltpu.roll(segment, LANES - shift, 1) for segment in segments[skip:]]
    lane = lax.broadcasted_iota(jnp.int32, turned[0].shape, 1)
    parts = [jnp.where(lane < LANES - shift, turned[i], turned[min(i + 1, len(turned) - 1)]) for i in range(len(turned))]
    return jnp.concatenate(parts, axis=1)


def pack_kernel(rows, levels, tracer_hbm, courant_hbm, up_ref, down_ref, tracer_ref, courant_ref, sems):
    tracer_count = tracer_ref.shape[0]
    copies = [pltpu.make_async_copy(tracer_hbm.at[t], tracer_ref.at[t], sems.at[t]) for t in range(tracer_count)]
    copies.append(pltpu.make_async_copy(courant_hbm, courant_ref, sems.at[tracer_count]))
    for copy in copies:
        copy.start()
    for t in range(tracer_count):
        copies[t].wait()
        place = slice(levels * t, levels * (t + 1))
        up_ref[place, :] = pack_rows(tracer_ref[t, :, rows - 2, :], tracer_ref[t, :, rows - 1, :])
        down_ref[place, :] = pack_rows(tracer_ref[t, :, 0, :], tracer_ref[t, :, 1, :])
    copies[tracer_count].wait()
    courant = courant_ref[:, 0, :]
    down_ref[levels * tracer_count :, :] = pack_rows(courant[: levels // 2], courant[levels // 2 :])


def base_kernel(width, not_pole_ref, tracer_hbm, lat_hbm, lon_hbm, side_ref, base_ref, north_ref, courant_ref, *scratch):
    tracer_ref, lat_ref, lon_ref, sems = scratch
    tracer_count, levels, rows, sector = tracer_ref.shape
    whole = sector // LANES * LANES
    copies = [pltpu.make_async_copy(source, target, sems.at[i]) for i, (source, target) in enumerate(((lat_hbm, lat_ref), (lon_hbm, lon_ref)))]
    copies += [pltpu.make_async_copy(tracer_hbm.at[t], tracer_ref.at[t], sems.at[t + 2]) for t in range(tracer_count)]
    for copy in copies:
        copy.start()

    def beside(values, side):
        return jnp.concatenate([values[:, :whole], values[:, whole:], side[:, sector - whole :]], axis=1)

    copies[0].wait()
    copies[1].wait()
    nothing = jnp.zeros((levels, LANES), jnp.float32)
    for r in range(rows):
        courant = lat_ref[:, r, :] if r else lat_ref[:, r, :] * not_pole_ref[0]
        courant_ref[r] = beside(courant, nothing)
    for t in range(tracer_count):
        copies[t + 2].wait()
        q = [beside(tracer_ref[t, :, r, :], side_ref[t, r]) for r in range(rows)]
        north_ref[t] = NEAR * q[3] - FAR * q[2]
        own_flux = [
            courant_ref[0] * (NEAR * q[0] - FAR * q[1]),
            courant_ref[1] * (NEAR * (q[1] + q[0]) - FAR * q[2]),
            courant_ref[2] * (NEAR * (q[2] + q[1]) - FAR * (q[3] + q[0])),
            courant_ref[3] * (NEAR * (q[3] + q[2]) - FAR * q[1]),
        ]
        for r in range(rows):
            west, west2, east = pltpu.roll(q[r], 1, 1), pltpu.roll(q[r], 2, 1), pltpu.roll(q[r], width - 1, 1)
            flux = beside(lon_ref[:, r, :], side_ref[tracer_count, r]) * (NEAR * (q[r] + west) - FAR * (east + west2))
            value = q[r] - (pltpu.roll(flux, width - 1, 1) - flux) + own_flux[r]
            if r + 1 < rows:
                value = value - own_flux[r + 1]
            base_ref[t, r] = value


def physics_kernel(levels, sector, owner_count, first_ref, *refs):
    base_ref, north_ref, low_ref, high_ref, courant_ref, surface_ref, mixing_ref, decay_ref, owner_ref, energy_in_ref = refs[:10]
    physics_refs, energy_ref = refs[10:-1], refs[-1]
    if len(physics_refs) == 1:
        physics_refs = [physics_refs[0].at[i] for i in range(physics_refs[0].shape[0])]
    rows, width = base_ref.shape[1], base_ref.shape[-1]
    courant = [courant_ref[r] for r in range(rows)]
    top = high_ref[high_ref.shape[0] - levels // 2 :, :]
    top = jnp.concatenate([top[:, :width], second_half(top, sector)], axis=0)
    mix_high, mix_low = split_high_low(mixing_ref[...])
    mix = jnp.concatenate([mix_high, mix_high, mix_low, mix_low], axis=1)
    level = lax.broadcasted_iota(jnp.int32, (8, width), 0)
    lane = lax.broadcasted_iota(jnp.int32, (8, width), 1)
    energies = [energy_in_ref[r] for r in range(rows)]
    for i, physics_ref in enumerate(physics_refs):
        t = first_ref[0] + i
        place = pl.ds(pl.multiple_of(levels * t, levels), levels)
        low, high = low_ref[place, :], high_ref[place, :]
        low_a, low_b = low[:, :width], second_half(low, sector)
        high_a, high_b = high[:, :width], second_half(high, sector)
        south = courant[0] * (NEAR * low_b - FAR * low_a)
        south_in = courant[1] * (FAR * low_b)
        north_in = courant[3] * (FAR * high_a)
        north = top * (NEAR * high_a - FAR * high_b + north_ref[t])
        extra = [south + south_in, -south_in, north_in, -north_in - north]
        for r in range(rows):
            advected = base_ref[t, r] + extra[r]
            part_high, part_low = split_high_low(advected)
            stacked = jnp.concatenate([part_high, part_low, part_high, part_low], axis=0)
            mixed = jnp.dot(mix, stacked, preferred_element_type=jnp.float32)
            surface = jnp.where(level == 7, surface_ref[t, r : r + 1, :], 0.0)
            mixed = jnp.concatenate([mixed[: levels - 8], mixed[levels - 8 :] + surface], axis=0)
            physics = mixed / (1.0 + decay_ref[t] * mixed * mixed)
            physics_ref[r] = physics
            gap = physics - advected
            squared = gap * gap
            for k in range(levels // 8):
                energies[r] = energies[r] + squared[8 * k : 8 * k + 8]
    if not owner_count:
        for r in range(rows):
            energy_ref[r] = energies[r]
        return
    energies = [jnp.where(lane < sector, energy, 0.0) for energy in energies]
    spot = lax.broadcasted_iota(jnp.int32, (1, LANES), 1)
    result = jnp.zeros((1, LANES), jnp.float32)
    for owner in range(owner_count):
        chosen = jnp.zeros((8, LANES), jnp.float32)
        for r in range(rows):
            picked = jnp.where(owner_ref[r : r + 1, :] == owner, energies[r], 0.0)
            for k in range(width // LANES):
                chosen = chosen + picked[:, LANES * k : LANES * (k + 1)]
        total = jnp.sum(jnp.sum(chosen, axis=0, keepdims=True), axis=1, keepdims=True)
        result = jnp.where(spot == owner, total, result)
    energy_ref[...] = result


def send_result(result_ref, out_hbm, tracer, sems):
    piece = result_ref.shape[0] // RESULT_PIECES
    copies = []
    for part in range(RESULT_PIECES):
        span = pl.ds(piece * part, piece)
        copies.append(pltpu.make_async_copy(result_ref.at[span], out_hbm.at[tracer, span], sems.at[part]))
        copies[-1].start()
    return copies


def waves_of(radix):
    pairs = (radix - 1) // 2
    cosine = lambda k, i: math.cos(2.0 * math.pi * ((k * i) % radix) / radix)
    sine = lambda k, i: math.sin(2.0 * math.pi * ((k * i) % radix) / radix)
    return pairs, cosine, sine


def stacked_table(high_ref, low_ref, begin, size):
    high = high_ref[begin : begin + size, :]
    return jnp.concatenate([high, high, low_ref[begin : begin + size, :]], axis=0)


def product_of(high_ref, low_ref, begin, size, table):
    high = high_ref[:, begin : begin + size]
    stacked = jnp.concatenate([high, low_ref[:, begin : begin + size], high], axis=1)
    return jnp.dot(stacked, table, preferred_element_type=jnp.float32)


def forward_kernel(radix, count, *refs):
    own_refs, refs = refs[:count], refs[count:]
    other_ref, table_high_ref, table_low_ref, first_high_ref, first_low_ref, scale_ref = refs[:6]
    out_high_ref, out_low_ref, high_ref, low_ref = refs[6:]
    rows, levels, width = own_refs[0].shape
    pairs, cosine, sine = waves_of(radix)
    segments = width // LANES
    shift = radix * LANES // 2 % LANES
    lane = lax.broadcasted_iota(jnp.int32, (levels, LANES), 1)

    def store(place, column, wave):
        high_ref[place, column : column + LANES], low_ref[place, column : column + LANES] = split_high_low(wave)

    for i, own_ref in enumerate(own_refs):
        for r in range(rows):
            place = slice(levels * (rows * i + r), levels * (rows * i + r + 1))
            own = [own_ref[r, :, LANES * n : LANES * (n + 1)] for n in range(segments)]
            turned = [pltpu.roll(other_ref[i, r, :, LANES * n : LANES * (n + 1)], shift, 1) for n in range(segments)]
            joined = own[:-1] + [jnp.where(lane < shift, own[-1], turned[0])]
            joined += [jnp.where(lane < shift, turned[n], turned[n + 1]) for n in range(segments - 1)]
            plus = [joined[n] + joined[radix - n] for n in range(1, pairs + 1)]
            minus = [joined[radix - n] - joined[n] for n in range(1, pairs + 1)]
            store(place, 0, sum(plus, joined[0]))
            for k in range(1, pairs + 1):
                real = sum((cosine(k, n) * plus[n - 1] for n in range(1, pairs + 1)), joined[0])
                imaginary = sine(k, 1) * minus[0]
                for n in range(2, pairs + 1):
                    imaginary = imaginary + sine(k, n) * minus[n - 1]
                store(place, LANES * (2 * k - 1), real)
                store(place, LANES * 2 * k, imaginary)

    def transform(begin, size, table):
        spectrum = product_of(high_ref, low_ref, begin, size, table)
        for i in range(count * rows):
            place = slice(levels * i, levels * (i + 1))
            damped = spectrum[place] * scale_ref[i % rows : i % rows + 1, begin : begin + size]
            out_high_ref[place, begin : begin + size], out_low_ref[place, begin : begin + size] = split_high_low(damped)

    transform(0, LANES, stacked_table(first_high_ref, first_low_ref, 0, LANES))
    for k in range(pairs):
        transform(LANES * (2 * k + 1), 2 * LANES, stacked_table(table_high_ref, table_low_ref, 2 * LANES * k, 2 * LANES))


def inverse_kernel(radix, count, mask_ref, *refs):
    own_refs, refs = refs[:count], refs[count:]
    other_ref, high_ref, low_ref, table_high_ref, table_low_ref, first_high_ref, first_low_ref = refs[:7]
    result_refs, back_ref, wave_ref = refs[7 : 7 + count], refs[7 + count], refs[8 + count]
    rows, levels, width = own_refs[0].shape
    sector = result_refs[0].shape[-1]
    pairs, cosine, sine = waves_of(radix)
    segments = width // LANES
    shift = radix * LANES // 2 % LANES
    lane = lax.broadcasted_iota(jnp.int32, (levels, LANES), 1)

    def transform(begin, size, table):
        wave_ref[:, begin : begin + size] = product_of(high_ref, low_ref, begin, size, table)

    transform(0, LANES, stacked_table(first_high_ref, first_low_ref, 0, LANES))
    for k in range(pairs):
        transform(LANES * (2 * k + 1), 2 * LANES, stacked_table(table_high_ref, table_low_ref, 2 * LANES * k, 2 * LANES))

    for i, (own_ref, result_ref) in enumerate(zip(own_refs, result_refs)):
        for r in range(rows):
            place = slice(levels * (rows * i + r), levels * (rows * i + r + 1))
            waves = [wave_ref[place, LANES * n : LANES * (n + 1)] for n in range(radix)]
            results = [None] * radix
            results[0] = sum((waves[2 * k - 1] for k in range(1, pairs + 1)), waves[0])
            for n in range(1, pairs + 1):
                even = sum((cosine(k, n) * waves[2 * k - 1] for k in range(1, pairs + 1)), waves[0])
                odd = sine(1, n) * waves[2]
                for k in range(2, pairs + 1):
                    odd = odd + sine(k, n) * waves[2 * k]
                results[n], results[radix - n] = even - odd, even + odd
            filtered_row = mask_ref[r] == 1
            turned = [pltpu.roll(result, LANES - shift, 1) for result in results[segments - 1 :]]
            for n in range(segments):
                begin = LANES * n
                size = min(LANES, sector - begin)
                value = jnp.where(filtered_row, results[n], own_ref[r, :, begin : begin + LANES])
                result_ref[:, r, begin : begin + size] = value[:, :size]
                value = jnp.where(lane < LANES - shift, turned[n], turned[min(n + 1, segments - 1)])
                back_ref[i, r, :, begin : begin + LANES] = jnp.where(
                    filtered_row, value, other_ref[i, r, :, begin : begin + LANES]
                )


def finish_kernel(keep_ref, give_ref, *refs):
    result_refs, (received_ref, out_hbm, turned_ref, sems) = refs[:-4], refs[-4:]
    count, rows, levels, width = received_ref.shape
    sector = out_hbm.shape[-1]
    piece = levels // RESULT_PIECES
    copies = []

    def send(source_ref, tracer, slot):
        for part in range(RESULT_PIECES):
            span = pl.ds(piece * part, piece)
            copies.append(pltpu.make_async_copy(source_ref.at[span], out_hbm.at[tracer, span], sems.at[slot, part]))
            copies[-1].start()

    for i, result_ref in enumerate(result_refs):
        send(result_ref, keep_ref[0] + i, i)
    for i in range(count):
        for r in range(rows):
            turned_ref[i, :, r, :] = received_ref[i, r, :, :sector]
        send(turned_ref.at[i], give_ref[0] + i, count + i)
    for copy in copies:
        copy.wait()


def on_device(tracers, courant_lat, courant_lon, surface_flux, mixing, decay_rate, owners, polar_mask):
    tracer_count, levels, rows, sector = tracers.shape
    assert rows == 4 and sector % 64 == 0 and lax.axis_size("lon") == 2
    f32 = jnp.float32
    lat_count, lat = lax.axis_size("lat"), lax.axis_index("lat")
    length = 2 * sector
    width = -(-sector // LANES) * LANES
    radix = length // LANES
    upward = [(i, i + 1) for i in range(lat_count - 1)]
    downward = [(i + 1, i) for i in range(lat_count - 1)]
    swap = [(0, 1), (1, 0)]

    whole = pl.BlockSpec(memory_space=pltpu.VMEM)
    in_hbm = pl.BlockSpec(memory_space=pltpu.HBM)
    scalars = pl.BlockSpec(memory_space=pltpu.SMEM)
    up, down = pl.pallas_call(
        functools.partial(pack_kernel, rows, levels),
        in_specs=[in_hbm, in_hbm],
        out_specs=[whole, whole],
        out_shape=[
            jax.ShapeDtypeStruct((levels * tracer_count, length), f32),
            jax.ShapeDtypeStruct((levels * tracer_count + levels // 2, length), f32),
        ],
        scratch_shapes=[
            pltpu.VMEM(tracers.shape, f32),
            pltpu.VMEM(courant_lat.shape, f32),
            pltpu.SemaphoreType.DMA((tracer_count + 1,)),
        ],
        compiler_params=params(),
        cost_estimate=cost(0, 600_000),
        name="pack",
    )(*(pltpu.with_memory_space_constraint(array, pltpu.HBM) for array in (tracers, courant_lat)))
    from_north = lax.ppermute(down, "lat", downward)
    from_south = lax.ppermute(up, "lat", upward)
    tracers, courant_lat, courant_lon, up, down = lax.optimization_barrier((tracers, courant_lat, courant_lon, up, down))

    ends = [jnp.concatenate([tracers[..., -2:], tracers[..., :2]], axis=-1), jnp.pad(courant_lon[None, ..., :1], ((0, 0),) * 3 + ((2, 1),))]
    sides = lax.ppermute(jnp.concatenate(ends, axis=0), "lon", swap)
    sides = jnp.transpose(sides, (0, 2, 1, 3))
    gap = jnp.zeros(sides.shape[:-1] + (width - sector - 4,), f32)
    sides = jnp.concatenate([jnp.zeros(sides.shape[:-1] + (LANES + sector - width,), f32), sides[..., 2:], gap, sides[..., :2]], axis=-1)
    not_pole = (lat > 0).astype(f32).reshape(1)
    base, north, lat_courant = pl.pallas_call(
        functools.partial(base_kernel, width),
        in_specs=[scalars, in_hbm, in_hbm, in_hbm, whole],
        out_specs=[whole] * 3,
        out_shape=[
            jax.ShapeDtypeStruct((tracer_count, rows, levels, width), f32),
            jax.ShapeDtypeStruct((tracer_count, levels, width), f32),
            jax.ShapeDtypeStruct((rows, levels, width), f32),
        ],
        scratch_shapes=[
            pltpu.VMEM(tracers.shape, f32),
            pltpu.VMEM(courant_lat.shape, f32),
            pltpu.VMEM(courant_lon.shape, f32),
            pltpu.SemaphoreType.DMA((tracer_count + 2,)),
        ],
        compiler_params=params(),
        cost_estimate=cost(0, 3_000_000),
        name="base",
    )(not_pole, *(pltpu.with_memory_space_constraint(array, pltpu.HBM) for array in (tracers, courant_lat, courant_lon)), sides)

    surface = jnp.pad(surface_flux, ((0, 0), (0, 0), (0, width - sector)))
    decay = decay_rate[:, :, None]
    block_count = rows * sector // BLOCK
    block_of = (np.arange(rows)[:, None] * sector + np.minimum(np.arange(width), sector - 1)[None]) // BLOCK
    owner_of = jnp.repeat(owners.reshape(block_count), BLOCK).reshape(rows, sector)
    owner_of = jnp.pad(owner_of, ((0, 0), (0, width - sector)))
    forward, inverse, numbers, weights = spectral_tables(length)
    row_ids = (lat * rows + jnp.arange(rows)).astype(f32)
    latitude = (-0.5 + (row_ids + 0.5) / (lat_count * rows)) * math.pi
    inverse_sine = np.where(numbers == 0, 1.0, 1.0 / np.where(numbers == 0, 1.0, np.sin(np.pi * numbers / length)))
    ratio = 2.0 * jnp.cos(latitude)[:, None] * jnp.asarray(inverse_sine, f32)[None]
    damping = jnp.where(jnp.asarray(numbers == 0)[None], 1.0, jnp.minimum(1.0, ratio * ratio))
    scale = damping * jnp.asarray(weights, f32)[None]

    base, scale, owner_of, surface, decay = lax.optimization_barrier((base, scale, owner_of, surface, decay))

    half = tracer_count // 2
    keep = (half * lax.axis_index("lon")).reshape(1)
    give = half - keep
    circles = jax.ShapeDtypeStruct((half, rows, levels, width), f32)
    result_shape = jax.ShapeDtypeStruct((levels, rows, sector), f32)
    spectra = jax.ShapeDtypeStruct((half * rows * levels, length), jnp.bfloat16)
    out_shape = jax.ShapeDtypeStruct(tracers.shape, f32)

    def run_physics(first, energy, shapes, last):
        shapes = shapes + [jax.ShapeDtypeStruct((1, LANES) if last else energy.shape, f32)]
        *results, energy = pl.pallas_call(
            functools.partial(physics_kernel, levels, sector, lat_count if last else 0),
            in_specs=[scalars] + [whole] * 10,
            out_specs=[whole] * len(shapes),
            out_shape=shapes,
            compiler_params=params(),
            cost_estimate=cost(50_000_000, 2_000_000),
            name="physics",
        )(first, base, north, from_south, from_north, lat_courant, surface, mixing, decay, owner_of, energy)
        return results, energy

    (given,), energy = run_physics(give, jnp.zeros((rows, 8, width), f32), [circles], False)
    other = lax.ppermute(given, "lon", swap)
    kept, energy = run_physics(keep, energy, [jax.ShapeDtypeStruct(circles.shape[1:], f32)] * half, True)

    forward, inverse = ([jnp.asarray(part) for table in tables for part in split_table(table)] for tables in (forward, inverse))
    distances = [1 << i for i in range(lat_count.bit_length() - 1)]

    def send_energy(energy):
        distance = distances.pop(0)
        return lax.ppermute(energy, "lat", [(i, i ^ distance) for i in range(lat_count)])

    coming = send_energy(energy)
    high, low = pl.pallas_call(
        functools.partial(forward_kernel, radix, half),
        in_specs=[whole] * (half + 6),
        out_specs=[whole] * 2,
        out_shape=[spectra] * 2,
        scratch_shapes=[pltpu.VMEM(spectra.shape, jnp.bfloat16)] * 2,
        compiler_params=params(),
        cost_estimate=cost(2_000_000_000, 6_000_000),
        name="forward",
    )(*kept, other, *forward, scale)
    coming, high = lax.optimization_barrier((coming, high))
    energy = energy + coming
    energy, high = lax.optimization_barrier((energy, high))

    coming = send_energy(energy)
    *results, back = pl.pallas_call(
        functools.partial(inverse_kernel, radix, half),
        in_specs=[scalars] + [whole] * (half + 7),
        out_specs=[whole] * (half + 1),
        out_shape=[result_shape] * half + [circles],
        scratch_shapes=[pltpu.VMEM(spectra.shape, f32)],
        compiler_params=params(),
        cost_estimate=cost(2_000_000_000, 6_000_000),
        name="inverse",
    )(polar_mask, *kept, other, high, low, *inverse)
    coming, back = lax.optimization_barrier((coming, back))
    energy = energy + coming
    energy, back = lax.optimization_barrier((energy, back))
    received = lax.ppermute(back, "lon", swap)

    coming = send_energy(energy)
    out = pl.pallas_call(
        finish_kernel,
        in_specs=[scalars] * 2 + [whole] * (half + 1),
        out_specs=in_hbm,
        out_shape=out_shape,
        scratch_shapes=[
            pltpu.VMEM((half,) + result_shape.shape, f32),
            pltpu.SemaphoreType.DMA((2 * half, RESULT_PIECES)),
        ],
        compiler_params=params(),
        cost_estimate=cost(0, 3_000_000),
        name="finish",
    )(keep, give, *results, received)
    coming, out = lax.optimization_barrier((coming, out))
    energy = energy + coming
    while distances:
        energy = energy + send_energy(energy)

    owner_energy = lax.dynamic_slice(energy, (0, lat), (1, 1)) / (block_count * BLOCK)
    return out, owner_energy


def solution(mesh):
    placed = (
        P("group", None, "lat", "lon"),
        P("group", "lat", "lon"),
        P("group", "lat", "lon"),
        P("group", "lat", "lon"),
        P(),
        P(),
        P(("group", "lat"), "lon", None, None),
        P(("group", "lat")),
    )
    return jax.shard_map(
        on_device,
        mesh=mesh,
        in_specs=placed,
        out_specs=(P("group", None, "lat", "lon"), P(("group", "lat"), "lon")),
        check_vma=False,
    )
```

```python
import functools
import math

import jax
import jax.numpy as jnp
import numpy as np
from jax import lax
from jax.experimental import pallas as pl
from jax.experimental.pallas import tpu as pltpu
from jax.sharding import PartitionSpec as P

LANES = 128
BLOCK = 128
VMEM_BYTES = 6 * 1024 * 1024
RESULT_PIECES = 4
NEAR = 7.0 / 12.0
FAR = 1.0 / 12.0


def params():
    return pltpu.CompilerParams(vmem_limit_bytes=VMEM_BYTES)


def cost(flops, bytes_accessed):
    return pl.CostEstimate(flops=flops, bytes_accessed=bytes_accessed, transcendentals=0)


def split_high_low(value):
    high = value.astype(jnp.bfloat16)
    low = (value - high.astype(jnp.float32)).astype(jnp.bfloat16)
    return high, low


def split_table(table):
    high = table.astype(jnp.bfloat16.dtype)
    return high, (table - high.astype(np.float64)).astype(jnp.bfloat16.dtype)


def spectral_tables(length):
    radix = length // LANES
    pairs = (radix - 1) // 2
    spot = np.arange(LANES)[:, None]
    number = np.arange(LANES)[None, :]
    is_cosine = number <= LANES // 2
    wave = np.where(is_cosine, number, number - LANES // 2)
    angle = 2.0 * np.pi * ((spot * wave) % LANES) / LANES
    first = np.where(is_cosine, np.cos(angle), np.sin(angle))
    others, numbers = [], [radix * wave[0]]
    weights = [np.where((wave[0] == 0) | (wave[0] == LANES // 2), 1.0, 2.0) / length]
    for residue in range(1, pairs + 1):
        whole = residue + radix * number
        angle = 2.0 * np.pi * ((spot * whole) % length) / length
        cosine, sine = np.cos(angle), np.sin(angle)
        others.append(np.block([[cosine, -sine], [sine, cosine]]))
        folded = np.minimum(whole[0], length - whole[0])
        numbers += [folded, folded]
        weights.append(np.full(2 * LANES, 2.0 / length))
    forward = np.concatenate(others), first
    inverse = np.concatenate([table.T for table in others]), first.T
    return forward, inverse, np.concatenate(numbers), np.concatenate(weights)


def pack_rows(first, second):
    return jnp.concatenate([first, second], axis=1)


def second_half(packed, sector):
    skip, shift = sector // LANES, sector % LANES
    segments = [packed[:, LANES * i : LANES * (i + 1)] for i in range(packed.shape[1] // LANES)]
    if shift == 0:
        return jnp.concatenate(segments[skip:], axis=1)
    turned = [pltpu.roll(segment, LANES - shift, 1) for segment in segments[skip:]]
    lane = lax.broadcasted_iota(jnp.int32, turned[0].shape, 1)
    parts = [jnp.where(lane < LANES - shift, turned[i], turned[min(i + 1, len(turned) - 1)]) for i in range(len(turned))]
    return jnp.concatenate(parts, axis=1)


def start_copies(pairs, sems):
    copies = [pltpu.make_async_copy(source, target, sems.at[i]) for i, (source, target) in enumerate(pairs)]
    for copy in copies:
        copy.start()
    return copies


def pack_halo(tracer_ref, t, out_ref, upward):
    levels, rows = tracer_ref.shape[1:3]
    place = slice(levels * t, levels * (t + 1))

    @pl.when(upward)
    def _():
        out_ref[place, :] = pack_rows(tracer_ref[t, :, rows - 2, :], tracer_ref[t, :, rows - 1, :])

    @pl.when(jnp.logical_not(upward))
    def _():
        out_ref[place, :] = pack_rows(tracer_ref[t, :, 0, :], tracer_ref[t, :, 1, :])


def pack_kernel(even_ref, tracer_hbm, lat_hbm, inner_ref, outer_ref, courant_ref, tracer_ref, lat_ref, sems):
    count = tracer_ref.shape[0]
    levels = tracer_ref.shape[1]
    copies = start_copies([(tracer_hbm.at[t], tracer_ref.at[t]) for t in range(count)] + [(lat_hbm, lat_ref)], sems)
    even = even_ref[0] == 1
    for t in range(count):
        copies[t].wait()
        pack_halo(tracer_ref, t, inner_ref, even)
        pack_halo(tracer_ref, t, outer_ref, jnp.logical_not(even))
    copies[count].wait()
    courant = lat_ref[:, 0, :]
    courant_ref[...] = pack_rows(courant[: levels // 2], courant[levels // 2 :])


def side_kernel(tracer_hbm, lon_hbm, side_ref, tracer_ref, lon_ref, sems):
    count, levels, rows, sector = tracer_ref.shape
    copies = start_copies([(tracer_hbm.at[t], tracer_ref.at[t]) for t in range(count)] + [(lon_hbm, lon_ref)], sems)
    shift, whole = sector % LANES, sector // LANES * LANES
    lane = lax.broadcasted_iota(jnp.int32, (levels, LANES), 1)
    for i in range(count + 1):
        copies[i].wait()
        for r in range(rows):
            values = tracer_ref[i, :, r, :] if i < count else lon_ref[:, r, :]
            first = pltpu.roll(values[:, :LANES], shift, 1)
            last = jnp.concatenate([values[:, whole:], values[:, whole:]], axis=1)
            side_ref[i, r] = jnp.where(lane < LANES - 2, first, last)


def base_kernel(width, not_pole_ref, tracer_hbm, lat_hbm, lon_hbm, side_ref, base_ref, north_ref, courant_ref, *scratch):
    tracer_ref, lat_ref, lon_ref, sems = scratch
    tracer_count, levels, rows, sector = tracer_ref.shape
    whole = sector // LANES * LANES
    pairs = [(lat_hbm, lat_ref), (lon_hbm, lon_ref)] + [(tracer_hbm.at[t], tracer_ref.at[t]) for t in range(tracer_count)]
    copies = start_copies(pairs, sems)

    def beside(values, side):
        return jnp.concatenate([values[:, :whole], values[:, whole:], side[:, sector - whole :]], axis=1)

    copies[0].wait()
    copies[1].wait()
    nothing = jnp.zeros((levels, LANES), jnp.float32)
    for r in range(rows):
        courant = lat_ref[:, r, :] if r else lat_ref[:, r, :] * not_pole_ref[0]
        courant_ref[r] = beside(courant, nothing)
    for t in range(tracer_count):
        copies[t + 2].wait()
        q = [beside(tracer_ref[t, :, r, :], side_ref[t, r]) for r in range(rows)]
        north_ref[t] = NEAR * q[3] - FAR * q[2]
        own_flux = [
            courant_ref[0] * (NEAR * q[0] - FAR * q[1]),
            courant_ref[1] * (NEAR * (q[1] + q[0]) - FAR * q[2]),
            courant_ref[2] * (NEAR * (q[2] + q[1]) - FAR * (q[3] + q[0])),
            courant_ref[3] * (NEAR * (q[3] + q[2]) - FAR * q[1]),
        ]
        for r in range(rows):
            west, west2, east = pltpu.roll(q[r], 1, 1), pltpu.roll(q[r], 2, 1), pltpu.roll(q[r], width - 1, 1)
            flux = beside(lon_ref[:, r, :], side_ref[tracer_count, r]) * (NEAR * (q[r] + west) - FAR * (east + west2))
            value = q[r] - (pltpu.roll(flux, width - 1, 1) - flux) + own_flux[r]
            if r + 1 < rows:
                value = value - own_flux[r + 1]
            base_ref[t, r] = value


def physics_kernel(levels, sector, owner_count, first_ref, even_ref, *refs):
    base_ref, north_ref, inner_ref, outer_ref, top_ref, courant_ref, surface_ref, mixing_ref, decay_ref, owner_ref = refs[:10]
    energy_in_ref, physics_refs, energy_ref = refs[10], refs[11:-1], refs[-1]
    if len(physics_refs) == 1:
        physics_refs = [physics_refs[0].at[i] for i in range(physics_refs[0].shape[0])]
    rows, width = base_ref.shape[1], base_ref.shape[-1]
    courant = [courant_ref[r] for r in range(rows)]
    even = even_ref[0] == 1
    top = top_ref[...]
    top = jnp.concatenate([top[:, :width], second_half(top, sector)], axis=0)
    mix_high, mix_low = split_high_low(mixing_ref[...])
    mix = jnp.concatenate([mix_high, mix_high, mix_low, mix_low], axis=1)
    level = lax.broadcasted_iota(jnp.int32, (8, width), 0)
    lane = lax.broadcasted_iota(jnp.int32, (8, width), 1)
    energies = [energy_in_ref[r] for r in range(rows)]
    for i, physics_ref in enumerate(physics_refs):
        t = first_ref[0] + i
        place = pl.ds(pl.multiple_of(levels * t, levels), levels)
        inner, outer = inner_ref[place, :], outer_ref[place, :]
        low, high = jnp.where(even, outer, inner), jnp.where(even, inner, outer)
        low_a, low_b = low[:, :width], second_half(low, sector)
        high_a, high_b = high[:, :width], second_half(high, sector)
        south = courant[0] * (NEAR * low_b - FAR * low_a)
        south_in = courant[1] * (FAR * low_b)
        north_in = courant[3] * (FAR * high_a)
        north = top * (NEAR * high_a - FAR * high_b + north_ref[t])
        extra = [south + south_in, -south_in, north_in, -north_in - north]
        for r in range(rows):
            advected = base_ref[t, r] + extra[r]
            part_high, part_low = split_high_low(advected)
            stacked = jnp.concatenate([part_high, part_low, part_high, part_low], axis=0)
            mixed = jnp.dot(mix, stacked, preferred_element_type=jnp.float32)
            surface = jnp.where(level == 7, surface_ref[t, r : r + 1, :], 0.0)
            mixed = jnp.concatenate([mixed[: levels - 8], mixed[levels - 8 :] + surface], axis=0)
            physics = mixed / (1.0 + decay_ref[t] * mixed * mixed)
            physics_ref[r] = physics
            gap = physics - advected
            squared = gap * gap
            for k in range(levels // 8):
                energies[r] = energies[r] + squared[8 * k : 8 * k + 8]
    if not owner_count:
        for r in range(rows):
            energy_ref[r] = energies[r]
        return
    energies = [jnp.where(lane < sector, energy, 0.0) for energy in energies]
    spot = lax.broadcasted_iota(jnp.int32, (1, LANES), 1)
    result = jnp.zeros((1, LANES), jnp.float32)
    for owner in range(owner_count):
        chosen = jnp.zeros((8, LANES), jnp.float32)
        for r in range(rows):
            picked = jnp.where(owner_ref[r : r + 1, :] == owner, energies[r], 0.0)
            for k in range(width // LANES):
                chosen = chosen + picked[:, LANES * k : LANES * (k + 1)]
        total = jnp.sum(jnp.sum(chosen, axis=0, keepdims=True), axis=1, keepdims=True)
        result = jnp.where(spot == owner, total, result)
    energy_ref[...] = result


def send_result(result_ref, out_hbm, tracer, sems):
    piece = result_ref.shape[0] // RESULT_PIECES
    copies = []
    for part in range(RESULT_PIECES):
        span = pl.ds(piece * part, piece)
        copies.append(pltpu.make_async_copy(result_ref.at[span], out_hbm.at[tracer, span], sems.at[part]))
        copies[-1].start()
    return copies


def waves_of(radix):
    pairs = (radix - 1) // 2
    cosine = lambda k, i: math.cos(2.0 * math.pi * ((k * i) % radix) / radix)
    sine = lambda k, i: math.sin(2.0 * math.pi * ((k * i) % radix) / radix)
    return pairs, cosine, sine


def stacked_table(high_ref, low_ref, begin, size):
    high = high_ref[begin : begin + size, :]
    return jnp.concatenate([high, high, low_ref[begin : begin + size, :]], axis=0)


def product_of(high_ref, low_ref, begin, size, table):
    high = high_ref[:, begin : begin + size]
    stacked = jnp.concatenate([high, low_ref[:, begin : begin + size], high], axis=1)
    return jnp.dot(stacked, table, preferred_element_type=jnp.float32)


def forward_kernel(radix, count, *refs):
    own_refs, refs = refs[:count], refs[count:]
    other_ref, table_high_ref, table_low_ref, first_high_ref, first_low_ref, scale_ref = refs[:6]
    out_high_ref, out_low_ref, high_ref, low_ref = refs[6:]
    rows, levels, width = own_refs[0].shape
    pairs, cosine, sine = waves_of(radix)
    segments = width // LANES
    shift = radix * LANES // 2 % LANES
    lane = lax.broadcasted_iota(jnp.int32, (levels, LANES), 1)

    def store(place, column, wave):
        high_ref[place, column : column + LANES], low_ref[place, column : column + LANES] = split_high_low(wave)

    for i, own_ref in enumerate(own_refs):
        for r in range(rows):
            place = slice(levels * (rows * i + r), levels * (rows * i + r + 1))
            own = [own_ref[r, :, LANES * n : LANES * (n + 1)] for n in range(segments)]
            turned = [pltpu.roll(other_ref[i, r, :, LANES * n : LANES * (n + 1)], shift, 1) for n in range(segments)]
            joined = own[:-1] + [jnp.where(lane < shift, own[-1], turned[0])]
            joined += [jnp.where(lane < shift, turned[n], turned[n + 1]) for n in range(segments - 1)]
            plus = [joined[n] + joined[radix - n] for n in range(1, pairs + 1)]
            minus = [joined[radix - n] - joined[n] for n in range(1, pairs + 1)]
            store(place, 0, sum(plus, joined[0]))
            for k in range(1, pairs + 1):
                real = sum((cosine(k, n) * plus[n - 1] for n in range(1, pairs + 1)), joined[0])
                imaginary = sine(k, 1) * minus[0]
                for n in range(2, pairs + 1):
                    imaginary = imaginary + sine(k, n) * minus[n - 1]
                store(place, LANES * (2 * k - 1), real)
                store(place, LANES * 2 * k, imaginary)

    def transform(begin, size, table):
        spectrum = product_of(high_ref, low_ref, begin, size, table)
        for i in range(count * rows):
            place = slice(levels * i, levels * (i + 1))
            damped = spectrum[place] * scale_ref[i % rows : i % rows + 1, begin : begin + size]
            out_high_ref[place, begin : begin + size], out_low_ref[place, begin : begin + size] = split_high_low(damped)

    transform(0, LANES, stacked_table(first_high_ref, first_low_ref, 0, LANES))
    for k in range(pairs):
        transform(LANES * (2 * k + 1), 2 * LANES, stacked_table(table_high_ref, table_low_ref, 2 * LANES * k, 2 * LANES))


def inverse_kernel(radix, count, mask_ref, *refs):
    own_refs, refs = refs[:count], refs[count:]
    other_ref, high_ref, low_ref, table_high_ref, table_low_ref, first_high_ref, first_low_ref = refs[:7]
    result_refs, back_ref, wave_ref = refs[7 : 7 + count], refs[7 + count], refs[8 + count]
    rows, levels, width = own_refs[0].shape
    sector = result_refs[0].shape[-1]
    pairs, cosine, sine = waves_of(radix)
    segments = width // LANES
    shift = radix * LANES // 2 % LANES
    lane = lax.broadcasted_iota(jnp.int32, (levels, LANES), 1)

    def transform(begin, size, table):
        wave_ref[:, begin : begin + size] = product_of(high_ref, low_ref, begin, size, table)

    transform(0, LANES, stacked_table(first_high_ref, first_low_ref, 0, LANES))
    for k in range(pairs):
        transform(LANES * (2 * k + 1), 2 * LANES, stacked_table(table_high_ref, table_low_ref, 2 * LANES * k, 2 * LANES))

    for i, (own_ref, result_ref) in enumerate(zip(own_refs, result_refs)):
        for r in range(rows):
            place = slice(levels * (rows * i + r), levels * (rows * i + r + 1))
            waves = [wave_ref[place, LANES * n : LANES * (n + 1)] for n in range(radix)]
            results = [None] * radix
            results[0] = sum((waves[2 * k - 1] for k in range(1, pairs + 1)), waves[0])
            for n in range(1, pairs + 1):
                even = sum((cosine(k, n) * waves[2 * k - 1] for k in range(1, pairs + 1)), waves[0])
                odd = sine(1, n) * waves[2]
                for k in range(2, pairs + 1):
                    odd = odd + sine(k, n) * waves[2 * k]
                results[n], results[radix - n] = even - odd, even + odd
            filtered_row = mask_ref[r] == 1
            turned = [pltpu.roll(result, LANES - shift, 1) for result in results[segments - 1 :]]
            for n in range(segments):
                begin = LANES * n
                size = min(LANES, sector - begin)
                value = jnp.where(filtered_row, results[n], own_ref[r, :, begin : begin + LANES])
                result_ref[:, r, begin : begin + size] = value[:, :size]
                value = jnp.where(lane < LANES - shift, turned[n], turned[min(n + 1, segments - 1)])
                back_ref[i, r, :, begin : begin + LANES] = jnp.where(
                    filtered_row, value, other_ref[i, r, :, begin : begin + LANES]
                )


def finish_kernel(keep_ref, give_ref, *refs):
    result_refs, (received_ref, out_hbm, turned_ref, sems) = refs[:-4], refs[-4:]
    count, rows, levels, width = received_ref.shape
    sector = out_hbm.shape[-1]
    piece = levels // RESULT_PIECES
    copies = []

    def send(source_ref, tracer, slot):
        for part in range(RESULT_PIECES):
            span = pl.ds(piece * part, piece)
            copies.append(pltpu.make_async_copy(source_ref.at[span], out_hbm.at[tracer, span], sems.at[slot, part]))
            copies[-1].start()

    for i, result_ref in enumerate(result_refs):
        send(result_ref, keep_ref[0] + i, i)
    for i in range(count):
        for r in range(rows):
            turned_ref[i, :, r, :] = received_ref[i, r, :, :sector]
        send(turned_ref.at[i], give_ref[0] + i, count + i)
    for copy in copies:
        copy.wait()


def on_device(tracers, courant_lat, courant_lon, surface_flux, mixing, decay_rate, owners, polar_mask):
    tracer_count, levels, rows, sector = tracers.shape
    assert rows == 4 and sector % 64 == 0 and lax.axis_size("lon") == 2
    f32 = jnp.float32
    lat_count, lat = lax.axis_size("lat"), lax.axis_index("lat")
    length = 2 * sector
    width = -(-sector // LANES) * LANES
    radix = length // LANES
    downward = [(i + 1, i) for i in range(lat_count - 1)]
    swap = [(0, 1), (1, 0)]

    whole = pl.BlockSpec(memory_space=pltpu.VMEM)
    in_hbm = pl.BlockSpec(memory_space=pltpu.HBM)
    scalars = pl.BlockSpec(memory_space=pltpu.SMEM)
    even = (1 - lat % 2).reshape(1)
    inside = [pair for i in range(0, lat_count - 1, 2) for pair in ((i, i + 1), (i + 1, i))]
    across = [pair for i in range(1, lat_count - 1, 2) for pair in ((i, i + 1), (i + 1, i))]
    fields = [pltpu.with_memory_space_constraint(array, pltpu.HBM) for array in (tracers, courant_lat, courant_lon)]
    field_buffers = [pltpu.VMEM(array.shape, f32) for array in (tracers, courant_lat, courant_lon)]
    inner, outer, courant_row = pl.pallas_call(
        pack_kernel,
        in_specs=[scalars] + [in_hbm] * 2,
        out_specs=[whole] * 3,
        out_shape=[pltpu.VMEM((levels * tracer_count, length), f32)] * 2 + [pltpu.VMEM((levels // 2, length), f32)],
        scratch_shapes=field_buffers[:2] + [pltpu.SemaphoreType.DMA((tracer_count + 1,))],
        compiler_params=params(),
        cost_estimate=cost(0, 600_000),
        name="pack",
    )(even, *fields[:2])
    from_inside = lax.ppermute(inner, "lat", inside)
    from_across = lax.ppermute(outer, "lat", across)
    top = lax.ppermute(courant_row, "lat", downward)

    fields, inner = lax.optimization_barrier((fields, inner))
    fields = [pltpu.with_memory_space_constraint(array, pltpu.HBM) for array in fields]
    sides = pl.pallas_call(
        side_kernel,
        in_specs=[in_hbm] * 2,
        out_specs=whole,
        out_shape=jax.ShapeDtypeStruct((tracer_count + 1, rows, levels, LANES), f32),
        scratch_shapes=[field_buffers[0], field_buffers[2], pltpu.SemaphoreType.DMA((tracer_count + 1,))],
        compiler_params=params(),
        cost_estimate=cost(0, 0),
        name="side",
    )(fields[0], fields[2])
    sides = lax.ppermute(sides, "lon", swap)
    not_pole = (lat > 0).astype(f32).reshape(1)
    base, north, lat_courant = pl.pallas_call(
        functools.partial(base_kernel, width),
        in_specs=[scalars, in_hbm, in_hbm, in_hbm, whole],
        out_specs=[whole] * 3,
        out_shape=[
            jax.ShapeDtypeStruct((tracer_count, rows, levels, width), f32),
            jax.ShapeDtypeStruct((tracer_count, levels, width), f32),
            jax.ShapeDtypeStruct((rows, levels, width), f32),
        ],
        scratch_shapes=field_buffers + [pltpu.SemaphoreType.DMA((tracer_count + 2,))],
        compiler_params=params(),
        cost_estimate=cost(0, 0),
        name="base",
    )(not_pole, *fields, sides)

    surface = jnp.pad(surface_flux, ((0, 0), (0, 0), (0, width - sector)))
    decay = decay_rate[:, :, None]
    block_count = rows * sector // BLOCK
    block_of = (np.arange(rows)[:, None] * sector + np.minimum(np.arange(width), sector - 1)[None]) // BLOCK
    owner_of = jnp.repeat(owners.reshape(block_count), BLOCK).reshape(rows, sector)
    owner_of = jnp.pad(owner_of, ((0, 0), (0, width - sector)))
    forward, inverse, numbers, weights = spectral_tables(length)
    row_ids = (lat * rows + jnp.arange(rows)).astype(f32)
    latitude = (-0.5 + (row_ids + 0.5) / (lat_count * rows)) * math.pi
    inverse_sine = np.where(numbers == 0, 1.0, 1.0 / np.where(numbers == 0, 1.0, np.sin(np.pi * numbers / length)))
    ratio = 2.0 * jnp.cos(latitude)[:, None] * jnp.asarray(inverse_sine, f32)[None]
    damping = jnp.where(jnp.asarray(numbers == 0)[None], 1.0, jnp.minimum(1.0, ratio * ratio))
    scale = damping * jnp.asarray(weights, f32)[None]

    base, scale, owner_of, surface, decay = lax.optimization_barrier((base, scale, owner_of, surface, decay))

    half = tracer_count // 2
    keep = (half * lax.axis_index("lon")).reshape(1)
    give = half - keep
    circles = jax.ShapeDtypeStruct((half, rows, levels, width), f32)
    result_shape = jax.ShapeDtypeStruct((levels, rows, sector), f32)
    spectra = jax.ShapeDtypeStruct((half * rows * levels, length), jnp.bfloat16)
    out_shape = jax.ShapeDtypeStruct(tracers.shape, f32)

    def run_physics(first, energy, shapes, last):
        shapes = shapes + [jax.ShapeDtypeStruct((1, LANES) if last else energy.shape, f32)]
        *results, energy = pl.pallas_call(
            functools.partial(physics_kernel, levels, sector, lat_count if last else 0),
            in_specs=[scalars] * 2 + [whole] * 11,
            out_specs=[whole] * len(shapes),
            out_shape=shapes,
            compiler_params=params(),
            cost_estimate=cost(50_000_000, 2_000_000),
            name="physics",
        )(first, even, base, north, from_inside, from_across, top, lat_courant, surface, mixing, decay, owner_of, energy)
        return results, energy

    (given,), energy = run_physics(give, jnp.zeros((rows, 8, width), f32), [circles], False)
    other = lax.ppermute(given, "lon", swap)
    kept, energy = run_physics(keep, energy, [jax.ShapeDtypeStruct(circles.shape[1:], f32)] * half, True)

    forward, inverse = ([jnp.asarray(part) for table in tables for part in split_table(table)] for tables in (forward, inverse))
    distances = [1 << i for i in range(lat_count.bit_length() - 1)]

    def send_energy(energy):
        distance = distances.pop(0)
        return lax.ppermute(energy, "lat", [(i, i ^ distance) for i in range(lat_count)])

    coming = send_energy(energy)
    high, low = pl.pallas_call(
        functools.partial(forward_kernel, radix, half),
        in_specs=[whole] * (half + 6),
        out_specs=[whole] * 2,
        out_shape=[spectra] * 2,
        scratch_shapes=[pltpu.VMEM(spectra.shape, jnp.bfloat16)] * 2,
        compiler_params=params(),
        cost_estimate=cost(2_000_000_000, 6_000_000),
        name="forward",
    )(*kept, other, *forward, scale)
    coming, high = lax.optimization_barrier((coming, high))
    energy = energy + coming
    energy, high = lax.optimization_barrier((energy, high))

    coming = send_energy(energy)
    *results, back = pl.pallas_call(
        functools.partial(inverse_kernel, radix, half),
        in_specs=[scalars] + [whole] * (half + 7),
        out_specs=[whole] * (half + 1),
        out_shape=[result_shape] * half + [circles],
        scratch_shapes=[pltpu.VMEM(spectra.shape, f32)],
        compiler_params=params(),
        cost_estimate=cost(2_000_000_000, 6_000_000),
        name="inverse",
    )(polar_mask, *kept, other, high, low, *inverse)
    coming, back = lax.optimization_barrier((coming, back))
    energy = energy + coming
    energy, back = lax.optimization_barrier((energy, back))
    received = lax.ppermute(back, "lon", swap)

    coming = send_energy(energy)
    out = pl.pallas_call(
        finish_kernel,
        in_specs=[scalars] * 2 + [whole] * (half + 1),
        out_specs=in_hbm,
        out_shape=out_shape,
        scratch_shapes=[
            pltpu.VMEM((half,) + result_shape.shape, f32),
            pltpu.SemaphoreType.DMA((2 * half, RESULT_PIECES)),
        ],
        compiler_params=params(),
        cost_estimate=cost(0, 3_000_000),
        name="finish",
    )(keep, give, *results, received)
    coming, out = lax.optimization_barrier((coming, out))
    energy = energy + coming
    while distances:
        energy = energy + send_energy(energy)

    owner_energy = lax.dynamic_slice(energy, (0, lat), (1, 1)) / (block_count * BLOCK)
    return out, owner_energy


def solution(mesh):
    placed = (
        P("group", None, "lat", "lon"),
        P("group", "lat", "lon"),
        P("group", "lat", "lon"),
        P("group", "lat", "lon"),
        P(),
        P(),
        P(("group", "lat"), "lon", None, None),
        P(("group", "lat")),
    )
    return jax.shard_map(
        on_device,
        mesh=mesh,
        in_specs=placed,
        out_specs=(P("group", None, "lat", "lon"), P(("group", "lat"), "lon")),
        check_vma=False,
    )
```

```python
import functools
import math

import jax
import jax.numpy as jnp
import numpy as np
from jax import lax
from jax.experimental import pallas as pl
from jax.experimental.pallas import tpu as pltpu
from jax.sharding import PartitionSpec as P

LANES = 128
BLOCK = 128
VMEM_BYTES = 6 * 1024 * 1024
PIECES = 4
NEAR = 7.0 / 12.0
FAR = 1.0 / 12.0


def params():
    return pltpu.CompilerParams(vmem_limit_bytes=VMEM_BYTES)


def cost(flops, bytes_accessed):
    return pl.CostEstimate(flops=flops, bytes_accessed=bytes_accessed, transcendentals=0)


def split_high_low(value):
    high = value.astype(jnp.bfloat16)
    low = (value - high.astype(jnp.float32)).astype(jnp.bfloat16)
    return high, low


def split_table(table):
    high = table.astype(jnp.bfloat16.dtype)
    return high, (table - high.astype(np.float64)).astype(jnp.bfloat16.dtype)


def spectral_tables(length):
    radix = length // LANES
    pairs = (radix - 1) // 2
    spot = np.arange(LANES)[:, None]
    number = np.arange(LANES)[None, :]
    is_cosine = number <= LANES // 2
    wave = np.where(is_cosine, number, number - LANES // 2)
    angle = 2.0 * np.pi * ((spot * wave) % LANES) / LANES
    first = np.where(is_cosine, np.cos(angle), np.sin(angle))
    others, numbers = [], [radix * wave[0]]
    weights = [np.where((wave[0] == 0) | (wave[0] == LANES // 2), 1.0, 2.0) / length]
    for residue in range(1, pairs + 1):
        whole = residue + radix * number
        angle = 2.0 * np.pi * ((spot * whole) % length) / length
        cosine, sine = np.cos(angle), np.sin(angle)
        others.append(np.block([[cosine, -sine], [sine, cosine]]))
        folded = np.minimum(whole[0], length - whole[0])
        numbers += [folded, folded]
        weights.append(np.full(2 * LANES, 2.0 / length))
    forward = np.concatenate(others), first
    inverse = np.concatenate([table.T for table in others]), first.T
    return forward, inverse, np.concatenate(numbers), np.concatenate(weights)


def pack_rows(first, second):
    return jnp.concatenate([first, second], axis=1)


def second_half(packed, sector):
    skip, shift = sector // LANES, sector % LANES
    segments = [packed[:, LANES * i : LANES * (i + 1)] for i in range(packed.shape[1] // LANES)]
    if shift == 0:
        return jnp.concatenate(segments[skip:], axis=1)
    turned = [pltpu.roll(segment, LANES - shift, 1) for segment in segments[skip:]]
    lane = lax.broadcasted_iota(jnp.int32, turned[0].shape, 1)
    parts = [jnp.where(lane < LANES - shift, turned[i], turned[min(i + 1, len(turned) - 1)]) for i in range(len(turned))]
    return jnp.concatenate(parts, axis=1)


def start_copies(pairs, sems):
    copies = [pltpu.make_async_copy(source, target, sems.at[i]) for i, (source, target) in enumerate(pairs)]
    for copy in copies:
        copy.start()
    return copies


def pack_halo(tracer_ref, t, out_ref, slot, upward):
    levels, rows = tracer_ref.shape[1:3]
    place = slice(levels * slot, levels * (slot + 1))

    @pl.when(upward)
    def _():
        out_ref[place, :] = pack_rows(tracer_ref[t, :, rows - 2, :], tracer_ref[t, :, rows - 1, :])

    @pl.when(jnp.logical_not(upward))
    def _():
        out_ref[place, :] = pack_rows(tracer_ref[t, :, 0, :], tracer_ref[t, :, 1, :])


def copies_in_pieces(source, target, sems, pieces):
    size = target.shape[0] // pieces
    spans = [pl.ds(size * i, size) for i in range(pieces)]
    copies = [pltpu.make_async_copy(source.at[span], target.at[span], sems.at[i]) for i, span in enumerate(spans)]
    for copy in copies:
        copy.start()
    return copies


def pack_kernel(even_ref, tracer_hbm, *refs):
    inner_ref, outer_refs, (tracer_ref, sems) = refs[0], refs[1:-2], refs[-2:]
    count = tracer_ref.shape[0]
    copies = [copies_in_pieces(tracer_hbm.at[t], tracer_ref.at[t], sems.at[t], PIECES) for t in range(count)]
    even = even_ref[0] == 1
    share = count // len(outer_refs)
    for t in range(count):
        for copy in copies[t]:
            copy.wait()
        pack_halo(tracer_ref, t, inner_ref, t, even)
        pack_halo(tracer_ref, t, outer_refs[t // share], t % share, jnp.logical_not(even))


def side_kernel(tracer_hbm, lat_hbm, lon_hbm, side_ref, courant_ref, tracer_ref, lat_ref, lon_ref, sems):
    count, levels, rows, sector = tracer_ref.shape
    pairs = [(lat_hbm, lat_ref)] + [(tracer_hbm.at[t], tracer_ref.at[t]) for t in range(count)] + [(lon_hbm, lon_ref)]
    copies = start_copies(pairs, sems)
    shift, whole = sector % LANES, sector // LANES * LANES
    lane = lax.broadcasted_iota(jnp.int32, (levels, LANES), 1)
    copies[0].wait()
    courant = lat_ref[:, 0, :]
    courant_ref[...] = pack_rows(courant[: levels // 2], courant[levels // 2 :])
    for i in range(count + 1):
        copies[i + 1].wait()
        for r in range(rows):
            values = tracer_ref[i, :, r, :] if i < count else lon_ref[:, r, :]
            first = pltpu.roll(values[:, :LANES], shift, 1)
            last = jnp.concatenate([values[:, whole:], values[:, whole:]], axis=1)
            side_ref[i, r] = jnp.where(lane < LANES - 2, first, last)


def base_kernel(width, not_pole_ref, tracer_hbm, lat_hbm, lon_hbm, side_ref, base_ref, north_ref, courant_ref, *scratch):
    tracer_ref, lat_ref, lon_ref, sems = scratch
    tracer_count, levels, rows, sector = tracer_ref.shape
    whole = sector // LANES * LANES
    pairs = [(lat_hbm, lat_ref), (lon_hbm, lon_ref)] + [(tracer_hbm.at[t], tracer_ref.at[t]) for t in range(tracer_count)]
    copies = start_copies(pairs, sems)

    def beside(values, side):
        return jnp.concatenate([values[:, :whole], values[:, whole:], side[:, sector - whole :]], axis=1)

    copies[0].wait()
    copies[1].wait()
    nothing = jnp.zeros((levels, LANES), jnp.float32)
    for r in range(rows):
        courant = lat_ref[:, r, :] if r else lat_ref[:, r, :] * not_pole_ref[0]
        courant_ref[r] = beside(courant, nothing)
    for t in range(tracer_count):
        copies[t + 2].wait()
        q = [beside(tracer_ref[t, :, r, :], side_ref[t, r]) for r in range(rows)]
        north_ref[t] = NEAR * q[3] - FAR * q[2]
        own_flux = [
            courant_ref[0] * (NEAR * q[0] - FAR * q[1]),
            courant_ref[1] * (NEAR * (q[1] + q[0]) - FAR * q[2]),
            courant_ref[2] * (NEAR * (q[2] + q[1]) - FAR * (q[3] + q[0])),
            courant_ref[3] * (NEAR * (q[3] + q[2]) - FAR * q[1]),
        ]
        for r in range(rows):
            west, west2, east = pltpu.roll(q[r], 1, 1), pltpu.roll(q[r], 2, 1), pltpu.roll(q[r], width - 1, 1)
            flux = beside(lon_ref[:, r, :], side_ref[tracer_count, r]) * (NEAR * (q[r] + west) - FAR * (east + west2))
            value = q[r] - (pltpu.roll(flux, width - 1, 1) - flux) + own_flux[r]
            if r + 1 < rows:
                value = value - own_flux[r + 1]
            base_ref[t, r] = value


def physics_kernel(levels, sector, owner_count, first_ref, even_ref, *refs):
    base_ref, north_ref, inner_ref, *outer_refs = refs[:5]
    top_ref, courant_ref, surface_ref, mixing_ref, decay_ref, owner_ref, energy_in_ref = refs[5:12]
    physics_refs, energy_ref = refs[12:-1], refs[-1]
    if len(physics_refs) == 1:
        physics_refs = [physics_refs[0].at[i] for i in range(physics_refs[0].shape[0])]
    rows, width = base_ref.shape[1], base_ref.shape[-1]
    courant = [courant_ref[r] for r in range(rows)]
    even = even_ref[0] == 1
    top = top_ref[...]
    top = jnp.concatenate([top[:, :width], second_half(top, sector)], axis=0)
    mix_high, mix_low = split_high_low(mixing_ref[...])
    mix = jnp.concatenate([mix_high, mix_high, mix_low, mix_low], axis=1)
    level = lax.broadcasted_iota(jnp.int32, (8, width), 0)
    lane = lax.broadcasted_iota(jnp.int32, (8, width), 1)
    energies = [energy_in_ref[r] for r in range(rows)]
    for i, physics_ref in enumerate(physics_refs):
        t = first_ref[0] + i
        inner = inner_ref[pl.ds(pl.multiple_of(levels * t, levels), levels), :]
        outer = [outer_ref[levels * i : levels * (i + 1), :] for outer_ref in outer_refs]
        outer = jnp.where(first_ref[0] == 0, *outer)
        low, high = jnp.where(even, outer, inner), jnp.where(even, inner, outer)
        low_a, low_b = low[:, :width], second_half(low, sector)
        high_a, high_b = high[:, :width], second_half(high, sector)
        south = courant[0] * (NEAR * low_b - FAR * low_a)
        south_in = courant[1] * (FAR * low_b)
        north_in = courant[3] * (FAR * high_a)
        north = top * (NEAR * high_a - FAR * high_b + north_ref[t])
        extra = [south + south_in, -south_in, north_in, -north_in - north]
        for r in range(rows):
            advected = base_ref[t, r] + extra[r]
            part_high, part_low = split_high_low(advected)
            stacked = jnp.concatenate([part_high, part_low, part_high, part_low], axis=0)
            mixed = jnp.dot(mix, stacked, preferred_element_type=jnp.float32)
            surface = jnp.where(level == 7, surface_ref[t, r : r + 1, :], 0.0)
            mixed = jnp.concatenate([mixed[: levels - 8], mixed[levels - 8 :] + surface], axis=0)
            physics = mixed / (1.0 + decay_ref[t] * mixed * mixed)
            physics_ref[r] = physics
            gap = physics - advected
            squared = gap * gap
            for k in range(levels // 8):
                energies[r] = energies[r] + squared[8 * k : 8 * k + 8]
    if not owner_count:
        for r in range(rows):
            energy_ref[r] = energies[r]
        return
    energies = [jnp.where(lane < sector, energy, 0.0) for energy in energies]
    spot = lax.broadcasted_iota(jnp.int32, (1, LANES), 1)
    result = jnp.zeros((1, LANES), jnp.float32)
    for owner in range(owner_count):
        chosen = jnp.zeros((8, LANES), jnp.float32)
        for r in range(rows):
            picked = jnp.where(owner_ref[r : r + 1, :] == owner, energies[r], 0.0)
            for k in range(width // LANES):
                chosen = chosen + picked[:, LANES * k : LANES * (k + 1)]
        total = jnp.sum(jnp.sum(chosen, axis=0, keepdims=True), axis=1, keepdims=True)
        result = jnp.where(spot == owner, total, result)
    energy_ref[...] = result


def send_result(result_ref, out_hbm, tracer, sems):
    piece = result_ref.shape[0] // PIECES
    copies = []
    for part in range(PIECES):
        span = pl.ds(piece * part, piece)
        copies.append(pltpu.make_async_copy(result_ref.at[span], out_hbm.at[tracer, span], sems.at[part]))
        copies[-1].start()
    return copies


def waves_of(radix):
    pairs = (radix - 1) // 2
    cosine = lambda k, i: math.cos(2.0 * math.pi * ((k * i) % radix) / radix)
    sine = lambda k, i: math.sin(2.0 * math.pi * ((k * i) % radix) / radix)
    return pairs, cosine, sine


def stacked_table(high_ref, low_ref, begin, size):
    high = high_ref[begin : begin + size, :]
    return jnp.concatenate([high, high, low_ref[begin : begin + size, :]], axis=0)


def product_of(high_ref, low_ref, begin, size, table):
    high = high_ref[:, begin : begin + size]
    stacked = jnp.concatenate([high, low_ref[:, begin : begin + size], high], axis=1)
    return jnp.dot(stacked, table, preferred_element_type=jnp.float32)


def forward_kernel(radix, count, *refs):
    own_refs, refs = refs[:count], refs[count:]
    other_ref, table_high_ref, table_low_ref, first_high_ref, first_low_ref, scale_ref = refs[:6]
    out_high_ref, out_low_ref, high_ref, low_ref = refs[6:]
    rows, levels, width = own_refs[0].shape
    pairs, cosine, sine = waves_of(radix)
    segments = width // LANES
    shift = radix * LANES // 2 % LANES
    lane = lax.broadcasted_iota(jnp.int32, (levels, LANES), 1)

    def store(place, column, wave):
        high_ref[place, column : column + LANES], low_ref[place, column : column + LANES] = split_high_low(wave)

    for i, own_ref in enumerate(own_refs):
        for r in range(rows):
            place = slice(levels * (rows * i + r), levels * (rows * i + r + 1))
            own = [own_ref[r, :, LANES * n : LANES * (n + 1)] for n in range(segments)]
            turned = [pltpu.roll(other_ref[i, r, :, LANES * n : LANES * (n + 1)], shift, 1) for n in range(segments)]
            joined = own[:-1] + [jnp.where(lane < shift, own[-1], turned[0])]
            joined += [jnp.where(lane < shift, turned[n], turned[n + 1]) for n in range(segments - 1)]
            plus = [joined[n] + joined[radix - n] for n in range(1, pairs + 1)]
            minus = [joined[radix - n] - joined[n] for n in range(1, pairs + 1)]
            store(place, 0, sum(plus, joined[0]))
            for k in range(1, pairs + 1):
                real = sum((cosine(k, n) * plus[n - 1] for n in range(1, pairs + 1)), joined[0])
                imaginary = sine(k, 1) * minus[0]
                for n in range(2, pairs + 1):
                    imaginary = imaginary + sine(k, n) * minus[n - 1]
                store(place, LANES * (2 * k - 1), real)
                store(place, LANES * 2 * k, imaginary)

    def transform(begin, size, table):
        spectrum = product_of(high_ref, low_ref, begin, size, table)
        for i in range(count * rows):
            place = slice(levels * i, levels * (i + 1))
            damped = spectrum[place] * scale_ref[i % rows : i % rows + 1, begin : begin + size]
            out_high_ref[place, begin : begin + size], out_low_ref[place, begin : begin + size] = split_high_low(damped)

    transform(0, LANES, stacked_table(first_high_ref, first_low_ref, 0, LANES))
    for k in range(pairs):
        transform(LANES * (2 * k + 1), 2 * LANES, stacked_table(table_high_ref, table_low_ref, 2 * LANES * k, 2 * LANES))


def inverse_kernel(radix, count, mask_ref, *refs):
    own_refs, refs = refs[:count], refs[count:]
    other_ref, high_ref, low_ref, table_high_ref, table_low_ref, first_high_ref, first_low_ref = refs[:7]
    result_refs, back_ref, wave_ref = refs[7 : 7 + count], refs[7 + count], refs[8 + count]
    rows, levels, width = own_refs[0].shape
    sector = result_refs[0].shape[-1]
    pairs, cosine, sine = waves_of(radix)
    segments = width // LANES
    shift = radix * LANES // 2 % LANES
    lane = lax.broadcasted_iota(jnp.int32, (levels, LANES), 1)

    def transform(begin, size, table):
        wave_ref[:, begin : begin + size] = product_of(high_ref, low_ref, begin, size, table)

    transform(0, LANES, stacked_table(first_high_ref, first_low_ref, 0, LANES))
    for k in range(pairs):
        transform(LANES * (2 * k + 1), 2 * LANES, stacked_table(table_high_ref, table_low_ref, 2 * LANES * k, 2 * LANES))

    for i, (own_ref, result_ref) in enumerate(zip(own_refs, result_refs)):
        for r in range(rows):
            place = slice(levels * (rows * i + r), levels * (rows * i + r + 1))
            waves = [wave_ref[place, LANES * n : LANES * (n + 1)] for n in range(radix)]
            results = [None] * radix
            results[0] = sum((waves[2 * k - 1] for k in range(1, pairs + 1)), waves[0])
            for n in range(1, pairs + 1):
                even = sum((cosine(k, n) * waves[2 * k - 1] for k in range(1, pairs + 1)), waves[0])
                odd = sine(1, n) * waves[2]
                for k in range(2, pairs + 1):
                    odd = odd + sine(k, n) * waves[2 * k]
                results[n], results[radix - n] = even - odd, even + odd
            filtered_row = mask_ref[r] == 1
            turned = [pltpu.roll(result, LANES - shift, 1) for result in results[segments - 1 :]]
            for n in range(segments):
                begin = LANES * n
                size = min(LANES, sector - begin)
                value = jnp.where(filtered_row, results[n], own_ref[r, :, begin : begin + LANES])
                result_ref[:, r, begin : begin + size] = value[:, :size]
                value = jnp.where(lane < LANES - shift, turned[n], turned[min(n + 1, segments - 1)])
                back_ref[i, r, :, begin : begin + LANES] = jnp.where(
                    filtered_row, value, other_ref[i, r, :, begin : begin + LANES]
                )


def finish_kernel(keep_ref, give_ref, *refs):
    result_refs, (received_ref, out_hbm, turned_ref, sems) = refs[:-4], refs[-4:]
    count, rows, levels, width = received_ref.shape
    sector = out_hbm.shape[-1]
    piece = levels // PIECES
    copies = []

    def send(source_ref, tracer, slot):
        for part in range(PIECES):
            span = pl.ds(piece * part, piece)
            copies.append(pltpu.make_async_copy(source_ref.at[span], out_hbm.at[tracer, span], sems.at[slot, part]))
            copies[-1].start()

    for i, result_ref in enumerate(result_refs):
        send(result_ref, keep_ref[0] + i, i)
    for i in range(count):
        for r in range(rows):
            turned_ref[i, :, r, :] = received_ref[i, r, :, :sector]
        send(turned_ref.at[i], give_ref[0] + i, count + i)
    for copy in copies:
        copy.wait()


def on_device(tracers, courant_lat, courant_lon, surface_flux, mixing, decay_rate, owners, polar_mask):
    tracer_count, levels, rows, sector = tracers.shape
    assert rows == 4 and sector % 64 == 0 and lax.axis_size("lon") == 2
    f32 = jnp.float32
    lat_count, lat = lax.axis_size("lat"), lax.axis_index("lat")
    length = 2 * sector
    width = -(-sector // LANES) * LANES
    radix = length // LANES
    downward = [(i + 1, i) for i in range(lat_count - 1)]
    swap = [(0, 1), (1, 0)]

    whole = pl.BlockSpec(memory_space=pltpu.VMEM)
    in_hbm = pl.BlockSpec(memory_space=pltpu.HBM)
    scalars = pl.BlockSpec(memory_space=pltpu.SMEM)
    even = (1 - lat % 2).reshape(1)
    inside = [pair for i in range(0, lat_count - 1, 2) for pair in ((i, i + 1), (i + 1, i))]
    across = [pair for i in range(1, lat_count - 1, 2) for pair in ((i, i + 1), (i + 1, i))]
    fields = [pltpu.with_memory_space_constraint(array, pltpu.HBM) for array in (tracers, courant_lat, courant_lon)]
    field_buffers = [pltpu.VMEM(array.shape, f32) for array in (tracers, courant_lat, courant_lon)]
    half = tracer_count // 2
    inner, *outer = pl.pallas_call(
        pack_kernel,
        in_specs=[scalars, in_hbm],
        out_specs=[whole] * 3,
        out_shape=[pltpu.VMEM((levels * count, length), f32) for count in (tracer_count, half, half)],
        scratch_shapes=[field_buffers[0], pltpu.SemaphoreType.DMA((tracer_count, PIECES))],
        compiler_params=params(),
        cost_estimate=cost(0, 600_000),
        name="pack",
    )(even, fields[0])
    from_inside = lax.ppermute(inner, "lat", inside)
    from_across = [lax.ppermute(part, "lat", across) for part in outer]

    fields, inner = lax.optimization_barrier((fields, inner))
    fields = [pltpu.with_memory_space_constraint(array, pltpu.HBM) for array in fields]
    sides, courant_row = pl.pallas_call(
        side_kernel,
        in_specs=[in_hbm] * 3,
        out_specs=[whole] * 2,
        out_shape=[
            jax.ShapeDtypeStruct((tracer_count + 1, rows, levels, LANES), f32),
            jax.ShapeDtypeStruct((levels // 2, length), f32),
        ],
        scratch_shapes=field_buffers + [pltpu.SemaphoreType.DMA((tracer_count + 2,))],
        compiler_params=params(),
        cost_estimate=cost(0, 0),
        name="side",
    )(*fields)
    top = lax.ppermute(courant_row, "lat", downward)
    sides = lax.ppermute(sides, "lon", swap)
    not_pole = (lat > 0).astype(f32).reshape(1)
    base, north, lat_courant = pl.pallas_call(
        functools.partial(base_kernel, width),
        in_specs=[scalars, in_hbm, in_hbm, in_hbm, whole],
        out_specs=[whole] * 3,
        out_shape=[
            jax.ShapeDtypeStruct((tracer_count, rows, levels, width), f32),
            jax.ShapeDtypeStruct((tracer_count, levels, width), f32),
            jax.ShapeDtypeStruct((rows, levels, width), f32),
        ],
        scratch_shapes=field_buffers + [pltpu.SemaphoreType.DMA((tracer_count + 2,))],
        compiler_params=params(),
        cost_estimate=cost(0, 0),
        name="base",
    )(not_pole, *fields, sides)

    surface = jnp.pad(surface_flux, ((0, 0), (0, 0), (0, width - sector)))
    decay = decay_rate[:, :, None]
    block_count = rows * sector // BLOCK
    block_of = (np.arange(rows)[:, None] * sector + np.minimum(np.arange(width), sector - 1)[None]) // BLOCK
    owner_of = jnp.repeat(owners.reshape(block_count), BLOCK).reshape(rows, sector)
    owner_of = jnp.pad(owner_of, ((0, 0), (0, width - sector)))
    forward, inverse, numbers, weights = spectral_tables(length)
    row_ids = (lat * rows + jnp.arange(rows)).astype(f32)
    latitude = (-0.5 + (row_ids + 0.5) / (lat_count * rows)) * math.pi
    inverse_sine = np.where(numbers == 0, 1.0, 1.0 / np.where(numbers == 0, 1.0, np.sin(np.pi * numbers / length)))
    ratio = 2.0 * jnp.cos(latitude)[:, None] * jnp.asarray(inverse_sine, f32)[None]
    damping = jnp.where(jnp.asarray(numbers == 0)[None], 1.0, jnp.minimum(1.0, ratio * ratio))
    scale = damping * jnp.asarray(weights, f32)[None]

    base, scale, owner_of, surface, decay = lax.optimization_barrier((base, scale, owner_of, surface, decay))

    keep = (half * lax.axis_index("lon")).reshape(1)
    give = half - keep
    circles = jax.ShapeDtypeStruct((half, rows, levels, width), f32)
    result_shape = jax.ShapeDtypeStruct((levels, rows, sector), f32)
    spectra = jax.ShapeDtypeStruct((half * rows * levels, length), jnp.bfloat16)
    out_shape = jax.ShapeDtypeStruct(tracers.shape, f32)

    def run_physics(first, energy, shapes, last):
        shapes = shapes + [jax.ShapeDtypeStruct((1, LANES) if last else energy.shape, f32)]
        *results, energy = pl.pallas_call(
            functools.partial(physics_kernel, levels, sector, lat_count if last else 0),
            in_specs=[scalars] * 2 + [whole] * 12,
            out_specs=[whole] * len(shapes),
            out_shape=shapes,
            compiler_params=params(),
            cost_estimate=cost(50_000_000, 2_000_000),
            name="physics",
        )(first, even, base, north, from_inside, *from_across, top, lat_courant, surface, mixing, decay, owner_of, energy)
        return results, energy

    (given,), energy = run_physics(give, jnp.zeros((rows, 8, width), f32), [circles], False)
    other = lax.ppermute(given, "lon", swap)
    kept, energy = run_physics(keep, energy, [jax.ShapeDtypeStruct(circles.shape[1:], f32)] * half, True)

    forward, inverse = ([jnp.asarray(part) for table in tables for part in split_table(table)] for tables in (forward, inverse))
    distances = [1 << i for i in range(lat_count.bit_length() - 1)]

    def send_energy(energy):
        distance = distances.pop(0)
        return lax.ppermute(energy, "lat", [(i, i ^ distance) for i in range(lat_count)])

    coming = send_energy(energy)
    high, low = pl.pallas_call(
        functools.partial(forward_kernel, radix, half),
        in_specs=[whole] * (half + 6),
        out_specs=[whole] * 2,
        out_shape=[spectra] * 2,
        scratch_shapes=[pltpu.VMEM(spectra.shape, jnp.bfloat16)] * 2,
        compiler_params=params(),
        cost_estimate=cost(2_000_000_000, 6_000_000),
        name="forward",
    )(*kept, other, *forward, scale)
    coming, high = lax.optimization_barrier((coming, high))
    energy = energy + coming
    energy, high = lax.optimization_barrier((energy, high))

    coming = send_energy(energy)
    *results, back = pl.pallas_call(
        functools.partial(inverse_kernel, radix, half),
        in_specs=[scalars] + [whole] * (half + 7),
        out_specs=[whole] * (half + 1),
        out_shape=[result_shape] * half + [circles],
        scratch_shapes=[pltpu.VMEM(spectra.shape, f32)],
        compiler_params=params(),
        cost_estimate=cost(2_000_000_000, 6_000_000),
        name="inverse",
    )(polar_mask, *kept, other, high, low, *inverse)
    coming, back = lax.optimization_barrier((coming, back))
    energy = energy + coming
    energy, back = lax.optimization_barrier((energy, back))
    received = lax.ppermute(back, "lon", swap)

    coming = send_energy(energy)
    out = pl.pallas_call(
        finish_kernel,
        in_specs=[scalars] * 2 + [whole] * (half + 1),
        out_specs=in_hbm,
        out_shape=out_shape,
        scratch_shapes=[
            pltpu.VMEM((half,) + result_shape.shape, f32),
            pltpu.SemaphoreType.DMA((2 * half, PIECES)),
        ],
        compiler_params=params(),
        cost_estimate=cost(0, 3_000_000),
        name="finish",
    )(keep, give, *results, received)
    coming, out = lax.optimization_barrier((coming, out))
    energy = energy + coming
    while distances:
        energy = energy + send_energy(energy)

    owner_energy = lax.dynamic_slice(energy, (0, lat), (1, 1)) / (block_count * BLOCK)
    return out, owner_energy


def solution(mesh):
    placed = (
        P("group", None, "lat", "lon"),
        P("group", "lat", "lon"),
        P("group", "lat", "lon"),
        P("group", "lat", "lon"),
        P(),
        P(),
        P(("group", "lat"), "lon", None, None),
        P(("group", "lat")),
    )
    return jax.shard_map(
        on_device,
        mesh=mesh,
        in_specs=placed,
        out_specs=(P("group", None, "lat", "lon"), P(("group", "lat"), "lon")),
        check_vma=False,
    )
```

```python
import functools
import math

import jax
import jax.numpy as jnp
import numpy as np
from jax import lax
from jax.experimental import pallas as pl
from jax.experimental.pallas import tpu as pltpu
from jax.sharding import PartitionSpec as P

LANES = 128
BLOCK = 128
VMEM_BYTES = 6 * 1024 * 1024
PIECES = 4
NEAR = 7.0 / 12.0
FAR = 1.0 / 12.0


def params():
    return pltpu.CompilerParams(vmem_limit_bytes=VMEM_BYTES)


def cost(flops, bytes_accessed):
    return pl.CostEstimate(flops=flops, bytes_accessed=bytes_accessed, transcendentals=0)


def split_high_low(value):
    high = value.astype(jnp.bfloat16)
    low = (value - high.astype(jnp.float32)).astype(jnp.bfloat16)
    return high, low


def split_table(table):
    high = table.astype(jnp.bfloat16.dtype)
    return high, (table - high.astype(np.float64)).astype(jnp.bfloat16.dtype)


def spectral_tables(length):
    radix = length // LANES
    pairs = (radix - 1) // 2
    spot = np.arange(LANES)[:, None]
    number = np.arange(LANES)[None, :]
    is_cosine = number <= LANES // 2
    wave = np.where(is_cosine, number, number - LANES // 2)
    angle = 2.0 * np.pi * ((spot * wave) % LANES) / LANES
    first = np.where(is_cosine, np.cos(angle), np.sin(angle))
    others, numbers = [], [radix * wave[0]]
    weights = [np.where((wave[0] == 0) | (wave[0] == LANES // 2), 1.0, 2.0) / length]
    for residue in range(1, pairs + 1):
        whole = residue + radix * number
        angle = 2.0 * np.pi * ((spot * whole) % length) / length
        cosine, sine = np.cos(angle), np.sin(angle)
        others.append(np.block([[cosine, -sine], [sine, cosine]]))
        folded = np.minimum(whole[0], length - whole[0])
        numbers += [folded, folded]
        weights.append(np.full(2 * LANES, 2.0 / length))
    forward = np.concatenate(others), first
    inverse = np.concatenate([table.T for table in others]), first.T
    return forward, inverse, np.concatenate(numbers), np.concatenate(weights)


def pack_rows(first, second):
    return jnp.concatenate([first, second], axis=1)


def second_half(packed, sector):
    skip, shift = sector // LANES, sector % LANES
    segments = [packed[:, LANES * i : LANES * (i + 1)] for i in range(packed.shape[1] // LANES)]
    if shift == 0:
        return jnp.concatenate(segments[skip:], axis=1)
    turned = [pltpu.roll(segment, LANES - shift, 1) for segment in segments[skip:]]
    lane = lax.broadcasted_iota(jnp.int32, turned[0].shape, 1)
    parts = [jnp.where(lane < LANES - shift, turned[i], turned[min(i + 1, len(turned) - 1)]) for i in range(len(turned))]
    return jnp.concatenate(parts, axis=1)


def start_copies(pairs, sems):
    copies = [pltpu.make_async_copy(source, target, sems.at[i]) for i, (source, target) in enumerate(pairs)]
    for copy in copies:
        copy.start()
    return copies


def pack_kernel(even_ref, tracer_hbm, out_ref, row_ref, sems):
    count, levels = row_ref.shape[:2]
    first_row = pl.multiple_of(jnp.where(even_ref[0] == 1, tracer_hbm.shape[2] - 2, 0), 2)
    sources = [tracer_hbm.at[t, :, pl.ds(first_row, 2), :] for t in range(count)]
    copies = start_copies([(sources[t], row_ref.at[t]) for t in range(count)], sems)
    for t in range(count):
        copies[t].wait()
        out_ref[levels * t : levels * (t + 1), :] = pack_rows(row_ref[t, :, 0, :], row_ref[t, :, 1, :])


def rest_kernel(even_ref, tracer_hbm, lat_hbm, lon_hbm, *refs):
    courant_ref, side_ref, tracer_ref, lat_ref, lon_ref, sems = refs[-6:]
    outer_refs = refs[:-6]
    count, levels, rows, sector = tracer_ref.shape
    pairs = [(tracer_hbm.at[t], tracer_ref.at[t]) for t in range(count)] + [(lat_hbm, lat_ref), (lon_hbm, lon_ref)]
    copies = start_copies(pairs, sems)
    shift, whole = sector % LANES, sector // LANES * LANES
    lane = lax.broadcasted_iota(jnp.int32, (levels, LANES), 1)
    even = even_ref[0] == 1

    def store_side(i, r, values):
        first = pltpu.roll(values[:, :LANES], shift, 1)
        last = jnp.concatenate([values[:, whole:], values[:, whole:]], axis=1)
        side_ref[i, r] = jnp.where(lane < LANES - 2, first, last)

    for t in range(count):
        copies[t].wait()
        row = [tracer_ref[t, :, r, :] for r in range(rows)]
        slot = t // len(outer_refs)
        outer_refs[t % len(outer_refs)][levels * slot : levels * (slot + 1), :] = pack_rows(
            jnp.where(even, row[0], row[rows - 2]), jnp.where(even, row[1], row[rows - 1])
        )
        for r in range(rows):
            store_side(t, r, row[r])
    copies[count].wait()
    courant = lat_ref[:, 0, :]
    courant_ref[...] = pack_rows(courant[: levels // 2], courant[levels // 2 :])
    copies[count + 1].wait()
    for r in range(rows):
        store_side(count, r, lon_ref[:, r, :])


def base_kernel(width, not_pole_ref, tracer_hbm, lat_hbm, lon_hbm, side_ref, base_ref, north_ref, courant_ref, *scratch):
    tracer_ref, lat_ref, lon_ref, sems = scratch
    tracer_count, levels, rows, sector = tracer_ref.shape
    whole = sector // LANES * LANES
    pairs = [(lat_hbm, lat_ref), (lon_hbm, lon_ref)] + [(tracer_hbm.at[t], tracer_ref.at[t]) for t in range(tracer_count)]
    copies = start_copies(pairs, sems)

    def beside(values, side):
        return jnp.concatenate([values[:, :whole], values[:, whole:], side[:, sector - whole :]], axis=1)

    copies[0].wait()
    copies[1].wait()
    nothing = jnp.zeros((levels, LANES), jnp.float32)
    for r in range(rows):
        courant = lat_ref[:, r, :] if r else lat_ref[:, r, :] * not_pole_ref[0]
        courant_ref[r] = beside(courant, nothing)
    for t in range(tracer_count):
        copies[t + 2].wait()
        q = [beside(tracer_ref[t, :, r, :], side_ref[t, r]) for r in range(rows)]
        north_ref[t] = NEAR * q[3] - FAR * q[2]
        own_flux = [
            courant_ref[0] * (NEAR * q[0] - FAR * q[1]),
            courant_ref[1] * (NEAR * (q[1] + q[0]) - FAR * q[2]),
            courant_ref[2] * (NEAR * (q[2] + q[1]) - FAR * (q[3] + q[0])),
            courant_ref[3] * (NEAR * (q[3] + q[2]) - FAR * q[1]),
        ]
        for r in range(rows):
            west, west2, east = pltpu.roll(q[r], 1, 1), pltpu.roll(q[r], 2, 1), pltpu.roll(q[r], width - 1, 1)
            flux = beside(lon_ref[:, r, :], side_ref[tracer_count, r]) * (NEAR * (q[r] + west) - FAR * (east + west2))
            value = q[r] - (pltpu.roll(flux, width - 1, 1) - flux) + own_flux[r]
            if r + 1 < rows:
                value = value - own_flux[r + 1]
            base_ref[t, r] = value


def physics_kernel(levels, sector, owner_count, chunk, even_ref, *refs):
    count = len(refs) - 12 >> 1
    first_refs, refs = refs[:count], refs[count:]
    base_ref, north_ref, inner_ref, outer_ref = refs[:4]
    top_ref, courant_ref, surface_ref, mixing_ref, decay_ref, owner_ref, energy_in_ref = refs[4:11]
    physics_refs, energy_ref = refs[11:-1], refs[-1]
    rows, width = base_ref.shape[1], base_ref.shape[-1]
    courant = [courant_ref[r] for r in range(rows)]
    even = even_ref[0] == 1
    top = top_ref[...]
    top = jnp.concatenate([top[:, :width], second_half(top, sector)], axis=0)
    mix_high, mix_low = split_high_low(mixing_ref[...])
    mix = jnp.concatenate([mix_high, mix_high, mix_low, mix_low], axis=1)
    level = lax.broadcasted_iota(jnp.int32, (8, width), 0)
    lane = lax.broadcasted_iota(jnp.int32, (8, width), 1)
    energies = [energy_in_ref[r] for r in range(rows)]
    for first_ref, physics_ref in zip(first_refs, physics_refs):
        t = first_ref[0] + chunk
        inner = inner_ref[pl.ds(pl.multiple_of(levels * t, levels), levels), :]
        outer = jnp.where(first_ref[0] == 0, outer_ref[:levels, :], outer_ref[levels:, :])
        low, high = jnp.where(even, outer, inner), jnp.where(even, inner, outer)
        low_a, low_b = low[:, :width], second_half(low, sector)
        high_a, high_b = high[:, :width], second_half(high, sector)
        south = courant[0] * (NEAR * low_b - FAR * low_a)
        south_in = courant[1] * (FAR * low_b)
        north_in = courant[3] * (FAR * high_a)
        north = top * (NEAR * high_a - FAR * high_b + north_ref[t])
        extra = [south + south_in, -south_in, north_in, -north_in - north]
        for r in range(rows):
            advected = base_ref[t, r] + extra[r]
            part_high, part_low = split_high_low(advected)
            stacked = jnp.concatenate([part_high, part_low, part_high, part_low], axis=0)
            mixed = jnp.dot(mix, stacked, preferred_element_type=jnp.float32)
            surface = jnp.where(level == 7, surface_ref[t, r : r + 1, :], 0.0)
            mixed = jnp.concatenate([mixed[: levels - 8], mixed[levels - 8 :] + surface], axis=0)
            physics = mixed / (1.0 + decay_ref[t] * mixed * mixed)
            physics_ref[r] = physics
            gap = physics - advected
            squared = gap * gap
            for k in range(levels // 8):
                energies[r] = energies[r] + squared[8 * k : 8 * k + 8]
    if not owner_count:
        for r in range(rows):
            energy_ref[r] = energies[r]
        return
    energies = [jnp.where(lane < sector, energy, 0.0) for energy in energies]
    spot = lax.broadcasted_iota(jnp.int32, (1, LANES), 1)
    result = jnp.zeros((1, LANES), jnp.float32)
    for owner in range(owner_count):
        chosen = jnp.zeros((8, LANES), jnp.float32)
        for r in range(rows):
            picked = jnp.where(owner_ref[r : r + 1, :] == owner, energies[r], 0.0)
            for k in range(width // LANES):
                chosen = chosen + picked[:, LANES * k : LANES * (k + 1)]
        total = jnp.sum(jnp.sum(chosen, axis=0, keepdims=True), axis=1, keepdims=True)
        result = jnp.where(spot == owner, total, result)
    energy_ref[...] = result


def send_result(result_ref, out_hbm, tracer, sems):
    piece = result_ref.shape[0] // PIECES
    copies = []
    for part in range(PIECES):
        span = pl.ds(piece * part, piece)
        copies.append(pltpu.make_async_copy(result_ref.at[span], out_hbm.at[tracer, span], sems.at[part]))
        copies[-1].start()
    return copies


def waves_of(radix):
    pairs = (radix - 1) // 2
    cosine = lambda k, i: math.cos(2.0 * math.pi * ((k * i) % radix) / radix)
    sine = lambda k, i: math.sin(2.0 * math.pi * ((k * i) % radix) / radix)
    return pairs, cosine, sine


def row_of(piece_refs, r):
    return piece_refs[0].at[r] if len(piece_refs) == 1 else piece_refs[r].at[0]


def stacked_table(high_ref, low_ref, begin, size):
    high = high_ref[begin : begin + size, :]
    return jnp.concatenate([high, high, low_ref[begin : begin + size, :]], axis=0)


def product_of(high_ref, low_ref, begin, size, table):
    high = high_ref[:, begin : begin + size]
    stacked = jnp.concatenate([high, low_ref[:, begin : begin + size], high], axis=1)
    return jnp.dot(stacked, table, preferred_element_type=jnp.float32)


def forward_kernel(radix, pieces, own_ref, *refs):
    other_refs, refs = refs[:pieces], refs[pieces:]
    table_high_ref, table_low_ref, first_high_ref, first_low_ref, scale_ref, *refs = refs
    out_high_ref, out_low_ref, high_ref, low_ref = refs
    rows, levels, width = own_ref.shape
    pairs, cosine, sine = waves_of(radix)
    segments = width // LANES
    shift = radix * LANES // 2 % LANES
    lane = lax.broadcasted_iota(jnp.int32, (levels, LANES), 1)

    def store(place, column, wave):
        high_ref[place, column : column + LANES], low_ref[place, column : column + LANES] = split_high_low(wave)

    for r in range(rows):
        place = slice(levels * r, levels * (r + 1))
        other_ref = row_of(other_refs, r)
        own = [own_ref[r, :, LANES * n : LANES * (n + 1)] for n in range(segments)]
        turned = [pltpu.roll(other_ref[:, LANES * n : LANES * (n + 1)], shift, 1) for n in range(segments)]
        joined = own[:-1] + [jnp.where(lane < shift, own[-1], turned[0])]
        joined += [jnp.where(lane < shift, turned[n], turned[n + 1]) for n in range(segments - 1)]
        plus = [joined[n] + joined[radix - n] for n in range(1, pairs + 1)]
        minus = [joined[radix - n] - joined[n] for n in range(1, pairs + 1)]
        store(place, 0, sum(plus, joined[0]))
        for k in range(1, pairs + 1):
            real = sum((cosine(k, n) * plus[n - 1] for n in range(1, pairs + 1)), joined[0])
            imaginary = sine(k, 1) * minus[0]
            for n in range(2, pairs + 1):
                imaginary = imaginary + sine(k, n) * minus[n - 1]
            store(place, LANES * (2 * k - 1), real)
            store(place, LANES * 2 * k, imaginary)

    def transform(begin, size, table):
        spectrum = product_of(high_ref, low_ref, begin, size, table)
        for r in range(rows):
            place = slice(levels * r, levels * (r + 1))
            damped = spectrum[place] * scale_ref[r : r + 1, begin : begin + size]
            out_high_ref[place, begin : begin + size], out_low_ref[place, begin : begin + size] = split_high_low(damped)

    transform(0, LANES, stacked_table(first_high_ref, first_low_ref, 0, LANES))
    for k in range(pairs):
        transform(LANES * (2 * k + 1), 2 * LANES, stacked_table(table_high_ref, table_low_ref, 2 * LANES * k, 2 * LANES))


def inverse_kernel(radix, pieces, mask_ref, own_ref, *refs):
    other_refs, refs = refs[:pieces], refs[pieces:]
    high_ref, low_ref, table_high_ref, table_low_ref, first_high_ref, first_low_ref, *refs = refs
    result_ref, back_ref, wave_ref = refs
    rows, levels, width = own_ref.shape
    sector = result_ref.shape[-1]
    pairs, cosine, sine = waves_of(radix)
    segments = width // LANES
    shift = radix * LANES // 2 % LANES
    lane = lax.broadcasted_iota(jnp.int32, (levels, LANES), 1)

    def transform(begin, size, table):
        wave_ref[:, begin : begin + size] = product_of(high_ref, low_ref, begin, size, table)

    transform(0, LANES, stacked_table(first_high_ref, first_low_ref, 0, LANES))
    for k in range(pairs):
        transform(LANES * (2 * k + 1), 2 * LANES, stacked_table(table_high_ref, table_low_ref, 2 * LANES * k, 2 * LANES))

    for r in range(rows):
        place = slice(levels * r, levels * (r + 1))
        other_ref = row_of(other_refs, r)
        waves = [wave_ref[place, LANES * n : LANES * (n + 1)] for n in range(radix)]
        results = [None] * radix
        results[0] = sum((waves[2 * k - 1] for k in range(1, pairs + 1)), waves[0])
        for n in range(1, pairs + 1):
            even = sum((cosine(k, n) * waves[2 * k - 1] for k in range(1, pairs + 1)), waves[0])
            odd = sine(1, n) * waves[2]
            for k in range(2, pairs + 1):
                odd = odd + sine(k, n) * waves[2 * k]
            results[n], results[radix - n] = even - odd, even + odd
        filtered_row = mask_ref[r] == 1
        turned = [pltpu.roll(result, LANES - shift, 1) for result in results[segments - 1 :]]
        for n in range(segments):
            begin = LANES * n
            size = min(LANES, sector - begin)
            value = jnp.where(filtered_row, results[n], own_ref[r, :, begin : begin + LANES])
            result_ref[:, r, begin : begin + size] = value[:, :size]
            value = jnp.where(lane < LANES - shift, turned[n], turned[min(n + 1, segments - 1)])
            back_ref[r, :, begin : begin + LANES] = jnp.where(filtered_row, value, other_ref[:, begin : begin + LANES])


def finish_kernel(keep_ref, give_ref, *refs):
    out_hbm, turned_ref, sems = refs[-3:]
    count = turned_ref.shape[0]
    result_refs, received_refs = refs[:count], refs[count : 2 * count]
    rows, levels, width = received_refs[0].shape
    sector = out_hbm.shape[-1]
    piece = levels // PIECES
    copies = []

    def send(source_ref, tracer, slot):
        for part in range(PIECES):
            span = pl.ds(piece * part, piece)
            copies.append(pltpu.make_async_copy(source_ref.at[span], out_hbm.at[tracer, span], sems.at[slot, part]))
            copies[-1].start()

    for i, result_ref in enumerate(result_refs):
        send(result_ref, keep_ref[0] + i, i)
    for i in range(count):
        for r in range(rows):
            turned_ref[i, :, r, :] = received_refs[i][r, :, :sector]
        send(turned_ref.at[i], give_ref[0] + i, count + i)
    for copy in copies:
        copy.wait()


def on_device(tracers, courant_lat, courant_lon, surface_flux, mixing, decay_rate, owners, polar_mask):
    tracer_count, levels, rows, sector = tracers.shape
    assert rows == 4 and sector % 64 == 0 and lax.axis_size("lon") == 2
    f32 = jnp.float32
    lat_count, lat = lax.axis_size("lat"), lax.axis_index("lat")
    length = 2 * sector
    width = -(-sector // LANES) * LANES
    radix = length // LANES
    downward = [(i + 1, i) for i in range(lat_count - 1)]
    swap = [(0, 1), (1, 0)]

    whole = pl.BlockSpec(memory_space=pltpu.VMEM)
    in_hbm = pl.BlockSpec(memory_space=pltpu.HBM)
    scalars = pl.BlockSpec(memory_space=pltpu.SMEM)
    even = (1 - lat % 2).reshape(1)
    inside = [pair for i in range(0, lat_count - 1, 2) for pair in ((i, i + 1), (i + 1, i))]
    across = [pair for i in range(1, lat_count - 1, 2) for pair in ((i, i + 1), (i + 1, i))]
    fields = [pltpu.with_memory_space_constraint(array, pltpu.HBM) for array in (tracers, courant_lat, courant_lon)]
    field_buffers = [pltpu.VMEM(array.shape, f32) for array in (tracers, courant_lat, courant_lon)]
    half = tracer_count // 2
    inner = pl.pallas_call(
        pack_kernel,
        in_specs=[scalars, in_hbm],
        out_specs=whole,
        out_shape=pltpu.VMEM((levels * tracer_count, length), f32),
        scratch_shapes=[pltpu.VMEM((tracer_count, levels, 2, sector), f32), pltpu.SemaphoreType.DMA((tracer_count,))],
        compiler_params=params(),
        cost_estimate=cost(0, 600_000),
        name="pack",
    )(even, fields[0])
    from_inside = lax.ppermute(inner, "lat", inside)
    even_rest, inner = lax.optimization_barrier((even, inner))
    *outer, courant_row, sides = pl.pallas_call(
        rest_kernel,
        in_specs=[scalars] + [in_hbm] * 3,
        out_specs=[whole] * (half + 2),
        out_shape=[pltpu.VMEM((levels * 2, length), f32)] * half
        + [
            jax.ShapeDtypeStruct((levels // 2, length), f32),
            jax.ShapeDtypeStruct((tracer_count + 1, rows, levels, LANES), f32),
        ],
        scratch_shapes=field_buffers + [pltpu.SemaphoreType.DMA((tracer_count + 2,))],
        compiler_params=params(),
        cost_estimate=cost(0, 0),
        name="rest",
    )(even_rest, *fields)
    from_across = [lax.ppermute(part, "lat", across) for part in outer[:-1]]
    top = lax.ppermute(courant_row, "lat", downward)

    sides = lax.ppermute(sides, "lon", swap)
    not_pole = (lat > 0).astype(f32).reshape(1)
    base, north, lat_courant = pl.pallas_call(
        functools.partial(base_kernel, width),
        in_specs=[scalars, in_hbm, in_hbm, in_hbm, whole],
        out_specs=[whole] * 3,
        out_shape=[
            jax.ShapeDtypeStruct((tracer_count, rows, levels, width), f32),
            jax.ShapeDtypeStruct((tracer_count, levels, width), f32),
            jax.ShapeDtypeStruct((rows, levels, width), f32),
        ],
        scratch_shapes=field_buffers + [pltpu.SemaphoreType.DMA((tracer_count + 2,))],
        compiler_params=params(),
        cost_estimate=cost(0, 0),
        name="base",
    )(not_pole, *fields, sides)

    surface = jnp.pad(surface_flux, ((0, 0), (0, 0), (0, width - sector)))
    decay = decay_rate[:, :, None]
    block_count = rows * sector // BLOCK
    block_of = (np.arange(rows)[:, None] * sector + np.minimum(np.arange(width), sector - 1)[None]) // BLOCK
    owner_of = jnp.repeat(owners.reshape(block_count), BLOCK).reshape(rows, sector)
    owner_of = jnp.pad(owner_of, ((0, 0), (0, width - sector)))
    forward, inverse, numbers, weights = spectral_tables(length)
    row_ids = (lat * rows + jnp.arange(rows)).astype(f32)
    latitude = (-0.5 + (row_ids + 0.5) / (lat_count * rows)) * math.pi
    inverse_sine = np.where(numbers == 0, 1.0, 1.0 / np.where(numbers == 0, 1.0, np.sin(np.pi * numbers / length)))
    ratio = 2.0 * jnp.cos(latitude)[:, None] * jnp.asarray(inverse_sine, f32)[None]
    damping = jnp.where(jnp.asarray(numbers == 0)[None], 1.0, jnp.minimum(1.0, ratio * ratio))
    scale = damping * jnp.asarray(weights, f32)[None]

    base, scale, owner_of, surface, decay = lax.optimization_barrier((base, scale, owner_of, surface, decay))

    base, outer = lax.optimization_barrier((base, outer))
    from_across.append(lax.ppermute(outer[-1], "lat", across))

    keep = (half * lax.axis_index("lon")).reshape(1)
    give = half - keep
    circles = jax.ShapeDtypeStruct((half, rows, levels, width), f32)
    result_shape = jax.ShapeDtypeStruct((levels, rows, sector), f32)
    out_shape = jax.ShapeDtypeStruct(tracers.shape, f32)

    def run_physics(chunk, firsts, energy, last=False):
        shapes = [jax.ShapeDtypeStruct(circles.shape[1:], f32)] * len(firsts)
        shapes.append(jax.ShapeDtypeStruct((1, LANES) if last else energy.shape, f32))
        *results, energy = pl.pallas_call(
            functools.partial(physics_kernel, levels, sector, lat_count if last else 0, chunk),
            in_specs=[scalars] * (1 + len(firsts)) + [whole] * 11,
            out_specs=[whole] * len(shapes),
            out_shape=shapes,
            compiler_params=params(),
            cost_estimate=cost(0, 0),
            name="physics",
        )(even, *firsts, base, north, from_inside, from_across[chunk], top, lat_courant, surface, mixing, decay, owner_of, energy)
        return results, energy

    forward, inverse = ([jnp.asarray(part) for table in tables for part in split_table(table)] for tables in (forward, inverse))
    circle = jax.ShapeDtypeStruct(circles.shape[1:], f32)
    spectra = jax.ShapeDtypeStruct((rows * levels, length), jnp.bfloat16)

    def run_forward(own, other):
        return pl.pallas_call(
            functools.partial(forward_kernel, radix, len(other)),
            in_specs=[whole] * (6 + len(other)),
            out_specs=[whole] * 2,
            out_shape=[spectra] * 2,
            scratch_shapes=[pltpu.VMEM(spectra.shape, jnp.bfloat16)] * 2,
            compiler_params=params(),
            cost_estimate=cost(0, 0),
            name="forward",
        )(own, *other, *forward, scale)

    def run_inverse(own, other, high, low):
        return pl.pallas_call(
            functools.partial(inverse_kernel, radix, len(other)),
            in_specs=[scalars] + [whole] * (7 + len(other)),
            out_specs=[whole] * 2,
            out_shape=[result_shape, circle],
            scratch_shapes=[pltpu.VMEM(spectra.shape, f32)],
            compiler_params=params(),
            cost_estimate=cost(0, 0),
            name="inverse",
        )(polar_mask, own, *other, high, low, *inverse)

    energy = jnp.zeros((rows, 8, width), f32)
    results, received = [], []
    for chunk in range(half - 1):
        (given, own), energy = run_physics(chunk, [give, keep], energy)
        other = [lax.ppermute(given[r : r + 1], "lon", swap) for r in range(rows)]
        spectrum = run_forward(own, other)
        result, back = run_inverse(own, other, *spectrum)
        results.append(result)
        received.append(lax.ppermute(back, "lon", swap))
        energy, back = lax.optimization_barrier((energy, back))

    distances = [1 << i for i in range(lat_count.bit_length() - 1)]

    def send_energy(energy):
        distance = distances.pop(0)
        return lax.ppermute(energy, "lat", [(i, i ^ distance) for i in range(lat_count)])

    (given,), energy = run_physics(half - 1, [give], energy)
    other = [lax.ppermute(given, "lon", swap)]
    (own,), energy = run_physics(half - 1, [keep], energy, True)

    coming = send_energy(energy)
    high, low = run_forward(own, other)
    coming, high = lax.optimization_barrier((coming, high))
    energy = energy + coming
    energy, high = lax.optimization_barrier((energy, high))

    coming = send_energy(energy)
    result, back = run_inverse(own, other, high, low)
    coming, back = lax.optimization_barrier((coming, back))
    energy = energy + coming
    energy, back = lax.optimization_barrier((energy, back))
    results.append(result)
    received.append(lax.ppermute(back, "lon", swap))

    coming = send_energy(energy)
    out = pl.pallas_call(
        finish_kernel,
        in_specs=[scalars] * 2 + [whole] * (2 * half),
        out_specs=in_hbm,
        out_shape=out_shape,
        scratch_shapes=[
            pltpu.VMEM((half,) + result_shape.shape, f32),
            pltpu.SemaphoreType.DMA((2 * half, PIECES)),
        ],
        compiler_params=params(),
        cost_estimate=cost(0, 3_000_000),
        name="finish",
    )(keep, give, *results, *received)
    coming, out = lax.optimization_barrier((coming, out))
    energy = energy + coming
    while distances:
        energy = energy + send_energy(energy)

    owner_energy = lax.dynamic_slice(energy, (0, lat), (1, 1)) / (block_count * BLOCK)
    return out, owner_energy


def solution(mesh):
    placed = (
        P("group", None, "lat", "lon"),
        P("group", "lat", "lon"),
        P("group", "lat", "lon"),
        P("group", "lat", "lon"),
        P(),
        P(),
        P(("group", "lat"), "lon", None, None),
        P(("group", "lat")),
    )
    return jax.shard_map(
        on_device,
        mesh=mesh,
        in_specs=placed,
        out_specs=(P("group", None, "lat", "lon"), P(("group", "lat"), "lon")),
        check_vma=False,
    )
```

```python
import functools
import math

import jax
import jax.numpy as jnp
import numpy as np
from jax import lax
from jax.experimental import pallas as pl
from jax.experimental.pallas import tpu as pltpu
from jax.sharding import PartitionSpec as P

LANES = 128
BLOCK = 128
VMEM_BYTES = 6 * 1024 * 1024
PIECES = 4
NEAR = 7.0 / 12.0
FAR = 1.0 / 12.0


def params():
    return pltpu.CompilerParams(vmem_limit_bytes=VMEM_BYTES)


def cost(flops, bytes_accessed):
    return pl.CostEstimate(flops=flops, bytes_accessed=bytes_accessed, transcendentals=0)


def split_high_low(value):
    high = value.astype(jnp.bfloat16)
    low = (value - high.astype(jnp.float32)).astype(jnp.bfloat16)
    return high, low


def split_table(table):
    high = table.astype(jnp.bfloat16.dtype)
    return high, (table - high.astype(np.float64)).astype(jnp.bfloat16.dtype)


def spectral_tables(length):
    radix = length // LANES
    pairs = (radix - 1) // 2
    spot = np.arange(LANES)[:, None]
    number = np.arange(LANES)[None, :]
    is_cosine = number <= LANES // 2
    wave = np.where(is_cosine, number, number - LANES // 2)
    angle = 2.0 * np.pi * ((spot * wave) % LANES) / LANES
    first = np.where(is_cosine, np.cos(angle), np.sin(angle))
    others, numbers = [], [radix * wave[0]]
    weights = [np.where((wave[0] == 0) | (wave[0] == LANES // 2), 1.0, 2.0) / length]
    for residue in range(1, pairs + 1):
        whole = residue + radix * number
        angle = 2.0 * np.pi * ((spot * whole) % length) / length
        cosine, sine = np.cos(angle), np.sin(angle)
        others.append(np.block([[cosine, -sine], [sine, cosine]]))
        folded = np.minimum(whole[0], length - whole[0])
        numbers += [folded, folded]
        weights.append(np.full(2 * LANES, 2.0 / length))
    forward = np.concatenate(others), first
    inverse = np.concatenate([table.T for table in others]), first.T
    return forward, inverse, np.concatenate(numbers), np.concatenate(weights)


def pack_rows(first, second):
    return jnp.concatenate([first, second], axis=1)


def second_half(packed, sector):
    skip, shift = sector // LANES, sector % LANES
    segments = [packed[:, LANES * i : LANES * (i + 1)] for i in range(packed.shape[1] // LANES)]
    if shift == 0:
        return jnp.concatenate(segments[skip:], axis=1)
    turned = [pltpu.roll(segment, LANES - shift, 1) for segment in segments[skip:]]
    lane = lax.broadcasted_iota(jnp.int32, turned[0].shape, 1)
    parts = [jnp.where(lane < LANES - shift, turned[i], turned[min(i + 1, len(turned) - 1)]) for i in range(len(turned))]
    return jnp.concatenate(parts, axis=1)


def start_copies(pairs, sems):
    copies = [pltpu.make_async_copy(source, target, sems.at[i]) for i, (source, target) in enumerate(pairs)]
    for copy in copies:
        copy.start()
    return copies


def pack_kernel(even_ref, tracer_hbm, out_ref, row_ref, sems):
    count, levels = row_ref.shape[:2]
    first_row = pl.multiple_of(jnp.where(even_ref[0] == 1, tracer_hbm.shape[2] - 2, 0), 2)
    sources = [tracer_hbm.at[t, :, pl.ds(first_row, 2), :] for t in range(count)]
    copies = start_copies([(sources[t], row_ref.at[t]) for t in range(count)], sems)
    for t in range(count):
        copies[t].wait()
        out_ref[levels * t : levels * (t + 1), :] = pack_rows(row_ref[t, :, 0, :], row_ref[t, :, 1, :])


def rest_kernel(even_ref, tracer_hbm, lat_hbm, lon_hbm, *refs):
    courant_ref, side_ref, tracer_ref, lat_ref, lon_ref, sems = refs[-6:]
    outer_refs = refs[:-6]
    count, levels, rows, sector = tracer_ref.shape
    pairs = [(tracer_hbm.at[t], tracer_ref.at[t]) for t in range(count)] + [(lat_hbm, lat_ref), (lon_hbm, lon_ref)]
    copies = start_copies(pairs, sems)
    shift, whole = sector % LANES, sector // LANES * LANES
    lane = lax.broadcasted_iota(jnp.int32, (levels, LANES), 1)
    even = even_ref[0] == 1

    def store_side(i, r, values):
        first = pltpu.roll(values[:, :LANES], shift, 1)
        last = jnp.concatenate([values[:, whole:], values[:, whole:]], axis=1)
        side_ref[i, r] = jnp.where(lane < LANES - 2, first, last)

    for t in range(count):
        copies[t].wait()
        row = [tracer_ref[t, :, r, :] for r in range(rows)]
        slot = t // len(outer_refs)
        outer_refs[t % len(outer_refs)][levels * slot : levels * (slot + 1), :] = pack_rows(
            jnp.where(even, row[0], row[rows - 2]), jnp.where(even, row[1], row[rows - 1])
        )
        for r in range(rows):
            store_side(t, r, row[r])
    copies[count].wait()
    courant = lat_ref[:, 0, :]
    courant_ref[...] = pack_rows(courant[: levels // 2], courant[levels // 2 :])
    copies[count + 1].wait()
    for r in range(rows):
        store_side(count, r, lon_ref[:, r, :])


def base_kernel(width, not_pole_ref, tracer_hbm, lat_hbm, lon_hbm, side_ref, base_ref, north_ref, courant_ref, *scratch):
    tracer_ref, lat_ref, lon_ref, sems = scratch
    tracer_count, levels, rows, sector = tracer_ref.shape
    whole = sector // LANES * LANES
    pairs = [(lat_hbm, lat_ref), (lon_hbm, lon_ref)] + [(tracer_hbm.at[t], tracer_ref.at[t]) for t in range(tracer_count)]
    copies = start_copies(pairs, sems)

    def beside(values, side):
        return jnp.concatenate([values[:, :whole], values[:, whole:], side[:, sector - whole :]], axis=1)

    copies[0].wait()
    copies[1].wait()
    nothing = jnp.zeros((levels, LANES), jnp.float32)
    for r in range(rows):
        courant = lat_ref[:, r, :] if r else lat_ref[:, r, :] * not_pole_ref[0]
        courant_ref[r] = beside(courant, nothing)
    for t in range(tracer_count):
        copies[t + 2].wait()
        q = [beside(tracer_ref[t, :, r, :], side_ref[t, r]) for r in range(rows)]
        north_ref[t] = NEAR * q[3] - FAR * q[2]
        own_flux = [
            courant_ref[0] * (NEAR * q[0] - FAR * q[1]),
            courant_ref[1] * (NEAR * (q[1] + q[0]) - FAR * q[2]),
            courant_ref[2] * (NEAR * (q[2] + q[1]) - FAR * (q[3] + q[0])),
            courant_ref[3] * (NEAR * (q[3] + q[2]) - FAR * q[1]),
        ]
        for r in range(rows):
            west, west2, east = pltpu.roll(q[r], 1, 1), pltpu.roll(q[r], 2, 1), pltpu.roll(q[r], width - 1, 1)
            flux = beside(lon_ref[:, r, :], side_ref[tracer_count, r]) * (NEAR * (q[r] + west) - FAR * (east + west2))
            value = q[r] - (pltpu.roll(flux, width - 1, 1) - flux) + own_flux[r]
            if r + 1 < rows:
                value = value - own_flux[r + 1]
            base_ref[t, r] = value


def physics_kernel(levels, sector, owner_count, chunk, even_ref, *refs):
    count = len(refs) - 12 >> 1
    first_refs, refs = refs[:count], refs[count:]
    base_ref, north_ref, inner_ref, outer_ref = refs[:4]
    top_ref, courant_ref, surface_ref, mixing_ref, decay_ref, owner_ref, energy_in_ref = refs[4:11]
    physics_refs, energy_ref = refs[11:-1], refs[-1]
    rows, width = base_ref.shape[1], base_ref.shape[-1]
    courant = [courant_ref[r] for r in range(rows)]
    even = even_ref[0] == 1
    top = top_ref[...]
    top = jnp.concatenate([top[:, :width], second_half(top, sector)], axis=0)
    mix_high, mix_low = split_high_low(mixing_ref[...])
    mix = jnp.concatenate([mix_high, mix_high, mix_low, mix_low], axis=1)
    level = lax.broadcasted_iota(jnp.int32, (8, width), 0)
    lane = lax.broadcasted_iota(jnp.int32, (8, width), 1)
    energies = [energy_in_ref[r] for r in range(rows)]
    for first_ref, physics_ref in zip(first_refs, physics_refs):
        t = first_ref[0] + chunk
        inner = inner_ref[pl.ds(pl.multiple_of(levels * t, levels), levels), :]
        outer = jnp.where(first_ref[0] == 0, outer_ref[:levels, :], outer_ref[levels:, :])
        low, high = jnp.where(even, outer, inner), jnp.where(even, inner, outer)
        low_a, low_b = low[:, :width], second_half(low, sector)
        high_a, high_b = high[:, :width], second_half(high, sector)
        south = courant[0] * (NEAR * low_b - FAR * low_a)
        south_in = courant[1] * (FAR * low_b)
        north_in = courant[3] * (FAR * high_a)
        north = top * (NEAR * high_a - FAR * high_b + north_ref[t])
        extra = [south + south_in, -south_in, north_in, -north_in - north]
        for r in range(rows):
            advected = base_ref[t, r] + extra[r]
            part_high, part_low = split_high_low(advected)
            stacked = jnp.concatenate([part_high, part_low, part_high, part_low], axis=0)
            mixed = jnp.dot(mix, stacked, preferred_element_type=jnp.float32)
            surface = jnp.where(level == 7, surface_ref[t, r : r + 1, :], 0.0)
            mixed = jnp.concatenate([mixed[: levels - 8], mixed[levels - 8 :] + surface], axis=0)
            physics = mixed / (1.0 + decay_ref[t] * mixed * mixed)
            physics_ref[r] = physics
            gap = physics - advected
            squared = gap * gap
            for k in range(levels // 8):
                energies[r] = energies[r] + squared[8 * k : 8 * k + 8]
    if not owner_count:
        for r in range(rows):
            energy_ref[r] = energies[r]
        return
    energies = [jnp.where(lane < sector, energy, 0.0) for energy in energies]
    spot = lax.broadcasted_iota(jnp.int32, (1, LANES), 1)
    result = jnp.zeros((1, LANES), jnp.float32)
    for owner in range(owner_count):
        chosen = jnp.zeros((8, LANES), jnp.float32)
        for r in range(rows):
            picked = jnp.where(owner_ref[r : r + 1, :] == owner, energies[r], 0.0)
            for k in range(width // LANES):
                chosen = chosen + picked[:, LANES * k : LANES * (k + 1)]
        total = jnp.sum(jnp.sum(chosen, axis=0, keepdims=True), axis=1, keepdims=True)
        result = jnp.where(spot == owner, total, result)
    energy_ref[...] = result


def waves_of(radix):
    pairs = (radix - 1) // 2
    cosine = lambda k, i: math.cos(2.0 * math.pi * ((k * i) % radix) / radix)
    sine = lambda k, i: math.sin(2.0 * math.pi * ((k * i) % radix) / radix)
    return pairs, cosine, sine


def row_of(piece_refs, r):
    return piece_refs[0].at[r] if len(piece_refs) == 1 else piece_refs[r].at[0]


def stacked_table(high_ref, low_ref, begin, size):
    high = high_ref[begin : begin + size, :]
    return jnp.concatenate([high, high, low_ref[begin : begin + size, :]], axis=0)


def product_of(high_ref, low_ref, begin, size, table):
    high = high_ref[:, begin : begin + size]
    stacked = jnp.concatenate([high, low_ref[:, begin : begin + size], high], axis=1)
    return jnp.dot(stacked, table, preferred_element_type=jnp.float32)


def forward_kernel(radix, pieces, own_ref, *refs):
    other_refs, refs = refs[:pieces], refs[pieces:]
    table_high_ref, table_low_ref, first_high_ref, first_low_ref, scale_ref, *refs = refs
    out_high_ref, out_low_ref, high_ref, low_ref = refs
    rows, levels, width = own_ref.shape
    pairs, cosine, sine = waves_of(radix)
    segments = width // LANES
    shift = radix * LANES // 2 % LANES
    lane = lax.broadcasted_iota(jnp.int32, (levels, LANES), 1)

    def store(place, column, wave):
        high_ref[place, column : column + LANES], low_ref[place, column : column + LANES] = split_high_low(wave)

    for r in range(rows):
        place = slice(levels * r, levels * (r + 1))
        other_ref = row_of(other_refs, r)
        own = [own_ref[r, :, LANES * n : LANES * (n + 1)] for n in range(segments)]
        turned = [pltpu.roll(other_ref[:, LANES * n : LANES * (n + 1)], shift, 1) for n in range(segments)]
        joined = own[:-1] + [jnp.where(lane < shift, own[-1], turned[0])]
        joined += [jnp.where(lane < shift, turned[n], turned[n + 1]) for n in range(segments - 1)]
        plus = [joined[n] + joined[radix - n] for n in range(1, pairs + 1)]
        minus = [joined[radix - n] - joined[n] for n in range(1, pairs + 1)]
        store(place, 0, sum(plus, joined[0]))
        for k in range(1, pairs + 1):
            real = sum((cosine(k, n) * plus[n - 1] for n in range(1, pairs + 1)), joined[0])
            imaginary = sine(k, 1) * minus[0]
            for n in range(2, pairs + 1):
                imaginary = imaginary + sine(k, n) * minus[n - 1]
            store(place, LANES * (2 * k - 1), real)
            store(place, LANES * 2 * k, imaginary)

    def transform(begin, size, table):
        spectrum = product_of(high_ref, low_ref, begin, size, table)
        for r in range(rows):
            place = slice(levels * r, levels * (r + 1))
            damped = spectrum[place] * scale_ref[r : r + 1, begin : begin + size]
            out_high_ref[place, begin : begin + size], out_low_ref[place, begin : begin + size] = split_high_low(damped)

    transform(0, LANES, stacked_table(first_high_ref, first_low_ref, 0, LANES))
    for k in range(pairs):
        transform(LANES * (2 * k + 1), 2 * LANES, stacked_table(table_high_ref, table_low_ref, 2 * LANES * k, 2 * LANES))


def inverse_kernel(radix, pieces, mask_ref, own_ref, *refs):
    other_refs, refs = refs[:pieces], refs[pieces:]
    high_ref, low_ref, table_high_ref, table_low_ref, first_high_ref, first_low_ref, *refs = refs
    result_ref, back_ref, wave_ref = refs
    rows, levels, width = own_ref.shape
    sector = result_ref.shape[-1]
    pairs, cosine, sine = waves_of(radix)
    segments = width // LANES
    shift = radix * LANES // 2 % LANES
    lane = lax.broadcasted_iota(jnp.int32, (levels, LANES), 1)

    def transform(begin, size, table):
        wave_ref[:, begin : begin + size] = product_of(high_ref, low_ref, begin, size, table)

    transform(0, LANES, stacked_table(first_high_ref, first_low_ref, 0, LANES))
    for k in range(pairs):
        transform(LANES * (2 * k + 1), 2 * LANES, stacked_table(table_high_ref, table_low_ref, 2 * LANES * k, 2 * LANES))

    for r in range(rows):
        place = slice(levels * r, levels * (r + 1))
        other_ref = row_of(other_refs, r)
        waves = [wave_ref[place, LANES * n : LANES * (n + 1)] for n in range(radix)]
        results = [None] * radix
        results[0] = sum((waves[2 * k - 1] for k in range(1, pairs + 1)), waves[0])
        for n in range(1, pairs + 1):
            even = sum((cosine(k, n) * waves[2 * k - 1] for k in range(1, pairs + 1)), waves[0])
            odd = sine(1, n) * waves[2]
            for k in range(2, pairs + 1):
                odd = odd + sine(k, n) * waves[2 * k]
            results[n], results[radix - n] = even - odd, even + odd
        filtered_row = mask_ref[r] == 1
        turned = [pltpu.roll(result, LANES - shift, 1) for result in results[segments - 1 :]]
        for n in range(segments):
            begin = LANES * n
            size = min(LANES, sector - begin)
            value = jnp.where(filtered_row, results[n], own_ref[r, :, begin : begin + LANES])
            result_ref[:, r, begin : begin + size] = value[:, :size]
            value = jnp.where(lane < LANES - shift, turned[n], turned[min(n + 1, segments - 1)])
            back_ref[r, :, begin : begin + LANES] = jnp.where(filtered_row, value, other_ref[:, begin : begin + LANES])


def finish_kernel(keep_ref, give_ref, *refs):
    out_hbm, turned_ref, sems = refs[-3:]
    count = turned_ref.shape[0]
    result_refs, received_refs = refs[:count], refs[count : 2 * count]
    rows, levels, width = received_refs[0].shape
    sector = out_hbm.shape[-1]
    piece = levels // PIECES
    copies = []

    def send(source_ref, tracer, slot):
        for part in range(PIECES):
            span = pl.ds(piece * part, piece)
            copies.append(pltpu.make_async_copy(source_ref.at[span], out_hbm.at[tracer, span], sems.at[slot, part]))
            copies[-1].start()

    for i, result_ref in enumerate(result_refs):
        send(result_ref, keep_ref[0] + i, i)
    for i in range(count):
        for r in range(rows):
            turned_ref[i, :, r, :] = received_refs[i][r, :, :sector]
        send(turned_ref.at[i], give_ref[0] + i, count + i)
    for copy in copies:
        copy.wait()


def on_device(tracers, courant_lat, courant_lon, surface_flux, mixing, decay_rate, owners, polar_mask):
    tracer_count, levels, rows, sector = tracers.shape
    assert rows == 4 and sector % 64 == 0 and lax.axis_size("lon") == 2
    f32 = jnp.float32
    lat_count, lat = lax.axis_size("lat"), lax.axis_index("lat")
    length = 2 * sector
    width = -(-sector // LANES) * LANES
    radix = length // LANES
    downward = [(i + 1, i) for i in range(lat_count - 1)]
    swap = [(0, 1), (1, 0)]

    whole = pl.BlockSpec(memory_space=pltpu.VMEM)
    in_hbm = pl.BlockSpec(memory_space=pltpu.HBM)
    scalars = pl.BlockSpec(memory_space=pltpu.SMEM)
    even = (1 - lat % 2).reshape(1)
    inside = [pair for i in range(0, lat_count - 1, 2) for pair in ((i, i + 1), (i + 1, i))]
    across = [pair for i in range(1, lat_count - 1, 2) for pair in ((i, i + 1), (i + 1, i))]
    fields = [pltpu.with_memory_space_constraint(array, pltpu.HBM) for array in (tracers, courant_lat, courant_lon)]
    field_buffers = [pltpu.VMEM(array.shape, f32) for array in (tracers, courant_lat, courant_lon)]
    half = tracer_count // 2
    inner = pl.pallas_call(
        pack_kernel,
        in_specs=[scalars, in_hbm],
        out_specs=whole,
        out_shape=pltpu.VMEM((levels * tracer_count, length), f32),
        scratch_shapes=[pltpu.VMEM((tracer_count, levels, 2, sector), f32), pltpu.SemaphoreType.DMA((tracer_count,))],
        compiler_params=params(),
        cost_estimate=cost(0, 600_000),
        name="pack",
    )(even, fields[0])
    from_inside = lax.ppermute(inner, "lat", inside)
    even_rest, inner = lax.optimization_barrier((even, inner))
    *outer, courant_row, sides = pl.pallas_call(
        rest_kernel,
        in_specs=[scalars] + [in_hbm] * 3,
        out_specs=[whole] * (half + 2),
        out_shape=[pltpu.VMEM((levels * 2, length), f32)] * half
        + [
            jax.ShapeDtypeStruct((levels // 2, length), f32),
            jax.ShapeDtypeStruct((tracer_count + 1, rows, levels, LANES), f32),
        ],
        scratch_shapes=field_buffers + [pltpu.SemaphoreType.DMA((tracer_count + 2,))],
        compiler_params=params(),
        cost_estimate=cost(0, 0),
        name="rest",
    )(even_rest, *fields)
    from_across = [lax.ppermute(part, "lat", across) for part in outer[:-1]]
    top = lax.ppermute(courant_row, "lat", downward)

    sides = lax.ppermute(sides, "lon", swap)
    not_pole = (lat > 0).astype(f32).reshape(1)
    base, north, lat_courant = pl.pallas_call(
        functools.partial(base_kernel, width),
        in_specs=[scalars, in_hbm, in_hbm, in_hbm, whole],
        out_specs=[whole] * 3,
        out_shape=[
            jax.ShapeDtypeStruct((tracer_count, rows, levels, width), f32),
            jax.ShapeDtypeStruct((tracer_count, levels, width), f32),
            jax.ShapeDtypeStruct((rows, levels, width), f32),
        ],
        scratch_shapes=field_buffers + [pltpu.SemaphoreType.DMA((tracer_count + 2,))],
        compiler_params=params(),
        cost_estimate=cost(0, 0),
        name="base",
    )(not_pole, *fields, sides)

    surface = jnp.pad(surface_flux, ((0, 0), (0, 0), (0, width - sector)))
    decay = decay_rate[:, :, None]
    block_count = rows * sector // BLOCK
    block_of = (np.arange(rows)[:, None] * sector + np.minimum(np.arange(width), sector - 1)[None]) // BLOCK
    owner_of = jnp.repeat(owners.reshape(block_count), BLOCK).reshape(rows, sector)
    owner_of = jnp.pad(owner_of, ((0, 0), (0, width - sector)))
    forward, inverse, numbers, weights = spectral_tables(length)
    row_ids = (lat * rows + jnp.arange(rows)).astype(f32)
    latitude = (-0.5 + (row_ids + 0.5) / (lat_count * rows)) * math.pi
    inverse_sine = np.where(numbers == 0, 1.0, 1.0 / np.where(numbers == 0, 1.0, np.sin(np.pi * numbers / length)))
    ratio = 2.0 * jnp.cos(latitude)[:, None] * jnp.asarray(inverse_sine, f32)[None]
    damping = jnp.where(jnp.asarray(numbers == 0)[None], 1.0, jnp.minimum(1.0, ratio * ratio))
    scale = damping * jnp.asarray(weights, f32)[None]

    base, scale, owner_of, surface, decay = lax.optimization_barrier((base, scale, owner_of, surface, decay))

    base, outer = lax.optimization_barrier((base, outer))
    from_across.append(lax.ppermute(outer[-1], "lat", across))

    keep = (half * lax.axis_index("lon")).reshape(1)
    give = half - keep
    circles = jax.ShapeDtypeStruct((half, rows, levels, width), f32)
    result_shape = jax.ShapeDtypeStruct((levels, rows, sector), f32)
    out_shape = jax.ShapeDtypeStruct(tracers.shape, f32)

    def run_physics(chunk, firsts, energy, last=False):
        shapes = [jax.ShapeDtypeStruct(circles.shape[1:], f32)] * len(firsts)
        shapes.append(jax.ShapeDtypeStruct((1, LANES) if last else energy.shape, f32))
        *results, energy = pl.pallas_call(
            functools.partial(physics_kernel, levels, sector, lat_count if last else 0, chunk),
            in_specs=[scalars] * (1 + len(firsts)) + [whole] * 11,
            out_specs=[whole] * len(shapes),
            out_shape=shapes,
            compiler_params=params(),
            cost_estimate=cost(0, 0),
            name="physics",
        )(even, *firsts, base, north, from_inside, from_across[chunk], top, lat_courant, surface, mixing, decay, owner_of, energy)
        return results, energy

    forward, inverse = ([jnp.asarray(part) for table in tables for part in split_table(table)] for tables in (forward, inverse))
    circle = jax.ShapeDtypeStruct(circles.shape[1:], f32)
    spectra = jax.ShapeDtypeStruct((rows * levels, length), jnp.bfloat16)

    def run_forward(own, other):
        return pl.pallas_call(
            functools.partial(forward_kernel, radix, len(other)),
            in_specs=[whole] * (6 + len(other)),
            out_specs=[whole] * 2,
            out_shape=[spectra] * 2,
            scratch_shapes=[pltpu.VMEM(spectra.shape, jnp.bfloat16)] * 2,
            compiler_params=params(),
            cost_estimate=cost(0, 0),
            name="forward",
        )(own, *other, *forward, scale)

    def run_inverse(own, other, high, low):
        return pl.pallas_call(
            functools.partial(inverse_kernel, radix, len(other)),
            in_specs=[scalars] + [whole] * (7 + len(other)),
            out_specs=[whole] * 2,
            out_shape=[result_shape, circle],
            scratch_shapes=[pltpu.VMEM(spectra.shape, f32)],
            compiler_params=params(),
            cost_estimate=cost(0, 0),
            name="inverse",
        )(polar_mask, own, *other, high, low, *inverse)

    energy = jnp.zeros((rows, 8, width), f32)
    results, received = [], []
    for chunk in range(half - 1):
        (given, own), energy = run_physics(chunk, [give, keep], energy)
        other = [lax.ppermute(given[r : r + 1], "lon", swap) for r in range(rows)]
        spectrum = run_forward(own, other)
        result, back = run_inverse(own, other, *spectrum)
        results.append(result)
        received.append(lax.ppermute(back, "lon", swap))
        energy, back = lax.optimization_barrier((energy, back))

    distances = [1 << i for i in range(lat_count.bit_length() - 1)]

    def send_energy(energy):
        distance = distances.pop(0)
        return lax.ppermute(energy, "lat", [(i, i ^ distance) for i in range(lat_count)])

    (given, own), energy = run_physics(half - 1, [give, keep], energy, True)
    other = [lax.ppermute(given, "lon", swap)]

    coming = send_energy(energy)
    high, low = run_forward(own, other)
    coming, high = lax.optimization_barrier((coming, high))
    energy = energy + coming
    energy, high = lax.optimization_barrier((energy, high))

    coming = send_energy(energy)
    result, back = run_inverse(own, other, high, low)
    coming, back = lax.optimization_barrier((coming, back))
    energy = energy + coming
    energy, back = lax.optimization_barrier((energy, back))
    results.append(result)
    received.append(lax.ppermute(back, "lon", swap))

    coming = send_energy(energy)
    out = pl.pallas_call(
        finish_kernel,
        in_specs=[scalars] * 2 + [whole] * (2 * half),
        out_specs=in_hbm,
        out_shape=out_shape,
        scratch_shapes=[
            pltpu.VMEM((half,) + result_shape.shape, f32),
            pltpu.SemaphoreType.DMA((2 * half, PIECES)),
        ],
        compiler_params=params(),
        cost_estimate=cost(0, 3_000_000),
        name="finish",
    )(keep, give, *results, *received)
    coming, out = lax.optimization_barrier((coming, out))
    energy = energy + coming
    while distances:
        energy = energy + send_energy(energy)

    owner_energy = lax.dynamic_slice(energy, (0, lat), (1, 1)) / (block_count * BLOCK)
    return out, owner_energy


def solution(mesh):
    placed = (
        P("group", None, "lat", "lon"),
        P("group", "lat", "lon"),
        P("group", "lat", "lon"),
        P("group", "lat", "lon"),
        P(),
        P(),
        P(("group", "lat"), "lon", None, None),
        P(("group", "lat")),
    )
    return jax.shard_map(
        on_device,
        mesh=mesh,
        in_specs=placed,
        out_specs=(P("group", None, "lat", "lon"), P(("group", "lat"), "lon")),
        check_vma=False,
    )
```

```python
import functools
import math

import jax
import jax.numpy as jnp
import numpy as np
from jax import lax
from jax.experimental import pallas as pl
from jax.experimental.pallas import tpu as pltpu
from jax.sharding import PartitionSpec as P

LANES = 128
BLOCK = 128
VMEM_BYTES = 6 * 1024 * 1024
PIECES = 4
NEAR = 7.0 / 12.0
FAR = 1.0 / 12.0


def params():
    return pltpu.CompilerParams(vmem_limit_bytes=VMEM_BYTES)


def cost(flops, bytes_accessed):
    return pl.CostEstimate(flops=flops, bytes_accessed=bytes_accessed, transcendentals=0)


def split_high_low(value):
    high = value.astype(jnp.bfloat16)
    low = (value - high.astype(jnp.float32)).astype(jnp.bfloat16)
    return high, low


def split_table(table):
    high = table.astype(jnp.bfloat16.dtype)
    return high, (table - high.astype(np.float64)).astype(jnp.bfloat16.dtype)


def spectral_tables(length):
    radix = length // LANES
    pairs = (radix - 1) // 2
    spot = np.arange(LANES)[:, None]
    number = np.arange(LANES)[None, :]
    is_cosine = number <= LANES // 2
    wave = np.where(is_cosine, number, number - LANES // 2)
    angle = 2.0 * np.pi * ((spot * wave) % LANES) / LANES
    first = np.where(is_cosine, np.cos(angle), np.sin(angle))
    others, numbers = [], [radix * wave[0]]
    weights = [np.where((wave[0] == 0) | (wave[0] == LANES // 2), 1.0, 2.0) / length]
    for residue in range(1, pairs + 1):
        whole = residue + radix * number
        angle = 2.0 * np.pi * ((spot * whole) % length) / length
        cosine, sine = np.cos(angle), np.sin(angle)
        others.append(np.block([[cosine, -sine], [sine, cosine]]))
        folded = np.minimum(whole[0], length - whole[0])
        numbers += [folded, folded]
        weights.append(np.full(2 * LANES, 2.0 / length))
    forward = np.concatenate(others), first
    inverse = np.concatenate([table.T for table in others]), first.T
    return forward, inverse, np.concatenate(numbers), np.concatenate(weights)


def pack_rows(first, second):
    return jnp.concatenate([first, second], axis=1)


def second_half(packed, sector):
    skip, shift = sector // LANES, sector % LANES
    segments = [packed[:, LANES * i : LANES * (i + 1)] for i in range(packed.shape[1] // LANES)]
    if shift == 0:
        return jnp.concatenate(segments[skip:], axis=1)
    turned = [pltpu.roll(segment, LANES - shift, 1) for segment in segments[skip:]]
    lane = lax.broadcasted_iota(jnp.int32, turned[0].shape, 1)
    parts = [jnp.where(lane < LANES - shift, turned[i], turned[min(i + 1, len(turned) - 1)]) for i in range(len(turned))]
    return jnp.concatenate(parts, axis=1)


def start_copies(pairs, sems):
    copies = [pltpu.make_async_copy(source, target, sems.at[i]) for i, (source, target) in enumerate(pairs)]
    for copy in copies:
        copy.start()
    return copies


def pack_kernel(even_ref, tracer_hbm, out_ref, row_ref, sems):
    count, levels = row_ref.shape[:2]
    first_row = pl.multiple_of(jnp.where(even_ref[0] == 1, tracer_hbm.shape[2] - 2, 0), 2)
    sources = [tracer_hbm.at[t, :, pl.ds(first_row, 2), :] for t in range(count)]
    copies = start_copies([(sources[t], row_ref.at[t]) for t in range(count)], sems)
    for t in range(count):
        copies[t].wait()
        out_ref[levels * t : levels * (t + 1), :] = pack_rows(row_ref[t, :, 0, :], row_ref[t, :, 1, :])


def rest_kernel(even_ref, tracer_hbm, lat_hbm, lon_hbm, *refs):
    courant_ref, side_ref, tracer_ref, lat_ref, lon_ref, sems = refs[-6:]
    outer_refs = refs[:-6]
    count, levels, rows, sector = tracer_ref.shape
    pairs = [(tracer_hbm.at[t], tracer_ref.at[t]) for t in range(count)] + [(lat_hbm, lat_ref), (lon_hbm, lon_ref)]
    copies = start_copies(pairs, sems)
    shift, whole = sector % LANES, sector // LANES * LANES
    lane = lax.broadcasted_iota(jnp.int32, (levels, LANES), 1)
    even = even_ref[0] == 1

    def store_side(i, r, values):
        first = pltpu.roll(values[:, :LANES], shift, 1)
        last = jnp.concatenate([values[:, whole:], values[:, whole:]], axis=1)
        side_ref[i, r] = jnp.where(lane < LANES - 2, first, last)

    for t in range(count):
        copies[t].wait()
        row = [tracer_ref[t, :, r, :] for r in range(rows)]
        slot = t // len(outer_refs)
        outer_refs[t % len(outer_refs)][levels * slot : levels * (slot + 1), :] = pack_rows(
            jnp.where(even, row[0], row[rows - 2]), jnp.where(even, row[1], row[rows - 1])
        )
        for r in range(rows):
            store_side(t, r, row[r])
    copies[count].wait()
    courant = lat_ref[:, 0, :]
    courant_ref[...] = pack_rows(courant[: levels // 2], courant[levels // 2 :])
    copies[count + 1].wait()
    for r in range(rows):
        store_side(count, r, lon_ref[:, r, :])


def base_kernel(width, not_pole_ref, tracer_hbm, lat_hbm, lon_hbm, side_ref, base_ref, north_ref, courant_ref, *scratch):
    tracer_ref, lat_ref, lon_ref, sems = scratch
    tracer_count, levels, rows, sector = tracer_ref.shape
    whole = sector // LANES * LANES
    pairs = [(lat_hbm, lat_ref), (lon_hbm, lon_ref)] + [(tracer_hbm.at[t], tracer_ref.at[t]) for t in range(tracer_count)]
    copies = start_copies(pairs, sems)

    def beside(values, side):
        return jnp.concatenate([values[:, :whole], values[:, whole:], side[:, sector - whole :]], axis=1)

    copies[0].wait()
    copies[1].wait()
    nothing = jnp.zeros((levels, LANES), jnp.float32)
    for r in range(rows):
        courant = lat_ref[:, r, :] if r else lat_ref[:, r, :] * not_pole_ref[0]
        courant_ref[r] = beside(courant, nothing)
    for t in range(tracer_count):
        copies[t + 2].wait()
        q = [beside(tracer_ref[t, :, r, :], side_ref[t, r]) for r in range(rows)]
        north_ref[t] = NEAR * q[3] - FAR * q[2]
        own_flux = [
            courant_ref[0] * (NEAR * q[0] - FAR * q[1]),
            courant_ref[1] * (NEAR * (q[1] + q[0]) - FAR * q[2]),
            courant_ref[2] * (NEAR * (q[2] + q[1]) - FAR * (q[3] + q[0])),
            courant_ref[3] * (NEAR * (q[3] + q[2]) - FAR * q[1]),
        ]
        for r in range(rows):
            west, west2, east = pltpu.roll(q[r], 1, 1), pltpu.roll(q[r], 2, 1), pltpu.roll(q[r], width - 1, 1)
            flux = beside(lon_ref[:, r, :], side_ref[tracer_count, r]) * (NEAR * (q[r] + west) - FAR * (east + west2))
            value = q[r] - (pltpu.roll(flux, width - 1, 1) - flux) + own_flux[r]
            if r + 1 < rows:
                value = value - own_flux[r + 1]
            base_ref[t, r] = value


def physics_kernel(levels, sector, owner_count, chunk, even_ref, *refs):
    count = len(refs) - 12 >> 1
    first_refs, refs = refs[:count], refs[count:]
    base_ref, north_ref, inner_ref, outer_ref = refs[:4]
    top_ref, courant_ref, surface_ref, mixing_ref, decay_ref, owner_ref, energy_in_ref = refs[4:11]
    physics_refs, energy_ref = refs[11:-1], refs[-1]
    rows, width = base_ref.shape[1], base_ref.shape[-1]
    courant = [courant_ref[r] for r in range(rows)]
    even = even_ref[0] == 1
    top = top_ref[...]
    top = jnp.concatenate([top[:, :width], second_half(top, sector)], axis=0)
    mix_high, mix_low = split_high_low(mixing_ref[...])
    mix = jnp.concatenate([mix_high, mix_high, mix_low, mix_low], axis=1)
    level = lax.broadcasted_iota(jnp.int32, (8, width), 0)
    lane = lax.broadcasted_iota(jnp.int32, (8, width), 1)
    energies = [energy_in_ref[r] for r in range(rows)]
    for first_ref, physics_ref in zip(first_refs, physics_refs):
        t = first_ref[0] + chunk
        inner = inner_ref[pl.ds(pl.multiple_of(levels * t, levels), levels), :]
        outer = jnp.where(first_ref[0] == 0, outer_ref[:levels, :], outer_ref[levels:, :])
        low, high = jnp.where(even, outer, inner), jnp.where(even, inner, outer)
        low_a, low_b = low[:, :width], second_half(low, sector)
        high_a, high_b = high[:, :width], second_half(high, sector)
        south = courant[0] * (NEAR * low_b - FAR * low_a)
        south_in = courant[1] * (FAR * low_b)
        north_in = courant[3] * (FAR * high_a)
        north = top * (NEAR * high_a - FAR * high_b + north_ref[t])
        extra = [south + south_in, -south_in, north_in, -north_in - north]
        for r in range(rows):
            advected = base_ref[t, r] + extra[r]
            part_high, part_low = split_high_low(advected)
            stacked = jnp.concatenate([part_high, part_low, part_high, part_low], axis=0)
            mixed = jnp.dot(mix, stacked, preferred_element_type=jnp.float32)
            surface = jnp.where(level == 7, surface_ref[t, r : r + 1, :], 0.0)
            mixed = jnp.concatenate([mixed[: levels - 8], mixed[levels - 8 :] + surface], axis=0)
            physics = mixed / (1.0 + decay_ref[t] * mixed * mixed)
            physics_ref[r] = physics
            gap = physics - advected
            squared = gap * gap
            for k in range(levels // 8):
                energies[r] = energies[r] + squared[8 * k : 8 * k + 8]
    if not owner_count:
        for r in range(rows):
            energy_ref[r] = energies[r]
        return
    energies = [jnp.where(lane < sector, energy, 0.0) for energy in energies]
    spot = lax.broadcasted_iota(jnp.int32, (1, LANES), 1)
    result = jnp.zeros((1, LANES), jnp.float32)
    for owner in range(owner_count):
        chosen = jnp.zeros((8, LANES), jnp.float32)
        for r in range(rows):
            picked = jnp.where(owner_ref[r : r + 1, :] == owner, energies[r], 0.0)
            for k in range(width // LANES):
                chosen = chosen + picked[:, LANES * k : LANES * (k + 1)]
        total = jnp.sum(jnp.sum(chosen, axis=0, keepdims=True), axis=1, keepdims=True)
        result = jnp.where(spot == owner, total, result)
    energy_ref[...] = result


def waves_of(radix):
    pairs = (radix - 1) // 2
    cosine = lambda k, i: math.cos(2.0 * math.pi * ((k * i) % radix) / radix)
    sine = lambda k, i: math.sin(2.0 * math.pi * ((k * i) % radix) / radix)
    return pairs, cosine, sine


def row_of(piece_refs, r):
    return piece_refs[0].at[r] if len(piece_refs) == 1 else piece_refs[r].at[0]


def stacked_table(high_ref, low_ref, begin, size):
    high = high_ref[begin : begin + size, :]
    return jnp.concatenate([high, high, low_ref[begin : begin + size, :]], axis=0)


def product_of(high_ref, low_ref, begin, size, table):
    high = high_ref[:, begin : begin + size]
    stacked = jnp.concatenate([high, low_ref[:, begin : begin + size], high], axis=1)
    return jnp.dot(stacked, table, preferred_element_type=jnp.float32)


def forward_kernel(radix, pieces, own_ref, *refs):
    other_refs, refs = refs[:pieces], refs[pieces:]
    table_high_ref, table_low_ref, first_high_ref, first_low_ref, scale_ref, *refs = refs
    out_high_ref, out_low_ref, high_ref, low_ref = refs
    rows, levels, width = own_ref.shape
    pairs, cosine, sine = waves_of(radix)
    segments = width // LANES
    shift = radix * LANES // 2 % LANES
    lane = lax.broadcasted_iota(jnp.int32, (levels, LANES), 1)

    def store(place, column, wave):
        high_ref[place, column : column + LANES], low_ref[place, column : column + LANES] = split_high_low(wave)

    for r in range(rows):
        place = slice(levels * r, levels * (r + 1))
        other_ref = row_of(other_refs, r)
        own = [own_ref[r, :, LANES * n : LANES * (n + 1)] for n in range(segments)]
        turned = [pltpu.roll(other_ref[:, LANES * n : LANES * (n + 1)], shift, 1) for n in range(segments)]
        joined = own[:-1] + [jnp.where(lane < shift, own[-1], turned[0])]
        joined += [jnp.where(lane < shift, turned[n], turned[n + 1]) for n in range(segments - 1)]
        plus = [joined[n] + joined[radix - n] for n in range(1, pairs + 1)]
        minus = [joined[radix - n] - joined[n] for n in range(1, pairs + 1)]
        store(place, 0, sum(plus, joined[0]))
        for k in range(1, pairs + 1):
            real = sum((cosine(k, n) * plus[n - 1] for n in range(1, pairs + 1)), joined[0])
            imaginary = sine(k, 1) * minus[0]
            for n in range(2, pairs + 1):
                imaginary = imaginary + sine(k, n) * minus[n - 1]
            store(place, LANES * (2 * k - 1), real)
            store(place, LANES * 2 * k, imaginary)

    def transform(begin, size, table):
        spectrum = product_of(high_ref, low_ref, begin, size, table)
        for r in range(rows):
            place = slice(levels * r, levels * (r + 1))
            damped = spectrum[place] * scale_ref[r : r + 1, begin : begin + size]
            out_high_ref[place, begin : begin + size], out_low_ref[place, begin : begin + size] = split_high_low(damped)

    transform(0, LANES, stacked_table(first_high_ref, first_low_ref, 0, LANES))
    for k in range(pairs):
        transform(LANES * (2 * k + 1), 2 * LANES, stacked_table(table_high_ref, table_low_ref, 2 * LANES * k, 2 * LANES))


def inverse_kernel(radix, pieces, mask_ref, own_ref, *refs):
    other_refs, refs = refs[:pieces], refs[pieces:]
    high_ref, low_ref, table_high_ref, table_low_ref, first_high_ref, first_low_ref, *refs = refs
    result_ref, back_ref, wave_ref = refs
    rows, levels, width = own_ref.shape
    sector = result_ref.shape[-1]
    pairs, cosine, sine = waves_of(radix)
    segments = width // LANES
    shift = radix * LANES // 2 % LANES
    lane = lax.broadcasted_iota(jnp.int32, (levels, LANES), 1)

    def transform(begin, size, table):
        wave_ref[:, begin : begin + size] = product_of(high_ref, low_ref, begin, size, table)

    transform(0, LANES, stacked_table(first_high_ref, first_low_ref, 0, LANES))
    for k in range(pairs):
        transform(LANES * (2 * k + 1), 2 * LANES, stacked_table(table_high_ref, table_low_ref, 2 * LANES * k, 2 * LANES))

    for r in range(rows):
        place = slice(levels * r, levels * (r + 1))
        other_ref = row_of(other_refs, r)
        waves = [wave_ref[place, LANES * n : LANES * (n + 1)] for n in range(radix)]
        results = [None] * radix
        results[0] = sum((waves[2 * k - 1] for k in range(1, pairs + 1)), waves[0])
        for n in range(1, pairs + 1):
            even = sum((cosine(k, n) * waves[2 * k - 1] for k in range(1, pairs + 1)), waves[0])
            odd = sine(1, n) * waves[2]
            for k in range(2, pairs + 1):
                odd = odd + sine(k, n) * waves[2 * k]
            results[n], results[radix - n] = even - odd, even + odd
        filtered_row = mask_ref[r] == 1
        turned = [pltpu.roll(result, LANES - shift, 1) for result in results[segments - 1 :]]
        for n in range(segments):
            begin = LANES * n
            size = min(LANES, sector - begin)
            value = jnp.where(filtered_row, results[n], own_ref[r, :, begin : begin + LANES])
            result_ref[:, r, begin : begin + size] = value[:, :size]
            value = jnp.where(lane < LANES - shift, turned[n], turned[min(n + 1, segments - 1)])
            back_ref[r, :, begin : begin + LANES] = jnp.where(filtered_row, value, other_ref[:, begin : begin + LANES])


def finish_kernel(keep_ref, give_ref, *refs):
    out_hbm, turned_ref, sems = refs[-3:]
    count = turned_ref.shape[0]
    result_refs, received_refs = refs[:count], refs[count : 2 * count]
    rows, levels, width = received_refs[0].shape
    sector = out_hbm.shape[-1]
    piece = levels // PIECES
    copies = []

    def send(source_ref, tracer, slot):
        for part in range(PIECES):
            span = pl.ds(piece * part, piece)
            copies.append(pltpu.make_async_copy(source_ref.at[span], out_hbm.at[tracer, span], sems.at[slot, part]))
            copies[-1].start()

    for i, result_ref in enumerate(result_refs):
        send(result_ref, keep_ref[0] + i, i)
    for i in range(count):
        for r in range(rows):
            turned_ref[i, :, r, :] = received_refs[i][r, :, :sector]
        send(turned_ref.at[i], give_ref[0] + i, count + i)
    for copy in copies:
        copy.wait()


def on_device(tracers, courant_lat, courant_lon, surface_flux, mixing, decay_rate, owners, polar_mask):
    tracer_count, levels, rows, sector = tracers.shape
    assert rows == 4 and sector % 64 == 0 and lax.axis_size("lon") == 2
    f32 = jnp.float32
    lat_count, lat = lax.axis_size("lat"), lax.axis_index("lat")
    length = 2 * sector
    width = -(-sector // LANES) * LANES
    radix = length // LANES
    downward = [(i + 1, i) for i in range(lat_count - 1)]
    swap = [(0, 1), (1, 0)]

    whole = pl.BlockSpec(memory_space=pltpu.VMEM)
    in_hbm = pl.BlockSpec(memory_space=pltpu.HBM)
    scalars = pl.BlockSpec(memory_space=pltpu.SMEM)
    even = (1 - lat % 2).reshape(1)
    inside = [pair for i in range(0, lat_count - 1, 2) for pair in ((i, i + 1), (i + 1, i))]
    across = [pair for i in range(1, lat_count - 1, 2) for pair in ((i, i + 1), (i + 1, i))]
    fields = [pltpu.with_memory_space_constraint(array, pltpu.HBM) for array in (tracers, courant_lat, courant_lon)]
    field_buffers = [pltpu.VMEM(array.shape, f32) for array in (tracers, courant_lat, courant_lon)]
    half = tracer_count // 2
    inner = pl.pallas_call(
        pack_kernel,
        in_specs=[scalars, in_hbm],
        out_specs=whole,
        out_shape=pltpu.VMEM((levels * tracer_count, length), f32),
        scratch_shapes=[pltpu.VMEM((tracer_count, levels, 2, sector), f32), pltpu.SemaphoreType.DMA((tracer_count,))],
        compiler_params=params(),
        cost_estimate=cost(0, 600_000),
        name="pack",
    )(even, fields[0])
    from_inside = lax.ppermute(inner, "lat", inside)
    even_rest, inner = lax.optimization_barrier((even, inner))
    *outer, courant_row, sides = pl.pallas_call(
        rest_kernel,
        in_specs=[scalars] + [in_hbm] * 3,
        out_specs=[whole] * (half + 2),
        out_shape=[pltpu.VMEM((levels * 2, length), f32)] * half
        + [
            jax.ShapeDtypeStruct((levels // 2, length), f32),
            jax.ShapeDtypeStruct((tracer_count + 1, rows, levels, LANES), f32),
        ],
        scratch_shapes=field_buffers + [pltpu.SemaphoreType.DMA((tracer_count + 2,))],
        compiler_params=params(),
        cost_estimate=cost(0, 0),
        name="rest",
    )(even_rest, *fields)
    top = lax.ppermute(courant_row, "lat", downward)

    sides = lax.ppermute(sides, "lon", swap)
    not_pole = (lat > 0).astype(f32).reshape(1)
    base, north, lat_courant = pl.pallas_call(
        functools.partial(base_kernel, width),
        in_specs=[scalars, in_hbm, in_hbm, in_hbm, whole],
        out_specs=[whole] * 3,
        out_shape=[
            jax.ShapeDtypeStruct((tracer_count, rows, levels, width), f32),
            jax.ShapeDtypeStruct((tracer_count, levels, width), f32),
            jax.ShapeDtypeStruct((rows, levels, width), f32),
        ],
        scratch_shapes=field_buffers + [pltpu.SemaphoreType.DMA((tracer_count + 2,))],
        compiler_params=params(),
        cost_estimate=cost(0, 0),
        name="base",
    )(not_pole, *fields, sides)

    surface = jnp.pad(surface_flux, ((0, 0), (0, 0), (0, width - sector)))
    decay = decay_rate[:, :, None]
    block_count = rows * sector // BLOCK
    block_of = (np.arange(rows)[:, None] * sector + np.minimum(np.arange(width), sector - 1)[None]) // BLOCK
    owner_of = jnp.repeat(owners.reshape(block_count), BLOCK).reshape(rows, sector)
    owner_of = jnp.pad(owner_of, ((0, 0), (0, width - sector)))
    forward, inverse, numbers, weights = spectral_tables(length)
    row_ids = (lat * rows + jnp.arange(rows)).astype(f32)
    latitude = (-0.5 + (row_ids + 0.5) / (lat_count * rows)) * math.pi
    inverse_sine = np.where(numbers == 0, 1.0, 1.0 / np.where(numbers == 0, 1.0, np.sin(np.pi * numbers / length)))
    ratio = 2.0 * jnp.cos(latitude)[:, None] * jnp.asarray(inverse_sine, f32)[None]
    damping = jnp.where(jnp.asarray(numbers == 0)[None], 1.0, jnp.minimum(1.0, ratio * ratio))
    scale = damping * jnp.asarray(weights, f32)[None]

    base, scale, owner_of, surface, decay = lax.optimization_barrier((base, scale, owner_of, surface, decay))

    base, outer = lax.optimization_barrier((base, outer))
    from_across = [lax.ppermute(part, "lat", across) for part in outer]

    keep = (half * lax.axis_index("lon")).reshape(1)
    give = half - keep
    circles = jax.ShapeDtypeStruct((half, rows, levels, width), f32)
    result_shape = jax.ShapeDtypeStruct((levels, rows, sector), f32)
    out_shape = jax.ShapeDtypeStruct(tracers.shape, f32)

    def run_physics(chunk, firsts, energy, last=False):
        shapes = [jax.ShapeDtypeStruct(circles.shape[1:], f32)] * len(firsts)
        shapes.append(jax.ShapeDtypeStruct((1, LANES) if last else energy.shape, f32))
        *results, energy = pl.pallas_call(
            functools.partial(physics_kernel, levels, sector, lat_count if last else 0, chunk),
            in_specs=[scalars] * (1 + len(firsts)) + [whole] * 11,
            out_specs=[whole] * len(shapes),
            out_shape=shapes,
            compiler_params=params(),
            cost_estimate=cost(0, 0),
            name="physics",
        )(even, *firsts, base, north, from_inside, from_across[chunk], top, lat_courant, surface, mixing, decay, owner_of, energy)
        return results, energy

    forward, inverse = ([jnp.asarray(part) for table in tables for part in split_table(table)] for tables in (forward, inverse))
    circle = jax.ShapeDtypeStruct(circles.shape[1:], f32)
    spectra = jax.ShapeDtypeStruct((rows * levels, length), jnp.bfloat16)

    def run_forward(own, other):
        return pl.pallas_call(
            functools.partial(forward_kernel, radix, len(other)),
            in_specs=[whole] * (6 + len(other)),
            out_specs=[whole] * 2,
            out_shape=[spectra] * 2,
            scratch_shapes=[pltpu.VMEM(spectra.shape, jnp.bfloat16)] * 2,
            compiler_params=params(),
            cost_estimate=cost(0, 0),
            name="forward",
        )(own, *other, *forward, scale)

    def run_inverse(own, other, high, low):
        return pl.pallas_call(
            functools.partial(inverse_kernel, radix, len(other)),
            in_specs=[scalars] + [whole] * (7 + len(other)),
            out_specs=[whole] * 2,
            out_shape=[result_shape, circle],
            scratch_shapes=[pltpu.VMEM(spectra.shape, f32)],
            compiler_params=params(),
            cost_estimate=cost(0, 0),
            name="inverse",
        )(polar_mask, own, *other, high, low, *inverse)

    energy = jnp.zeros((rows, 8, width), f32)
    results, received = [], []
    for chunk in range(half - 1):
        (given, own), energy = run_physics(chunk, [give, keep], energy)
        other = [lax.ppermute(given[r : r + 1], "lon", swap) for r in range(rows)]
        spectrum = run_forward(own, other)
        result, back = run_inverse(own, other, *spectrum)
        results.append(result)
        received.append(lax.ppermute(back, "lon", swap))
        energy, back = lax.optimization_barrier((energy, back))

    distances = [1 << i for i in range(lat_count.bit_length() - 1)]

    def send_energy(energy):
        distance = distances.pop(0)
        return lax.ppermute(energy, "lat", [(i, i ^ distance) for i in range(lat_count)])

    (given, own), energy = run_physics(half - 1, [give, keep], energy, True)
    other = [lax.ppermute(given, "lon", swap)]

    coming = send_energy(energy)
    high, low = run_forward(own, other)
    coming, high = lax.optimization_barrier((coming, high))
    energy = energy + coming
    energy, high = lax.optimization_barrier((energy, high))

    coming = send_energy(energy)
    result, back = run_inverse(own, other, high, low)
    coming, back = lax.optimization_barrier((coming, back))
    energy = energy + coming
    energy, back = lax.optimization_barrier((energy, back))
    results.append(result)
    received.append(lax.ppermute(back, "lon", swap))

    coming = send_energy(energy)
    out = pl.pallas_call(
        finish_kernel,
        in_specs=[scalars] * 2 + [whole] * (2 * half),
        out_specs=in_hbm,
        out_shape=out_shape,
        scratch_shapes=[
            pltpu.VMEM((half,) + result_shape.shape, f32),
            pltpu.SemaphoreType.DMA((2 * half, PIECES)),
        ],
        compiler_params=params(),
        cost_estimate=cost(0, 3_000_000),
        name="finish",
    )(keep, give, *results, *received)
    coming, out = lax.optimization_barrier((coming, out))
    energy = energy + coming
    while distances:
        energy = energy + send_energy(energy)

    owner_energy = lax.dynamic_slice(energy, (0, lat), (1, 1)) / (block_count * BLOCK)
    return out, owner_energy


def solution(mesh):
    placed = (
        P("group", None, "lat", "lon"),
        P("group", "lat", "lon"),
        P("group", "lat", "lon"),
        P("group", "lat", "lon"),
        P(),
        P(),
        P(("group", "lat"), "lon", None, None),
        P(("group", "lat")),
    )
    return jax.shard_map(
        on_device,
        mesh=mesh,
        in_specs=placed,
        out_specs=(P("group", None, "lat", "lon"), P(("group", "lat"), "lon")),
        check_vma=False,
    )
```

```python
import functools
import math

import jax
import jax.numpy as jnp
import numpy as np
from jax import lax
from jax.experimental import pallas as pl
from jax.experimental.pallas import tpu as pltpu
from jax.sharding import PartitionSpec as P

LANES = 128
BLOCK = 128
VMEM_BYTES = 6 * 1024 * 1024
PIECES = 4
NEAR = 7.0 / 12.0
FAR = 1.0 / 12.0


def params():
    return pltpu.CompilerParams(vmem_limit_bytes=VMEM_BYTES)


def cost(flops, bytes_accessed):
    return pl.CostEstimate(flops=flops, bytes_accessed=bytes_accessed, transcendentals=0)


def split_high_low(value):
    high = value.astype(jnp.bfloat16)
    low = (value - high.astype(jnp.float32)).astype(jnp.bfloat16)
    return high, low


def split_table(table):
    high = table.astype(jnp.bfloat16.dtype)
    return high, (table - high.astype(np.float64)).astype(jnp.bfloat16.dtype)


def spectral_tables(length):
    radix = length // LANES
    pairs = (radix - 1) // 2
    spot = np.arange(LANES)[:, None]
    number = np.arange(LANES)[None, :]
    is_cosine = number <= LANES // 2
    wave = np.where(is_cosine, number, number - LANES // 2)
    angle = 2.0 * np.pi * ((spot * wave) % LANES) / LANES
    first = np.where(is_cosine, np.cos(angle), np.sin(angle))
    others, numbers = [], [radix * wave[0]]
    weights = [np.where((wave[0] == 0) | (wave[0] == LANES // 2), 1.0, 2.0) / length]
    for residue in range(1, pairs + 1):
        whole = residue + radix * number
        angle = 2.0 * np.pi * ((spot * whole) % length) / length
        cosine, sine = np.cos(angle), np.sin(angle)
        others.append(np.block([[cosine, -sine], [sine, cosine]]))
        folded = np.minimum(whole[0], length - whole[0])
        numbers += [folded, folded]
        weights.append(np.full(2 * LANES, 2.0 / length))
    forward = np.concatenate(others), first
    inverse = np.concatenate([table.T for table in others]), first.T
    return forward, inverse, np.concatenate(numbers), np.concatenate(weights)


def pack_rows(first, second):
    return jnp.concatenate([first, second], axis=1)


def second_half(packed, sector):
    skip, shift = sector // LANES, sector % LANES
    segments = [packed[:, LANES * i : LANES * (i + 1)] for i in range(packed.shape[1] // LANES)]
    if shift == 0:
        return jnp.concatenate(segments[skip:], axis=1)
    turned = [pltpu.roll(segment, LANES - shift, 1) for segment in segments[skip:]]
    lane = lax.broadcasted_iota(jnp.int32, turned[0].shape, 1)
    parts = [jnp.where(lane < LANES - shift, turned[i], turned[min(i + 1, len(turned) - 1)]) for i in range(len(turned))]
    return jnp.concatenate(parts, axis=1)


def start_copies(pairs, sems):
    copies = [pltpu.make_async_copy(source, target, sems.at[i]) for i, (source, target) in enumerate(pairs)]
    for copy in copies:
        copy.start()
    return copies


def pack_kernel(even_ref, tracer_hbm, out_ref, row_ref, sems):
    count, levels = row_ref.shape[:2]
    first_row = pl.multiple_of(jnp.where(even_ref[0] == 1, tracer_hbm.shape[2] - 2, 0), 2)
    sources = [tracer_hbm.at[t, :, pl.ds(first_row, 2), :] for t in range(count)]
    copies = start_copies([(sources[t], row_ref.at[t]) for t in range(count)], sems)
    for t in range(count):
        copies[t].wait()
        out_ref[levels * t : levels * (t + 1), :] = pack_rows(row_ref[t, :, 0, :], row_ref[t, :, 1, :])


def rest_kernel(even_ref, tracer_hbm, lat_hbm, lon_hbm, *refs):
    courant_ref, side_ref, tracer_ref, lat_ref, lon_ref, sems = refs[-6:]
    outer_refs = refs[:-6]
    count, levels, rows, sector = tracer_ref.shape
    pairs = [(tracer_hbm.at[t], tracer_ref.at[t]) for t in range(count)] + [(lat_hbm, lat_ref), (lon_hbm, lon_ref)]
    copies = start_copies(pairs, sems)
    shift, whole = sector % LANES, sector // LANES * LANES
    lane = lax.broadcasted_iota(jnp.int32, (levels, LANES), 1)
    even = even_ref[0] == 1

    def store_side(i, r, values):
        first = pltpu.roll(values[:, :LANES], shift, 1)
        last = jnp.concatenate([values[:, whole:], values[:, whole:]], axis=1)
        side_ref[i, r] = jnp.where(lane < LANES - 2, first, last)

    for t in range(count):
        copies[t].wait()
        row = [tracer_ref[t, :, r, :] for r in range(rows)]
        slot = t // len(outer_refs)
        outer_refs[t % len(outer_refs)][levels * slot : levels * (slot + 1), :] = pack_rows(
            jnp.where(even, row[0], row[rows - 2]), jnp.where(even, row[1], row[rows - 1])
        )
        for r in range(rows):
            store_side(t, r, row[r])
    copies[count].wait()
    courant = lat_ref[:, 0, :]
    courant_ref[...] = pack_rows(courant[: levels // 2], courant[levels // 2 :])
    copies[count + 1].wait()
    for r in range(rows):
        store_side(count, r, lon_ref[:, r, :])


def base_kernel(width, not_pole_ref, tracer_hbm, lat_hbm, lon_hbm, side_ref, base_ref, north_ref, courant_ref, *scratch):
    tracer_ref, lat_ref, lon_ref, sems = scratch
    tracer_count, levels, rows, sector = tracer_ref.shape
    whole = sector // LANES * LANES
    pairs = [(lat_hbm, lat_ref), (lon_hbm, lon_ref)] + [(tracer_hbm.at[t], tracer_ref.at[t]) for t in range(tracer_count)]
    copies = start_copies(pairs, sems)

    def beside(values, side):
        return jnp.concatenate([values[:, :whole], values[:, whole:], side[:, sector - whole :]], axis=1)

    copies[0].wait()
    copies[1].wait()
    nothing = jnp.zeros((levels, LANES), jnp.float32)
    for r in range(rows):
        courant = lat_ref[:, r, :] if r else lat_ref[:, r, :] * not_pole_ref[0]
        courant_ref[r] = beside(courant, nothing)
    for t in range(tracer_count):
        copies[t + 2].wait()
        q = [beside(tracer_ref[t, :, r, :], side_ref[t, r]) for r in range(rows)]
        north_ref[t] = NEAR * q[3] - FAR * q[2]
        own_flux = [
            courant_ref[0] * (NEAR * q[0] - FAR * q[1]),
            courant_ref[1] * (NEAR * (q[1] + q[0]) - FAR * q[2]),
            courant_ref[2] * (NEAR * (q[2] + q[1]) - FAR * (q[3] + q[0])),
            courant_ref[3] * (NEAR * (q[3] + q[2]) - FAR * q[1]),
        ]
        for r in range(rows):
            west, west2, east = pltpu.roll(q[r], 1, 1), pltpu.roll(q[r], 2, 1), pltpu.roll(q[r], width - 1, 1)
            flux = beside(lon_ref[:, r, :], side_ref[tracer_count, r]) * (NEAR * (q[r] + west) - FAR * (east + west2))
            value = q[r] - (pltpu.roll(flux, width - 1, 1) - flux) + own_flux[r]
            if r + 1 < rows:
                value = value - own_flux[r + 1]
            base_ref[t, r] = value


def physics_kernel(levels, sector, owner_count, chunk, even_ref, *refs):
    count = len(refs) - 12 >> 1
    first_refs, refs = refs[:count], refs[count:]
    base_ref, north_ref, inner_ref, outer_ref = refs[:4]
    top_ref, courant_ref, surface_ref, mixing_ref, decay_ref, owner_ref, energy_in_ref = refs[4:11]
    physics_refs, energy_ref = refs[11:-1], refs[-1]
    rows, width = base_ref.shape[1], base_ref.shape[-1]
    courant = [courant_ref[r] for r in range(rows)]
    even = even_ref[0] == 1
    top = top_ref[...]
    top = jnp.concatenate([top[:, :width], second_half(top, sector)], axis=0)
    mix_high, mix_low = split_high_low(mixing_ref[...])
    mix = jnp.concatenate([mix_high, mix_high, mix_low, mix_low], axis=1)
    level = lax.broadcasted_iota(jnp.int32, (8, width), 0)
    lane = lax.broadcasted_iota(jnp.int32, (8, width), 1)
    energies = [energy_in_ref[r] for r in range(rows)]
    for first_ref, physics_ref in zip(first_refs, physics_refs):
        t = first_ref[0] + chunk
        inner = inner_ref[pl.ds(pl.multiple_of(levels * t, levels), levels), :]
        outer = jnp.where(first_ref[0] == 0, outer_ref[:levels, :], outer_ref[levels:, :])
        low, high = jnp.where(even, outer, inner), jnp.where(even, inner, outer)
        low_a, low_b = low[:, :width], second_half(low, sector)
        high_a, high_b = high[:, :width], second_half(high, sector)
        south = courant[0] * (NEAR * low_b - FAR * low_a)
        south_in = courant[1] * (FAR * low_b)
        north_in = courant[3] * (FAR * high_a)
        north = top * (NEAR * high_a - FAR * high_b + north_ref[t])
        extra = [south + south_in, -south_in, north_in, -north_in - north]
        for r in range(rows):
            advected = base_ref[t, r] + extra[r]
            part_high, part_low = split_high_low(advected)
            stacked = jnp.concatenate([part_high, part_low, part_high, part_low], axis=0)
            mixed = jnp.dot(mix, stacked, preferred_element_type=jnp.float32)
            surface = jnp.where(level == 7, surface_ref[t, r : r + 1, :], 0.0)
            mixed = jnp.concatenate([mixed[: levels - 8], mixed[levels - 8 :] + surface], axis=0)
            physics = mixed / (1.0 + decay_ref[t] * mixed * mixed)
            physics_ref[r] = physics
            gap = physics - advected
            squared = gap * gap
            for k in range(levels // 8):
                energies[r] = energies[r] + squared[8 * k : 8 * k + 8]
    if not owner_count:
        for r in range(rows):
            energy_ref[r] = energies[r]
        return
    energies = [jnp.where(lane < sector, energy, 0.0) for energy in energies]
    spot = lax.broadcasted_iota(jnp.int32, (1, LANES), 1)
    result = jnp.zeros((1, LANES), jnp.float32)
    for owner in range(owner_count):
        chosen = jnp.zeros((8, LANES), jnp.float32)
        for r in range(rows):
            picked = jnp.where(owner_ref[r : r + 1, :] == owner, energies[r], 0.0)
            for k in range(width // LANES):
                chosen = chosen + picked[:, LANES * k : LANES * (k + 1)]
        total = jnp.sum(jnp.sum(chosen, axis=0, keepdims=True), axis=1, keepdims=True)
        result = jnp.where(spot == owner, total, result)
    energy_ref[...] = result


def waves_of(radix):
    pairs = (radix - 1) // 2
    cosine = lambda k, i: math.cos(2.0 * math.pi * ((k * i) % radix) / radix)
    sine = lambda k, i: math.sin(2.0 * math.pi * ((k * i) % radix) / radix)
    return pairs, cosine, sine


def row_of(piece_refs, r):
    return piece_refs[0].at[r] if len(piece_refs) == 1 else piece_refs[r].at[0]


def stacked_table(high_ref, low_ref, begin, size):
    high = high_ref[begin : begin + size, :]
    return jnp.concatenate([high, high, low_ref[begin : begin + size, :]], axis=0)


def product_of(high_ref, low_ref, begin, size, table):
    high = high_ref[:, begin : begin + size]
    stacked = jnp.concatenate([high, low_ref[:, begin : begin + size], high], axis=1)
    return jnp.dot(stacked, table, preferred_element_type=jnp.float32)


def forward_kernel(radix, pieces, own_ref, *refs):
    other_refs, refs = refs[:pieces], refs[pieces:]
    table_high_ref, table_low_ref, first_high_ref, first_low_ref, scale_ref, *refs = refs
    out_high_ref, out_low_ref, high_ref, low_ref = refs
    rows, levels, width = own_ref.shape
    pairs, cosine, sine = waves_of(radix)
    segments = width // LANES
    shift = radix * LANES // 2 % LANES
    lane = lax.broadcasted_iota(jnp.int32, (levels, LANES), 1)

    def store(place, column, wave):
        high_ref[place, column : column + LANES], low_ref[place, column : column + LANES] = split_high_low(wave)

    for r in range(rows):
        place = slice(levels * r, levels * (r + 1))
        other_ref = row_of(other_refs, r)
        own = [own_ref[r, :, LANES * n : LANES * (n + 1)] for n in range(segments)]
        turned = [pltpu.roll(other_ref[:, LANES * n : LANES * (n + 1)], shift, 1) for n in range(segments)]
        joined = own[:-1] + [jnp.where(lane < shift, own[-1], turned[0])]
        joined += [jnp.where(lane < shift, turned[n], turned[n + 1]) for n in range(segments - 1)]
        plus = [joined[n] + joined[radix - n] for n in range(1, pairs + 1)]
        minus = [joined[radix - n] - joined[n] for n in range(1, pairs + 1)]
        store(place, 0, sum(plus, joined[0]))
        for k in range(1, pairs + 1):
            real = sum((cosine(k, n) * plus[n - 1] for n in range(1, pairs + 1)), joined[0])
            imaginary = sine(k, 1) * minus[0]
            for n in range(2, pairs + 1):
                imaginary = imaginary + sine(k, n) * minus[n - 1]
            store(place, LANES * (2 * k - 1), real)
            store(place, LANES * 2 * k, imaginary)

    def transform(begin, size, table):
        spectrum = product_of(high_ref, low_ref, begin, size, table)
        for r in range(rows):
            place = slice(levels * r, levels * (r + 1))
            damped = spectrum[place] * scale_ref[r : r + 1, begin : begin + size]
            out_high_ref[place, begin : begin + size], out_low_ref[place, begin : begin + size] = split_high_low(damped)

    transform(0, LANES, stacked_table(first_high_ref, first_low_ref, 0, LANES))
    for k in range(pairs):
        transform(LANES * (2 * k + 1), 2 * LANES, stacked_table(table_high_ref, table_low_ref, 2 * LANES * k, 2 * LANES))


def inverse_kernel(radix, pieces, mask_ref, own_ref, *refs):
    other_refs, refs = refs[:pieces], refs[pieces:]
    high_ref, low_ref, table_high_ref, table_low_ref, first_high_ref, first_low_ref, *refs = refs
    result_ref, back_ref, wave_ref = refs
    rows, levels, width = own_ref.shape
    sector = result_ref.shape[-1]
    pairs, cosine, sine = waves_of(radix)
    segments = width // LANES
    shift = radix * LANES // 2 % LANES
    lane = lax.broadcasted_iota(jnp.int32, (levels, LANES), 1)

    def transform(begin, size, table):
        wave_ref[:, begin : begin + size] = product_of(high_ref, low_ref, begin, size, table)

    transform(0, LANES, stacked_table(first_high_ref, first_low_ref, 0, LANES))
    for k in range(pairs):
        transform(LANES * (2 * k + 1), 2 * LANES, stacked_table(table_high_ref, table_low_ref, 2 * LANES * k, 2 * LANES))

    for r in range(rows):
        place = slice(levels * r, levels * (r + 1))
        other_ref = row_of(other_refs, r)
        waves = [wave_ref[place, LANES * n : LANES * (n + 1)] for n in range(radix)]
        results = [None] * radix
        results[0] = sum((waves[2 * k - 1] for k in range(1, pairs + 1)), waves[0])
        for n in range(1, pairs + 1):
            even = sum((cosine(k, n) * waves[2 * k - 1] for k in range(1, pairs + 1)), waves[0])
            odd = sine(1, n) * waves[2]
            for k in range(2, pairs + 1):
                odd = odd + sine(k, n) * waves[2 * k]
            results[n], results[radix - n] = even - odd, even + odd
        filtered_row = mask_ref[r] == 1
        turned = [pltpu.roll(result, LANES - shift, 1) for result in results[segments - 1 :]]
        for n in range(segments):
            begin = LANES * n
            size = min(LANES, sector - begin)
            value = jnp.where(filtered_row, results[n], own_ref[r, :, begin : begin + LANES])
            result_ref[:, r, begin : begin + size] = value[:, :size]
            value = jnp.where(lane < LANES - shift, turned[n], turned[min(n + 1, segments - 1)])
            back_ref[r, :, begin : begin + LANES] = jnp.where(filtered_row, value, other_ref[:, begin : begin + LANES])


def finish_kernel(keep_ref, give_ref, *refs):
    out_hbm, turned_ref, sems = refs[-3:]
    count = turned_ref.shape[0]
    result_refs, received_refs = refs[:count], refs[count : 2 * count]
    rows, levels, width = received_refs[0].shape
    sector = out_hbm.shape[-1]
    piece = levels // PIECES
    copies = []

    def send(source_ref, tracer, slot):
        for part in range(PIECES):
            span = pl.ds(piece * part, piece)
            copies.append(pltpu.make_async_copy(source_ref.at[span], out_hbm.at[tracer, span], sems.at[slot, part]))
            copies[-1].start()

    for i, result_ref in enumerate(result_refs):
        send(result_ref, keep_ref[0] + i, i)
    for i in range(count):
        for r in range(rows):
            turned_ref[i, :, r, :] = received_refs[i][r, :, :sector]
        send(turned_ref.at[i], give_ref[0] + i, count + i)
    for copy in copies:
        copy.wait()


def on_device(tracers, courant_lat, courant_lon, surface_flux, mixing, decay_rate, owners, polar_mask):
    tracer_count, levels, rows, sector = tracers.shape
    assert rows == 4 and sector % 64 == 0 and lax.axis_size("lon") == 2
    f32 = jnp.float32
    lat_count, lat = lax.axis_size("lat"), lax.axis_index("lat")
    length = 2 * sector
    width = -(-sector // LANES) * LANES
    radix = length // LANES
    downward = [(i + 1, i) for i in range(lat_count - 1)]
    swap = [(0, 1), (1, 0)]

    whole = pl.BlockSpec(memory_space=pltpu.VMEM)
    in_hbm = pl.BlockSpec(memory_space=pltpu.HBM)
    scalars = pl.BlockSpec(memory_space=pltpu.SMEM)
    even = (1 - lat % 2).reshape(1)
    inside = [pair for i in range(0, lat_count - 1, 2) for pair in ((i, i + 1), (i + 1, i))]
    across = [pair for i in range(1, lat_count - 1, 2) for pair in ((i, i + 1), (i + 1, i))]
    fields = [pltpu.with_memory_space_constraint(array, pltpu.HBM) for array in (tracers, courant_lat, courant_lon)]
    field_buffers = [pltpu.VMEM(array.shape, f32) for array in (tracers, courant_lat, courant_lon)]
    half = tracer_count // 2
    inner = pl.pallas_call(
        pack_kernel,
        in_specs=[scalars, in_hbm],
        out_specs=whole,
        out_shape=pltpu.VMEM((levels * tracer_count, length), f32),
        scratch_shapes=[pltpu.VMEM((tracer_count, levels, 2, sector), f32), pltpu.SemaphoreType.DMA((tracer_count,))],
        compiler_params=params(),
        cost_estimate=cost(0, 600_000),
        name="pack",
    )(even, fields[0])
    from_inside = lax.ppermute(inner, "lat", inside)
    even_rest, inner = lax.optimization_barrier((even, inner))
    *outer, courant_row, sides = pl.pallas_call(
        rest_kernel,
        in_specs=[scalars] + [in_hbm] * 3,
        out_specs=[whole] * (half + 2),
        out_shape=[pltpu.VMEM((levels * 2, length), f32)] * half
        + [
            jax.ShapeDtypeStruct((levels // 2, length), f32),
            jax.ShapeDtypeStruct((tracer_count + 1, rows, levels, LANES), f32),
        ],
        scratch_shapes=field_buffers + [pltpu.SemaphoreType.DMA((tracer_count + 2,))],
        compiler_params=params(),
        cost_estimate=cost(0, 0),
        name="rest",
    )(even_rest, *fields)
    from_across = [lax.ppermute(part, "lat", across) for part in outer[:-1]]
    top = lax.ppermute(courant_row, "lat", downward)

    sides = lax.ppermute(sides, "lon", swap)
    sides, outer = lax.optimization_barrier((sides, outer))
    from_across.append(lax.ppermute(outer[-1], "lat", across))
    not_pole = (lat > 0).astype(f32).reshape(1)
    base, north, lat_courant = pl.pallas_call(
        functools.partial(base_kernel, width),
        in_specs=[scalars, in_hbm, in_hbm, in_hbm, whole],
        out_specs=[whole] * 3,
        out_shape=[
            jax.ShapeDtypeStruct((tracer_count, rows, levels, width), f32),
            jax.ShapeDtypeStruct((tracer_count, levels, width), f32),
            jax.ShapeDtypeStruct((rows, levels, width), f32),
        ],
        scratch_shapes=field_buffers + [pltpu.SemaphoreType.DMA((tracer_count + 2,))],
        compiler_params=params(),
        cost_estimate=cost(0, 0),
        name="base",
    )(not_pole, *fields, sides)

    surface = jnp.pad(surface_flux, ((0, 0), (0, 0), (0, width - sector)))
    decay = decay_rate[:, :, None]
    block_count = rows * sector // BLOCK
    block_of = (np.arange(rows)[:, None] * sector + np.minimum(np.arange(width), sector - 1)[None]) // BLOCK
    owner_of = jnp.repeat(owners.reshape(block_count), BLOCK).reshape(rows, sector)
    owner_of = jnp.pad(owner_of, ((0, 0), (0, width - sector)))
    forward, inverse, numbers, weights = spectral_tables(length)
    row_ids = (lat * rows + jnp.arange(rows)).astype(f32)
    latitude = (-0.5 + (row_ids + 0.5) / (lat_count * rows)) * math.pi
    inverse_sine = np.where(numbers == 0, 1.0, 1.0 / np.where(numbers == 0, 1.0, np.sin(np.pi * numbers / length)))
    ratio = 2.0 * jnp.cos(latitude)[:, None] * jnp.asarray(inverse_sine, f32)[None]
    damping = jnp.where(jnp.asarray(numbers == 0)[None], 1.0, jnp.minimum(1.0, ratio * ratio))
    scale = damping * jnp.asarray(weights, f32)[None]

    base, scale, owner_of, surface, decay = lax.optimization_barrier((base, scale, owner_of, surface, decay))

    keep = (half * lax.axis_index("lon")).reshape(1)
    give = half - keep
    circles = jax.ShapeDtypeStruct((half, rows, levels, width), f32)
    result_shape = jax.ShapeDtypeStruct((levels, rows, sector), f32)
    out_shape = jax.ShapeDtypeStruct(tracers.shape, f32)

    def run_physics(chunk, firsts, energy, last=False):
        shapes = [jax.ShapeDtypeStruct(circles.shape[1:], f32)] * len(firsts)
        shapes.append(jax.ShapeDtypeStruct((1, LANES) if last else energy.shape, f32))
        *results, energy = pl.pallas_call(
            functools.partial(physics_kernel, levels, sector, lat_count if last else 0, chunk),
            in_specs=[scalars] * (1 + len(firsts)) + [whole] * 11,
            out_specs=[whole] * len(shapes),
            out_shape=shapes,
            compiler_params=params(),
            cost_estimate=cost(0, 0),
            name="physics",
        )(even, *firsts, base, north, from_inside, from_across[chunk], top, lat_courant, surface, mixing, decay, owner_of, energy)
        return results, energy

    forward, inverse = ([jnp.asarray(part) for table in tables for part in split_table(table)] for tables in (forward, inverse))
    circle = jax.ShapeDtypeStruct(circles.shape[1:], f32)
    spectra = jax.ShapeDtypeStruct((rows * levels, length), jnp.bfloat16)

    def run_forward(own, other):
        return pl.pallas_call(
            functools.partial(forward_kernel, radix, len(other)),
            in_specs=[whole] * (6 + len(other)),
            out_specs=[whole] * 2,
            out_shape=[spectra] * 2,
            scratch_shapes=[pltpu.VMEM(spectra.shape, jnp.bfloat16)] * 2,
            compiler_params=params(),
            cost_estimate=cost(0, 0),
            name="forward",
        )(own, *other, *forward, scale)

    def run_inverse(own, other, high, low):
        return pl.pallas_call(
            functools.partial(inverse_kernel, radix, len(other)),
            in_specs=[scalars] + [whole] * (7 + len(other)),
            out_specs=[whole] * 2,
            out_shape=[result_shape, circle],
            scratch_shapes=[pltpu.VMEM(spectra.shape, f32)],
            compiler_params=params(),
            cost_estimate=cost(0, 0),
            name="inverse",
        )(polar_mask, own, *other, high, low, *inverse)

    energy = jnp.zeros((rows, 8, width), f32)
    results, received = [], []
    for chunk in range(half - 1):
        (given, own), energy = run_physics(chunk, [give, keep], energy)
        other = [lax.ppermute(given[r : r + 1], "lon", swap) for r in range(rows)]
        spectrum = run_forward(own, other)
        result, back = run_inverse(own, other, *spectrum)
        results.append(result)
        received.append(lax.ppermute(back, "lon", swap))
        energy, back = lax.optimization_barrier((energy, back))

    distances = [1 << i for i in range(lat_count.bit_length() - 1)]

    def send_energy(energy):
        distance = distances.pop(0)
        return lax.ppermute(energy, "lat", [(i, i ^ distance) for i in range(lat_count)])

    (given, own), energy = run_physics(half - 1, [give, keep], energy, True)
    other = [lax.ppermute(given, "lon", swap)]

    coming = send_energy(energy)
    high, low = run_forward(own, other)
    coming, high = lax.optimization_barrier((coming, high))
    energy = energy + coming
    energy, high = lax.optimization_barrier((energy, high))

    coming = send_energy(energy)
    result, back = run_inverse(own, other, high, low)
    coming, back = lax.optimization_barrier((coming, back))
    energy = energy + coming
    energy, back = lax.optimization_barrier((energy, back))
    results.append(result)
    received.append(lax.ppermute(back, "lon", swap))

    coming = send_energy(energy)
    out = pl.pallas_call(
        finish_kernel,
        in_specs=[scalars] * 2 + [whole] * (2 * half),
        out_specs=in_hbm,
        out_shape=out_shape,
        scratch_shapes=[
            pltpu.VMEM((half,) + result_shape.shape, f32),
            pltpu.SemaphoreType.DMA((2 * half, PIECES)),
        ],
        compiler_params=params(),
        cost_estimate=cost(0, 3_000_000),
        name="finish",
    )(keep, give, *results, *received)
    coming, out = lax.optimization_barrier((coming, out))
    energy = energy + coming
    while distances:
        energy = energy + send_energy(energy)

    owner_energy = lax.dynamic_slice(energy, (0, lat), (1, 1)) / (block_count * BLOCK)
    return out, owner_energy


def solution(mesh):
    placed = (
        P("group", None, "lat", "lon"),
        P("group", "lat", "lon"),
        P("group", "lat", "lon"),
        P("group", "lat", "lon"),
        P(),
        P(),
        P(("group", "lat"), "lon", None, None),
        P(("group", "lat")),
    )
    return jax.shard_map(
        on_device,
        mesh=mesh,
        in_specs=placed,
        out_specs=(P("group", None, "lat", "lon"), P(("group", "lat"), "lon")),
        check_vma=False,
    )
```

```python
import functools
import math

import jax
import jax.numpy as jnp
import numpy as np
from jax import lax
from jax.experimental import pallas as pl
from jax.experimental.pallas import tpu as pltpu
from jax.sharding import PartitionSpec as P

LANES = 128
BLOCK = 128
VMEM_BYTES = 6 * 1024 * 1024
PIECES = 4
NEAR = 7.0 / 12.0
FAR = 1.0 / 12.0


def params():
    return pltpu.CompilerParams(vmem_limit_bytes=VMEM_BYTES)


def cost(flops, bytes_accessed):
    return pl.CostEstimate(flops=flops, bytes_accessed=bytes_accessed, transcendentals=0)


def split_high_low(value):
    high = value.astype(jnp.bfloat16)
    low = (value - high.astype(jnp.float32)).astype(jnp.bfloat16)
    return high, low


def split_table(table):
    high = table.astype(jnp.bfloat16.dtype)
    return high, (table - high.astype(np.float64)).astype(jnp.bfloat16.dtype)


def spectral_tables(length):
    radix = length // LANES
    pairs = (radix - 1) // 2
    spot = np.arange(LANES)[:, None]
    number = np.arange(LANES)[None, :]
    is_cosine = number <= LANES // 2
    wave = np.where(is_cosine, number, number - LANES // 2)
    angle = 2.0 * np.pi * ((spot * wave) % LANES) / LANES
    first = np.where(is_cosine, np.cos(angle), np.sin(angle))
    others, numbers = [], [radix * wave[0]]
    weights = [np.where((wave[0] == 0) | (wave[0] == LANES // 2), 1.0, 2.0) / length]
    for residue in range(1, pairs + 1):
        whole = residue + radix * number
        angle = 2.0 * np.pi * ((spot * whole) % length) / length
        cosine, sine = np.cos(angle), np.sin(angle)
        others.append(np.block([[cosine, -sine], [sine, cosine]]))
        folded = np.minimum(whole[0], length - whole[0])
        numbers += [folded, folded]
        weights.append(np.full(2 * LANES, 2.0 / length))
    forward = np.concatenate(others), first
    inverse = np.concatenate([table.T for table in others]), first.T
    return forward, inverse, np.concatenate(numbers), np.concatenate(weights)


def pack_rows(first, second):
    return jnp.concatenate([first, second], axis=1)


def second_half(packed, sector):
    skip, shift = sector // LANES, sector % LANES
    segments = [packed[:, LANES * i : LANES * (i + 1)] for i in range(packed.shape[1] // LANES)]
    if shift == 0:
        return jnp.concatenate(segments[skip:], axis=1)
    turned = [pltpu.roll(segment, LANES - shift, 1) for segment in segments[skip:]]
    lane = lax.broadcasted_iota(jnp.int32, turned[0].shape, 1)
    parts = [jnp.where(lane < LANES - shift, turned[i], turned[min(i + 1, len(turned) - 1)]) for i in range(len(turned))]
    return jnp.concatenate(parts, axis=1)


def start_copies(pairs, sems):
    copies = [pltpu.make_async_copy(source, target, sems.at[i]) for i, (source, target) in enumerate(pairs)]
    for copy in copies:
        copy.start()
    return copies


def pack_kernel(even_ref, tracer_hbm, out_ref, row_ref, sems):
    count, levels = row_ref.shape[:2]
    first_row = pl.multiple_of(jnp.where(even_ref[0] == 1, tracer_hbm.shape[2] - 2, 0), 2)
    sources = [tracer_hbm.at[t, :, pl.ds(first_row, 2), :] for t in range(count)]
    copies = start_copies([(sources[t], row_ref.at[t]) for t in range(count)], sems)
    for t in range(count):
        copies[t].wait()
        out_ref[levels * t : levels * (t + 1), :] = pack_rows(row_ref[t, :, 0, :], row_ref[t, :, 1, :])


def rest_kernel(even_ref, tracer_hbm, lat_hbm, lon_hbm, *refs):
    courant_ref, side_ref, tracer_ref, lat_ref, lon_ref, sems = refs[-6:]
    outer_refs = refs[:-6]
    count, levels, rows, sector = tracer_ref.shape
    pairs = [(tracer_hbm.at[t], tracer_ref.at[t]) for t in range(count)] + [(lat_hbm, lat_ref), (lon_hbm, lon_ref)]
    copies = start_copies(pairs, sems)
    shift, whole = sector % LANES, sector // LANES * LANES
    lane = lax.broadcasted_iota(jnp.int32, (levels, LANES), 1)
    even = even_ref[0] == 1

    def store_side(i, r, values):
        first = pltpu.roll(values[:, :LANES], shift, 1)
        last = jnp.concatenate([values[:, whole:], values[:, whole:]], axis=1)
        side_ref[i, r] = jnp.where(lane < LANES - 2, first, last)

    for copy in copies:
        copy.wait()
    for t in range(count):
        row = [tracer_ref[t, :, r, :] for r in range(rows)]
        slot = t // len(outer_refs)
        outer_refs[t % len(outer_refs)][levels * slot : levels * (slot + 1), :] = pack_rows(
            jnp.where(even, row[0], row[rows - 2]), jnp.where(even, row[1], row[rows - 1])
        )
        for r in range(rows):
            store_side(t, r, row[r])
    courant = lat_ref[:, 0, :]
    courant_ref[...] = pack_rows(courant[: levels // 2], courant[levels // 2 :])
    for r in range(rows):
        store_side(count, r, lon_ref[:, r, :])


def base_kernel(width, not_pole_ref, tracer_hbm, lat_hbm, lon_hbm, side_ref, base_ref, north_ref, courant_ref, *scratch):
    tracer_ref, lat_ref, lon_ref, sems = scratch
    tracer_count, levels, rows, sector = tracer_ref.shape
    whole = sector // LANES * LANES
    pairs = [(lat_hbm, lat_ref), (lon_hbm, lon_ref)] + [(tracer_hbm.at[t], tracer_ref.at[t]) for t in range(tracer_count)]
    copies = start_copies(pairs, sems)

    def beside(values, side):
        return jnp.concatenate([values[:, :whole], values[:, whole:], side[:, sector - whole :]], axis=1)

    copies[0].wait()
    copies[1].wait()
    nothing = jnp.zeros((levels, LANES), jnp.float32)
    for r in range(rows):
        courant = lat_ref[:, r, :] if r else lat_ref[:, r, :] * not_pole_ref[0]
        courant_ref[r] = beside(courant, nothing)
    for t in range(tracer_count):
        copies[t + 2].wait()
        q = [beside(tracer_ref[t, :, r, :], side_ref[t, r]) for r in range(rows)]
        north_ref[t] = NEAR * q[3] - FAR * q[2]
        own_flux = [
            courant_ref[0] * (NEAR * q[0] - FAR * q[1]),
            courant_ref[1] * (NEAR * (q[1] + q[0]) - FAR * q[2]),
            courant_ref[2] * (NEAR * (q[2] + q[1]) - FAR * (q[3] + q[0])),
            courant_ref[3] * (NEAR * (q[3] + q[2]) - FAR * q[1]),
        ]
        for r in range(rows):
            west, west2, east = pltpu.roll(q[r], 1, 1), pltpu.roll(q[r], 2, 1), pltpu.roll(q[r], width - 1, 1)
            flux = beside(lon_ref[:, r, :], side_ref[tracer_count, r]) * (NEAR * (q[r] + west) - FAR * (east + west2))
            value = q[r] - (pltpu.roll(flux, width - 1, 1) - flux) + own_flux[r]
            if r + 1 < rows:
                value = value - own_flux[r + 1]
            base_ref[t, r] = value


def physics_kernel(levels, sector, owner_count, chunk, even_ref, *refs):
    count = len(refs) - 12 >> 1
    first_refs, refs = refs[:count], refs[count:]
    base_ref, north_ref, inner_ref, outer_ref = refs[:4]
    top_ref, courant_ref, surface_ref, mixing_ref, decay_ref, owner_ref, energy_in_ref = refs[4:11]
    physics_refs, energy_ref = refs[11:-1], refs[-1]
    rows, width = base_ref.shape[1], base_ref.shape[-1]
    courant = [courant_ref[r] for r in range(rows)]
    even = even_ref[0] == 1
    top = top_ref[...]
    top = jnp.concatenate([top[:, :width], second_half(top, sector)], axis=0)
    mix_high, mix_low = split_high_low(mixing_ref[...])
    mix = jnp.concatenate([mix_high, mix_high, mix_low, mix_low], axis=1)
    level = lax.broadcasted_iota(jnp.int32, (8, width), 0)
    lane = lax.broadcasted_iota(jnp.int32, (8, width), 1)
    energies = [energy_in_ref[r] for r in range(rows)]
    for first_ref, physics_ref in zip(first_refs, physics_refs):
        t = first_ref[0] + chunk
        inner = inner_ref[pl.ds(pl.multiple_of(levels * t, levels), levels), :]
        outer = jnp.where(first_ref[0] == 0, outer_ref[:levels, :], outer_ref[levels:, :])
        low, high = jnp.where(even, outer, inner), jnp.where(even, inner, outer)
        low_a, low_b = low[:, :width], second_half(low, sector)
        high_a, high_b = high[:, :width], second_half(high, sector)
        south = courant[0] * (NEAR * low_b - FAR * low_a)
        south_in = courant[1] * (FAR * low_b)
        north_in = courant[3] * (FAR * high_a)
        north = top * (NEAR * high_a - FAR * high_b + north_ref[t])
        extra = [south + south_in, -south_in, north_in, -north_in - north]
        for r in range(rows):
            advected = base_ref[t, r] + extra[r]
            part_high, part_low = split_high_low(advected)
            stacked = jnp.concatenate([part_high, part_low, part_high, part_low], axis=0)
            mixed = jnp.dot(mix, stacked, preferred_element_type=jnp.float32)
            surface = jnp.where(level == 7, surface_ref[t, r : r + 1, :], 0.0)
            mixed = jnp.concatenate([mixed[: levels - 8], mixed[levels - 8 :] + surface], axis=0)
            physics = mixed / (1.0 + decay_ref[t] * mixed * mixed)
            physics_ref[r] = physics
            gap = physics - advected
            squared = gap * gap
            for k in range(levels // 8):
                energies[r] = energies[r] + squared[8 * k : 8 * k + 8]
    if not owner_count:
        for r in range(rows):
            energy_ref[r] = energies[r]
        return
    energies = [jnp.where(lane < sector, energy, 0.0) for energy in energies]
    spot = lax.broadcasted_iota(jnp.int32, (1, LANES), 1)
    result = jnp.zeros((1, LANES), jnp.float32)
    for owner in range(owner_count):
        chosen = jnp.zeros((8, LANES), jnp.float32)
        for r in range(rows):
            picked = jnp.where(owner_ref[r : r + 1, :] == owner, energies[r], 0.0)
            for k in range(width // LANES):
                chosen = chosen + picked[:, LANES * k : LANES * (k + 1)]
        total = jnp.sum(jnp.sum(chosen, axis=0, keepdims=True), axis=1, keepdims=True)
        result = jnp.where(spot == owner, total, result)
    energy_ref[...] = result


def waves_of(radix):
    pairs = (radix - 1) // 2
    cosine = lambda k, i: math.cos(2.0 * math.pi * ((k * i) % radix) / radix)
    sine = lambda k, i: math.sin(2.0 * math.pi * ((k * i) % radix) / radix)
    return pairs, cosine, sine


def row_of(piece_refs, r):
    return piece_refs[0].at[r] if len(piece_refs) == 1 else piece_refs[r].at[0]


def stacked_table(high_ref, low_ref, begin, size):
    high = high_ref[begin : begin + size, :]
    return jnp.concatenate([high, high, low_ref[begin : begin + size, :]], axis=0)


def product_of(high_ref, low_ref, begin, size, table):
    high = high_ref[:, begin : begin + size]
    stacked = jnp.concatenate([high, low_ref[:, begin : begin + size], high], axis=1)
    return jnp.dot(stacked, table, preferred_element_type=jnp.float32)


def forward_kernel(radix, pieces, own_ref, *refs):
    other_refs, refs = refs[:pieces], refs[pieces:]
    table_high_ref, table_low_ref, first_high_ref, first_low_ref, scale_ref, *refs = refs
    out_high_ref, out_low_ref, high_ref, low_ref = refs
    rows, levels, width = own_ref.shape
    pairs, cosine, sine = waves_of(radix)
    segments = width // LANES
    shift = radix * LANES // 2 % LANES
    lane = lax.broadcasted_iota(jnp.int32, (levels, LANES), 1)

    def store(place, column, wave):
        high_ref[place, column : column + LANES], low_ref[place, column : column + LANES] = split_high_low(wave)

    for r in range(rows):
        place = slice(levels * r, levels * (r + 1))
        other_ref = row_of(other_refs, r)
        own = [own_ref[r, :, LANES * n : LANES * (n + 1)] for n in range(segments)]
        turned = [pltpu.roll(other_ref[:, LANES * n : LANES * (n + 1)], shift, 1) for n in range(segments)]
        joined = own[:-1] + [jnp.where(lane < shift, own[-1], turned[0])]
        joined += [jnp.where(lane < shift, turned[n], turned[n + 1]) for n in range(segments - 1)]
        plus = [joined[n] + joined[radix - n] for n in range(1, pairs + 1)]
        minus = [joined[radix - n] - joined[n] for n in range(1, pairs + 1)]
        store(place, 0, sum(plus, joined[0]))
        for k in range(1, pairs + 1):
            real = sum((cosine(k, n) * plus[n - 1] for n in range(1, pairs + 1)), joined[0])
            imaginary = sine(k, 1) * minus[0]
            for n in range(2, pairs + 1):
                imaginary = imaginary + sine(k, n) * minus[n - 1]
            store(place, LANES * (2 * k - 1), real)
            store(place, LANES * 2 * k, imaginary)

    def transform(begin, size, table):
        spectrum = product_of(high_ref, low_ref, begin, size, table)
        for r in range(rows):
            place = slice(levels * r, levels * (r + 1))
            damped = spectrum[place] * scale_ref[r : r + 1, begin : begin + size]
            out_high_ref[place, begin : begin + size], out_low_ref[place, begin : begin + size] = split_high_low(damped)

    transform(0, LANES, stacked_table(first_high_ref, first_low_ref, 0, LANES))
    for k in range(pairs):
        transform(LANES * (2 * k + 1), 2 * LANES, stacked_table(table_high_ref, table_low_ref, 2 * LANES * k, 2 * LANES))


def inverse_kernel(radix, pieces, mask_ref, own_ref, *refs):
    other_refs, refs = refs[:pieces], refs[pieces:]
    high_ref, low_ref, table_high_ref, table_low_ref, first_high_ref, first_low_ref, *refs = refs
    result_ref, back_ref, wave_ref = refs
    rows, levels, width = own_ref.shape
    sector = result_ref.shape[-1]
    pairs, cosine, sine = waves_of(radix)
    segments = width // LANES
    shift = radix * LANES // 2 % LANES
    lane = lax.broadcasted_iota(jnp.int32, (levels, LANES), 1)

    def transform(begin, size, table):
        wave_ref[:, begin : begin + size] = product_of(high_ref, low_ref, begin, size, table)

    transform(0, LANES, stacked_table(first_high_ref, first_low_ref, 0, LANES))
    for k in range(pairs):
        transform(LANES * (2 * k + 1), 2 * LANES, stacked_table(table_high_ref, table_low_ref, 2 * LANES * k, 2 * LANES))

    for r in range(rows):
        place = slice(levels * r, levels * (r + 1))
        other_ref = row_of(other_refs, r)
        waves = [wave_ref[place, LANES * n : LANES * (n + 1)] for n in range(radix)]
        results = [None] * radix
        results[0] = sum((waves[2 * k - 1] for k in range(1, pairs + 1)), waves[0])
        for n in range(1, pairs + 1):
            even = sum((cosine(k, n) * waves[2 * k - 1] for k in range(1, pairs + 1)), waves[0])
            odd = sine(1, n) * waves[2]
            for k in range(2, pairs + 1):
                odd = odd + sine(k, n) * waves[2 * k]
            results[n], results[radix - n] = even - odd, even + odd
        filtered_row = mask_ref[r] == 1
        turned = [pltpu.roll(result, LANES - shift, 1) for result in results[segments - 1 :]]
        for n in range(segments):
            begin = LANES * n
            size = min(LANES, sector - begin)
            value = jnp.where(filtered_row, results[n], own_ref[r, :, begin : begin + LANES])
            result_ref[:, r, begin : begin + size] = value[:, :size]
            value = jnp.where(lane < LANES - shift, turned[n], turned[min(n + 1, segments - 1)])
            back_ref[r, :, begin : begin + LANES] = jnp.where(filtered_row, value, other_ref[:, begin : begin + LANES])


def finish_kernel(keep_ref, give_ref, *refs):
    out_hbm, turned_ref, sems = refs[-3:]
    count = turned_ref.shape[0]
    result_refs, received_refs = refs[:count], refs[count : 2 * count]
    rows, levels, width = received_refs[0].shape
    sector = out_hbm.shape[-1]
    piece = levels // PIECES
    copies = []

    def send(source_ref, tracer, slot):
        for part in range(PIECES):
            span = pl.ds(piece * part, piece)
            copies.append(pltpu.make_async_copy(source_ref.at[span], out_hbm.at[tracer, span], sems.at[slot, part]))
            copies[-1].start()

    for i, result_ref in enumerate(result_refs):
        send(result_ref, keep_ref[0] + i, i)
    for i in range(count):
        for r in range(rows):
            turned_ref[i, :, r, :] = received_refs[i][r, :, :sector]
        send(turned_ref.at[i], give_ref[0] + i, count + i)
    for copy in copies:
        copy.wait()


def on_device(tracers, courant_lat, courant_lon, surface_flux, mixing, decay_rate, owners, polar_mask):
    tracer_count, levels, rows, sector = tracers.shape
    assert rows == 4 and sector % 64 == 0 and lax.axis_size("lon") == 2
    f32 = jnp.float32
    lat_count, lat = lax.axis_size("lat"), lax.axis_index("lat")
    length = 2 * sector
    width = -(-sector // LANES) * LANES
    radix = length // LANES
    downward = [(i + 1, i) for i in range(lat_count - 1)]
    swap = [(0, 1), (1, 0)]

    whole = pl.BlockSpec(memory_space=pltpu.VMEM)
    in_hbm = pl.BlockSpec(memory_space=pltpu.HBM)
    scalars = pl.BlockSpec(memory_space=pltpu.SMEM)
    even = (1 - lat % 2).reshape(1)
    inside = [pair for i in range(0, lat_count - 1, 2) for pair in ((i, i + 1), (i + 1, i))]
    across = [pair for i in range(1, lat_count - 1, 2) for pair in ((i, i + 1), (i + 1, i))]
    fields = [pltpu.with_memory_space_constraint(array, pltpu.HBM) for array in (tracers, courant_lat, courant_lon)]
    field_buffers = [pltpu.VMEM(array.shape, f32) for array in (tracers, courant_lat, courant_lon)]
    half = tracer_count // 2
    inner = pl.pallas_call(
        pack_kernel,
        in_specs=[scalars, in_hbm],
        out_specs=whole,
        out_shape=pltpu.VMEM((levels * tracer_count, length), f32),
        scratch_shapes=[pltpu.VMEM((tracer_count, levels, 2, sector), f32), pltpu.SemaphoreType.DMA((tracer_count,))],
        compiler_params=params(),
        cost_estimate=cost(0, 600_000),
        name="pack",
    )(even, fields[0])
    from_inside = lax.ppermute(inner, "lat", inside)
    even_rest, inner = lax.optimization_barrier((even, inner))
    *outer, courant_row, sides = pl.pallas_call(
        rest_kernel,
        in_specs=[scalars] + [in_hbm] * 3,
        out_specs=[whole] * (half + 2),
        out_shape=[pltpu.VMEM((levels * 2, length), f32)] * half
        + [
            jax.ShapeDtypeStruct((levels // 2, length), f32),
            jax.ShapeDtypeStruct((tracer_count + 1, rows, levels, LANES), f32),
        ],
        scratch_shapes=field_buffers + [pltpu.SemaphoreType.DMA((tracer_count + 2,))],
        compiler_params=params(),
        cost_estimate=cost(0, 0),
        name="rest",
    )(even_rest, *fields)
    from_across = [lax.ppermute(part, "lat", across) for part in outer[:-1]]
    top = lax.ppermute(courant_row, "lat", downward)

    sides = lax.ppermute(sides, "lon", swap)
    not_pole = (lat > 0).astype(f32).reshape(1)
    base, north, lat_courant = pl.pallas_call(
        functools.partial(base_kernel, width),
        in_specs=[scalars, in_hbm, in_hbm, in_hbm, whole],
        out_specs=[whole] * 3,
        out_shape=[
            jax.ShapeDtypeStruct((tracer_count, rows, levels, width), f32),
            jax.ShapeDtypeStruct((tracer_count, levels, width), f32),
            jax.ShapeDtypeStruct((rows, levels, width), f32),
        ],
        scratch_shapes=field_buffers + [pltpu.SemaphoreType.DMA((tracer_count + 2,))],
        compiler_params=params(),
        cost_estimate=cost(0, 0),
        name="base",
    )(not_pole, *fields, sides)

    surface = jnp.pad(surface_flux, ((0, 0), (0, 0), (0, width - sector)))
    decay = decay_rate[:, :, None]
    block_count = rows * sector // BLOCK
    block_of = (np.arange(rows)[:, None] * sector + np.minimum(np.arange(width), sector - 1)[None]) // BLOCK
    owner_of = jnp.repeat(owners.reshape(block_count), BLOCK).reshape(rows, sector)
    owner_of = jnp.pad(owner_of, ((0, 0), (0, width - sector)))
    forward, inverse, numbers, weights = spectral_tables(length)
    row_ids = (lat * rows + jnp.arange(rows)).astype(f32)
    latitude = (-0.5 + (row_ids + 0.5) / (lat_count * rows)) * math.pi
    inverse_sine = np.where(numbers == 0, 1.0, 1.0 / np.where(numbers == 0, 1.0, np.sin(np.pi * numbers / length)))
    ratio = 2.0 * jnp.cos(latitude)[:, None] * jnp.asarray(inverse_sine, f32)[None]
    damping = jnp.where(jnp.asarray(numbers == 0)[None], 1.0, jnp.minimum(1.0, ratio * ratio))
    scale = damping * jnp.asarray(weights, f32)[None]

    base, scale, owner_of, surface, decay = lax.optimization_barrier((base, scale, owner_of, surface, decay))

    base, outer = lax.optimization_barrier((base, outer))
    from_across.append(lax.ppermute(outer[-1], "lat", across))

    keep = (half * lax.axis_index("lon")).reshape(1)
    give = half - keep
    circles = jax.ShapeDtypeStruct((half, rows, levels, width), f32)
    result_shape = jax.ShapeDtypeStruct((levels, rows, sector), f32)
    out_shape = jax.ShapeDtypeStruct(tracers.shape, f32)

    def run_physics(chunk, firsts, energy, last=False):
        shapes = [jax.ShapeDtypeStruct(circles.shape[1:], f32)] * len(firsts)
        shapes.append(jax.ShapeDtypeStruct((1, LANES) if last else energy.shape, f32))
        *results, energy = pl.pallas_call(
            functools.partial(physics_kernel, levels, sector, lat_count if last else 0, chunk),
            in_specs=[scalars] * (1 + len(firsts)) + [whole] * 11,
            out_specs=[whole] * len(shapes),
            out_shape=shapes,
            compiler_params=params(),
            cost_estimate=cost(0, 0),
            name="physics",
        )(even, *firsts, base, north, from_inside, from_across[chunk], top, lat_courant, surface, mixing, decay, owner_of, energy)
        return results, energy

    forward, inverse = ([jnp.asarray(part) for table in tables for part in split_table(table)] for tables in (forward, inverse))
    circle = jax.ShapeDtypeStruct(circles.shape[1:], f32)
    spectra = jax.ShapeDtypeStruct((rows * levels, length), jnp.bfloat16)

    def run_forward(own, other):
        return pl.pallas_call(
            functools.partial(forward_kernel, radix, len(other)),
            in_specs=[whole] * (6 + len(other)),
            out_specs=[whole] * 2,
            out_shape=[spectra] * 2,
            scratch_shapes=[pltpu.VMEM(spectra.shape, jnp.bfloat16)] * 2,
            compiler_params=params(),
            cost_estimate=cost(0, 0),
            name="forward",
        )(own, *other, *forward, scale)

    def run_inverse(own, other, high, low):
        return pl.pallas_call(
            functools.partial(inverse_kernel, radix, len(other)),
            in_specs=[scalars] + [whole] * (7 + len(other)),
            out_specs=[whole] * 2,
            out_shape=[result_shape, circle],
            scratch_shapes=[pltpu.VMEM(spectra.shape, f32)],
            compiler_params=params(),
            cost_estimate=cost(0, 0),
            name="inverse",
        )(polar_mask, own, *other, high, low, *inverse)

    energy = jnp.zeros((rows, 8, width), f32)
    results, received = [], []
    for chunk in range(half - 1):
        (given, own), energy = run_physics(chunk, [give, keep], energy)
        other = [lax.ppermute(given[r : r + 1], "lon", swap) for r in range(rows)]
        spectrum = run_forward(own, other)
        result, back = run_inverse(own, other, *spectrum)
        results.append(result)
        received.append(lax.ppermute(back, "lon", swap))
        energy, back = lax.optimization_barrier((energy, back))

    distances = [1 << i for i in range(lat_count.bit_length() - 1)]

    def send_energy(energy):
        distance = distances.pop(0)
        return lax.ppermute(energy, "lat", [(i, i ^ distance) for i in range(lat_count)])

    (given, own), energy = run_physics(half - 1, [give, keep], energy, True)
    other = [lax.ppermute(given, "lon", swap)]

    coming = send_energy(energy)
    high, low = run_forward(own, other)
    coming, high = lax.optimization_barrier((coming, high))
    energy = energy + coming
    energy, high = lax.optimization_barrier((energy, high))

    coming = send_energy(energy)
    result, back = run_inverse(own, other, high, low)
    coming, back = lax.optimization_barrier((coming, back))
    energy = energy + coming
    energy, back = lax.optimization_barrier((energy, back))
    results.append(result)
    received.append(lax.ppermute(back, "lon", swap))

    coming = send_energy(energy)
    out = pl.pallas_call(
        finish_kernel,
        in_specs=[scalars] * 2 + [whole] * (2 * half),
        out_specs=in_hbm,
        out_shape=out_shape,
        scratch_shapes=[
            pltpu.VMEM((half,) + result_shape.shape, f32),
            pltpu.SemaphoreType.DMA((2 * half, PIECES)),
        ],
        compiler_params=params(),
        cost_estimate=cost(0, 3_000_000),
        name="finish",
    )(keep, give, *results, *received)
    coming, out = lax.optimization_barrier((coming, out))
    energy = energy + coming
    while distances:
        energy = energy + send_energy(energy)

    owner_energy = lax.dynamic_slice(energy, (0, lat), (1, 1)) / (block_count * BLOCK)
    return out, owner_energy


def solution(mesh):
    placed = (
        P("group", None, "lat", "lon"),
        P("group", "lat", "lon"),
        P("group", "lat", "lon"),
        P("group", "lat", "lon"),
        P(),
        P(),
        P(("group", "lat"), "lon", None, None),
        P(("group", "lat")),
    )
    return jax.shard_map(
        on_device,
        mesh=mesh,
        in_specs=placed,
        out_specs=(P("group", None, "lat", "lon"), P(("group", "lat"), "lon")),
        check_vma=False,
    )
```

```python
import functools
import math

import jax
import jax.numpy as jnp
import numpy as np
from jax import lax
from jax.experimental import pallas as pl
from jax.experimental.pallas import tpu as pltpu
from jax.sharding import PartitionSpec as P

LANES = 128
BLOCK = 128
VMEM_BYTES = 6 * 1024 * 1024
PIECES = 4
NEAR = 7.0 / 12.0
FAR = 1.0 / 12.0


def params():
    return pltpu.CompilerParams(vmem_limit_bytes=VMEM_BYTES)


def cost(flops, bytes_accessed):
    return pl.CostEstimate(flops=flops, bytes_accessed=bytes_accessed, transcendentals=0)


def split_high_low(value):
    high = value.astype(jnp.bfloat16)
    low = (value - high.astype(jnp.float32)).astype(jnp.bfloat16)
    return high, low


def split_table(table):
    high = table.astype(jnp.bfloat16.dtype)
    return high, (table - high.astype(np.float64)).astype(jnp.bfloat16.dtype)


def spectral_tables(length):
    radix = length // LANES
    pairs = (radix - 1) // 2
    spot = np.arange(LANES)[:, None]
    number = np.arange(LANES)[None, :]
    is_cosine = number <= LANES // 2
    wave = np.where(is_cosine, number, number - LANES // 2)
    angle = 2.0 * np.pi * ((spot * wave) % LANES) / LANES
    first = np.where(is_cosine, np.cos(angle), np.sin(angle))
    others, numbers = [], [radix * wave[0]]
    weights = [np.where((wave[0] == 0) | (wave[0] == LANES // 2), 1.0, 2.0) / length]
    for residue in range(1, pairs + 1):
        whole = residue + radix * number
        angle = 2.0 * np.pi * ((spot * whole) % length) / length
        cosine, sine = np.cos(angle), np.sin(angle)
        others.append(np.block([[cosine, -sine], [sine, cosine]]))
        folded = np.minimum(whole[0], length - whole[0])
        numbers += [folded, folded]
        weights.append(np.full(2 * LANES, 2.0 / length))
    forward = np.concatenate(others), first
    inverse = np.concatenate([table.T for table in others]), first.T
    return forward, inverse, np.concatenate(numbers), np.concatenate(weights)


def pack_rows(first, second):
    return jnp.concatenate([first, second], axis=1)


def second_half(packed, sector):
    skip, shift = sector // LANES, sector % LANES
    segments = [packed[:, LANES * i : LANES * (i + 1)] for i in range(packed.shape[1] // LANES)]
    if shift == 0:
        return jnp.concatenate(segments[skip:], axis=1)
    turned = [pltpu.roll(segment, LANES - shift, 1) for segment in segments[skip:]]
    lane = lax.broadcasted_iota(jnp.int32, turned[0].shape, 1)
    parts = [jnp.where(lane < LANES - shift, turned[i], turned[min(i + 1, len(turned) - 1)]) for i in range(len(turned))]
    return jnp.concatenate(parts, axis=1)


def start_copies(pairs, sems):
    copies = [pltpu.make_async_copy(source, target, sems.at[i]) for i, (source, target) in enumerate(pairs)]
    for copy in copies:
        copy.start()
    return copies


def pack_kernel(even_ref, tracer_hbm, out_ref, row_ref, sems):
    count, levels = row_ref.shape[:2]
    first_row = pl.multiple_of(jnp.where(even_ref[0] == 1, tracer_hbm.shape[2] - 2, 0), 2)
    sources = [tracer_hbm.at[t, :, pl.ds(first_row, 2), :] for t in range(count)]
    copies = start_copies([(sources[t], row_ref.at[t]) for t in range(count)], sems)
    for t in range(count):
        copies[t].wait()
        out_ref[levels * t : levels * (t + 1), :] = pack_rows(row_ref[t, :, 0, :], row_ref[t, :, 1, :])


def rest_kernel(even_ref, tracer_hbm, lat_hbm, lon_hbm, *refs):
    courant_ref, side_ref, tracer_ref, lat_ref, lon_ref, sems = refs[-6:]
    outer_refs = refs[:-6]
    count, levels, rows, sector = tracer_ref.shape
    pairs = [(tracer_hbm.at[t], tracer_ref.at[t]) for t in range(count)] + [(lat_hbm, lat_ref), (lon_hbm, lon_ref)]
    copies = start_copies(pairs, sems)
    shift, whole = sector % LANES, sector // LANES * LANES
    lane = lax.broadcasted_iota(jnp.int32, (levels, LANES), 1)
    even = even_ref[0] == 1

    def store_side(i, r, values):
        first = pltpu.roll(values[:, :LANES], shift, 1)
        last = jnp.concatenate([values[:, whole:], values[:, whole:]], axis=1)
        side_ref[i, r] = jnp.where(lane < LANES - 2, first, last)

    for copy in copies:
        copy.wait()
    for t in range(count):
        row = [tracer_ref[t, :, r, :] for r in range(rows)]
        slot = t // len(outer_refs)
        outer_refs[t % len(outer_refs)][levels * slot : levels * (slot + 1), :] = pack_rows(
            jnp.where(even, row[0], row[rows - 2]), jnp.where(even, row[1], row[rows - 1])
        )
        for r in range(rows):
            store_side(t, r, row[r])
    courant = lat_ref[:, 0, :]
    courant_ref[...] = pack_rows(courant[: levels // 2], courant[levels // 2 :])
    for r in range(rows):
        store_side(count, r, lon_ref[:, r, :])


def base_kernel(width, not_pole_ref, tracer_hbm, lat_hbm, lon_hbm, side_ref, base_ref, north_ref, courant_ref, *scratch):
    tracer_ref, lat_ref, lon_ref, sems = scratch
    tracer_count, levels, rows, sector = tracer_ref.shape
    whole = sector // LANES * LANES
    pairs = [(lat_hbm, lat_ref), (lon_hbm, lon_ref)] + [(tracer_hbm.at[t], tracer_ref.at[t]) for t in range(tracer_count)]
    copies = start_copies(pairs, sems)

    def beside(values, side):
        return jnp.concatenate([values[:, :whole], values[:, whole:], side[:, sector - whole :]], axis=1)

    copies[0].wait()
    copies[1].wait()
    nothing = jnp.zeros((levels, LANES), jnp.float32)
    for r in range(rows):
        courant = lat_ref[:, r, :] if r else lat_ref[:, r, :] * not_pole_ref[0]
        courant_ref[r] = beside(courant, nothing)
    for t in range(tracer_count):
        copies[t + 2].wait()
        q = [beside(tracer_ref[t, :, r, :], side_ref[t, r]) for r in range(rows)]
        north_ref[t] = NEAR * q[3] - FAR * q[2]
        own_flux = [
            courant_ref[0] * (NEAR * q[0] - FAR * q[1]),
            courant_ref[1] * (NEAR * (q[1] + q[0]) - FAR * q[2]),
            courant_ref[2] * (NEAR * (q[2] + q[1]) - FAR * (q[3] + q[0])),
            courant_ref[3] * (NEAR * (q[3] + q[2]) - FAR * q[1]),
        ]
        for r in range(rows):
            west, west2, east = pltpu.roll(q[r], 1, 1), pltpu.roll(q[r], 2, 1), pltpu.roll(q[r], width - 1, 1)
            flux = beside(lon_ref[:, r, :], side_ref[tracer_count, r]) * (NEAR * (q[r] + west) - FAR * (east + west2))
            value = q[r] - (pltpu.roll(flux, width - 1, 1) - flux) + own_flux[r]
            if r + 1 < rows:
                value = value - own_flux[r + 1]
            base_ref[t, r] = value


def physics_kernel(levels, sector, owner_count, chunk, even_ref, *refs):
    count = len(refs) - 12 >> 1
    first_refs, refs = refs[:count], refs[count:]
    base_ref, north_ref, inner_ref, outer_ref = refs[:4]
    top_ref, courant_ref, surface_ref, mixing_ref, decay_ref, owner_ref, energy_in_ref = refs[4:11]
    physics_refs, energy_ref = refs[11:-1], refs[-1]
    rows, width = base_ref.shape[1], base_ref.shape[-1]
    courant = [courant_ref[r] for r in range(rows)]
    even = even_ref[0] == 1
    top = top_ref[...]
    top = jnp.concatenate([top[:, :width], second_half(top, sector)], axis=0)
    mix_high, mix_low = split_high_low(mixing_ref[...])
    mix = jnp.concatenate([mix_high, mix_high, mix_low, mix_low], axis=1)
    level = lax.broadcasted_iota(jnp.int32, (8, width), 0)
    lane = lax.broadcasted_iota(jnp.int32, (8, width), 1)
    energies = [energy_in_ref[r] for r in range(rows)]
    for first_ref, physics_ref in zip(first_refs, physics_refs):
        t = first_ref[0] + chunk
        inner = inner_ref[pl.ds(pl.multiple_of(levels * t, levels), levels), :]
        outer = jnp.where(first_ref[0] == 0, outer_ref[:levels, :], outer_ref[levels:, :])
        low, high = jnp.where(even, outer, inner), jnp.where(even, inner, outer)
        low_a, low_b = low[:, :width], second_half(low, sector)
        high_a, high_b = high[:, :width], second_half(high, sector)
        south = courant[0] * (NEAR * low_b - FAR * low_a)
        south_in = courant[1] * (FAR * low_b)
        north_in = courant[3] * (FAR * high_a)
        north = top * (NEAR * high_a - FAR * high_b + north_ref[t])
        extra = [south + south_in, -south_in, north_in, -north_in - north]
        for r in range(rows):
            advected = base_ref[t, r] + extra[r]
            part_high, part_low = split_high_low(advected)
            stacked = jnp.concatenate([part_high, part_low, part_high, part_low], axis=0)
            mixed = jnp.dot(mix, stacked, preferred_element_type=jnp.float32)
            surface = jnp.where(level == 7, surface_ref[t, r : r + 1, :], 0.0)
            mixed = jnp.concatenate([mixed[: levels - 8], mixed[levels - 8 :] + surface], axis=0)
            physics = mixed / (1.0 + decay_ref[t] * mixed * mixed)
            physics_ref[r] = physics
            gap = physics - advected
            squared = gap * gap
            for k in range(levels // 8):
                energies[r] = energies[r] + squared[8 * k : 8 * k + 8]
    if not owner_count:
        for r in range(rows):
            energy_ref[r] = energies[r]
        return
    energies = [jnp.where(lane < sector, energy, 0.0) for energy in energies]
    spot = lax.broadcasted_iota(jnp.int32, (1, LANES), 1)
    result = jnp.zeros((1, LANES), jnp.float32)
    for owner in range(owner_count):
        chosen = jnp.zeros((8, LANES), jnp.float32)
        for r in range(rows):
            picked = jnp.where(owner_ref[r : r + 1, :] == owner, energies[r], 0.0)
            for k in range(width // LANES):
                chosen = chosen + picked[:, LANES * k : LANES * (k + 1)]
        total = jnp.sum(jnp.sum(chosen, axis=0, keepdims=True), axis=1, keepdims=True)
        result = jnp.where(spot == owner, total, result)
    energy_ref[...] = result


def waves_of(radix):
    pairs = (radix - 1) // 2
    cosine = lambda k, i: math.cos(2.0 * math.pi * ((k * i) % radix) / radix)
    sine = lambda k, i: math.sin(2.0 * math.pi * ((k * i) % radix) / radix)
    return pairs, cosine, sine


def row_of(piece_refs, r):
    return piece_refs[0].at[r] if len(piece_refs) == 1 else piece_refs[r].at[0]


def stacked_table(high_ref, low_ref, begin, size):
    high = high_ref[begin : begin + size, :]
    return jnp.concatenate([high, high, low_ref[begin : begin + size, :]], axis=0)


def product_of(high_ref, low_ref, begin, size, table):
    high = high_ref[:, begin : begin + size]
    stacked = jnp.concatenate([high, low_ref[:, begin : begin + size], high], axis=1)
    return jnp.dot(stacked, table, preferred_element_type=jnp.float32)


def forward_kernel(radix, pieces, own_ref, *refs):
    other_refs, refs = refs[:pieces], refs[pieces:]
    table_high_ref, table_low_ref, first_high_ref, first_low_ref, scale_ref, *refs = refs
    out_high_ref, out_low_ref, high_ref, low_ref = refs
    rows, levels, width = own_ref.shape
    pairs, cosine, sine = waves_of(radix)
    segments = width // LANES
    shift = radix * LANES // 2 % LANES
    lane = lax.broadcasted_iota(jnp.int32, (levels, LANES), 1)

    def store(place, column, wave):
        high_ref[place, column : column + LANES], low_ref[place, column : column + LANES] = split_high_low(wave)

    for r in range(rows):
        place = slice(levels * r, levels * (r + 1))
        other_ref = row_of(other_refs, r)
        own = [own_ref[r, :, LANES * n : LANES * (n + 1)] for n in range(segments)]
        turned = [pltpu.roll(other_ref[:, LANES * n : LANES * (n + 1)], shift, 1) for n in range(segments)]
        joined = own[:-1] + [jnp.where(lane < shift, own[-1], turned[0])]
        joined += [jnp.where(lane < shift, turned[n], turned[n + 1]) for n in range(segments - 1)]
        plus = [joined[n] + joined[radix - n] for n in range(1, pairs + 1)]
        minus = [joined[radix - n] - joined[n] for n in range(1, pairs + 1)]
        store(place, 0, sum(plus, joined[0]))
        for k in range(1, pairs + 1):
            real = sum((cosine(k, n) * plus[n - 1] for n in range(1, pairs + 1)), joined[0])
            imaginary = sine(k, 1) * minus[0]
            for n in range(2, pairs + 1):
                imaginary = imaginary + sine(k, n) * minus[n - 1]
            store(place, LANES * (2 * k - 1), real)
            store(place, LANES * 2 * k, imaginary)

    def transform(begin, size, table):
        spectrum = product_of(high_ref, low_ref, begin, size, table)
        for r in range(rows):
            place = slice(levels * r, levels * (r + 1))
            damped = spectrum[place] * scale_ref[r : r + 1, begin : begin + size]
            out_high_ref[place, begin : begin + size], out_low_ref[place, begin : begin + size] = split_high_low(damped)

    transform(0, LANES, stacked_table(first_high_ref, first_low_ref, 0, LANES))
    for k in range(pairs):
        transform(LANES * (2 * k + 1), 2 * LANES, stacked_table(table_high_ref, table_low_ref, 2 * LANES * k, 2 * LANES))


def inverse_kernel(radix, pieces, mask_ref, own_ref, *refs):
    other_refs, refs = refs[:pieces], refs[pieces:]
    high_ref, low_ref, table_high_ref, table_low_ref, first_high_ref, first_low_ref, *refs = refs
    result_ref, back_ref, wave_ref = refs
    rows, levels, width = own_ref.shape
    sector = result_ref.shape[-1]
    pairs, cosine, sine = waves_of(radix)
    segments = width // LANES
    shift = radix * LANES // 2 % LANES
    lane = lax.broadcasted_iota(jnp.int32, (levels, LANES), 1)

    def transform(begin, size, table):
        wave_ref[:, begin : begin + size] = product_of(high_ref, low_ref, begin, size, table)

    transform(0, LANES, stacked_table(first_high_ref, first_low_ref, 0, LANES))
    for k in range(pairs):
        transform(LANES * (2 * k + 1), 2 * LANES, stacked_table(table_high_ref, table_low_ref, 2 * LANES * k, 2 * LANES))

    for r in range(rows):
        place = slice(levels * r, levels * (r + 1))
        other_ref = row_of(other_refs, r)
        waves = [wave_ref[place, LANES * n : LANES * (n + 1)] for n in range(radix)]
        results = [None] * radix
        results[0] = sum((waves[2 * k - 1] for k in range(1, pairs + 1)), waves[0])
        for n in range(1, pairs + 1):
            even = sum((cosine(k, n) * waves[2 * k - 1] for k in range(1, pairs + 1)), waves[0])
            odd = sine(1, n) * waves[2]
            for k in range(2, pairs + 1):
                odd = odd + sine(k, n) * waves[2 * k]
            results[n], results[radix - n] = even - odd, even + odd
        filtered_row = mask_ref[r] == 1
        turned = [pltpu.roll(result, LANES - shift, 1) for result in results[segments - 1 :]]
        for n in range(segments):
            begin = LANES * n
            size = min(LANES, sector - begin)
            value = jnp.where(filtered_row, results[n], own_ref[r, :, begin : begin + LANES])
            result_ref[:, r, begin : begin + size] = value[:, :size]
            value = jnp.where(lane < LANES - shift, turned[n], turned[min(n + 1, segments - 1)])
            back_ref[r, :, begin : begin + LANES] = jnp.where(filtered_row, value, other_ref[:, begin : begin + LANES])


def finish_kernel(keep_ref, give_ref, *refs):
    out_hbm, turned_ref, sems = refs[-3:]
    count = turned_ref.shape[0]
    result_refs, received_refs = refs[:count], refs[count : 2 * count]
    rows, levels, width = received_refs[0].shape
    sector = out_hbm.shape[-1]
    piece = levels // PIECES
    copies = []

    def send(source_ref, tracer, slot):
        for part in range(PIECES):
            span = pl.ds(piece * part, piece)
            copies.append(pltpu.make_async_copy(source_ref.at[span], out_hbm.at[tracer, span], sems.at[slot, part]))
            copies[-1].start()

    for i, result_ref in enumerate(result_refs):
        send(result_ref, keep_ref[0] + i, i)
    for i in range(count):
        for r in range(rows):
            turned_ref[i, :, r, :] = received_refs[i][r, :, :sector]
        send(turned_ref.at[i], give_ref[0] + i, count + i)
    for copy in copies:
        copy.wait()


def on_device(tracers, courant_lat, courant_lon, surface_flux, mixing, decay_rate, owners, polar_mask):
    tracer_count, levels, rows, sector = tracers.shape
    assert rows == 4 and sector % 64 == 0 and lax.axis_size("lon") == 2
    f32 = jnp.float32
    lat_count, lat = lax.axis_size("lat"), lax.axis_index("lat")
    length = 2 * sector
    width = -(-sector // LANES) * LANES
    radix = length // LANES
    downward = [(i + 1, i) for i in range(lat_count - 1)]
    swap = [(0, 1), (1, 0)]

    whole = pl.BlockSpec(memory_space=pltpu.VMEM)
    in_hbm = pl.BlockSpec(memory_space=pltpu.HBM)
    scalars = pl.BlockSpec(memory_space=pltpu.SMEM)
    even = (1 - lat % 2).reshape(1)
    inside = [pair for i in range(0, lat_count - 1, 2) for pair in ((i, i + 1), (i + 1, i))]
    across = [pair for i in range(1, lat_count - 1, 2) for pair in ((i, i + 1), (i + 1, i))]
    fields = [pltpu.with_memory_space_constraint(array, pltpu.HBM) for array in (tracers, courant_lat, courant_lon)]
    field_buffers = [pltpu.VMEM(array.shape, f32) for array in (tracers, courant_lat, courant_lon)]
    half = tracer_count // 2
    inner = pl.pallas_call(
        pack_kernel,
        in_specs=[scalars, in_hbm],
        out_specs=whole,
        out_shape=pltpu.VMEM((levels * tracer_count, length), f32),
        scratch_shapes=[pltpu.VMEM((tracer_count, levels, 2, sector), f32), pltpu.SemaphoreType.DMA((tracer_count,))],
        compiler_params=params(),
        cost_estimate=cost(0, 600_000),
        name="pack",
    )(even, fields[0])
    from_inside = lax.ppermute(inner, "lat", inside)
    even_rest, inner = lax.optimization_barrier((even, inner))
    *outer, courant_row, sides = pl.pallas_call(
        rest_kernel,
        in_specs=[scalars] + [in_hbm] * 3,
        out_specs=[whole] * (half + 2),
        out_shape=[pltpu.VMEM((levels * 2, length), f32)] * half
        + [
            jax.ShapeDtypeStruct((levels // 2, length), f32),
            jax.ShapeDtypeStruct((tracer_count + 1, rows, levels, LANES), f32),
        ],
        scratch_shapes=field_buffers + [pltpu.SemaphoreType.DMA((tracer_count + 2,))],
        compiler_params=params(),
        cost_estimate=cost(0, 0),
        name="rest",
    )(even_rest, *fields)
    from_across = [lax.ppermute(part, "lat", across) for part in outer[:-1]]
    top = lax.ppermute(courant_row, "lat", downward)

    sides = lax.ppermute(sides, "lon", swap)
    not_pole = (lat > 0).astype(f32).reshape(1)
    base, north, lat_courant = pl.pallas_call(
        functools.partial(base_kernel, width),
        in_specs=[scalars, in_hbm, in_hbm, in_hbm, whole],
        out_specs=[whole] * 3,
        out_shape=[
            jax.ShapeDtypeStruct((tracer_count, rows, levels, width), f32),
            jax.ShapeDtypeStruct((tracer_count, levels, width), f32),
            jax.ShapeDtypeStruct((rows, levels, width), f32),
        ],
        scratch_shapes=field_buffers + [pltpu.SemaphoreType.DMA((tracer_count + 2,))],
        compiler_params=params(),
        cost_estimate=cost(0, 0),
        name="base",
    )(not_pole, *fields, sides)

    surface = jnp.pad(surface_flux, ((0, 0), (0, 0), (0, width - sector)))
    decay = decay_rate[:, :, None]
    block_count = rows * sector // BLOCK
    block_of = (np.arange(rows)[:, None] * sector + np.minimum(np.arange(width), sector - 1)[None]) // BLOCK
    owner_of = jnp.repeat(owners.reshape(block_count), BLOCK).reshape(rows, sector)
    owner_of = jnp.pad(owner_of, ((0, 0), (0, width - sector)))
    forward, inverse, numbers, weights = spectral_tables(length)
    row_ids = (lat * rows + jnp.arange(rows)).astype(f32)
    latitude = (-0.5 + (row_ids + 0.5) / (lat_count * rows)) * math.pi
    inverse_sine = np.where(numbers == 0, 1.0, 1.0 / np.where(numbers == 0, 1.0, np.sin(np.pi * numbers / length)))
    ratio = 2.0 * jnp.cos(latitude)[:, None] * jnp.asarray(inverse_sine, f32)[None]
    damping = jnp.where(jnp.asarray(numbers == 0)[None], 1.0, jnp.minimum(1.0, ratio * ratio))
    scale = damping * jnp.asarray(weights, f32)[None]

    base, scale, owner_of, surface, decay = lax.optimization_barrier((base, scale, owner_of, surface, decay))

    base, outer = lax.optimization_barrier((base, outer))
    from_across.append(lax.ppermute(outer[-1], "lat", across))

    keep = (half * lax.axis_index("lon")).reshape(1)
    give = half - keep
    circles = jax.ShapeDtypeStruct((half, rows, levels, width), f32)
    result_shape = jax.ShapeDtypeStruct((levels, rows, sector), f32)
    out_shape = jax.ShapeDtypeStruct(tracers.shape, f32)

    def run_physics(chunk, firsts, energy, last=False):
        shapes = [jax.ShapeDtypeStruct(circles.shape[1:], f32)] * len(firsts)
        shapes.append(jax.ShapeDtypeStruct((1, LANES) if last else energy.shape, f32))
        *results, energy = pl.pallas_call(
            functools.partial(physics_kernel, levels, sector, lat_count if last else 0, chunk),
            in_specs=[scalars] * (1 + len(firsts)) + [whole] * 11,
            out_specs=[whole] * len(shapes),
            out_shape=shapes,
            compiler_params=params(),
            cost_estimate=cost(0, 0),
            name="physics",
        )(
            even, *firsts, base, north, from_inside, pltpu.with_memory_space_constraint(from_across[chunk], pltpu.VMEM), top,
            lat_courant, surface, mixing, decay, owner_of, energy,
        )
        return results, energy

    forward, inverse = ([jnp.asarray(part) for table in tables for part in split_table(table)] for tables in (forward, inverse))
    circle = jax.ShapeDtypeStruct(circles.shape[1:], f32)
    spectra = jax.ShapeDtypeStruct((rows * levels, length), jnp.bfloat16)

    def run_forward(own, other):
        return pl.pallas_call(
            functools.partial(forward_kernel, radix, len(other)),
            in_specs=[whole] * (6 + len(other)),
            out_specs=[whole] * 2,
            out_shape=[spectra] * 2,
            scratch_shapes=[pltpu.VMEM(spectra.shape, jnp.bfloat16)] * 2,
            compiler_params=params(),
            cost_estimate=cost(0, 0),
            name="forward",
        )(own, *other, *forward, scale)

    def run_inverse(own, other, high, low):
        return pl.pallas_call(
            functools.partial(inverse_kernel, radix, len(other)),
            in_specs=[scalars] + [whole] * (7 + len(other)),
            out_specs=[whole] * 2,
            out_shape=[result_shape, circle],
            scratch_shapes=[pltpu.VMEM(spectra.shape, f32)],
            compiler_params=params(),
            cost_estimate=cost(0, 0),
            name="inverse",
        )(polar_mask, own, *other, high, low, *inverse)

    energy = jnp.zeros((rows, 8, width), f32)
    results, received = [], []
    for chunk in range(half - 1):
        (given, own), energy = run_physics(chunk, [give, keep], energy)
        other = [lax.ppermute(given[r : r + 1], "lon", swap) for r in range(rows)]
        spectrum = run_forward(own, other)
        result, back = run_inverse(own, other, *spectrum)
        results.append(result)
        received.append(lax.ppermute(back, "lon", swap))
        energy, back = lax.optimization_barrier((energy, back))

    distances = [1 << i for i in range(lat_count.bit_length() - 1)]

    def send_energy(energy):
        distance = distances.pop(0)
        return lax.ppermute(energy, "lat", [(i, i ^ distance) for i in range(lat_count)])

    (given, own), energy = run_physics(half - 1, [give, keep], energy, True)
    other = [lax.ppermute(given, "lon", swap)]

    coming = send_energy(energy)
    high, low = run_forward(own, other)
    coming, high = lax.optimization_barrier((coming, high))
    energy = energy + coming
    energy, high = lax.optimization_barrier((energy, high))

    coming = send_energy(energy)
    result, back = run_inverse(own, other, high, low)
    coming, back = lax.optimization_barrier((coming, back))
    energy = energy + coming
    energy, back = lax.optimization_barrier((energy, back))
    results.append(result)
    received.append(lax.ppermute(back, "lon", swap))

    coming = send_energy(energy)
    out = pl.pallas_call(
        finish_kernel,
        in_specs=[scalars] * 2 + [whole] * (2 * half),
        out_specs=in_hbm,
        out_shape=out_shape,
        scratch_shapes=[
            pltpu.VMEM((half,) + result_shape.shape, f32),
            pltpu.SemaphoreType.DMA((2 * half, PIECES)),
        ],
        compiler_params=params(),
        cost_estimate=cost(0, 3_000_000),
        name="finish",
    )(keep, give, *results, *received)
    coming, out = lax.optimization_barrier((coming, out))
    energy = energy + coming
    while distances:
        energy = energy + send_energy(energy)

    owner_energy = lax.dynamic_slice(energy, (0, lat), (1, 1)) / (block_count * BLOCK)
    return out, owner_energy


def solution(mesh):
    placed = (
        P("group", None, "lat", "lon"),
        P("group", "lat", "lon"),
        P("group", "lat", "lon"),
        P("group", "lat", "lon"),
        P(),
        P(),
        P(("group", "lat"), "lon", None, None),
        P(("group", "lat")),
    )
    return jax.shard_map(
        on_device,
        mesh=mesh,
        in_specs=placed,
        out_specs=(P("group", None, "lat", "lon"), P(("group", "lat"), "lon")),
        check_vma=False,
    )
```

```python
import functools
import math

import jax
import jax.numpy as jnp
import numpy as np
from jax import lax
from jax.experimental import pallas as pl
from jax.experimental.pallas import tpu as pltpu
from jax.sharding import PartitionSpec as P

LANES = 128
BLOCK = 128
VMEM_BYTES = 6 * 1024 * 1024
PIECES = 4
NEAR = 7.0 / 12.0
FAR = 1.0 / 12.0


def params():
    return pltpu.CompilerParams(vmem_limit_bytes=VMEM_BYTES)


def cost(flops, bytes_accessed):
    return pl.CostEstimate(flops=flops, bytes_accessed=bytes_accessed, transcendentals=0)


def split_high_low(value):
    high = value.astype(jnp.bfloat16)
    low = (value - high.astype(jnp.float32)).astype(jnp.bfloat16)
    return high, low


def split_table(table):
    high = table.astype(jnp.bfloat16.dtype)
    return high, (table - high.astype(np.float64)).astype(jnp.bfloat16.dtype)


def spectral_tables(length):
    radix = length // LANES
    pairs = (radix - 1) // 2
    spot = np.arange(LANES)[:, None]
    number = np.arange(LANES)[None, :]
    is_cosine = number <= LANES // 2
    wave = np.where(is_cosine, number, number - LANES // 2)
    angle = 2.0 * np.pi * ((spot * wave) % LANES) / LANES
    first = np.where(is_cosine, np.cos(angle), np.sin(angle))
    others, numbers = [], [radix * wave[0]]
    weights = [np.where((wave[0] == 0) | (wave[0] == LANES // 2), 1.0, 2.0) / length]
    for residue in range(1, pairs + 1):
        whole = residue + radix * number
        angle = 2.0 * np.pi * ((spot * whole) % length) / length
        cosine, sine = np.cos(angle), np.sin(angle)
        others.append(np.block([[cosine, -sine], [sine, cosine]]))
        folded = np.minimum(whole[0], length - whole[0])
        numbers += [folded, folded]
        weights.append(np.full(2 * LANES, 2.0 / length))
    forward = np.concatenate(others), first
    inverse = np.concatenate([table.T for table in others]), first.T
    return forward, inverse, np.concatenate(numbers), np.concatenate(weights)


def pack_rows(first, second):
    return jnp.concatenate([first, second], axis=1)


def second_half(packed, sector):
    skip, shift = sector // LANES, sector % LANES
    segments = [packed[:, LANES * i : LANES * (i + 1)] for i in range(packed.shape[1] // LANES)]
    if shift == 0:
        return jnp.concatenate(segments[skip:], axis=1)
    turned = [pltpu.roll(segment, LANES - shift, 1) for segment in segments[skip:]]
    lane = lax.broadcasted_iota(jnp.int32, turned[0].shape, 1)
    parts = [jnp.where(lane < LANES - shift, turned[i], turned[min(i + 1, len(turned) - 1)]) for i in range(len(turned))]
    return jnp.concatenate(parts, axis=1)


def start_copies(pairs, sems):
    copies = [pltpu.make_async_copy(source, target, sems.at[i]) for i, (source, target) in enumerate(pairs)]
    for copy in copies:
        copy.start()
    return copies


def pack_kernel(even_ref, tracer_hbm, out_ref, row_ref, sems):
    count, levels = row_ref.shape[:2]
    first_row = pl.multiple_of(jnp.where(even_ref[0] == 1, tracer_hbm.shape[2] - 2, 0), 2)
    sources = [tracer_hbm.at[t, :, pl.ds(first_row, 2), :] for t in range(count)]
    copies = start_copies([(sources[t], row_ref.at[t]) for t in range(count)], sems)
    for t in range(count):
        copies[t].wait()
        out_ref[levels * t : levels * (t + 1), :] = pack_rows(row_ref[t, :, 0, :], row_ref[t, :, 1, :])


def rest_kernel(even_ref, tracer_hbm, lat_hbm, lon_hbm, *refs):
    courant_ref, side_ref, tracer_ref, lat_ref, lon_ref, sems = refs[-6:]
    outer_refs = refs[:-6]
    count, levels, rows, sector = tracer_ref.shape
    pairs = [(tracer_hbm.at[t], tracer_ref.at[t]) for t in range(count)] + [(lat_hbm, lat_ref), (lon_hbm, lon_ref)]
    copies = start_copies(pairs, sems)
    shift, whole = sector % LANES, sector // LANES * LANES
    lane = lax.broadcasted_iota(jnp.int32, (levels, LANES), 1)
    even = even_ref[0] == 1

    def store_side(i, r, values):
        first = pltpu.roll(values[:, :LANES], shift, 1)
        last = jnp.concatenate([values[:, whole:], values[:, whole:]], axis=1)
        side_ref[i, r] = jnp.where(lane < LANES - 2, first, last)

    for copy in copies:
        copy.wait()
    for t in range(count):
        row = [tracer_ref[t, :, r, :] for r in range(rows)]
        slot = t // len(outer_refs)
        outer_refs[t % len(outer_refs)][levels * slot : levels * (slot + 1), :] = pack_rows(
            jnp.where(even, row[0], row[rows - 2]), jnp.where(even, row[1], row[rows - 1])
        )
        for r in range(rows):
            store_side(t, r, row[r])
    courant = lat_ref[:, 0, :]
    courant_ref[...] = pack_rows(courant[: levels // 2], courant[levels // 2 :])
    for r in range(rows):
        store_side(count, r, lon_ref[:, r, :])


def base_kernel(width, not_pole_ref, tracer_hbm, lat_hbm, lon_hbm, side_ref, base_ref, north_ref, courant_ref, *scratch):
    tracer_ref, lat_ref, lon_ref, sems = scratch
    tracer_count, levels, rows, sector = tracer_ref.shape
    whole = sector // LANES * LANES
    pairs = [(lat_hbm, lat_ref), (lon_hbm, lon_ref)] + [(tracer_hbm.at[t], tracer_ref.at[t]) for t in range(tracer_count)]
    copies = start_copies(pairs, sems)

    def beside(values, side):
        return jnp.concatenate([values[:, :whole], values[:, whole:], side[:, sector - whole :]], axis=1)

    copies[0].wait()
    copies[1].wait()
    nothing = jnp.zeros((levels, LANES), jnp.float32)
    for r in range(rows):
        courant = lat_ref[:, r, :] if r else lat_ref[:, r, :] * not_pole_ref[0]
        courant_ref[r] = beside(courant, nothing)
    for t in range(tracer_count):
        copies[t + 2].wait()
        q = [beside(tracer_ref[t, :, r, :], side_ref[t, r]) for r in range(rows)]
        north_ref[t] = NEAR * q[3] - FAR * q[2]
        own_flux = [
            courant_ref[0] * (NEAR * q[0] - FAR * q[1]),
            courant_ref[1] * (NEAR * (q[1] + q[0]) - FAR * q[2]),
            courant_ref[2] * (NEAR * (q[2] + q[1]) - FAR * (q[3] + q[0])),
            courant_ref[3] * (NEAR * (q[3] + q[2]) - FAR * q[1]),
        ]
        for r in range(rows):
            west, west2, east = pltpu.roll(q[r], 1, 1), pltpu.roll(q[r], 2, 1), pltpu.roll(q[r], width - 1, 1)
            flux = beside(lon_ref[:, r, :], side_ref[tracer_count, r]) * (NEAR * (q[r] + west) - FAR * (east + west2))
            value = q[r] - (pltpu.roll(flux, width - 1, 1) - flux) + own_flux[r]
            if r + 1 < rows:
                value = value - own_flux[r + 1]
            base_ref[t, r] = value


def physics_kernel(levels, sector, owner_count, chunk, even_ref, *refs):
    count = len(refs) - 12 >> 1
    first_refs, refs = refs[:count], refs[count:]
    base_ref, north_ref, inner_ref, outer_ref = refs[:4]
    top_ref, courant_ref, surface_ref, mixing_ref, decay_ref, owner_ref, energy_in_ref = refs[4:11]
    physics_refs, energy_ref = refs[11:-1], refs[-1]
    rows, width = base_ref.shape[1], base_ref.shape[-1]
    courant = [courant_ref[r] for r in range(rows)]
    even = even_ref[0] == 1
    top = top_ref[...]
    top = jnp.concatenate([top[:, :width], second_half(top, sector)], axis=0)
    mix_high, mix_low = split_high_low(mixing_ref[...])
    mix = jnp.concatenate([mix_high, mix_high, mix_low, mix_low], axis=1)
    level = lax.broadcasted_iota(jnp.int32, (8, width), 0)
    lane = lax.broadcasted_iota(jnp.int32, (8, width), 1)
    energies = [energy_in_ref[r] for r in range(rows)]
    for first_ref, physics_ref in zip(first_refs, physics_refs):
        t = first_ref[0] + chunk
        inner = inner_ref[pl.ds(pl.multiple_of(levels * t, levels), levels), :]
        outer = jnp.where(first_ref[0] == 0, outer_ref[:levels, :], outer_ref[levels:, :])
        low, high = jnp.where(even, outer, inner), jnp.where(even, inner, outer)
        low_a, low_b = low[:, :width], second_half(low, sector)
        high_a, high_b = high[:, :width], second_half(high, sector)
        south = courant[0] * (NEAR * low_b - FAR * low_a)
        south_in = courant[1] * (FAR * low_b)
        north_in = courant[3] * (FAR * high_a)
        north = top * (NEAR * high_a - FAR * high_b + north_ref[t])
        extra = [south + south_in, -south_in, north_in, -north_in - north]
        for r in range(rows):
            advected = base_ref[t, r] + extra[r]
            part_high, part_low = split_high_low(advected)
            stacked = jnp.concatenate([part_high, part_low, part_high, part_low], axis=0)
            mixed = jnp.dot(mix, stacked, preferred_element_type=jnp.float32)
            surface = jnp.where(level == 7, surface_ref[t, r : r + 1, :], 0.0)
            mixed = jnp.concatenate([mixed[: levels - 8], mixed[levels - 8 :] + surface], axis=0)
            physics = mixed / (1.0 + decay_ref[t] * mixed * mixed)
            physics_ref[r] = physics
            gap = physics - advected
            squared = gap * gap
            for k in range(levels // 8):
                energies[r] = energies[r] + squared[8 * k : 8 * k + 8]
    if not owner_count:
        for r in range(rows):
            energy_ref[r] = energies[r]
        return
    energies = [jnp.where(lane < sector, energy, 0.0) for energy in energies]
    spot = lax.broadcasted_iota(jnp.int32, (1, LANES), 1)
    result = jnp.zeros((1, LANES), jnp.float32)
    for owner in range(owner_count):
        chosen = jnp.zeros((8, LANES), jnp.float32)
        for r in range(rows):
            picked = jnp.where(owner_ref[r : r + 1, :] == owner, energies[r], 0.0)
            for k in range(width // LANES):
                chosen = chosen + picked[:, LANES * k : LANES * (k + 1)]
        total = jnp.sum(jnp.sum(chosen, axis=0, keepdims=True), axis=1, keepdims=True)
        result = jnp.where(spot == owner, total, result)
    energy_ref[...] = result


def waves_of(radix):
    pairs = (radix - 1) // 2
    cosine = lambda k, i: math.cos(2.0 * math.pi * ((k * i) % radix) / radix)
    sine = lambda k, i: math.sin(2.0 * math.pi * ((k * i) % radix) / radix)
    return pairs, cosine, sine


def row_of(piece_refs, r):
    share = piece_refs[0].shape[0]
    return piece_refs[r // share].at[r % share]


def stacked_table(high_ref, low_ref, begin, size):
    high = high_ref[begin : begin + size, :]
    return jnp.concatenate([high, high, low_ref[begin : begin + size, :]], axis=0)


def product_of(high_ref, low_ref, begin, size, table):
    high = high_ref[:, begin : begin + size]
    stacked = jnp.concatenate([high, low_ref[:, begin : begin + size], high], axis=1)
    return jnp.dot(stacked, table, preferred_element_type=jnp.float32)


def forward_kernel(radix, pieces, own_ref, *refs):
    other_refs, refs = refs[:pieces], refs[pieces:]
    table_high_ref, table_low_ref, first_high_ref, first_low_ref, scale_ref, *refs = refs
    out_high_ref, out_low_ref, high_ref, low_ref = refs
    rows, levels, width = own_ref.shape
    pairs, cosine, sine = waves_of(radix)
    segments = width // LANES
    shift = radix * LANES // 2 % LANES
    lane = lax.broadcasted_iota(jnp.int32, (levels, LANES), 1)

    def store(place, column, wave):
        high_ref[place, column : column + LANES], low_ref[place, column : column + LANES] = split_high_low(wave)

    for r in range(rows):
        place = slice(levels * r, levels * (r + 1))
        other_ref = row_of(other_refs, r)
        own = [own_ref[r, :, LANES * n : LANES * (n + 1)] for n in range(segments)]
        turned = [pltpu.roll(other_ref[:, LANES * n : LANES * (n + 1)], shift, 1) for n in range(segments)]
        joined = own[:-1] + [jnp.where(lane < shift, own[-1], turned[0])]
        joined += [jnp.where(lane < shift, turned[n], turned[n + 1]) for n in range(segments - 1)]
        plus = [joined[n] + joined[radix - n] for n in range(1, pairs + 1)]
        minus = [joined[radix - n] - joined[n] for n in range(1, pairs + 1)]
        store(place, 0, sum(plus, joined[0]))
        for k in range(1, pairs + 1):
            real = sum((cosine(k, n) * plus[n - 1] for n in range(1, pairs + 1)), joined[0])
            imaginary = sine(k, 1) * minus[0]
            for n in range(2, pairs + 1):
                imaginary = imaginary + sine(k, n) * minus[n - 1]
            store(place, LANES * (2 * k - 1), real)
            store(place, LANES * 2 * k, imaginary)

    def transform(begin, size, table):
        spectrum = product_of(high_ref, low_ref, begin, size, table)
        for r in range(rows):
            place = slice(levels * r, levels * (r + 1))
            damped = spectrum[place] * scale_ref[r : r + 1, begin : begin + size]
            out_high_ref[place, begin : begin + size], out_low_ref[place, begin : begin + size] = split_high_low(damped)

    transform(0, LANES, stacked_table(first_high_ref, first_low_ref, 0, LANES))
    for k in range(pairs):
        transform(LANES * (2 * k + 1), 2 * LANES, stacked_table(table_high_ref, table_low_ref, 2 * LANES * k, 2 * LANES))


def inverse_kernel(radix, pieces, mask_ref, own_ref, *refs):
    other_refs, refs = refs[:pieces], refs[pieces:]
    high_ref, low_ref, table_high_ref, table_low_ref, first_high_ref, first_low_ref, *refs = refs
    result_ref, back_ref, wave_ref = refs
    rows, levels, width = own_ref.shape
    sector = result_ref.shape[-1]
    pairs, cosine, sine = waves_of(radix)
    segments = width // LANES
    shift = radix * LANES // 2 % LANES
    lane = lax.broadcasted_iota(jnp.int32, (levels, LANES), 1)

    def transform(begin, size, table):
        wave_ref[:, begin : begin + size] = product_of(high_ref, low_ref, begin, size, table)

    transform(0, LANES, stacked_table(first_high_ref, first_low_ref, 0, LANES))
    for k in range(pairs):
        transform(LANES * (2 * k + 1), 2 * LANES, stacked_table(table_high_ref, table_low_ref, 2 * LANES * k, 2 * LANES))

    for r in range(rows):
        place = slice(levels * r, levels * (r + 1))
        other_ref = row_of(other_refs, r)
        waves = [wave_ref[place, LANES * n : LANES * (n + 1)] for n in range(radix)]
        results = [None] * radix
        results[0] = sum((waves[2 * k - 1] for k in range(1, pairs + 1)), waves[0])
        for n in range(1, pairs + 1):
            even = sum((cosine(k, n) * waves[2 * k - 1] for k in range(1, pairs + 1)), waves[0])
            odd = sine(1, n) * waves[2]
            for k in range(2, pairs + 1):
                odd = odd + sine(k, n) * waves[2 * k]
            results[n], results[radix - n] = even - odd, even + odd
        filtered_row = mask_ref[r] == 1
        turned = [pltpu.roll(result, LANES - shift, 1) for result in results[segments - 1 :]]
        for n in range(segments):
            begin = LANES * n
            size = min(LANES, sector - begin)
            value = jnp.where(filtered_row, results[n], own_ref[r, :, begin : begin + LANES])
            result_ref[:, r, begin : begin + size] = value[:, :size]
            value = jnp.where(lane < LANES - shift, turned[n], turned[min(n + 1, segments - 1)])
            back_ref[r, :, begin : begin + LANES] = jnp.where(filtered_row, value, other_ref[:, begin : begin + LANES])


def finish_kernel(keep_ref, give_ref, *refs):
    out_hbm, turned_ref, sems = refs[-3:]
    count = turned_ref.shape[0]
    result_refs, received_refs = refs[:count], refs[count : 2 * count]
    rows, levels, width = received_refs[0].shape
    sector = out_hbm.shape[-1]
    piece = levels // PIECES
    copies = []

    def send(source_ref, tracer, slot):
        for part in range(PIECES):
            span = pl.ds(piece * part, piece)
            copies.append(pltpu.make_async_copy(source_ref.at[span], out_hbm.at[tracer, span], sems.at[slot, part]))
            copies[-1].start()

    for i, result_ref in enumerate(result_refs):
        send(result_ref, keep_ref[0] + i, i)
    for i in range(count):
        for r in range(rows):
            turned_ref[i, :, r, :] = received_refs[i][r, :, :sector]
        send(turned_ref.at[i], give_ref[0] + i, count + i)
    for copy in copies:
        copy.wait()


def on_device(tracers, courant_lat, courant_lon, surface_flux, mixing, decay_rate, owners, polar_mask):
    tracer_count, levels, rows, sector = tracers.shape
    assert rows == 4 and sector % 64 == 0 and lax.axis_size("lon") == 2
    f32 = jnp.float32
    lat_count, lat = lax.axis_size("lat"), lax.axis_index("lat")
    length = 2 * sector
    width = -(-sector // LANES) * LANES
    radix = length // LANES
    downward = [(i + 1, i) for i in range(lat_count - 1)]
    swap = [(0, 1), (1, 0)]

    whole = pl.BlockSpec(memory_space=pltpu.VMEM)
    in_hbm = pl.BlockSpec(memory_space=pltpu.HBM)
    scalars = pl.BlockSpec(memory_space=pltpu.SMEM)
    even = (1 - lat % 2).reshape(1)
    inside = [pair for i in range(0, lat_count - 1, 2) for pair in ((i, i + 1), (i + 1, i))]
    across = [pair for i in range(1, lat_count - 1, 2) for pair in ((i, i + 1), (i + 1, i))]
    fields = [pltpu.with_memory_space_constraint(array, pltpu.HBM) for array in (tracers, courant_lat, courant_lon)]
    field_buffers = [pltpu.VMEM(array.shape, f32) for array in (tracers, courant_lat, courant_lon)]
    half = tracer_count // 2
    inner = pl.pallas_call(
        pack_kernel,
        in_specs=[scalars, in_hbm],
        out_specs=whole,
        out_shape=pltpu.VMEM((levels * tracer_count, length), f32),
        scratch_shapes=[pltpu.VMEM((tracer_count, levels, 2, sector), f32), pltpu.SemaphoreType.DMA((tracer_count,))],
        compiler_params=params(),
        cost_estimate=cost(0, 600_000),
        name="pack",
    )(even, fields[0])
    from_inside = lax.ppermute(inner, "lat", inside)
    even_rest, inner = lax.optimization_barrier((even, inner))
    *outer, courant_row, sides = pl.pallas_call(
        rest_kernel,
        in_specs=[scalars] + [in_hbm] * 3,
        out_specs=[whole] * (half + 2),
        out_shape=[pltpu.VMEM((levels * 2, length), f32)] * half
        + [
            jax.ShapeDtypeStruct((levels // 2, length), f32),
            jax.ShapeDtypeStruct((tracer_count + 1, rows, levels, LANES), f32),
        ],
        scratch_shapes=field_buffers + [pltpu.SemaphoreType.DMA((tracer_count + 2,))],
        compiler_params=params(),
        cost_estimate=cost(0, 0),
        name="rest",
    )(even_rest, *fields)
    from_across = [lax.ppermute(part, "lat", across) for part in outer[:-1]]
    top = lax.ppermute(courant_row, "lat", downward)

    sides = lax.ppermute(sides, "lon", swap)
    not_pole = (lat > 0).astype(f32).reshape(1)
    base, north, lat_courant = pl.pallas_call(
        functools.partial(base_kernel, width),
        in_specs=[scalars, in_hbm, in_hbm, in_hbm, whole],
        out_specs=[whole] * 3,
        out_shape=[
            jax.ShapeDtypeStruct((tracer_count, rows, levels, width), f32),
            jax.ShapeDtypeStruct((tracer_count, levels, width), f32),
            jax.ShapeDtypeStruct((rows, levels, width), f32),
        ],
        scratch_shapes=field_buffers + [pltpu.SemaphoreType.DMA((tracer_count + 2,))],
        compiler_params=params(),
        cost_estimate=cost(0, 0),
        name="base",
    )(not_pole, *fields, sides)

    surface = jnp.pad(surface_flux, ((0, 0), (0, 0), (0, width - sector)))
    decay = decay_rate[:, :, None]
    block_count = rows * sector // BLOCK
    block_of = (np.arange(rows)[:, None] * sector + np.minimum(np.arange(width), sector - 1)[None]) // BLOCK
    owner_of = jnp.repeat(owners.reshape(block_count), BLOCK).reshape(rows, sector)
    owner_of = jnp.pad(owner_of, ((0, 0), (0, width - sector)))
    forward, inverse, numbers, weights = spectral_tables(length)
    row_ids = (lat * rows + jnp.arange(rows)).astype(f32)
    latitude = (-0.5 + (row_ids + 0.5) / (lat_count * rows)) * math.pi
    inverse_sine = np.where(numbers == 0, 1.0, 1.0 / np.where(numbers == 0, 1.0, np.sin(np.pi * numbers / length)))
    ratio = 2.0 * jnp.cos(latitude)[:, None] * jnp.asarray(inverse_sine, f32)[None]
    damping = jnp.where(jnp.asarray(numbers == 0)[None], 1.0, jnp.minimum(1.0, ratio * ratio))
    scale = damping * jnp.asarray(weights, f32)[None]

    base, scale, owner_of, surface, decay = lax.optimization_barrier((base, scale, owner_of, surface, decay))

    base, outer = lax.optimization_barrier((base, outer))
    from_across.append(lax.ppermute(outer[-1], "lat", across))

    keep = (half * lax.axis_index("lon")).reshape(1)
    give = half - keep
    circles = jax.ShapeDtypeStruct((half, rows, levels, width), f32)
    result_shape = jax.ShapeDtypeStruct((levels, rows, sector), f32)
    out_shape = jax.ShapeDtypeStruct(tracers.shape, f32)

    def run_physics(chunk, firsts, energy, last=False):
        shapes = [jax.ShapeDtypeStruct(circles.shape[1:], f32)] * len(firsts)
        shapes.append(jax.ShapeDtypeStruct((1, LANES) if last else energy.shape, f32))
        *results, energy = pl.pallas_call(
            functools.partial(physics_kernel, levels, sector, lat_count if last else 0, chunk),
            in_specs=[scalars] * (1 + len(firsts)) + [whole] * 11,
            out_specs=[whole] * len(shapes),
            out_shape=shapes,
            compiler_params=params(),
            cost_estimate=cost(0, 0),
            name="physics",
        )(even, *firsts, base, north, from_inside, from_across[chunk], top, lat_courant, surface, mixing, decay, owner_of, energy)
        return results, energy

    forward, inverse = ([jnp.asarray(part) for table in tables for part in split_table(table)] for tables in (forward, inverse))
    circle = jax.ShapeDtypeStruct(circles.shape[1:], f32)
    spectra = jax.ShapeDtypeStruct((rows * levels, length), jnp.bfloat16)

    def run_forward(own, other):
        return pl.pallas_call(
            functools.partial(forward_kernel, radix, len(other)),
            in_specs=[whole] * (6 + len(other)),
            out_specs=[whole] * 2,
            out_shape=[spectra] * 2,
            scratch_shapes=[pltpu.VMEM(spectra.shape, jnp.bfloat16)] * 2,
            compiler_params=params(),
            cost_estimate=cost(0, 0),
            name="forward",
        )(own, *other, *forward, scale)

    def run_inverse(own, other, high, low):
        return pl.pallas_call(
            functools.partial(inverse_kernel, radix, len(other)),
            in_specs=[scalars] + [whole] * (7 + len(other)),
            out_specs=[whole] * 2,
            out_shape=[result_shape, circle],
            scratch_shapes=[pltpu.VMEM(spectra.shape, f32)],
            compiler_params=params(),
            cost_estimate=cost(0, 0),
            name="inverse",
        )(polar_mask, own, *other, high, low, *inverse)

    energy = jnp.zeros((rows, 8, width), f32)
    results, received = [], []
    for chunk in range(half - 1):
        (given, own), energy = run_physics(chunk, [give, keep], energy)
        other = [lax.ppermute(given[r : r + 2], "lon", swap) for r in range(0, rows, 2)]
        spectrum = run_forward(own, other)
        result, back = run_inverse(own, other, *spectrum)
        results.append(result)
        received.append(lax.ppermute(back, "lon", swap))
        energy, back = lax.optimization_barrier((energy, back))

    distances = [1 << i for i in range(lat_count.bit_length() - 1)]

    def send_energy(energy):
        distance = distances.pop(0)
        return lax.ppermute(energy, "lat", [(i, i ^ distance) for i in range(lat_count)])

    (given, own), energy = run_physics(half - 1, [give, keep], energy, True)
    other = [lax.ppermute(given, "lon", swap)]

    coming = send_energy(energy)
    high, low = run_forward(own, other)
    coming, high = lax.optimization_barrier((coming, high))
    energy = energy + coming
    energy, high = lax.optimization_barrier((energy, high))

    coming = send_energy(energy)
    result, back = run_inverse(own, other, high, low)
    coming, back = lax.optimization_barrier((coming, back))
    energy = energy + coming
    energy, back = lax.optimization_barrier((energy, back))
    results.append(result)
    received.append(lax.ppermute(back, "lon", swap))

    coming = send_energy(energy)
    out = pl.pallas_call(
        finish_kernel,
        in_specs=[scalars] * 2 + [whole] * (2 * half),
        out_specs=in_hbm,
        out_shape=out_shape,
        scratch_shapes=[
            pltpu.VMEM((half,) + result_shape.shape, f32),
            pltpu.SemaphoreType.DMA((2 * half, PIECES)),
        ],
        compiler_params=params(),
        cost_estimate=cost(0, 3_000_000),
        name="finish",
    )(keep, give, *results, *received)
    coming, out = lax.optimization_barrier((coming, out))
    energy = energy + coming
    while distances:
        energy = energy + send_energy(energy)

    owner_energy = lax.dynamic_slice(energy, (0, lat), (1, 1)) / (block_count * BLOCK)
    return out, owner_energy


def solution(mesh):
    placed = (
        P("group", None, "lat", "lon"),
        P("group", "lat", "lon"),
        P("group", "lat", "lon"),
        P("group", "lat", "lon"),
        P(),
        P(),
        P(("group", "lat"), "lon", None, None),
        P(("group", "lat")),
    )
    return jax.shard_map(
        on_device,
        mesh=mesh,
        in_specs=placed,
        out_specs=(P("group", None, "lat", "lon"), P(("group", "lat"), "lon")),
        check_vma=False,
    )
```

```python
import functools
import math

import jax
import jax.numpy as jnp
import numpy as np
from jax import lax
from jax.experimental import pallas as pl
from jax.experimental.pallas import tpu as pltpu
from jax.sharding import PartitionSpec as P

LANES = 128
BLOCK = 128
VMEM_BYTES = 6 * 1024 * 1024
PIECES = 4
NEAR = 7.0 / 12.0
FAR = 1.0 / 12.0


def params():
    return pltpu.CompilerParams(vmem_limit_bytes=VMEM_BYTES)


def cost(flops, bytes_accessed):
    return pl.CostEstimate(flops=flops, bytes_accessed=bytes_accessed, transcendentals=0)


def split_high_low(value):
    high = value.astype(jnp.bfloat16)
    low = (value - high.astype(jnp.float32)).astype(jnp.bfloat16)
    return high, low


def split_table(table):
    high = table.astype(jnp.bfloat16.dtype)
    return high, (table - high.astype(np.float64)).astype(jnp.bfloat16.dtype)


def spectral_tables(length):
    radix = length // LANES
    pairs = (radix - 1) // 2
    spot = np.arange(LANES)[:, None]
    number = np.arange(LANES)[None, :]
    is_cosine = number <= LANES // 2
    wave = np.where(is_cosine, number, number - LANES // 2)
    angle = 2.0 * np.pi * ((spot * wave) % LANES) / LANES
    first = np.where(is_cosine, np.cos(angle), np.sin(angle))
    others, numbers = [], [radix * wave[0]]
    weights = [np.where((wave[0] == 0) | (wave[0] == LANES // 2), 1.0, 2.0) / length]
    for residue in range(1, pairs + 1):
        whole = residue + radix * number
        angle = 2.0 * np.pi * ((spot * whole) % length) / length
        cosine, sine = np.cos(angle), np.sin(angle)
        others.append(np.block([[cosine, -sine], [sine, cosine]]))
        folded = np.minimum(whole[0], length - whole[0])
        numbers += [folded, folded]
        weights.append(np.full(2 * LANES, 2.0 / length))
    forward = np.concatenate(others), first
    inverse = np.concatenate([table.T for table in others]), first.T
    return forward, inverse, np.concatenate(numbers), np.concatenate(weights)


def is_even():
    return lax.axis_index("lat") % 2 == 0


def first_of(half, tracer_count):
    lon = lax.axis_index("lon")
    return (tracer_count // 2) * (lon if half == "keep" else 1 - lon)


def pack_rows(first, second):
    return jnp.concatenate([first, second], axis=1)


def second_half(packed, sector):
    skip, shift = sector // LANES, sector % LANES
    segments = [packed[:, LANES * i : LANES * (i + 1)] for i in range(packed.shape[1] // LANES)]
    if shift == 0:
        return jnp.concatenate(segments[skip:], axis=1)
    turned = [pltpu.roll(segment, LANES - shift, 1) for segment in segments[skip:]]
    lane = lax.broadcasted_iota(jnp.int32, turned[0].shape, 1)
    parts = [jnp.where(lane < LANES - shift, turned[i], turned[min(i + 1, len(turned) - 1)]) for i in range(len(turned))]
    return jnp.concatenate(parts, axis=1)


def start_copies(pairs, sems):
    copies = [pltpu.make_async_copy(source, target, sems.at[i]) for i, (source, target) in enumerate(pairs)]
    for copy in copies:
        copy.start()
    return copies


def pack_kernel(tracer_hbm, out_ref, row_ref, sems):
    count, levels = row_ref.shape[:2]
    first_row = pl.multiple_of(jnp.where(is_even(), tracer_hbm.shape[2] - 2, 0), 2)
    sources = [tracer_hbm.at[t, :, pl.ds(first_row, 2), :] for t in range(count)]
    copies = start_copies([(sources[t], row_ref.at[t]) for t in range(count)], sems)
    for t in range(count):
        copies[t].wait()
        out_ref[levels * t : levels * (t + 1), :] = pack_rows(row_ref[t, :, 0, :], row_ref[t, :, 1, :])


def rest_kernel(tracer_hbm, lat_hbm, lon_hbm, *refs):
    courant_ref, side_ref, tracer_ref, lat_ref, lon_ref, sems = refs[-6:]
    outer_refs = refs[:-6]
    count, levels, rows, sector = tracer_ref.shape
    pairs = [(tracer_hbm.at[t], tracer_ref.at[t]) for t in range(count)] + [(lat_hbm, lat_ref), (lon_hbm, lon_ref)]
    copies = start_copies(pairs, sems)
    shift, whole = sector % LANES, sector // LANES * LANES
    lane = lax.broadcasted_iota(jnp.int32, (levels, LANES), 1)
    even = is_even()

    def store_side(i, r, values):
        first = pltpu.roll(values[:, :LANES], shift, 1)
        last = jnp.concatenate([values[:, whole:], values[:, whole:]], axis=1)
        side_ref[i, r] = jnp.where(lane < LANES - 2, first, last)

    for copy in copies:
        copy.wait()
    for t in range(count):
        row = [tracer_ref[t, :, r, :] for r in range(rows)]
        slot = t // len(outer_refs)
        outer_refs[t % len(outer_refs)][levels * slot : levels * (slot + 1), :] = pack_rows(
            jnp.where(even, row[0], row[rows - 2]), jnp.where(even, row[1], row[rows - 1])
        )
        for r in range(rows):
            store_side(t, r, row[r])
    courant = lat_ref[:, 0, :]
    courant_ref[...] = pack_rows(courant[: levels // 2], courant[levels // 2 :])
    for r in range(rows):
        store_side(count, r, lon_ref[:, r, :])


def base_kernel(width, tracer_hbm, lat_hbm, lon_hbm, side_ref, base_ref, north_ref, courant_ref, *scratch):
    tracer_ref, lat_ref, lon_ref, sems = scratch
    tracer_count, levels, rows, sector = tracer_ref.shape
    whole = sector // LANES * LANES
    pairs = [(lat_hbm, lat_ref), (lon_hbm, lon_ref)] + [(tracer_hbm.at[t], tracer_ref.at[t]) for t in range(tracer_count)]
    copies = start_copies(pairs, sems)

    def beside(values, side):
        return jnp.concatenate([values[:, :whole], values[:, whole:], side[:, sector - whole :]], axis=1)

    copies[0].wait()
    copies[1].wait()
    nothing = jnp.zeros((levels, LANES), jnp.float32)
    for r in range(rows):
        courant = lat_ref[:, r, :] if r else jnp.where(lax.axis_index("lat") > 0, lat_ref[:, r, :], 0.0)
        courant_ref[r] = beside(courant, nothing)
    for t in range(tracer_count):
        copies[t + 2].wait()
        q = [beside(tracer_ref[t, :, r, :], side_ref[t, r]) for r in range(rows)]
        north_ref[t] = NEAR * q[3] - FAR * q[2]
        own_flux = [
            courant_ref[0] * (NEAR * q[0] - FAR * q[1]),
            courant_ref[1] * (NEAR * (q[1] + q[0]) - FAR * q[2]),
            courant_ref[2] * (NEAR * (q[2] + q[1]) - FAR * (q[3] + q[0])),
            courant_ref[3] * (NEAR * (q[3] + q[2]) - FAR * q[1]),
        ]
        for r in range(rows):
            west, west2, east = pltpu.roll(q[r], 1, 1), pltpu.roll(q[r], 2, 1), pltpu.roll(q[r], width - 1, 1)
            flux = beside(lon_ref[:, r, :], side_ref[tracer_count, r]) * (NEAR * (q[r] + west) - FAR * (east + west2))
            value = q[r] - (pltpu.roll(flux, width - 1, 1) - flux) + own_flux[r]
            if r + 1 < rows:
                value = value - own_flux[r + 1]
            base_ref[t, r] = value


def physics_kernel(levels, sector, owner_count, chunk, halves, *refs):
    base_ref, north_ref, inner_ref, outer_ref = refs[:4]
    top_ref, courant_ref, surface_ref, mixing_ref, decay_ref, owner_ref, energy_in_ref = refs[4:11]
    physics_refs, energy_ref = refs[11:-1], refs[-1]
    rows, width = base_ref.shape[1], base_ref.shape[-1]
    courant = [courant_ref[r] for r in range(rows)]
    even = is_even()
    top = top_ref[...]
    top = jnp.concatenate([top[:, :width], second_half(top, sector)], axis=0)
    mix_high, mix_low = split_high_low(mixing_ref[...])
    mix = jnp.concatenate([mix_high, mix_high, mix_low, mix_low], axis=1)
    level = lax.broadcasted_iota(jnp.int32, (8, width), 0)
    lane = lax.broadcasted_iota(jnp.int32, (8, width), 1)
    energies = [energy_in_ref[r] for r in range(rows)]
    for half, physics_ref in zip(halves, physics_refs):
        first = first_of(half, base_ref.shape[0])
        t = first + chunk
        inner = inner_ref[pl.ds(pl.multiple_of(levels * t, levels), levels), :]
        outer = jnp.where(first == 0, outer_ref[:levels, :], outer_ref[levels:, :])
        low, high = jnp.where(even, outer, inner), jnp.where(even, inner, outer)
        low_a, low_b = low[:, :width], second_half(low, sector)
        high_a, high_b = high[:, :width], second_half(high, sector)
        south = courant[0] * (NEAR * low_b - FAR * low_a)
        south_in = courant[1] * (FAR * low_b)
        north_in = courant[3] * (FAR * high_a)
        north = top * (NEAR * high_a - FAR * high_b + north_ref[t])
        extra = [south + south_in, -south_in, north_in, -north_in - north]
        for r in range(rows):
            advected = base_ref[t, r] + extra[r]
            part_high, part_low = split_high_low(advected)
            stacked = jnp.concatenate([part_high, part_low, part_high, part_low], axis=0)
            mixed = jnp.dot(mix, stacked, preferred_element_type=jnp.float32)
            surface = jnp.where(level == 7, surface_ref[t, r : r + 1, :], 0.0)
            mixed = jnp.concatenate([mixed[: levels - 8], mixed[levels - 8 :] + surface], axis=0)
            physics = mixed / (1.0 + decay_ref[t] * mixed * mixed)
            physics_ref[r] = physics
            gap = physics - advected
            squared = gap * gap
            for k in range(levels // 8):
                energies[r] = energies[r] + squared[8 * k : 8 * k + 8]
    if not owner_count:
        for r in range(rows):
            energy_ref[r] = energies[r]
        return
    energies = [jnp.where(lane < sector, energy, 0.0) for energy in energies]
    spot = lax.broadcasted_iota(jnp.int32, (1, LANES), 1)
    result = jnp.zeros((1, LANES), jnp.float32)
    for owner in range(owner_count):
        chosen = jnp.zeros((8, LANES), jnp.float32)
        for r in range(rows):
            picked = jnp.where(owner_ref[r : r + 1, :] == owner, energies[r], 0.0)
            for k in range(width // LANES):
                chosen = chosen + picked[:, LANES * k : LANES * (k + 1)]
        total = jnp.sum(jnp.sum(chosen, axis=0, keepdims=True), axis=1, keepdims=True)
        result = jnp.where(spot == owner, total, result)
    energy_ref[...] = result


def waves_of(radix):
    pairs = (radix - 1) // 2
    cosine = lambda k, i: math.cos(2.0 * math.pi * ((k * i) % radix) / radix)
    sine = lambda k, i: math.sin(2.0 * math.pi * ((k * i) % radix) / radix)
    return pairs, cosine, sine


def row_of(piece_refs, r):
    share = piece_refs[0].shape[0]
    return piece_refs[r // share].at[r % share]


def stacked_table(high_ref, low_ref, begin, size):
    high = high_ref[begin : begin + size, :]
    return jnp.concatenate([high, high, low_ref[begin : begin + size, :]], axis=0)


def product_of(high_ref, low_ref, begin, size, table):
    high = high_ref[:, begin : begin + size]
    stacked = jnp.concatenate([high, low_ref[:, begin : begin + size], high], axis=1)
    return jnp.dot(stacked, table, preferred_element_type=jnp.float32)


def forward_kernel(radix, pieces, own_ref, *refs):
    other_refs, refs = refs[:pieces], refs[pieces:]
    table_high_ref, table_low_ref, first_high_ref, first_low_ref, scale_ref, *refs = refs
    out_high_ref, out_low_ref, high_ref, low_ref = refs
    rows, levels, width = own_ref.shape
    pairs, cosine, sine = waves_of(radix)
    segments = width // LANES
    shift = radix * LANES // 2 % LANES
    lane = lax.broadcasted_iota(jnp.int32, (levels, LANES), 1)

    def store(place, column, wave):
        high_ref[place, column : column + LANES], low_ref[place, column : column + LANES] = split_high_low(wave)

    for r in range(rows):
        place = slice(levels * r, levels * (r + 1))
        other_ref = row_of(other_refs, r)
        own = [own_ref[r, :, LANES * n : LANES * (n + 1)] for n in range(segments)]
        turned = [pltpu.roll(other_ref[:, LANES * n : LANES * (n + 1)], shift, 1) for n in range(segments)]
        joined = own[:-1] + [jnp.where(lane < shift, own[-1], turned[0])]
        joined += [jnp.where(lane < shift, turned[n], turned[n + 1]) for n in range(segments - 1)]
        plus = [joined[n] + joined[radix - n] for n in range(1, pairs + 1)]
        minus = [joined[radix - n] - joined[n] for n in range(1, pairs + 1)]
        store(place, 0, sum(plus, joined[0]))
        for k in range(1, pairs + 1):
            real = sum((cosine(k, n) * plus[n - 1] for n in range(1, pairs + 1)), joined[0])
            imaginary = sine(k, 1) * minus[0]
            for n in range(2, pairs + 1):
                imaginary = imaginary + sine(k, n) * minus[n - 1]
            store(place, LANES * (2 * k - 1), real)
            store(place, LANES * 2 * k, imaginary)

    def transform(begin, size, table):
        spectrum = product_of(high_ref, low_ref, begin, size, table)
        for r in range(rows):
            place = slice(levels * r, levels * (r + 1))
            damped = spectrum[place] * scale_ref[r : r + 1, begin : begin + size]
            out_high_ref[place, begin : begin + size], out_low_ref[place, begin : begin + size] = split_high_low(damped)

    transform(0, LANES, stacked_table(first_high_ref, first_low_ref, 0, LANES))
    for k in range(pairs):
        transform(LANES * (2 * k + 1), 2 * LANES, stacked_table(table_high_ref, table_low_ref, 2 * LANES * k, 2 * LANES))


def inverse_kernel(radix, pieces, mask_ref, own_ref, *refs):
    other_refs, refs = refs[:pieces], refs[pieces:]
    high_ref, low_ref, table_high_ref, table_low_ref, first_high_ref, first_low_ref, *refs = refs
    result_ref, back_ref, wave_ref = refs
    rows, levels, width = own_ref.shape
    sector = result_ref.shape[-1]
    pairs, cosine, sine = waves_of(radix)
    segments = width // LANES
    shift = radix * LANES // 2 % LANES
    lane = lax.broadcasted_iota(jnp.int32, (levels, LANES), 1)

    def transform(begin, size, table):
        wave_ref[:, begin : begin + size] = product_of(high_ref, low_ref, begin, size, table)

    transform(0, LANES, stacked_table(first_high_ref, first_low_ref, 0, LANES))
    for k in range(pairs):
        transform(LANES * (2 * k + 1), 2 * LANES, stacked_table(table_high_ref, table_low_ref, 2 * LANES * k, 2 * LANES))

    for r in range(rows):
        place = slice(levels * r, levels * (r + 1))
        other_ref = row_of(other_refs, r)
        waves = [wave_ref[place, LANES * n : LANES * (n + 1)] for n in range(radix)]
        results = [None] * radix
        results[0] = sum((waves[2 * k - 1] for k in range(1, pairs + 1)), waves[0])
        for n in range(1, pairs + 1):
            even = sum((cosine(k, n) * waves[2 * k - 1] for k in range(1, pairs + 1)), waves[0])
            odd = sine(1, n) * waves[2]
            for k in range(2, pairs + 1):
                odd = odd + sine(k, n) * waves[2 * k]
            results[n], results[radix - n] = even - odd, even + odd
        filtered_row = mask_ref[r] == 1
        turned = [pltpu.roll(result, LANES - shift, 1) for result in results[segments - 1 :]]
        for n in range(segments):
            begin = LANES * n
            size = min(LANES, sector - begin)
            value = jnp.where(filtered_row, results[n], own_ref[r, :, begin : begin + LANES])
            result_ref[:, r, begin : begin + size] = value[:, :size]
            value = jnp.where(lane < LANES - shift, turned[n], turned[min(n + 1, segments - 1)])
            back_ref[r, :, begin : begin + LANES] = jnp.where(filtered_row, value, other_ref[:, begin : begin + LANES])


def finish_kernel(*refs):
    out_hbm, turned_ref, sems = refs[-3:]
    count = turned_ref.shape[0]
    result_refs, received_refs = refs[:count], refs[count : 2 * count]
    rows, levels, width = received_refs[0].shape
    sector = out_hbm.shape[-1]
    piece = levels // PIECES
    copies = []

    def send(source_ref, tracer, slot):
        for part in range(PIECES):
            span = pl.ds(piece * part, piece)
            copies.append(pltpu.make_async_copy(source_ref.at[span], out_hbm.at[tracer, span], sems.at[slot, part]))
            copies[-1].start()

    for i, result_ref in enumerate(result_refs):
        send(result_ref, first_of("keep", 2 * count) + i, i)
    for i in range(count):
        for r in range(rows):
            turned_ref[i, :, r, :] = received_refs[i][r, :, :sector]
        send(turned_ref.at[i], first_of("give", 2 * count) + i, count + i)
    for copy in copies:
        copy.wait()


def on_device(tracers, courant_lat, courant_lon, surface_flux, mixing, decay_rate, owners, polar_mask):
    tracer_count, levels, rows, sector = tracers.shape
    assert rows == 4 and sector % 64 == 0 and lax.axis_size("lon") == 2
    f32 = jnp.float32
    lat_count, lat = lax.axis_size("lat"), lax.axis_index("lat")
    length = 2 * sector
    width = -(-sector // LANES) * LANES
    radix = length // LANES
    downward = [(i + 1, i) for i in range(lat_count - 1)]
    swap = [(0, 1), (1, 0)]

    whole = pl.BlockSpec(memory_space=pltpu.VMEM)
    in_hbm = pl.BlockSpec(memory_space=pltpu.HBM)
    scalars = pl.BlockSpec(memory_space=pltpu.SMEM)
    inside = [pair for i in range(0, lat_count - 1, 2) for pair in ((i, i + 1), (i + 1, i))]
    across = [pair for i in range(1, lat_count - 1, 2) for pair in ((i, i + 1), (i + 1, i))]
    fields = [pltpu.with_memory_space_constraint(array, pltpu.HBM) for array in (tracers, courant_lat, courant_lon)]
    field_buffers = [pltpu.VMEM(array.shape, f32) for array in (tracers, courant_lat, courant_lon)]
    half = tracer_count // 2
    inner = pl.pallas_call(
        pack_kernel,
        in_specs=[in_hbm],
        out_specs=whole,
        out_shape=pltpu.VMEM((levels * tracer_count, length), f32),
        scratch_shapes=[pltpu.VMEM((tracer_count, levels, 2, sector), f32), pltpu.SemaphoreType.DMA((tracer_count,))],
        compiler_params=params(),
        cost_estimate=cost(0, 600_000),
        name="pack",
    )(fields[0])
    from_inside = lax.ppermute(inner, "lat", inside)
    fields, inner = lax.optimization_barrier((fields, inner))
    fields = [pltpu.with_memory_space_constraint(array, pltpu.HBM) for array in fields]
    *outer, courant_row, sides = pl.pallas_call(
        rest_kernel,
        in_specs=[in_hbm] * 3,
        out_specs=[whole] * (half + 2),
        out_shape=[pltpu.VMEM((levels * 2, length), f32)] * half
        + [
            jax.ShapeDtypeStruct((levels // 2, length), f32),
            jax.ShapeDtypeStruct((tracer_count + 1, rows, levels, LANES), f32),
        ],
        scratch_shapes=field_buffers + [pltpu.SemaphoreType.DMA((tracer_count + 2,))],
        compiler_params=params(),
        cost_estimate=cost(0, 0),
        name="rest",
    )(*fields)
    from_across = [lax.ppermute(part, "lat", across) for part in outer[:-1]]
    top = lax.ppermute(courant_row, "lat", downward)

    sides = lax.ppermute(sides, "lon", swap)
    base, north, lat_courant = pl.pallas_call(
        functools.partial(base_kernel, width),
        in_specs=[in_hbm, in_hbm, in_hbm, whole],
        out_specs=[whole] * 3,
        out_shape=[
            jax.ShapeDtypeStruct((tracer_count, rows, levels, width), f32),
            jax.ShapeDtypeStruct((tracer_count, levels, width), f32),
            jax.ShapeDtypeStruct((rows, levels, width), f32),
        ],
        scratch_shapes=field_buffers + [pltpu.SemaphoreType.DMA((tracer_count + 2,))],
        compiler_params=params(),
        cost_estimate=cost(0, 0),
        name="base",
    )(*fields, sides)

    surface = jnp.pad(surface_flux, ((0, 0), (0, 0), (0, width - sector)))
    decay = decay_rate[:, :, None]
    block_count = rows * sector // BLOCK
    block_of = (np.arange(rows)[:, None] * sector + np.minimum(np.arange(width), sector - 1)[None]) // BLOCK
    owner_of = jnp.repeat(owners.reshape(block_count), BLOCK).reshape(rows, sector)
    owner_of = jnp.pad(owner_of, ((0, 0), (0, width - sector)))
    forward, inverse, numbers, weights = spectral_tables(length)
    row_ids = (lat * rows + jnp.arange(rows)).astype(f32)
    latitude = (-0.5 + (row_ids + 0.5) / (lat_count * rows)) * math.pi
    inverse_sine = np.where(numbers == 0, 1.0, 1.0 / np.where(numbers == 0, 1.0, np.sin(np.pi * numbers / length)))
    ratio = 2.0 * jnp.cos(latitude)[:, None] * jnp.asarray(inverse_sine, f32)[None]
    damping = jnp.where(jnp.asarray(numbers == 0)[None], 1.0, jnp.minimum(1.0, ratio * ratio))
    scale = damping * jnp.asarray(weights, f32)[None]

    base, scale, owner_of, surface, decay = lax.optimization_barrier((base, scale, owner_of, surface, decay))

    base, outer = lax.optimization_barrier((base, outer))
    from_across.append(lax.ppermute(outer[-1], "lat", across))

    circles = jax.ShapeDtypeStruct((half, rows, levels, width), f32)
    result_shape = jax.ShapeDtypeStruct((levels, rows, sector), f32)
    out_shape = jax.ShapeDtypeStruct(tracers.shape, f32)

    def run_physics(chunk, energy, last=False):
        shapes = [jax.ShapeDtypeStruct(circles.shape[1:], f32)] * 2
        shapes.append(jax.ShapeDtypeStruct((1, LANES) if last else energy.shape, f32))
        *results, energy = pl.pallas_call(
            functools.partial(physics_kernel, levels, sector, lat_count if last else 0, chunk, ("give", "keep")),
            in_specs=[whole] * 11,
            out_specs=[whole] * len(shapes),
            out_shape=shapes,
            compiler_params=params(),
            cost_estimate=cost(0, 0),
            name="physics",
        )(base, north, from_inside, from_across[chunk], top, lat_courant, surface, mixing, decay, owner_of, energy)
        return results, energy

    forward, inverse = ([jnp.asarray(part) for table in tables for part in split_table(table)] for tables in (forward, inverse))
    circle = jax.ShapeDtypeStruct(circles.shape[1:], f32)
    spectra = jax.ShapeDtypeStruct((rows * levels, length), jnp.bfloat16)

    def run_forward(own, other):
        return pl.pallas_call(
            functools.partial(forward_kernel, radix, len(other)),
            in_specs=[whole] * (6 + len(other)),
            out_specs=[whole] * 2,
            out_shape=[spectra] * 2,
            scratch_shapes=[pltpu.VMEM(spectra.shape, jnp.bfloat16)] * 2,
            compiler_params=params(),
            cost_estimate=cost(0, 0),
            name="forward",
        )(own, *other, *forward, scale)

    def run_inverse(own, other, high, low):
        return pl.pallas_call(
            functools.partial(inverse_kernel, radix, len(other)),
            in_specs=[scalars] + [whole] * (7 + len(other)),
            out_specs=[whole] * 2,
            out_shape=[result_shape, circle],
            scratch_shapes=[pltpu.VMEM(spectra.shape, f32)],
            compiler_params=params(),
            cost_estimate=cost(0, 0),
            name="inverse",
        )(polar_mask, own, *other, high, low, *inverse)

    energy = jnp.zeros((rows, 8, width), f32)
    results, received = [], []
    for chunk in range(half - 1):
        (given, own), energy = run_physics(chunk, energy)
        other = [lax.ppermute(given[r : r + 2], "lon", swap) for r in range(0, rows, 2)]
        spectrum = run_forward(own, other)
        result, back = run_inverse(own, other, *spectrum)
        results.append(result)
        received.append(lax.ppermute(back, "lon", swap))
        energy, back = lax.optimization_barrier((energy, back))

    distances = [1 << i for i in range(lat_count.bit_length() - 1)]

    def send_energy(energy):
        distance = distances.pop(0)
        return lax.ppermute(energy, "lat", [(i, i ^ distance) for i in range(lat_count)])

    (given, own), energy = run_physics(half - 1, energy, True)
    other = [lax.ppermute(given, "lon", swap)]

    coming = send_energy(energy)
    high, low = run_forward(own, other)
    coming, high = lax.optimization_barrier((coming, high))
    energy = energy + coming
    energy, high = lax.optimization_barrier((energy, high))

    coming = send_energy(energy)
    result, back = run_inverse(own, other, high, low)
    coming, back = lax.optimization_barrier((coming, back))
    energy = energy + coming
    energy, back = lax.optimization_barrier((energy, back))
    results.append(result)
    received.append(lax.ppermute(back, "lon", swap))

    coming = send_energy(energy)
    out = pl.pallas_call(
        finish_kernel,
        in_specs=[whole] * (2 * half),
        out_specs=in_hbm,
        out_shape=out_shape,
        scratch_shapes=[
            pltpu.VMEM((half,) + result_shape.shape, f32),
            pltpu.SemaphoreType.DMA((2 * half, PIECES)),
        ],
        compiler_params=params(),
        cost_estimate=cost(0, 3_000_000),
        name="finish",
    )(*results, *received)
    coming, out = lax.optimization_barrier((coming, out))
    energy = energy + coming
    while distances:
        energy = energy + send_energy(energy)

    owner_energy = lax.dynamic_slice(energy, (0, lat), (1, 1)) / (block_count * BLOCK)
    return out, owner_energy


def solution(mesh):
    placed = (
        P("group", None, "lat", "lon"),
        P("group", "lat", "lon"),
        P("group", "lat", "lon"),
        P("group", "lat", "lon"),
        P(),
        P(),
        P(("group", "lat"), "lon", None, None),
        P(("group", "lat")),
    )
    return jax.shard_map(
        on_device,
        mesh=mesh,
        in_specs=placed,
        out_specs=(P("group", None, "lat", "lon"), P(("group", "lat"), "lon")),
        check_vma=False,
    )
```

```python
import functools
import math

import jax
import jax.numpy as jnp
import numpy as np
from jax import lax
from jax.experimental import pallas as pl
from jax.experimental.pallas import tpu as pltpu
from jax.sharding import PartitionSpec as P

LANES = 128
BLOCK = 128
VMEM_BYTES = 6 * 1024 * 1024
PIECES = 4
NEAR = 7.0 / 12.0
FAR = 1.0 / 12.0


def params():
    return pltpu.CompilerParams(vmem_limit_bytes=VMEM_BYTES)


def cost(flops, bytes_accessed):
    return pl.CostEstimate(flops=flops, bytes_accessed=bytes_accessed, transcendentals=0)


def split_high_low(value):
    high = value.astype(jnp.bfloat16)
    low = (value - high.astype(jnp.float32)).astype(jnp.bfloat16)
    return high, low


def split_table(table):
    high = table.astype(jnp.bfloat16.dtype)
    return high, (table - high.astype(np.float64)).astype(jnp.bfloat16.dtype)


def spectral_tables(length):
    radix = length // LANES
    pairs = (radix - 1) // 2
    spot = np.arange(LANES)[:, None]
    number = np.arange(LANES)[None, :]
    is_cosine = number <= LANES // 2
    wave = np.where(is_cosine, number, number - LANES // 2)
    angle = 2.0 * np.pi * ((spot * wave) % LANES) / LANES
    first = np.where(is_cosine, np.cos(angle), np.sin(angle))
    others, numbers = [], [radix * wave[0]]
    weights = [np.where((wave[0] == 0) | (wave[0] == LANES // 2), 1.0, 2.0) / length]
    for residue in range(1, pairs + 1):
        whole = residue + radix * number
        angle = 2.0 * np.pi * ((spot * whole) % length) / length
        cosine, sine = np.cos(angle), np.sin(angle)
        others.append(np.block([[cosine, -sine], [sine, cosine]]))
        folded = np.minimum(whole[0], length - whole[0])
        numbers += [folded, folded]
        weights.append(np.full(2 * LANES, 2.0 / length))
    forward = np.concatenate(others), first
    inverse = np.concatenate([table.T for table in others]), first.T
    return forward, inverse, np.concatenate(numbers), np.concatenate(weights)


def is_even():
    return lax.axis_index("lat") % 2 == 0


def first_of(half, tracer_count):
    lon = lax.axis_index("lon")
    return (tracer_count // 2) * (lon if half == "keep" else 1 - lon)


def pack_rows(first, second):
    return jnp.concatenate([first, second], axis=1)


def second_half(packed, sector):
    skip, shift = sector // LANES, sector % LANES
    segments = [packed[:, LANES * i : LANES * (i + 1)] for i in range(packed.shape[1] // LANES)]
    if shift == 0:
        return jnp.concatenate(segments[skip:], axis=1)
    turned = [pltpu.roll(segment, LANES - shift, 1) for segment in segments[skip:]]
    lane = lax.broadcasted_iota(jnp.int32, turned[0].shape, 1)
    parts = [jnp.where(lane < LANES - shift, turned[i], turned[min(i + 1, len(turned) - 1)]) for i in range(len(turned))]
    return jnp.concatenate(parts, axis=1)


def start_copies(pairs, sems):
    copies = [pltpu.make_async_copy(source, target, sems.at[i]) for i, (source, target) in enumerate(pairs)]
    for copy in copies:
        copy.start()
    return copies


def pack_kernel(tracer_hbm, out_ref, row_ref, sems):
    count, levels = row_ref.shape[:2]
    first_row = pl.multiple_of(jnp.where(is_even(), tracer_hbm.shape[2] - 2, 0), 2)
    sources = [tracer_hbm.at[t, :, pl.ds(first_row, 2), :] for t in range(count)]
    copies = start_copies([(sources[t], row_ref.at[t]) for t in range(count)], sems)
    for t in range(count):
        copies[t].wait()
        out_ref[levels * t : levels * (t + 1), :] = pack_rows(row_ref[t, :, 0, :], row_ref[t, :, 1, :])


def rest_kernel(tracer_hbm, lat_hbm, lon_hbm, *refs):
    courant_ref, side_ref, tracer_ref, lat_ref, lon_ref, sems = refs[-6:]
    outer_refs = refs[:-6]
    count, levels, rows, sector = tracer_ref.shape
    pairs = [(tracer_hbm.at[t], tracer_ref.at[t]) for t in range(count)] + [(lat_hbm, lat_ref), (lon_hbm, lon_ref)]
    copies = start_copies(pairs, sems)
    shift, whole = sector % LANES, sector // LANES * LANES
    lane = lax.broadcasted_iota(jnp.int32, (levels, LANES), 1)
    even = is_even()

    def store_side(i, r, values):
        first = pltpu.roll(values[:, :LANES], shift, 1)
        last = jnp.concatenate([values[:, whole:], values[:, whole:]], axis=1)
        side_ref[i, r] = jnp.where(lane < LANES - 2, first, last)

    for copy in copies:
        copy.wait()
    for t in range(count):
        row = [tracer_ref[t, :, r, :] for r in range(rows)]
        slot = t // len(outer_refs)
        outer_refs[t % len(outer_refs)][levels * slot : levels * (slot + 1), :] = pack_rows(
            jnp.where(even, row[0], row[rows - 2]), jnp.where(even, row[1], row[rows - 1])
        )
        for r in range(rows):
            store_side(t, r, row[r])
    courant = lat_ref[:, 0, :]
    courant_ref[...] = pack_rows(courant[: levels // 2], courant[levels // 2 :])
    for r in range(rows):
        store_side(count, r, lon_ref[:, r, :])


def base_kernel(width, tracer_hbm, lat_hbm, lon_hbm, side_ref, base_ref, north_ref, courant_ref, *scratch):
    tracer_ref, lat_ref, lon_ref, sems = scratch
    tracer_count, levels, rows, sector = tracer_ref.shape
    whole = sector // LANES * LANES
    pairs = [(lat_hbm, lat_ref), (lon_hbm, lon_ref)] + [(tracer_hbm.at[t], tracer_ref.at[t]) for t in range(tracer_count)]
    copies = start_copies(pairs, sems)

    def beside(values, side):
        return jnp.concatenate([values[:, :whole], values[:, whole:], side[:, sector - whole :]], axis=1)

    copies[0].wait()
    copies[1].wait()
    nothing = jnp.zeros((levels, LANES), jnp.float32)
    for r in range(rows):
        courant = lat_ref[:, r, :] if r else jnp.where(lax.axis_index("lat") > 0, lat_ref[:, r, :], 0.0)
        courant_ref[r] = beside(courant, nothing)
    for t in range(tracer_count):
        copies[t + 2].wait()
        q = [beside(tracer_ref[t, :, r, :], side_ref[t, r]) for r in range(rows)]
        north_ref[t] = NEAR * q[3] - FAR * q[2]
        own_flux = [
            courant_ref[0] * (NEAR * q[0] - FAR * q[1]),
            courant_ref[1] * (NEAR * (q[1] + q[0]) - FAR * q[2]),
            courant_ref[2] * (NEAR * (q[2] + q[1]) - FAR * (q[3] + q[0])),
            courant_ref[3] * (NEAR * (q[3] + q[2]) - FAR * q[1]),
        ]
        for r in range(rows):
            west, west2, east = pltpu.roll(q[r], 1, 1), pltpu.roll(q[r], 2, 1), pltpu.roll(q[r], width - 1, 1)
            flux = beside(lon_ref[:, r, :], side_ref[tracer_count, r]) * (NEAR * (q[r] + west) - FAR * (east + west2))
            value = q[r] - (pltpu.roll(flux, width - 1, 1) - flux) + own_flux[r]
            if r + 1 < rows:
                value = value - own_flux[r + 1]
            base_ref[t, r] = value


def physics_kernel(levels, sector, owner_count, chunk, halves, *refs):
    base_ref, north_ref, inner_ref, outer_ref = refs[:4]
    top_ref, courant_ref, surface_ref, mixing_ref, decay_ref, owner_ref, energy_in_ref = refs[4:11]
    physics_refs, energy_ref = refs[11:-1], refs[-1]
    rows, width = base_ref.shape[1], base_ref.shape[-1]
    courant = [courant_ref[r] for r in range(rows)]
    even = is_even()
    top = top_ref[...]
    top = jnp.concatenate([top[:, :width], second_half(top, sector)], axis=0)
    mix_high, mix_low = split_high_low(mixing_ref[...])
    mix = jnp.concatenate([mix_high, mix_high, mix_low, mix_low], axis=1)
    level = lax.broadcasted_iota(jnp.int32, (8, width), 0)
    lane = lax.broadcasted_iota(jnp.int32, (8, width), 1)
    energies = [energy_in_ref[r] for r in range(rows)]
    for half, physics_ref in zip(halves, physics_refs):
        first = first_of(half, base_ref.shape[0])
        t = first + chunk
        inner = inner_ref[pl.ds(pl.multiple_of(levels * t, levels), levels), :]
        outer = jnp.where(first == 0, outer_ref[:levels, :], outer_ref[levels:, :])
        low, high = jnp.where(even, outer, inner), jnp.where(even, inner, outer)
        low_a, low_b = low[:, :width], second_half(low, sector)
        high_a, high_b = high[:, :width], second_half(high, sector)
        south = courant[0] * (NEAR * low_b - FAR * low_a)
        south_in = courant[1] * (FAR * low_b)
        north_in = courant[3] * (FAR * high_a)
        north = top * (NEAR * high_a - FAR * high_b + north_ref[t])
        extra = [south + south_in, -south_in, north_in, -north_in - north]
        for r in range(rows):
            advected = base_ref[t, r] + extra[r]
            part_high, part_low = split_high_low(advected)
            stacked = jnp.concatenate([part_high, part_low, part_high, part_low], axis=0)
            mixed = jnp.dot(mix, stacked, preferred_element_type=jnp.float32)
            surface = jnp.where(level == 7, surface_ref[t, r : r + 1, :], 0.0)
            mixed = jnp.concatenate([mixed[: levels - 8], mixed[levels - 8 :] + surface], axis=0)
            physics = mixed / (1.0 + decay_ref[t] * mixed * mixed)
            physics_ref[r] = physics
            gap = physics - advected
            squared = gap * gap
            for k in range(levels // 8):
                energies[r] = energies[r] + squared[8 * k : 8 * k + 8]
    if not owner_count:
        for r in range(rows):
            energy_ref[r] = energies[r]
        return
    energies = [jnp.where(lane < sector, energy, 0.0) for energy in energies]
    spot = lax.broadcasted_iota(jnp.int32, (1, LANES), 1)
    result = jnp.zeros((1, LANES), jnp.float32)
    for owner in range(owner_count):
        chosen = jnp.zeros((8, LANES), jnp.float32)
        for r in range(rows):
            picked = jnp.where(owner_ref[r : r + 1, :] == owner, energies[r], 0.0)
            for k in range(width // LANES):
                chosen = chosen + picked[:, LANES * k : LANES * (k + 1)]
        total = jnp.sum(jnp.sum(chosen, axis=0, keepdims=True), axis=1, keepdims=True)
        result = jnp.where(spot == owner, total, result)
    energy_ref[...] = result


def waves_of(radix):
    pairs = (radix - 1) // 2
    cosine = lambda k, i: math.cos(2.0 * math.pi * ((k * i) % radix) / radix)
    sine = lambda k, i: math.sin(2.0 * math.pi * ((k * i) % radix) / radix)
    return pairs, cosine, sine


def row_of(piece_refs, r):
    share = piece_refs[0].shape[0]
    return piece_refs[r // share].at[r % share]


def stacked_table(high_ref, low_ref, begin, size):
    high = high_ref[begin : begin + size, :]
    return jnp.concatenate([high, high, low_ref[begin : begin + size, :]], axis=0)


def product_of(high_ref, low_ref, begin, size, table):
    high = high_ref[:, begin : begin + size]
    stacked = jnp.concatenate([high, low_ref[:, begin : begin + size], high], axis=1)
    return jnp.dot(stacked, table, preferred_element_type=jnp.float32)


def forward_kernel(radix, pieces, own_ref, *refs):
    other_refs, refs = refs[:pieces], refs[pieces:]
    table_high_ref, table_low_ref, first_high_ref, first_low_ref, scale_ref, *refs = refs
    out_high_ref, out_low_ref, high_ref, low_ref = refs
    rows, levels, width = own_ref.shape
    pairs, cosine, sine = waves_of(radix)
    segments = width // LANES
    shift = radix * LANES // 2 % LANES
    lane = lax.broadcasted_iota(jnp.int32, (levels, LANES), 1)

    def store(place, column, wave):
        high_ref[place, column : column + LANES], low_ref[place, column : column + LANES] = split_high_low(wave)

    for r in range(rows):
        place = slice(levels * r, levels * (r + 1))
        other_ref = row_of(other_refs, r)
        own = [own_ref[r, :, LANES * n : LANES * (n + 1)] for n in range(segments)]
        turned = [pltpu.roll(other_ref[:, LANES * n : LANES * (n + 1)], shift, 1) for n in range(segments)]
        joined = own[:-1] + [jnp.where(lane < shift, own[-1], turned[0])]
        joined += [jnp.where(lane < shift, turned[n], turned[n + 1]) for n in range(segments - 1)]
        plus = [joined[n] + joined[radix - n] for n in range(1, pairs + 1)]
        minus = [joined[radix - n] - joined[n] for n in range(1, pairs + 1)]
        store(place, 0, sum(plus, joined[0]))
        for k in range(1, pairs + 1):
            real = sum((cosine(k, n) * plus[n - 1] for n in range(1, pairs + 1)), joined[0])
            imaginary = sine(k, 1) * minus[0]
            for n in range(2, pairs + 1):
                imaginary = imaginary + sine(k, n) * minus[n - 1]
            store(place, LANES * (2 * k - 1), real)
            store(place, LANES * 2 * k, imaginary)

    def transform(begin, size, table):
        spectrum = product_of(high_ref, low_ref, begin, size, table)
        for r in range(rows):
            place = slice(levels * r, levels * (r + 1))
            damped = spectrum[place] * scale_ref[r : r + 1, begin : begin + size]
            out_high_ref[place, begin : begin + size], out_low_ref[place, begin : begin + size] = split_high_low(damped)

    transform(0, LANES, stacked_table(first_high_ref, first_low_ref, 0, LANES))
    for k in range(pairs):
        transform(LANES * (2 * k + 1), 2 * LANES, stacked_table(table_high_ref, table_low_ref, 2 * LANES * k, 2 * LANES))


def inverse_kernel(radix, pieces, mask_ref, own_ref, *refs):
    other_refs, refs = refs[:pieces], refs[pieces:]
    high_ref, low_ref, table_high_ref, table_low_ref, first_high_ref, first_low_ref, *refs = refs
    result_ref, back_ref, wave_ref = refs
    rows, levels, width = own_ref.shape
    sector = result_ref.shape[-1]
    pairs, cosine, sine = waves_of(radix)
    segments = width // LANES
    shift = radix * LANES // 2 % LANES
    lane = lax.broadcasted_iota(jnp.int32, (levels, LANES), 1)

    def transform(begin, size, table):
        wave_ref[:, begin : begin + size] = product_of(high_ref, low_ref, begin, size, table)

    transform(0, LANES, stacked_table(first_high_ref, first_low_ref, 0, LANES))
    for k in range(pairs):
        transform(LANES * (2 * k + 1), 2 * LANES, stacked_table(table_high_ref, table_low_ref, 2 * LANES * k, 2 * LANES))

    for r in range(rows):
        place = slice(levels * r, levels * (r + 1))
        other_ref = row_of(other_refs, r)
        waves = [wave_ref[place, LANES * n : LANES * (n + 1)] for n in range(radix)]
        results = [None] * radix
        results[0] = sum((waves[2 * k - 1] for k in range(1, pairs + 1)), waves[0])
        for n in range(1, pairs + 1):
            even = sum((cosine(k, n) * waves[2 * k - 1] for k in range(1, pairs + 1)), waves[0])
            odd = sine(1, n) * waves[2]
            for k in range(2, pairs + 1):
                odd = odd + sine(k, n) * waves[2 * k]
            results[n], results[radix - n] = even - odd, even + odd
        filtered_row = mask_ref[r] == 1
        turned = [pltpu.roll(result, LANES - shift, 1) for result in results[segments - 1 :]]
        for n in range(segments):
            begin = LANES * n
            size = min(LANES, sector - begin)
            value = jnp.where(filtered_row, results[n], own_ref[r, :, begin : begin + LANES])
            result_ref[:, r, begin : begin + size] = value[:, :size]
            value = jnp.where(lane < LANES - shift, turned[n], turned[min(n + 1, segments - 1)])
            back_ref[r, :, begin : begin + LANES] = jnp.where(filtered_row, value, other_ref[:, begin : begin + LANES])


def finish_kernel(*refs):
    out_hbm, turned_ref, sems = refs[-3:]
    count = turned_ref.shape[0]
    result_refs, received_refs = refs[:count], refs[count : 2 * count]
    rows, levels, width = received_refs[0].shape
    sector = out_hbm.shape[-1]
    piece = levels // PIECES
    copies = []

    def send(source_ref, tracer, slot):
        for part in range(PIECES):
            span = pl.ds(piece * part, piece)
            copies.append(pltpu.make_async_copy(source_ref.at[span], out_hbm.at[tracer, span], sems.at[slot, part]))
            copies[-1].start()

    for i, result_ref in enumerate(result_refs):
        send(result_ref, first_of("keep", 2 * count) + i, i)
    for i in range(count):
        for r in range(rows):
            turned_ref[i, :, r, :] = received_refs[i][r, :, :sector]
        send(turned_ref.at[i], first_of("give", 2 * count) + i, count + i)
    for copy in copies:
        copy.wait()


def on_device(tracers, courant_lat, courant_lon, surface_flux, mixing, decay_rate, owners, polar_mask):
    tracer_count, levels, rows, sector = tracers.shape
    assert rows == 4 and sector % 64 == 0 and lax.axis_size("lon") == 2
    f32 = jnp.float32
    lat_count, lat = lax.axis_size("lat"), lax.axis_index("lat")
    length = 2 * sector
    width = -(-sector // LANES) * LANES
    radix = length // LANES
    downward = [(i + 1, i) for i in range(lat_count - 1)]
    swap = [(0, 1), (1, 0)]

    whole = pl.BlockSpec(memory_space=pltpu.VMEM)
    in_hbm = pl.BlockSpec(memory_space=pltpu.HBM)
    scalars = pl.BlockSpec(memory_space=pltpu.SMEM)
    inside = [pair for i in range(0, lat_count - 1, 2) for pair in ((i, i + 1), (i + 1, i))]
    across = [pair for i in range(1, lat_count - 1, 2) for pair in ((i, i + 1), (i + 1, i))]
    fields = [pltpu.with_memory_space_constraint(array, pltpu.HBM) for array in (tracers, courant_lat, courant_lon)]
    field_buffers = [pltpu.VMEM(array.shape, f32) for array in (tracers, courant_lat, courant_lon)]
    half = tracer_count // 2
    inner = pl.pallas_call(
        pack_kernel,
        in_specs=[in_hbm],
        out_specs=whole,
        out_shape=pltpu.VMEM((levels * tracer_count, length), f32),
        scratch_shapes=[pltpu.VMEM((tracer_count, levels, 2, sector), f32), pltpu.SemaphoreType.DMA((tracer_count,))],
        compiler_params=params(),
        cost_estimate=cost(0, 600_000),
        name="pack",
    )(fields[0])
    from_inside = lax.ppermute(inner, "lat", inside)
    fields, inner = lax.optimization_barrier((fields, inner))
    fields = [pltpu.with_memory_space_constraint(array, pltpu.HBM) for array in fields]
    *outer, courant_row, sides = pl.pallas_call(
        rest_kernel,
        in_specs=[in_hbm] * 3,
        out_specs=[whole] * (half + 2),
        out_shape=[pltpu.VMEM((levels * 2, length), f32)] * half
        + [
            jax.ShapeDtypeStruct((levels // 2, length), f32),
            jax.ShapeDtypeStruct((tracer_count + 1, rows, levels, LANES), f32),
        ],
        scratch_shapes=field_buffers + [pltpu.SemaphoreType.DMA((tracer_count + 2,))],
        compiler_params=params(),
        cost_estimate=cost(0, 0),
        name="rest",
    )(*fields)
    from_across = [lax.ppermute(part, "lat", across) for part in outer[:-1]]

    sides = lax.ppermute(sides, "lon", swap)
    base, north, lat_courant = pl.pallas_call(
        functools.partial(base_kernel, width),
        in_specs=[in_hbm, in_hbm, in_hbm, whole],
        out_specs=[whole] * 3,
        out_shape=[
            jax.ShapeDtypeStruct((tracer_count, rows, levels, width), f32),
            jax.ShapeDtypeStruct((tracer_count, levels, width), f32),
            jax.ShapeDtypeStruct((rows, levels, width), f32),
        ],
        scratch_shapes=field_buffers + [pltpu.SemaphoreType.DMA((tracer_count + 2,))],
        compiler_params=params(),
        cost_estimate=cost(0, 0),
        name="base",
    )(*fields, sides)

    surface = jnp.pad(surface_flux, ((0, 0), (0, 0), (0, width - sector)))
    decay = decay_rate[:, :, None]
    block_count = rows * sector // BLOCK
    block_of = (np.arange(rows)[:, None] * sector + np.minimum(np.arange(width), sector - 1)[None]) // BLOCK
    owner_of = jnp.repeat(owners.reshape(block_count), BLOCK).reshape(rows, sector)
    owner_of = jnp.pad(owner_of, ((0, 0), (0, width - sector)))
    forward, inverse, numbers, weights = spectral_tables(length)
    row_ids = (lat * rows + jnp.arange(rows)).astype(f32)
    latitude = (-0.5 + (row_ids + 0.5) / (lat_count * rows)) * math.pi
    inverse_sine = np.where(numbers == 0, 1.0, 1.0 / np.where(numbers == 0, 1.0, np.sin(np.pi * numbers / length)))
    ratio = 2.0 * jnp.cos(latitude)[:, None] * jnp.asarray(inverse_sine, f32)[None]
    damping = jnp.where(jnp.asarray(numbers == 0)[None], 1.0, jnp.minimum(1.0, ratio * ratio))
    scale = damping * jnp.asarray(weights, f32)[None]

    base, scale, owner_of, surface, decay = lax.optimization_barrier((base, scale, owner_of, surface, decay))

    base, outer, courant_row = lax.optimization_barrier((base, outer, courant_row))
    top = lax.ppermute(courant_row, "lat", downward)
    from_across.append(lax.ppermute(outer[-1], "lat", across))

    circles = jax.ShapeDtypeStruct((half, rows, levels, width), f32)
    result_shape = jax.ShapeDtypeStruct((levels, rows, sector), f32)
    out_shape = jax.ShapeDtypeStruct(tracers.shape, f32)

    def run_physics(chunk, energy, last=False):
        shapes = [jax.ShapeDtypeStruct(circles.shape[1:], f32)] * 2
        shapes.append(jax.ShapeDtypeStruct((1, LANES) if last else energy.shape, f32))
        *results, energy = pl.pallas_call(
            functools.partial(physics_kernel, levels, sector, lat_count if last else 0, chunk, ("give", "keep")),
            in_specs=[whole] * 11,
            out_specs=[whole] * len(shapes),
            out_shape=shapes,
            compiler_params=params(),
            cost_estimate=cost(0, 0),
            name="physics",
        )(base, north, from_inside, from_across[chunk], top, lat_courant, surface, mixing, decay, owner_of, energy)
        return results, energy

    forward, inverse = ([jnp.asarray(part) for table in tables for part in split_table(table)] for tables in (forward, inverse))
    circle = jax.ShapeDtypeStruct(circles.shape[1:], f32)
    spectra = jax.ShapeDtypeStruct((rows * levels, length), jnp.bfloat16)

    def run_forward(own, other):
        return pl.pallas_call(
            functools.partial(forward_kernel, radix, len(other)),
            in_specs=[whole] * (6 + len(other)),
            out_specs=[whole] * 2,
            out_shape=[spectra] * 2,
            scratch_shapes=[pltpu.VMEM(spectra.shape, jnp.bfloat16)] * 2,
            compiler_params=params(),
            cost_estimate=cost(0, 0),
            name="forward",
        )(own, *other, *forward, scale)

    def run_inverse(own, other, high, low):
        return pl.pallas_call(
            functools.partial(inverse_kernel, radix, len(other)),
            in_specs=[scalars] + [whole] * (7 + len(other)),
            out_specs=[whole] * 2,
            out_shape=[result_shape, circle],
            scratch_shapes=[pltpu.VMEM(spectra.shape, f32)],
            compiler_params=params(),
            cost_estimate=cost(0, 0),
            name="inverse",
        )(polar_mask, own, *other, high, low, *inverse)

    energy = jnp.zeros((rows, 8, width), f32)
    results, received = [], []
    for chunk in range(half - 1):
        (given, own), energy = run_physics(chunk, energy)
        other = [lax.ppermute(given[r : r + 2], "lon", swap) for r in range(0, rows, 2)]
        spectrum = run_forward(own, other)
        result, back = run_inverse(own, other, *spectrum)
        results.append(result)
        received.append(lax.ppermute(back, "lon", swap))
        energy, back = lax.optimization_barrier((energy, back))

    distances = [1 << i for i in range(lat_count.bit_length() - 1)]

    def send_energy(energy):
        distance = distances.pop(0)
        return lax.ppermute(energy, "lat", [(i, i ^ distance) for i in range(lat_count)])

    (given, own), energy = run_physics(half - 1, energy, True)
    other = [lax.ppermute(given, "lon", swap)]

    coming = send_energy(energy)
    high, low = run_forward(own, other)
    coming, high = lax.optimization_barrier((coming, high))
    energy = energy + coming
    energy, high = lax.optimization_barrier((energy, high))

    coming = send_energy(energy)
    result, back = run_inverse(own, other, high, low)
    coming, back = lax.optimization_barrier((coming, back))
    energy = energy + coming
    energy, back = lax.optimization_barrier((energy, back))
    results.append(result)
    received.append(lax.ppermute(back, "lon", swap))

    coming = send_energy(energy)
    out = pl.pallas_call(
        finish_kernel,
        in_specs=[whole] * (2 * half),
        out_specs=in_hbm,
        out_shape=out_shape,
        scratch_shapes=[
            pltpu.VMEM((half,) + result_shape.shape, f32),
            pltpu.SemaphoreType.DMA((2 * half, PIECES)),
        ],
        compiler_params=params(),
        cost_estimate=cost(0, 3_000_000),
        name="finish",
    )(*results, *received)
    coming, out = lax.optimization_barrier((coming, out))
    energy = energy + coming
    while distances:
        energy = energy + send_energy(energy)

    owner_energy = lax.dynamic_slice(energy, (0, lat), (1, 1)) / (block_count * BLOCK)
    return out, owner_energy


def solution(mesh):
    placed = (
        P("group", None, "lat", "lon"),
        P("group", "lat", "lon"),
        P("group", "lat", "lon"),
        P("group", "lat", "lon"),
        P(),
        P(),
        P(("group", "lat"), "lon", None, None),
        P(("group", "lat")),
    )
    return jax.shard_map(
        on_device,
        mesh=mesh,
        in_specs=placed,
        out_specs=(P("group", None, "lat", "lon"), P(("group", "lat"), "lon")),
        check_vma=False,
    )
```

```python
import functools
import math

import jax
import jax.numpy as jnp
import numpy as np
from jax import lax
from jax.experimental import pallas as pl
from jax.experimental.pallas import tpu as pltpu
from jax.sharding import PartitionSpec as P

LANES = 128
BLOCK = 128
VMEM_BYTES = 6 * 1024 * 1024
PIECES = 4
NEAR = 7.0 / 12.0
FAR = 1.0 / 12.0


def params():
    return pltpu.CompilerParams(vmem_limit_bytes=VMEM_BYTES)


def cost(flops, bytes_accessed):
    return pl.CostEstimate(flops=flops, bytes_accessed=bytes_accessed, transcendentals=0)


def split_high_low(value):
    high = value.astype(jnp.bfloat16)
    low = (value - high.astype(jnp.float32)).astype(jnp.bfloat16)
    return high, low


def split_table(table):
    high = table.astype(jnp.bfloat16.dtype)
    return high, (table - high.astype(np.float64)).astype(jnp.bfloat16.dtype)


def spectral_tables(length):
    radix = length // LANES
    pairs = (radix - 1) // 2
    spot = np.arange(LANES)[:, None]
    number = np.arange(LANES)[None, :]
    is_cosine = number <= LANES // 2
    wave = np.where(is_cosine, number, number - LANES // 2)
    angle = 2.0 * np.pi * ((spot * wave) % LANES) / LANES
    first = np.where(is_cosine, np.cos(angle), np.sin(angle))
    others, numbers = [], [radix * wave[0]]
    weights = [np.where((wave[0] == 0) | (wave[0] == LANES // 2), 1.0, 2.0) / length]
    for residue in range(1, pairs + 1):
        whole = residue + radix * number
        angle = 2.0 * np.pi * ((spot * whole) % length) / length
        cosine, sine = np.cos(angle), np.sin(angle)
        others.append(np.block([[cosine, -sine], [sine, cosine]]))
        folded = np.minimum(whole[0], length - whole[0])
        numbers += [folded, folded]
        weights.append(np.full(2 * LANES, 2.0 / length))
    forward = np.concatenate(others), first
    inverse = np.concatenate([table.T for table in others]), first.T
    return forward, inverse, np.concatenate(numbers), np.concatenate(weights)


def is_even():
    return lax.axis_index("lat") % 2 == 0


def first_of(half, tracer_count):
    lon = lax.axis_index("lon")
    return (tracer_count // 2) * (lon if half == "keep" else 1 - lon)


def pack_rows(first, second):
    return jnp.concatenate([first, second], axis=1)


def second_half(packed, sector):
    skip, shift = sector // LANES, sector % LANES
    segments = [packed[:, LANES * i : LANES * (i + 1)] for i in range(packed.shape[1] // LANES)]
    if shift == 0:
        return jnp.concatenate(segments[skip:], axis=1)
    turned = [pltpu.roll(segment, LANES - shift, 1) for segment in segments[skip:]]
    lane = lax.broadcasted_iota(jnp.int32, turned[0].shape, 1)
    parts = [jnp.where(lane < LANES - shift, turned[i], turned[min(i + 1, len(turned) - 1)]) for i in range(len(turned))]
    return jnp.concatenate(parts, axis=1)


def start_copies(pairs, sems):
    copies = [pltpu.make_async_copy(source, target, sems.at[i]) for i, (source, target) in enumerate(pairs)]
    for copy in copies:
        copy.start()
    return copies


def pack_kernel(tracer_hbm, out_ref, row_ref, sems):
    count, levels = row_ref.shape[:2]
    first_row = pl.multiple_of(jnp.where(is_even(), tracer_hbm.shape[2] - 2, 0), 2)
    sources = [tracer_hbm.at[t, :, pl.ds(first_row, 2), :] for t in range(count)]
    copies = start_copies([(sources[t], row_ref.at[t]) for t in range(count)], sems)
    for t in range(count):
        copies[t].wait()
        out_ref[levels * t : levels * (t + 1), :] = pack_rows(row_ref[t, :, 0, :], row_ref[t, :, 1, :])


def rest_kernel(tracer_hbm, lat_hbm, lon_hbm, *refs):
    courant_ref, side_ref, tracer_ref, lat_ref, lon_ref, sems = refs[-6:]
    outer_refs = refs[:-6]
    count, levels, rows, sector = tracer_ref.shape
    for pairs in (
        [(lat_hbm, lat_ref), (lon_hbm, lon_ref)],
        [(tracer_hbm.at[t], tracer_ref.at[t]) for t in range(count)],
    ):
        for copy in start_copies(pairs, sems):
            copy.wait()
    shift, whole = sector % LANES, sector // LANES * LANES
    lane = lax.broadcasted_iota(jnp.int32, (levels, LANES), 1)
    even = is_even()

    def store_side(i, r, values):
        first = pltpu.roll(values[:, :LANES], shift, 1)
        last = jnp.concatenate([values[:, whole:], values[:, whole:]], axis=1)
        side_ref[i, r] = jnp.where(lane < LANES - 2, first, last)

    for t in range(count):
        row = [tracer_ref[t, :, r, :] for r in range(rows)]
        slot = t // len(outer_refs)
        outer_refs[t % len(outer_refs)][levels * slot : levels * (slot + 1), :] = pack_rows(
            jnp.where(even, row[0], row[rows - 2]), jnp.where(even, row[1], row[rows - 1])
        )
        for r in range(rows):
            store_side(t, r, row[r])
    courant = lat_ref[:, 0, :]
    courant_ref[...] = pack_rows(courant[: levels // 2], courant[levels // 2 :])
    for r in range(rows):
        store_side(count, r, lon_ref[:, r, :])


def base_kernel(width, tracer_hbm, lat_hbm, lon_hbm, side_ref, base_ref, north_ref, courant_ref, *scratch):
    tracer_ref, lat_ref, lon_ref, sems = scratch
    tracer_count, levels, rows, sector = tracer_ref.shape
    whole = sector // LANES * LANES
    pairs = [(lat_hbm, lat_ref), (lon_hbm, lon_ref)] + [(tracer_hbm.at[t], tracer_ref.at[t]) for t in range(tracer_count)]
    copies = start_copies(pairs, sems)

    def beside(values, side):
        return jnp.concatenate([values[:, :whole], values[:, whole:], side[:, sector - whole :]], axis=1)

    copies[0].wait()
    copies[1].wait()
    nothing = jnp.zeros((levels, LANES), jnp.float32)
    for r in range(rows):
        courant = lat_ref[:, r, :] if r else jnp.where(lax.axis_index("lat") > 0, lat_ref[:, r, :], 0.0)
        courant_ref[r] = beside(courant, nothing)
    for t in range(tracer_count):
        copies[t + 2].wait()
        q = [beside(tracer_ref[t, :, r, :], side_ref[t, r]) for r in range(rows)]
        north_ref[t] = NEAR * q[3] - FAR * q[2]
        own_flux = [
            courant_ref[0] * (NEAR * q[0] - FAR * q[1]),
            courant_ref[1] * (NEAR * (q[1] + q[0]) - FAR * q[2]),
            courant_ref[2] * (NEAR * (q[2] + q[1]) - FAR * (q[3] + q[0])),
            courant_ref[3] * (NEAR * (q[3] + q[2]) - FAR * q[1]),
        ]
        for r in range(rows):
            west, west2, east = pltpu.roll(q[r], 1, 1), pltpu.roll(q[r], 2, 1), pltpu.roll(q[r], width - 1, 1)
            flux = beside(lon_ref[:, r, :], side_ref[tracer_count, r]) * (NEAR * (q[r] + west) - FAR * (east + west2))
            value = q[r] - (pltpu.roll(flux, width - 1, 1) - flux) + own_flux[r]
            if r + 1 < rows:
                value = value - own_flux[r + 1]
            base_ref[t, r] = value


def physics_kernel(levels, sector, owner_count, chunk, halves, *refs):
    base_ref, north_ref, inner_ref, outer_ref = refs[:4]
    top_ref, courant_ref, surface_ref, mixing_ref, decay_ref, owner_ref, energy_in_ref = refs[4:11]
    physics_refs, energy_ref = refs[11:-1], refs[-1]
    rows, width = base_ref.shape[1], base_ref.shape[-1]
    courant = [courant_ref[r] for r in range(rows)]
    even = is_even()
    top = top_ref[...]
    top = jnp.concatenate([top[:, :width], second_half(top, sector)], axis=0)
    mix_high, mix_low = split_high_low(mixing_ref[...])
    mix = jnp.concatenate([mix_high, mix_high, mix_low, mix_low], axis=1)
    level = lax.broadcasted_iota(jnp.int32, (8, width), 0)
    lane = lax.broadcasted_iota(jnp.int32, (8, width), 1)
    energies = [energy_in_ref[r] for r in range(rows)]
    for half, physics_ref in zip(halves, physics_refs):
        first = first_of(half, base_ref.shape[0])
        t = first + chunk
        inner = inner_ref[pl.ds(pl.multiple_of(levels * t, levels), levels), :]
        outer = jnp.where(first == 0, outer_ref[:levels, :], outer_ref[levels:, :])
        low, high = jnp.where(even, outer, inner), jnp.where(even, inner, outer)
        low_a, low_b = low[:, :width], second_half(low, sector)
        high_a, high_b = high[:, :width], second_half(high, sector)
        south = courant[0] * (NEAR * low_b - FAR * low_a)
        south_in = courant[1] * (FAR * low_b)
        north_in = courant[3] * (FAR * high_a)
        north = top * (NEAR * high_a - FAR * high_b + north_ref[t])
        extra = [south + south_in, -south_in, north_in, -north_in - north]
        for r in range(rows):
            advected = base_ref[t, r] + extra[r]
            part_high, part_low = split_high_low(advected)
            stacked = jnp.concatenate([part_high, part_low, part_high, part_low], axis=0)
            mixed = jnp.dot(mix, stacked, preferred_element_type=jnp.float32)
            surface = jnp.where(level == 7, surface_ref[t, r : r + 1, :], 0.0)
            mixed = jnp.concatenate([mixed[: levels - 8], mixed[levels - 8 :] + surface], axis=0)
            physics = mixed / (1.0 + decay_ref[t] * mixed * mixed)
            physics_ref[r] = physics
            gap = physics - advected
            squared = gap * gap
            for k in range(levels // 8):
                energies[r] = energies[r] + squared[8 * k : 8 * k + 8]
    if not owner_count:
        for r in range(rows):
            energy_ref[r] = energies[r]
        return
    energies = [jnp.where(lane < sector, energy, 0.0) for energy in energies]
    spot = lax.broadcasted_iota(jnp.int32, (1, LANES), 1)
    result = jnp.zeros((1, LANES), jnp.float32)
    for owner in range(owner_count):
        chosen = jnp.zeros((8, LANES), jnp.float32)
        for r in range(rows):
            picked = jnp.where(owner_ref[r : r + 1, :] == owner, energies[r], 0.0)
            for k in range(width // LANES):
                chosen = chosen + picked[:, LANES * k : LANES * (k + 1)]
        total = jnp.sum(jnp.sum(chosen, axis=0, keepdims=True), axis=1, keepdims=True)
        result = jnp.where(spot == owner, total, result)
    energy_ref[...] = result


def waves_of(radix):
    pairs = (radix - 1) // 2
    cosine = lambda k, i: math.cos(2.0 * math.pi * ((k * i) % radix) / radix)
    sine = lambda k, i: math.sin(2.0 * math.pi * ((k * i) % radix) / radix)
    return pairs, cosine, sine


def row_of(piece_refs, r):
    share = piece_refs[0].shape[0]
    return piece_refs[r // share].at[r % share]


def stacked_table(high_ref, low_ref, begin, size):
    high = high_ref[begin : begin + size, :]
    return jnp.concatenate([high, high, low_ref[begin : begin + size, :]], axis=0)


def product_of(high_ref, low_ref, begin, size, table):
    high = high_ref[:, begin : begin + size]
    stacked = jnp.concatenate([high, low_ref[:, begin : begin + size], high], axis=1)
    return jnp.dot(stacked, table, preferred_element_type=jnp.float32)


def forward_kernel(radix, pieces, own_ref, *refs):
    other_refs, refs = refs[:pieces], refs[pieces:]
    table_high_ref, table_low_ref, first_high_ref, first_low_ref, scale_ref, *refs = refs
    out_high_ref, out_low_ref, high_ref, low_ref = refs
    rows, levels, width = own_ref.shape
    pairs, cosine, sine = waves_of(radix)
    segments = width // LANES
    shift = radix * LANES // 2 % LANES
    lane = lax.broadcasted_iota(jnp.int32, (levels, LANES), 1)

    def store(place, column, wave):
        high_ref[place, column : column + LANES], low_ref[place, column : column + LANES] = split_high_low(wave)

    for r in range(rows):
        place = slice(levels * r, levels * (r + 1))
        other_ref = row_of(other_refs, r)
        own = [own_ref[r, :, LANES * n : LANES * (n + 1)] for n in range(segments)]
        turned = [pltpu.roll(other_ref[:, LANES * n : LANES * (n + 1)], shift, 1) for n in range(segments)]
        joined = own[:-1] + [jnp.where(lane < shift, own[-1], turned[0])]
        joined += [jnp.where(lane < shift, turned[n], turned[n + 1]) for n in range(segments - 1)]
        plus = [joined[n] + joined[radix - n] for n in range(1, pairs + 1)]
        minus = [joined[radix - n] - joined[n] for n in range(1, pairs + 1)]
        store(place, 0, sum(plus, joined[0]))
        for k in range(1, pairs + 1):
            real = sum((cosine(k, n) * plus[n - 1] for n in range(1, pairs + 1)), joined[0])
            imaginary = sine(k, 1) * minus[0]
            for n in range(2, pairs + 1):
                imaginary = imaginary + sine(k, n) * minus[n - 1]
            store(place, LANES * (2 * k - 1), real)
            store(place, LANES * 2 * k, imaginary)

    def transform(begin, size, table):
        spectrum = product_of(high_ref, low_ref, begin, size, table)
        for r in range(rows):
            place = slice(levels * r, levels * (r + 1))
            damped = spectrum[place] * scale_ref[r : r + 1, begin : begin + size]
            out_high_ref[place, begin : begin + size], out_low_ref[place, begin : begin + size] = split_high_low(damped)

    transform(0, LANES, stacked_table(first_high_ref, first_low_ref, 0, LANES))
    for k in range(pairs):
        transform(LANES * (2 * k + 1), 2 * LANES, stacked_table(table_high_ref, table_low_ref, 2 * LANES * k, 2 * LANES))


def inverse_kernel(radix, pieces, mask_ref, own_ref, *refs):
    other_refs, refs = refs[:pieces], refs[pieces:]
    high_ref, low_ref, table_high_ref, table_low_ref, first_high_ref, first_low_ref, *refs = refs
    result_ref, back_ref, wave_ref = refs
    rows, levels, width = own_ref.shape
    sector = result_ref.shape[-1]
    pairs, cosine, sine = waves_of(radix)
    segments = width // LANES
    shift = radix * LANES // 2 % LANES
    lane = lax.broadcasted_iota(jnp.int32, (levels, LANES), 1)

    def transform(begin, size, table):
        wave_ref[:, begin : begin + size] = product_of(high_ref, low_ref, begin, size, table)

    transform(0, LANES, stacked_table(first_high_ref, first_low_ref, 0, LANES))
    for k in range(pairs):
        transform(LANES * (2 * k + 1), 2 * LANES, stacked_table(table_high_ref, table_low_ref, 2 * LANES * k, 2 * LANES))

    for r in range(rows):
        place = slice(levels * r, levels * (r + 1))
        other_ref = row_of(other_refs, r)
        waves = [wave_ref[place, LANES * n : LANES * (n + 1)] for n in range(radix)]
        results = [None] * radix
        results[0] = sum((waves[2 * k - 1] for k in range(1, pairs + 1)), waves[0])
        for n in range(1, pairs + 1):
            even = sum((cosine(k, n) * waves[2 * k - 1] for k in range(1, pairs + 1)), waves[0])
            odd = sine(1, n) * waves[2]
            for k in range(2, pairs + 1):
                odd = odd + sine(k, n) * waves[2 * k]
            results[n], results[radix - n] = even - odd, even + odd
        filtered_row = mask_ref[r] == 1
        turned = [pltpu.roll(result, LANES - shift, 1) for result in results[segments - 1 :]]
        for n in range(segments):
            begin = LANES * n
            size = min(LANES, sector - begin)
            value = jnp.where(filtered_row, results[n], own_ref[r, :, begin : begin + LANES])
            result_ref[:, r, begin : begin + size] = value[:, :size]
            value = jnp.where(lane < LANES - shift, turned[n], turned[min(n + 1, segments - 1)])
            back_ref[r, :, begin : begin + LANES] = jnp.where(filtered_row, value, other_ref[:, begin : begin + LANES])


def finish_kernel(*refs):
    out_hbm, turned_ref, sems = refs[-3:]
    count = turned_ref.shape[0]
    result_refs, received_refs = refs[:count], refs[count : 2 * count]
    rows, levels, width = received_refs[0].shape
    sector = out_hbm.shape[-1]
    piece = levels // PIECES
    copies = []

    def send(source_ref, tracer, slot):
        for part in range(PIECES):
            span = pl.ds(piece * part, piece)
            copies.append(pltpu.make_async_copy(source_ref.at[span], out_hbm.at[tracer, span], sems.at[slot, part]))
            copies[-1].start()

    for i, result_ref in enumerate(result_refs):
        send(result_ref, first_of("keep", 2 * count) + i, i)
    for i in range(count):
        for r in range(rows):
            turned_ref[i, :, r, :] = received_refs[i][r, :, :sector]
        send(turned_ref.at[i], first_of("give", 2 * count) + i, count + i)
    for copy in copies:
        copy.wait()


def on_device(tracers, courant_lat, courant_lon, surface_flux, mixing, decay_rate, owners, polar_mask):
    tracer_count, levels, rows, sector = tracers.shape
    assert rows == 4 and sector % 64 == 0 and lax.axis_size("lon") == 2
    f32 = jnp.float32
    lat_count, lat = lax.axis_size("lat"), lax.axis_index("lat")
    length = 2 * sector
    width = -(-sector // LANES) * LANES
    radix = length // LANES
    downward = [(i + 1, i) for i in range(lat_count - 1)]
    swap = [(0, 1), (1, 0)]

    whole = pl.BlockSpec(memory_space=pltpu.VMEM)
    in_hbm = pl.BlockSpec(memory_space=pltpu.HBM)
    scalars = pl.BlockSpec(memory_space=pltpu.SMEM)
    inside = [pair for i in range(0, lat_count - 1, 2) for pair in ((i, i + 1), (i + 1, i))]
    across = [pair for i in range(1, lat_count - 1, 2) for pair in ((i, i + 1), (i + 1, i))]
    fields = [pltpu.with_memory_space_constraint(array, pltpu.HBM) for array in (tracers, courant_lat, courant_lon)]
    field_buffers = [pltpu.VMEM(array.shape, f32) for array in (tracers, courant_lat, courant_lon)]
    half = tracer_count // 2
    inner = pl.pallas_call(
        pack_kernel,
        in_specs=[in_hbm],
        out_specs=whole,
        out_shape=pltpu.VMEM((levels * tracer_count, length), f32),
        scratch_shapes=[pltpu.VMEM((tracer_count, levels, 2, sector), f32), pltpu.SemaphoreType.DMA((tracer_count,))],
        compiler_params=params(),
        cost_estimate=cost(0, 600_000),
        name="pack",
    )(fields[0])
    from_inside = lax.ppermute(inner, "lat", inside)
    fields, inner = lax.optimization_barrier((fields, inner))
    fields = [pltpu.with_memory_space_constraint(array, pltpu.HBM) for array in fields]
    *outer, courant_row, sides = pl.pallas_call(
        rest_kernel,
        in_specs=[in_hbm] * 3,
        out_specs=[whole] * (half + 2),
        out_shape=[pltpu.VMEM((levels * 2, length), f32)] * half
        + [
            jax.ShapeDtypeStruct((levels // 2, length), f32),
            jax.ShapeDtypeStruct((tracer_count + 1, rows, levels, LANES), f32),
        ],
        scratch_shapes=field_buffers + [pltpu.SemaphoreType.DMA((tracer_count + 2,))],
        compiler_params=params(),
        cost_estimate=cost(0, 0),
        name="rest",
    )(*fields)
    from_across = [lax.ppermute(part, "lat", across) for part in outer[:-1]]
    top = lax.ppermute(courant_row, "lat", downward)

    sides = lax.ppermute(sides, "lon", swap)
    base, north, lat_courant = pl.pallas_call(
        functools.partial(base_kernel, width),
        in_specs=[in_hbm, in_hbm, in_hbm, whole],
        out_specs=[whole] * 3,
        out_shape=[
            jax.ShapeDtypeStruct((tracer_count, rows, levels, width), f32),
            jax.ShapeDtypeStruct((tracer_count, levels, width), f32),
            jax.ShapeDtypeStruct((rows, levels, width), f32),
        ],
        scratch_shapes=field_buffers + [pltpu.SemaphoreType.DMA((tracer_count + 2,))],
        compiler_params=params(),
        cost_estimate=cost(0, 0),
        name="base",
    )(*fields, sides)

    surface = jnp.pad(surface_flux, ((0, 0), (0, 0), (0, width - sector)))
    decay = decay_rate[:, :, None]
    block_count = rows * sector // BLOCK
    block_of = (np.arange(rows)[:, None] * sector + np.minimum(np.arange(width), sector - 1)[None]) // BLOCK
    owner_of = jnp.repeat(owners.reshape(block_count), BLOCK).reshape(rows, sector)
    owner_of = jnp.pad(owner_of, ((0, 0), (0, width - sector)))
    forward, inverse, numbers, weights = spectral_tables(length)
    row_ids = (lat * rows + jnp.arange(rows)).astype(f32)
    latitude = (-0.5 + (row_ids + 0.5) / (lat_count * rows)) * math.pi
    inverse_sine = np.where(numbers == 0, 1.0, 1.0 / np.where(numbers == 0, 1.0, np.sin(np.pi * numbers / length)))
    ratio = 2.0 * jnp.cos(latitude)[:, None] * jnp.asarray(inverse_sine, f32)[None]
    damping = jnp.where(jnp.asarray(numbers == 0)[None], 1.0, jnp.minimum(1.0, ratio * ratio))
    scale = damping * jnp.asarray(weights, f32)[None]

    base, scale, owner_of, surface, decay = lax.optimization_barrier((base, scale, owner_of, surface, decay))

    base, outer = lax.optimization_barrier((base, outer))
    from_across.append(lax.ppermute(outer[-1], "lat", across))

    circles = jax.ShapeDtypeStruct((half, rows, levels, width), f32)
    result_shape = jax.ShapeDtypeStruct((levels, rows, sector), f32)
    out_shape = jax.ShapeDtypeStruct(tracers.shape, f32)

    def run_physics(chunk, energy, last=False):
        shapes = [jax.ShapeDtypeStruct(circles.shape[1:], f32)] * 2
        shapes.append(jax.ShapeDtypeStruct((1, LANES) if last else energy.shape, f32))
        *results, energy = pl.pallas_call(
            functools.partial(physics_kernel, levels, sector, lat_count if last else 0, chunk, ("give", "keep")),
            in_specs=[whole] * 11,
            out_specs=[whole] * len(shapes),
            out_shape=shapes,
            compiler_params=params(),
            cost_estimate=cost(0, 0),
            name="physics",
        )(base, north, from_inside, from_across[chunk], top, lat_courant, surface, mixing, decay, owner_of, energy)
        return results, energy

    forward, inverse = ([jnp.asarray(part) for table in tables for part in split_table(table)] for tables in (forward, inverse))
    circle = jax.ShapeDtypeStruct(circles.shape[1:], f32)
    spectra = jax.ShapeDtypeStruct((rows * levels, length), jnp.bfloat16)

    def run_forward(own, other):
        return pl.pallas_call(
            functools.partial(forward_kernel, radix, len(other)),
            in_specs=[whole] * (6 + len(other)),
            out_specs=[whole] * 2,
            out_shape=[spectra] * 2,
            scratch_shapes=[pltpu.VMEM(spectra.shape, jnp.bfloat16)] * 2,
            compiler_params=params(),
            cost_estimate=cost(0, 0),
            name="forward",
        )(own, *other, *forward, scale)

    def run_inverse(own, other, high, low):
        return pl.pallas_call(
            functools.partial(inverse_kernel, radix, len(other)),
            in_specs=[scalars] + [whole] * (7 + len(other)),
            out_specs=[whole] * 2,
            out_shape=[result_shape, circle],
            scratch_shapes=[pltpu.VMEM(spectra.shape, f32)],
            compiler_params=params(),
            cost_estimate=cost(0, 0),
            name="inverse",
        )(polar_mask, own, *other, high, low, *inverse)

    energy = jnp.zeros((rows, 8, width), f32)
    results, received = [], []
    for chunk in range(half - 1):
        (given, own), energy = run_physics(chunk, energy)
        other = [lax.ppermute(given[r : r + 2], "lon", swap) for r in range(0, rows, 2)]
        spectrum = run_forward(own, other)
        result, back = run_inverse(own, other, *spectrum)
        results.append(result)
        received.append(lax.ppermute(back, "lon", swap))
        energy, back = lax.optimization_barrier((energy, back))

    distances = [1 << i for i in range(lat_count.bit_length() - 1)]

    def send_energy(energy):
        distance = distances.pop(0)
        return lax.ppermute(energy, "lat", [(i, i ^ distance) for i in range(lat_count)])

    (given, own), energy = run_physics(half - 1, energy, True)
    other = [lax.ppermute(given, "lon", swap)]

    coming = send_energy(energy)
    high, low = run_forward(own, other)
    coming, high = lax.optimization_barrier((coming, high))
    energy = energy + coming
    energy, high = lax.optimization_barrier((energy, high))

    coming = send_energy(energy)
    result, back = run_inverse(own, other, high, low)
    coming, back = lax.optimization_barrier((coming, back))
    energy = energy + coming
    energy, back = lax.optimization_barrier((energy, back))
    results.append(result)
    received.append(lax.ppermute(back, "lon", swap))

    coming = send_energy(energy)
    out = pl.pallas_call(
        finish_kernel,
        in_specs=[whole] * (2 * half),
        out_specs=in_hbm,
        out_shape=out_shape,
        scratch_shapes=[
            pltpu.VMEM((half,) + result_shape.shape, f32),
            pltpu.SemaphoreType.DMA((2 * half, PIECES)),
        ],
        compiler_params=params(),
        cost_estimate=cost(0, 3_000_000),
        name="finish",
    )(*results, *received)
    coming, out = lax.optimization_barrier((coming, out))
    energy = energy + coming
    while distances:
        energy = energy + send_energy(energy)

    owner_energy = lax.dynamic_slice(energy, (0, lat), (1, 1)) / (block_count * BLOCK)
    return out, owner_energy


def solution(mesh):
    placed = (
        P("group", None, "lat", "lon"),
        P("group", "lat", "lon"),
        P("group", "lat", "lon"),
        P("group", "lat", "lon"),
        P(),
        P(),
        P(("group", "lat"), "lon", None, None),
        P(("group", "lat")),
    )
    return jax.shard_map(
        on_device,
        mesh=mesh,
        in_specs=placed,
        out_specs=(P("group", None, "lat", "lon"), P(("group", "lat"), "lon")),
        check_vma=False,
    )
```

```python
import functools
import math

import jax
import jax.numpy as jnp
import numpy as np
from jax import lax
from jax.experimental import pallas as pl
from jax.experimental.pallas import tpu as pltpu
from jax.sharding import PartitionSpec as P

LANES = 128
BLOCK = 128
VMEM_BYTES = 6 * 1024 * 1024
PIECES = 4
NEAR = 7.0 / 12.0
FAR = 1.0 / 12.0


def params():
    return pltpu.CompilerParams(vmem_limit_bytes=VMEM_BYTES)


def cost(flops, bytes_accessed):
    return pl.CostEstimate(flops=flops, bytes_accessed=bytes_accessed, transcendentals=0)


def split_high_low(value):
    high = value.astype(jnp.bfloat16)
    low = (value - high.astype(jnp.float32)).astype(jnp.bfloat16)
    return high, low


def split_table(table):
    high = table.astype(jnp.bfloat16.dtype)
    return high, (table - high.astype(np.float64)).astype(jnp.bfloat16.dtype)


def spectral_tables(length):
    radix = length // LANES
    pairs = (radix - 1) // 2
    spot = np.arange(LANES)[:, None]
    number = np.arange(LANES)[None, :]
    is_cosine = number <= LANES // 2
    wave = np.where(is_cosine, number, number - LANES // 2)
    angle = 2.0 * np.pi * ((spot * wave) % LANES) / LANES
    first = np.where(is_cosine, np.cos(angle), np.sin(angle))
    others, numbers = [], [radix * wave[0]]
    weights = [np.where((wave[0] == 0) | (wave[0] == LANES // 2), 1.0, 2.0) / length]
    for residue in range(1, pairs + 1):
        whole = residue + radix * number
        angle = 2.0 * np.pi * ((spot * whole) % length) / length
        cosine, sine = np.cos(angle), np.sin(angle)
        others.append(np.block([[cosine, -sine], [sine, cosine]]))
        folded = np.minimum(whole[0], length - whole[0])
        numbers += [folded, folded]
        weights.append(np.full(2 * LANES, 2.0 / length))
    forward = np.concatenate(others), first
    inverse = np.concatenate([table.T for table in others]), first.T
    return forward, inverse, np.concatenate(numbers), np.concatenate(weights)


def pack_rows(first, second):
    return jnp.concatenate([first, second], axis=1)


def second_half(packed, sector):
    skip, shift = sector // LANES, sector % LANES
    segments = [packed[:, LANES * i : LANES * (i + 1)] for i in range(packed.shape[1] // LANES)]
    if shift == 0:
        return jnp.concatenate(segments[skip:], axis=1)
    turned = [pltpu.roll(segment, LANES - shift, 1) for segment in segments[skip:]]
    lane = lax.broadcasted_iota(jnp.int32, turned[0].shape, 1)
    parts = [jnp.where(lane < LANES - shift, turned[i], turned[min(i + 1, len(turned) - 1)]) for i in range(len(turned))]
    return jnp.concatenate(parts, axis=1)


def start_copies(pairs, sems):
    copies = [pltpu.make_async_copy(source, target, sems.at[i]) for i, (source, target) in enumerate(pairs)]
    for copy in copies:
        copy.start()
    return copies


def pack_kernel(even_ref, tracer_hbm, out_ref, row_ref, sems):
    count, levels = row_ref.shape[:2]
    first_row = pl.multiple_of(jnp.where(even_ref[0] == 1, tracer_hbm.shape[2] - 2, 0), 2)
    sources = [tracer_hbm.at[t, :, pl.ds(first_row, 2), :] for t in range(count)]
    copies = start_copies([(sources[t], row_ref.at[t]) for t in range(count)], sems)
    for t in range(count):
        copies[t].wait()
        out_ref[levels * t : levels * (t + 1), :] = pack_rows(row_ref[t, :, 0, :], row_ref[t, :, 1, :])


def rest_kernel(even_ref, tracer_hbm, lat_hbm, lon_hbm, *refs):
    courant_ref, side_ref, tracer_ref, lat_ref, lon_ref, sems = refs[-6:]
    outer_refs = refs[:-6]
    count, levels, rows, sector = tracer_ref.shape
    pairs = [(tracer_hbm.at[t], tracer_ref.at[t]) for t in range(count)] + [(lat_hbm, lat_ref), (lon_hbm, lon_ref)]
    copies = start_copies(pairs, sems)
    shift, whole = sector % LANES, sector // LANES * LANES
    lane = lax.broadcasted_iota(jnp.int32, (levels, LANES), 1)
    even = even_ref[0] == 1

    def store_side(i, r, values):
        first = pltpu.roll(values[:, :LANES], shift, 1)
        last = jnp.concatenate([values[:, whole:], values[:, whole:]], axis=1)
        side_ref[i, r] = jnp.where(lane < LANES - 2, first, last)

    for copy in copies:
        copy.wait()
    for t in range(count):
        row = [tracer_ref[t, :, r, :] for r in range(rows)]
        slot = t // len(outer_refs)
        outer_refs[t % len(outer_refs)][levels * slot : levels * (slot + 1), :] = pack_rows(
            jnp.where(even, row[0], row[rows - 2]), jnp.where(even, row[1], row[rows - 1])
        )
        for r in range(rows):
            store_side(t, r, row[r])
    courant = lat_ref[:, 0, :]
    courant_ref[...] = pack_rows(courant[: levels // 2], courant[levels // 2 :])
    for r in range(rows):
        store_side(count, r, lon_ref[:, r, :])


def base_kernel(width, not_pole_ref, tracer_hbm, lat_hbm, lon_hbm, side_hbm, base_ref, north_ref, courant_ref, *scratch):
    tracer_ref, lat_ref, lon_ref, side_ref, sems = scratch
    tracer_count, levels, rows, sector = tracer_ref.shape
    whole = sector // LANES * LANES
    pairs = [(lat_hbm, lat_ref), (lon_hbm, lon_ref)] + [(tracer_hbm.at[t], tracer_ref.at[t]) for t in range(tracer_count)]
    copies = start_copies(pairs + [(side_hbm, side_ref)], sems)

    def beside(values, side):
        return jnp.concatenate([values[:, :whole], values[:, whole:], side[:, sector - whole :]], axis=1)

    copies[0].wait()
    copies[1].wait()
    copies[tracer_count + 2].wait()
    nothing = jnp.zeros((levels, LANES), jnp.float32)
    for r in range(rows):
        courant = lat_ref[:, r, :] if r else lat_ref[:, r, :] * not_pole_ref[0]
        courant_ref[r] = beside(courant, nothing)
    for t in range(tracer_count):
        copies[t + 2].wait()
        q = [beside(tracer_ref[t, :, r, :], side_ref[t, r]) for r in range(rows)]
        north_ref[t] = NEAR * q[3] - FAR * q[2]
        own_flux = [
            courant_ref[0] * (NEAR * q[0] - FAR * q[1]),
            courant_ref[1] * (NEAR * (q[1] + q[0]) - FAR * q[2]),
            courant_ref[2] * (NEAR * (q[2] + q[1]) - FAR * (q[3] + q[0])),
            courant_ref[3] * (NEAR * (q[3] + q[2]) - FAR * q[1]),
        ]
        for r in range(rows):
            west, west2, east = pltpu.roll(q[r], 1, 1), pltpu.roll(q[r], 2, 1), pltpu.roll(q[r], width - 1, 1)
            flux = beside(lon_ref[:, r, :], side_ref[tracer_count, r]) * (NEAR * (q[r] + west) - FAR * (east + west2))
            value = q[r] - (pltpu.roll(flux, width - 1, 1) - flux) + own_flux[r]
            if r + 1 < rows:
                value = value - own_flux[r + 1]
            base_ref[t, r] = value


def physics_kernel(levels, sector, owner_count, chunk, even_ref, *refs):
    count = len(refs) - 12 >> 1
    first_refs, refs = refs[:count], refs[count:]
    base_ref, north_ref, inner_ref, outer_ref = refs[:4]
    top_ref, courant_ref, surface_ref, mixing_ref, decay_ref, owner_ref, energy_in_ref = refs[4:11]
    physics_refs, energy_ref = refs[11:-1], refs[-1]
    rows, width = base_ref.shape[1], base_ref.shape[-1]
    courant = [courant_ref[r] for r in range(rows)]
    even = even_ref[0] == 1
    top = top_ref[...]
    top = jnp.concatenate([top[:, :width], second_half(top, sector)], axis=0)
    mix_high, mix_low = split_high_low(mixing_ref[...])
    mix = jnp.concatenate([mix_high, mix_high, mix_low, mix_low], axis=1)
    level = lax.broadcasted_iota(jnp.int32, (8, width), 0)
    lane = lax.broadcasted_iota(jnp.int32, (8, width), 1)
    energies = [energy_in_ref[r] for r in range(rows)]
    for first_ref, physics_ref in zip(first_refs, physics_refs):
        t = first_ref[0] + chunk
        inner = inner_ref[pl.ds(pl.multiple_of(levels * t, levels), levels), :]
        outer = jnp.where(first_ref[0] == 0, outer_ref[:levels, :], outer_ref[levels:, :])
        low, high = jnp.where(even, outer, inner), jnp.where(even, inner, outer)
        low_a, low_b = low[:, :width], second_half(low, sector)
        high_a, high_b = high[:, :width], second_half(high, sector)
        south = courant[0] * (NEAR * low_b - FAR * low_a)
        south_in = courant[1] * (FAR * low_b)
        north_in = courant[3] * (FAR * high_a)
        north = top * (NEAR * high_a - FAR * high_b + north_ref[t])
        extra = [south + south_in, -south_in, north_in, -north_in - north]
        for r in range(rows):
            advected = base_ref[t, r] + extra[r]
            part_high, part_low = split_high_low(advected)
            stacked = jnp.concatenate([part_high, part_low, part_high, part_low], axis=0)
            mixed = jnp.dot(mix, stacked, preferred_element_type=jnp.float32)
            surface = jnp.where(level == 7, surface_ref[t, r : r + 1, :], 0.0)
            mixed = jnp.concatenate([mixed[: levels - 8], mixed[levels - 8 :] + surface], axis=0)
            physics = mixed / (1.0 + decay_ref[t] * mixed * mixed)
            physics_ref[r] = physics
            gap = physics - advected
            squared = gap * gap
            for k in range(levels // 8):
                energies[r] = energies[r] + squared[8 * k : 8 * k + 8]
    if not owner_count:
        for r in range(rows):
            energy_ref[r] = energies[r]
        return
    energies = [jnp.where(lane < sector, energy, 0.0) for energy in energies]
    spot = lax.broadcasted_iota(jnp.int32, (1, LANES), 1)
    result = jnp.zeros((1, LANES), jnp.float32)
    for owner in range(owner_count):
        chosen = jnp.zeros((8, LANES), jnp.float32)
        for r in range(rows):
            picked = jnp.where(owner_ref[r : r + 1, :] == owner, energies[r], 0.0)
            for k in range(width // LANES):
                chosen = chosen + picked[:, LANES * k : LANES * (k + 1)]
        total = jnp.sum(jnp.sum(chosen, axis=0, keepdims=True), axis=1, keepdims=True)
        result = jnp.where(spot == owner, total, result)
    energy_ref[...] = result


def waves_of(radix):
    pairs = (radix - 1) // 2
    cosine = lambda k, i: math.cos(2.0 * math.pi * ((k * i) % radix) / radix)
    sine = lambda k, i: math.sin(2.0 * math.pi * ((k * i) % radix) / radix)
    return pairs, cosine, sine


def row_of(piece_refs, r):
    share = piece_refs[0].shape[0]
    return piece_refs[r // share].at[r % share]


def stacked_table(high_ref, low_ref, begin, size):
    high = high_ref[begin : begin + size, :]
    return jnp.concatenate([high, high, low_ref[begin : begin + size, :]], axis=0)


def product_of(high_ref, low_ref, begin, size, table):
    high = high_ref[:, begin : begin + size]
    stacked = jnp.concatenate([high, low_ref[:, begin : begin + size], high], axis=1)
    return jnp.dot(stacked, table, preferred_element_type=jnp.float32)


def forward_kernel(radix, pieces, own_ref, *refs):
    other_refs, refs = refs[:pieces], refs[pieces:]
    table_high_ref, table_low_ref, first_high_ref, first_low_ref, scale_ref, *refs = refs
    out_high_ref, out_low_ref, high_ref, low_ref = refs
    rows, levels, width = own_ref.shape
    pairs, cosine, sine = waves_of(radix)
    segments = width // LANES
    shift = radix * LANES // 2 % LANES
    lane = lax.broadcasted_iota(jnp.int32, (levels, LANES), 1)

    def store(place, column, wave):
        high_ref[place, column : column + LANES], low_ref[place, column : column + LANES] = split_high_low(wave)

    for r in range(rows):
        place = slice(levels * r, levels * (r + 1))
        other_ref = row_of(other_refs, r)
        own = [own_ref[r, :, LANES * n : LANES * (n + 1)] for n in range(segments)]
        turned = [pltpu.roll(other_ref[:, LANES * n : LANES * (n + 1)], shift, 1) for n in range(segments)]
        joined = own[:-1] + [jnp.where(lane < shift, own[-1], turned[0])]
        joined += [jnp.where(lane < shift, turned[n], turned[n + 1]) for n in range(segments - 1)]
        plus = [joined[n] + joined[radix - n] for n in range(1, pairs + 1)]
        minus = [joined[radix - n] - joined[n] for n in range(1, pairs + 1)]
        store(place, 0, sum(plus, joined[0]))
        for k in range(1, pairs + 1):
            real = sum((cosine(k, n) * plus[n - 1] for n in range(1, pairs + 1)), joined[0])
            imaginary = sine(k, 1) * minus[0]
            for n in range(2, pairs + 1):
                imaginary = imaginary + sine(k, n) * minus[n - 1]
            store(place, LANES * (2 * k - 1), real)
            store(place, LANES * 2 * k, imaginary)

    def transform(begin, size, table):
        spectrum = product_of(high_ref, low_ref, begin, size, table)
        for r in range(rows):
            place = slice(levels * r, levels * (r + 1))
            damped = spectrum[place] * scale_ref[r : r + 1, begin : begin + size]
            out_high_ref[place, begin : begin + size], out_low_ref[place, begin : begin + size] = split_high_low(damped)

    transform(0, LANES, stacked_table(first_high_ref, first_low_ref, 0, LANES))
    for k in range(pairs):
        transform(LANES * (2 * k + 1), 2 * LANES, stacked_table(table_high_ref, table_low_ref, 2 * LANES * k, 2 * LANES))


def inverse_kernel(radix, pieces, mask_ref, own_ref, *refs):
    other_refs, refs = refs[:pieces], refs[pieces:]
    high_ref, low_ref, table_high_ref, table_low_ref, first_high_ref, first_low_ref, *refs = refs
    result_ref, back_ref, wave_ref = refs
    rows, levels, width = own_ref.shape
    sector = result_ref.shape[-1]
    pairs, cosine, sine = waves_of(radix)
    segments = width // LANES
    shift = radix * LANES // 2 % LANES
    lane = lax.broadcasted_iota(jnp.int32, (levels, LANES), 1)

    def transform(begin, size, table):
        wave_ref[:, begin : begin + size] = product_of(high_ref, low_ref, begin, size, table)

    transform(0, LANES, stacked_table(first_high_ref, first_low_ref, 0, LANES))
    for k in range(pairs):
        transform(LANES * (2 * k + 1), 2 * LANES, stacked_table(table_high_ref, table_low_ref, 2 * LANES * k, 2 * LANES))

    for r in range(rows):
        place = slice(levels * r, levels * (r + 1))
        other_ref = row_of(other_refs, r)
        waves = [wave_ref[place, LANES * n : LANES * (n + 1)] for n in range(radix)]
        results = [None] * radix
        results[0] = sum((waves[2 * k - 1] for k in range(1, pairs + 1)), waves[0])
        for n in range(1, pairs + 1):
            even = sum((cosine(k, n) * waves[2 * k - 1] for k in range(1, pairs + 1)), waves[0])
            odd = sine(1, n) * waves[2]
            for k in range(2, pairs + 1):
                odd = odd + sine(k, n) * waves[2 * k]
            results[n], results[radix - n] = even - odd, even + odd
        filtered_row = mask_ref[r] == 1
        turned = [pltpu.roll(result, LANES - shift, 1) for result in results[segments - 1 :]]
        for n in range(segments):
            begin = LANES * n
            size = min(LANES, sector - begin)
            value = jnp.where(filtered_row, results[n], own_ref[r, :, begin : begin + LANES])
            result_ref[:, r, begin : begin + size] = value[:, :size]
            value = jnp.where(lane < LANES - shift, turned[n], turned[min(n + 1, segments - 1)])
            back_ref[r, :, begin : begin + LANES] = jnp.where(filtered_row, value, other_ref[:, begin : begin + LANES])


def finish_kernel(keep_ref, give_ref, *refs):
    out_hbm, turned_ref, sems = refs[-3:]
    count = turned_ref.shape[0]
    result_refs, received_refs = refs[:count], refs[count : 2 * count]
    rows, levels, width = received_refs[0].shape
    sector = out_hbm.shape[-1]
    piece = levels // PIECES
    copies = []

    def send(source_ref, tracer, slot):
        for part in range(PIECES):
            span = pl.ds(piece * part, piece)
            copies.append(pltpu.make_async_copy(source_ref.at[span], out_hbm.at[tracer, span], sems.at[slot, part]))
            copies[-1].start()

    for i, result_ref in enumerate(result_refs):
        send(result_ref, keep_ref[0] + i, i)
    for i in range(count):
        for r in range(rows):
            turned_ref[i, :, r, :] = received_refs[i][r, :, :sector]
        send(turned_ref.at[i], give_ref[0] + i, count + i)
    for copy in copies:
        copy.wait()


def on_device(tracers, courant_lat, courant_lon, surface_flux, mixing, decay_rate, owners, polar_mask):
    tracer_count, levels, rows, sector = tracers.shape
    assert rows == 4 and sector % 64 == 0 and lax.axis_size("lon") == 2
    f32 = jnp.float32
    lat_count, lat = lax.axis_size("lat"), lax.axis_index("lat")
    length = 2 * sector
    width = -(-sector // LANES) * LANES
    radix = length // LANES
    downward = [(i + 1, i) for i in range(lat_count - 1)]
    swap = [(0, 1), (1, 0)]

    whole = pl.BlockSpec(memory_space=pltpu.VMEM)
    in_hbm = pl.BlockSpec(memory_space=pltpu.HBM)
    scalars = pl.BlockSpec(memory_space=pltpu.SMEM)
    even = (1 - lat % 2).reshape(1)
    inside = [pair for i in range(0, lat_count - 1, 2) for pair in ((i, i + 1), (i + 1, i))]
    across = [pair for i in range(1, lat_count - 1, 2) for pair in ((i, i + 1), (i + 1, i))]
    fields = [pltpu.with_memory_space_constraint(array, pltpu.HBM) for array in (tracers, courant_lat, courant_lon)]
    field_buffers = [pltpu.VMEM(array.shape, f32) for array in (tracers, courant_lat, courant_lon)]
    half = tracer_count // 2
    inner = pl.pallas_call(
        pack_kernel,
        in_specs=[scalars, in_hbm],
        out_specs=whole,
        out_shape=pltpu.VMEM((levels * tracer_count, length), f32),
        scratch_shapes=[pltpu.VMEM((tracer_count, levels, 2, sector), f32), pltpu.SemaphoreType.DMA((tracer_count,))],
        compiler_params=params(),
        cost_estimate=cost(0, 600_000),
        name="pack",
    )(even, fields[0])
    from_inside = lax.ppermute(inner, "lat", inside)
    even_rest, inner = lax.optimization_barrier((even, inner))
    *outer, courant_row, sides = pl.pallas_call(
        rest_kernel,
        in_specs=[scalars] + [in_hbm] * 3,
        out_specs=[whole] * (half + 2),
        out_shape=[pltpu.VMEM((levels * 2, length), f32)] * half
        + [
            jax.ShapeDtypeStruct((levels // 2, length), f32),
            jax.ShapeDtypeStruct((tracer_count + 1, rows, levels, LANES), f32),
        ],
        scratch_shapes=field_buffers + [pltpu.SemaphoreType.DMA((tracer_count + 2,))],
        compiler_params=params(),
        cost_estimate=cost(0, 0),
        name="rest",
    )(even_rest, *fields)
    from_across = [lax.ppermute(part, "lat", across) for part in outer[:-1]]
    top = lax.ppermute(courant_row, "lat", downward)

    sides = lax.ppermute(sides, "lon", swap)
    not_pole = (lat > 0).astype(f32).reshape(1)
    base, north, lat_courant = pl.pallas_call(
        functools.partial(base_kernel, width),
        in_specs=[scalars] + [in_hbm] * 4,
        out_specs=[whole] * 3,
        out_shape=[
            jax.ShapeDtypeStruct((tracer_count, rows, levels, width), f32),
            jax.ShapeDtypeStruct((tracer_count, levels, width), f32),
            jax.ShapeDtypeStruct((rows, levels, width), f32),
        ],
        scratch_shapes=field_buffers + [pltpu.VMEM(sides.shape, f32), pltpu.SemaphoreType.DMA((tracer_count + 3,))],
        compiler_params=params(),
        cost_estimate=cost(0, 0),
        name="base",
    )(not_pole, *fields, pltpu.with_memory_space_constraint(sides, pltpu.HBM))

    surface = jnp.pad(surface_flux, ((0, 0), (0, 0), (0, width - sector)))
    decay = decay_rate[:, :, None]
    block_count = rows * sector // BLOCK
    block_of = (np.arange(rows)[:, None] * sector + np.minimum(np.arange(width), sector - 1)[None]) // BLOCK
    owner_of = jnp.repeat(owners.reshape(block_count), BLOCK).reshape(rows, sector)
    owner_of = jnp.pad(owner_of, ((0, 0), (0, width - sector)))
    forward, inverse, numbers, weights = spectral_tables(length)
    row_ids = (lat * rows + jnp.arange(rows)).astype(f32)
    latitude = (-0.5 + (row_ids + 0.5) / (lat_count * rows)) * math.pi
    inverse_sine = np.where(numbers == 0, 1.0, 1.0 / np.where(numbers == 0, 1.0, np.sin(np.pi * numbers / length)))
    ratio = 2.0 * jnp.cos(latitude)[:, None] * jnp.asarray(inverse_sine, f32)[None]
    damping = jnp.where(jnp.asarray(numbers == 0)[None], 1.0, jnp.minimum(1.0, ratio * ratio))
    scale = damping * jnp.asarray(weights, f32)[None]

    base, scale, owner_of, surface, decay = lax.optimization_barrier((base, scale, owner_of, surface, decay))

    base, outer = lax.optimization_barrier((base, outer))
    from_across.append(lax.ppermute(outer[-1], "lat", across))

    keep = (half * lax.axis_index("lon")).reshape(1)
    give = half - keep
    circles = jax.ShapeDtypeStruct((half, rows, levels, width), f32)
    result_shape = jax.ShapeDtypeStruct((levels, rows, sector), f32)
    out_shape = jax.ShapeDtypeStruct(tracers.shape, f32)

    def run_physics(chunk, firsts, energy, last=False):
        shapes = [jax.ShapeDtypeStruct(circles.shape[1:], f32)] * len(firsts)
        shapes.append(jax.ShapeDtypeStruct((1, LANES) if last else energy.shape, f32))
        *results, energy = pl.pallas_call(
            functools.partial(physics_kernel, levels, sector, lat_count if last else 0, chunk),
            in_specs=[scalars] * (1 + len(firsts)) + [whole] * 11,
            out_specs=[whole] * len(shapes),
            out_shape=shapes,
            compiler_params=params(),
            cost_estimate=cost(0, 0),
            name="physics",
        )(even, *firsts, base, north, from_inside, from_across[chunk], top, lat_courant, surface, mixing, decay, owner_of, energy)
        return results, energy

    forward, inverse = ([jnp.asarray(part) for table in tables for part in split_table(table)] for tables in (forward, inverse))
    circle = jax.ShapeDtypeStruct(circles.shape[1:], f32)
    spectra = jax.ShapeDtypeStruct((rows * levels, length), jnp.bfloat16)

    def run_forward(own, other):
        return pl.pallas_call(
            functools.partial(forward_kernel, radix, len(other)),
            in_specs=[whole] * (6 + len(other)),
            out_specs=[whole] * 2,
            out_shape=[spectra] * 2,
            scratch_shapes=[pltpu.VMEM(spectra.shape, jnp.bfloat16)] * 2,
            compiler_params=params(),
            cost_estimate=cost(0, 0),
            name="forward",
        )(own, *other, *forward, scale)

    def run_inverse(own, other, high, low):
        return pl.pallas_call(
            functools.partial(inverse_kernel, radix, len(other)),
            in_specs=[scalars] + [whole] * (7 + len(other)),
            out_specs=[whole] * 2,
            out_shape=[result_shape, circle],
            scratch_shapes=[pltpu.VMEM(spectra.shape, f32)],
            compiler_params=params(),
            cost_estimate=cost(0, 0),
            name="inverse",
        )(polar_mask, own, *other, high, low, *inverse)

    energy = jnp.zeros((rows, 8, width), f32)
    results, received = [], []
    for chunk in range(half - 1):
        (given, own), energy = run_physics(chunk, [give, keep], energy)
        other = [lax.ppermute(given[r : r + 2], "lon", swap) for r in range(0, rows, 2)]
        spectrum = run_forward(own, other)
        result, back = run_inverse(own, other, *spectrum)
        results.append(result)
        received.append(lax.ppermute(back, "lon", swap))
        energy, back = lax.optimization_barrier((energy, back))

    distances = [1 << i for i in range(lat_count.bit_length() - 1)]

    def send_energy(energy):
        distance = distances.pop(0)
        return lax.ppermute(energy, "lat", [(i, i ^ distance) for i in range(lat_count)])

    (given, own), energy = run_physics(half - 1, [give, keep], energy, True)
    other = [lax.ppermute(given, "lon", swap)]

    coming = send_energy(energy)
    high, low = run_forward(own, other)
    coming, high = lax.optimization_barrier((coming, high))
    energy = energy + coming
    energy, high = lax.optimization_barrier((energy, high))

    coming = send_energy(energy)
    result, back = run_inverse(own, other, high, low)
    coming, back = lax.optimization_barrier((coming, back))
    energy = energy + coming
    energy, back = lax.optimization_barrier((energy, back))
    results.append(result)
    received.append(lax.ppermute(back, "lon", swap))

    coming = send_energy(energy)
    out = pl.pallas_call(
        finish_kernel,
        in_specs=[scalars] * 2 + [whole] * (2 * half),
        out_specs=in_hbm,
        out_shape=out_shape,
        scratch_shapes=[
            pltpu.VMEM((half,) + result_shape.shape, f32),
            pltpu.SemaphoreType.DMA((2 * half, PIECES)),
        ],
        compiler_params=params(),
        cost_estimate=cost(0, 3_000_000),
        name="finish",
    )(keep, give, *results, *received)
    coming, out = lax.optimization_barrier((coming, out))
    energy = energy + coming
    while distances:
        energy = energy + send_energy(energy)

    owner_energy = lax.dynamic_slice(energy, (0, lat), (1, 1)) / (block_count * BLOCK)
    return out, owner_energy


def solution(mesh):
    placed = (
        P("group", None, "lat", "lon"),
        P("group", "lat", "lon"),
        P("group", "lat", "lon"),
        P("group", "lat", "lon"),
        P(),
        P(),
        P(("group", "lat"), "lon", None, None),
        P(("group", "lat")),
    )
    return jax.shard_map(
        on_device,
        mesh=mesh,
        in_specs=placed,
        out_specs=(P("group", None, "lat", "lon"), P(("group", "lat"), "lon")),
        check_vma=False,
    )
```

```python
import functools
import math

import jax
import jax.numpy as jnp
import numpy as np
from jax import lax
from jax.experimental import pallas as pl
from jax.experimental.pallas import tpu as pltpu
from jax.sharding import PartitionSpec as P

LANES = 128
BLOCK = 128
VMEM_BYTES = 6 * 1024 * 1024
PIECES = 4
NEAR = 7.0 / 12.0
FAR = 1.0 / 12.0


def params():
    return pltpu.CompilerParams(vmem_limit_bytes=VMEM_BYTES)


def cost(flops, bytes_accessed):
    return pl.CostEstimate(flops=flops, bytes_accessed=bytes_accessed, transcendentals=0)


def split_high_low(value):
    high = value.astype(jnp.bfloat16)
    low = (value - high.astype(jnp.float32)).astype(jnp.bfloat16)
    return high, low


def split_table(table):
    high = table.astype(jnp.bfloat16.dtype)
    return high, (table - high.astype(np.float64)).astype(jnp.bfloat16.dtype)


def spectral_tables(length):
    radix = length // LANES
    pairs = (radix - 1) // 2
    spot = np.arange(LANES)[:, None]
    number = np.arange(LANES)[None, :]
    is_cosine = number <= LANES // 2
    wave = np.where(is_cosine, number, number - LANES // 2)
    angle = 2.0 * np.pi * ((spot * wave) % LANES) / LANES
    first = np.where(is_cosine, np.cos(angle), np.sin(angle))
    others, numbers = [], [radix * wave[0]]
    weights = [np.where((wave[0] == 0) | (wave[0] == LANES // 2), 1.0, 2.0) / length]
    for residue in range(1, pairs + 1):
        whole = residue + radix * number
        angle = 2.0 * np.pi * ((spot * whole) % length) / length
        cosine, sine = np.cos(angle), np.sin(angle)
        others.append(np.block([[cosine, -sine], [sine, cosine]]))
        folded = np.minimum(whole[0], length - whole[0])
        numbers += [folded, folded]
        weights.append(np.full(2 * LANES, 2.0 / length))
    forward = np.concatenate(others), first
    inverse = np.concatenate([table.T for table in others]), first.T
    return forward, inverse, np.concatenate(numbers), np.concatenate(weights)


def is_even():
    return lax.axis_index("lat") % 2 == 0


def first_of(half, tracer_count):
    lon = lax.axis_index("lon")
    return (tracer_count // 2) * (lon if half == "keep" else 1 - lon)


def pack_rows(first, second):
    return jnp.concatenate([first, second], axis=1)


def second_half(packed, sector):
    skip, shift = sector // LANES, sector % LANES
    segments = [packed[:, LANES * i : LANES * (i + 1)] for i in range(packed.shape[1] // LANES)]
    if shift == 0:
        return jnp.concatenate(segments[skip:], axis=1)
    turned = [pltpu.roll(segment, LANES - shift, 1) for segment in segments[skip:]]
    lane = lax.broadcasted_iota(jnp.int32, turned[0].shape, 1)
    parts = [jnp.where(lane < LANES - shift, turned[i], turned[min(i + 1, len(turned) - 1)]) for i in range(len(turned))]
    return jnp.concatenate(parts, axis=1)


def start_copies(pairs, sems):
    copies = [pltpu.make_async_copy(source, target, sems.at[i]) for i, (source, target) in enumerate(pairs)]
    for copy in copies:
        copy.start()
    return copies


def pack_kernel(tracers, tracer_hbm, out_ref, row_ref, sems):
    levels = row_ref.shape[1]
    first_row = pl.multiple_of(jnp.where(is_even(), tracer_hbm.shape[2] - 2, 0), 2)
    sources = [tracer_hbm.at[t, :, pl.ds(first_row, 2), :] for t in tracers]
    copies = start_copies([(source, row_ref.at[i]) for i, source in enumerate(sources)], sems)
    for i, copy in enumerate(copies):
        copy.wait()
        out_ref[levels * i : levels * (i + 1), :] = pack_rows(row_ref[i, :, 0, :], row_ref[i, :, 1, :])


def rest_kernel(tracer_hbm, lat_hbm, lon_hbm, *refs):
    courant_ref, side_ref, tracer_ref, lat_ref, lon_ref, sems = refs[-6:]
    count, levels, rows, sector = tracer_ref.shape
    half = count // 2
    outer_refs, inner_refs = refs[:half], refs[half:-6]
    pairs = [(tracer_hbm.at[t], tracer_ref.at[t]) for t in range(count)] + [(lat_hbm, lat_ref), (lon_hbm, lon_ref)]
    for copy in start_copies(pairs, sems):
        copy.wait()
    shift, whole = sector % LANES, sector // LANES * LANES
    lane = lax.broadcasted_iota(jnp.int32, (levels, LANES), 1)
    even = is_even()

    def side_of(values):
        first = pltpu.roll(values[:, :LANES], shift, 1)
        last = jnp.concatenate([values[:, whole:], values[:, whole:]], axis=1)
        return jnp.where(lane < LANES - 2, first, last)

    def store_sides(i, values):
        for r in range(0, rows, 2):
            side_ref[i, r // 2] = jnp.where(lane < shift, pltpu.roll(side_of(values[r]), shift, 1), side_of(values[r + 1]))

    for t in range(count):
        row = [tracer_ref[t, :, r, :] for r in range(rows)]
        place = slice(levels * (t // half), levels * (t // half + 1))
        top, bottom = pack_rows(row[rows - 2], row[rows - 1]), pack_rows(row[0], row[1])
        outer_refs[t % half][place, :] = jnp.where(even, bottom, top)
        if t % half:
            inner_refs[t % half - 1][place, :] = jnp.where(even, top, bottom)
        store_sides(t, row)
    courant = lat_ref[:, 0, :]
    courant_ref[...] = pack_rows(courant[: levels // 2], courant[levels // 2 :])
    store_sides(count, [lon_ref[:, r, :] for r in range(rows)])


def base_kernel(width, tracer_hbm, lat_hbm, lon_hbm, side_ref, base_ref, north_ref, courant_ref, *scratch):
    tracer_ref, lat_ref, lon_ref, sems = scratch
    tracer_count, levels, rows, sector = tracer_ref.shape
    whole = sector // LANES * LANES
    pairs = [(lat_hbm, lat_ref), (lon_hbm, lon_ref)] + [(tracer_hbm.at[t], tracer_ref.at[t]) for t in range(tracer_count)]
    copies = start_copies(pairs, sems)

    def beside(values, side, part=0):
        begin = (sector - whole) * part
        return jnp.concatenate([values[:, :whole], values[:, whole:], side[:, begin : begin + width - sector]], axis=1)

    copies[0].wait()
    copies[1].wait()
    nothing = jnp.zeros((levels, LANES), jnp.float32)
    for r in range(rows):
        courant = lat_ref[:, r, :] if r else jnp.where(lax.axis_index("lat") > 0, lat_ref[:, r, :], 0.0)
        courant_ref[r] = beside(courant, nothing)
    for t in range(tracer_count):
        copies[t + 2].wait()
        q = [beside(tracer_ref[t, :, r, :], side_ref[t, r // 2], r % 2) for r in range(rows)]
        north_ref[t] = NEAR * q[3] - FAR * q[2]
        own_flux = [
            courant_ref[0] * (NEAR * q[0] - FAR * q[1]),
            courant_ref[1] * (NEAR * (q[1] + q[0]) - FAR * q[2]),
            courant_ref[2] * (NEAR * (q[2] + q[1]) - FAR * (q[3] + q[0])),
            courant_ref[3] * (NEAR * (q[3] + q[2]) - FAR * q[1]),
        ]
        for r in range(rows):
            west, west2, east = pltpu.roll(q[r], 1, 1), pltpu.roll(q[r], 2, 1), pltpu.roll(q[r], width - 1, 1)
            flux = beside(lon_ref[:, r, :], side_ref[tracer_count, r // 2], r % 2) * (NEAR * (q[r] + west) - FAR * (east + west2))
            value = q[r] - (pltpu.roll(flux, width - 1, 1) - flux) + own_flux[r]
            if r + 1 < rows:
                value = value - own_flux[r + 1]
            base_ref[t, r] = value


def physics_kernel(levels, sector, owner_count, chunk, halves, *refs):
    base_ref, north_ref, inner_ref, outer_ref = refs[:4]
    top_ref, courant_ref, surface_ref, mixing_ref, decay_ref, owner_ref, energy_in_ref = refs[4:11]
    physics_refs, energy_ref = refs[11:-1], refs[-1]
    rows, width = base_ref.shape[1], base_ref.shape[-1]
    courant = [courant_ref[r] for r in range(rows)]
    even = is_even()
    top = top_ref[...]
    top = jnp.concatenate([top[:, :width], second_half(top, sector)], axis=0)
    mix_high, mix_low = split_high_low(mixing_ref[...])
    mix = jnp.concatenate([mix_high, mix_high, mix_low, mix_low], axis=1)
    level = lax.broadcasted_iota(jnp.int32, (8, width), 0)
    lane = lax.broadcasted_iota(jnp.int32, (8, width), 1)
    energies = [energy_in_ref[r] for r in range(rows)]
    for half, physics_ref in zip(halves, physics_refs):
        first = first_of(half, base_ref.shape[0])
        t = first + chunk
        inner = jnp.where(first == 0, inner_ref[:levels, :], inner_ref[levels:, :])
        outer = jnp.where(first == 0, outer_ref[:levels, :], outer_ref[levels:, :])
        low, high = jnp.where(even, outer, inner), jnp.where(even, inner, outer)
        low_a, low_b = low[:, :width], second_half(low, sector)
        high_a, high_b = high[:, :width], second_half(high, sector)
        south = courant[0] * (NEAR * low_b - FAR * low_a)
        south_in = courant[1] * (FAR * low_b)
        north_in = courant[3] * (FAR * high_a)
        north = top * (NEAR * high_a - FAR * high_b + north_ref[t])
        extra = [south + south_in, -south_in, north_in, -north_in - north]
        for r in range(rows):
            advected = base_ref[t, r] + extra[r]
            part_high, part_low = split_high_low(advected)
            stacked = jnp.concatenate([part_high, part_low, part_high, part_low], axis=0)
            mixed = jnp.dot(mix, stacked, preferred_element_type=jnp.float32)
            surface = jnp.where(level == 7, surface_ref[t, r : r + 1, :], 0.0)
            mixed = jnp.concatenate([mixed[: levels - 8], mixed[levels - 8 :] + surface], axis=0)
            physics = mixed / (1.0 + decay_ref[t] * mixed * mixed)
            physics_ref[r] = physics
            gap = physics - advected
            squared = gap * gap
            for k in range(levels // 8):
                energies[r] = energies[r] + squared[8 * k : 8 * k + 8]
    if not owner_count:
        for r in range(rows):
            energy_ref[r] = energies[r]
        return
    energies = [jnp.where(lane < sector, energy, 0.0) for energy in energies]
    spot = lax.broadcasted_iota(jnp.int32, (1, LANES), 1)
    result = jnp.zeros((1, LANES), jnp.float32)
    for owner in range(owner_count):
        chosen = jnp.zeros((8, LANES), jnp.float32)
        for r in range(rows):
            picked = jnp.where(owner_ref[r : r + 1, :] == owner, energies[r], 0.0)
            for k in range(width // LANES):
                chosen = chosen + picked[:, LANES * k : LANES * (k + 1)]
        total = jnp.sum(jnp.sum(chosen, axis=0, keepdims=True), axis=1, keepdims=True)
        result = jnp.where(spot == owner, total, result)
    energy_ref[...] = result


def waves_of(radix):
    pairs = (radix - 1) // 2
    cosine = lambda k, i: math.cos(2.0 * math.pi * ((k * i) % radix) / radix)
    sine = lambda k, i: math.sin(2.0 * math.pi * ((k * i) % radix) / radix)
    return pairs, cosine, sine


def row_of(piece_refs, r):
    share = piece_refs[0].shape[0]
    return piece_refs[r // share].at[r % share]


def stacked_table(high_ref, low_ref, begin, size):
    high = high_ref[begin : begin + size, :]
    return jnp.concatenate([high, high, low_ref[begin : begin + size, :]], axis=0)


def product_of(high_ref, low_ref, begin, size, table):
    high = high_ref[:, begin : begin + size]
    stacked = jnp.concatenate([high, low_ref[:, begin : begin + size], high], axis=1)
    return jnp.dot(stacked, table, preferred_element_type=jnp.float32)


def forward_kernel(radix, pieces, own_ref, *refs):
    other_refs, refs = refs[:pieces], refs[pieces:]
    table_high_ref, table_low_ref, first_high_ref, first_low_ref, scale_ref, *refs = refs
    out_high_ref, out_low_ref, high_ref, low_ref = refs
    rows, levels, width = own_ref.shape
    pairs, cosine, sine = waves_of(radix)
    segments = width // LANES
    shift = radix * LANES // 2 % LANES
    lane = lax.broadcasted_iota(jnp.int32, (levels, LANES), 1)

    def store(place, column, wave):
        high_ref[place, column : column + LANES], low_ref[place, column : column + LANES] = split_high_low(wave)

    for r in range(rows):
        place = slice(levels * r, levels * (r + 1))
        other_ref = row_of(other_refs, r)
        own = [own_ref[r, :, LANES * n : LANES * (n + 1)] for n in range(segments)]
        turned = [pltpu.roll(other_ref[:, LANES * n : LANES * (n + 1)], shift, 1) for n in range(segments)]
        joined = own[:-1] + [jnp.where(lane < shift, own[-1], turned[0])]
        joined += [jnp.where(lane < shift, turned[n], turned[n + 1]) for n in range(segments - 1)]
        plus = [joined[n] + joined[radix - n] for n in range(1, pairs + 1)]
        minus = [joined[radix - n] - joined[n] for n in range(1, pairs + 1)]
        store(place, 0, sum(plus, joined[0]))
        for k in range(1, pairs + 1):
            real = sum((cosine(k, n) * plus[n - 1] for n in range(1, pairs + 1)), joined[0])
            imaginary = sine(k, 1) * minus[0]
            for n in range(2, pairs + 1):
                imaginary = imaginary + sine(k, n) * minus[n - 1]
            store(place, LANES * (2 * k - 1), real)
            store(place, LANES * 2 * k, imaginary)

    def transform(begin, size, table):
        spectrum = product_of(high_ref, low_ref, begin, size, table)
        for r in range(rows):
            place = slice(levels * r, levels * (r + 1))
            damped = spectrum[place] * scale_ref[r : r + 1, begin : begin + size]
            out_high_ref[place, begin : begin + size], out_low_ref[place, begin : begin + size] = split_high_low(damped)

    transform(0, LANES, stacked_table(first_high_ref, first_low_ref, 0, LANES))
    for k in range(pairs):
        transform(LANES * (2 * k + 1), 2 * LANES, stacked_table(table_high_ref, table_low_ref, 2 * LANES * k, 2 * LANES))


def inverse_kernel(radix, pieces, mask_ref, own_ref, *refs):
    other_refs, refs = refs[:pieces], refs[pieces:]
    high_ref, low_ref, table_high_ref, table_low_ref, first_high_ref, first_low_ref, *refs = refs
    result_ref, back_ref, wave_ref = refs
    rows, levels, width = own_ref.shape
    sector = result_ref.shape[-1]
    pairs, cosine, sine = waves_of(radix)
    segments = width // LANES
    shift = radix * LANES // 2 % LANES
    lane = lax.broadcasted_iota(jnp.int32, (levels, LANES), 1)

    def transform(begin, size, table):
        wave_ref[:, begin : begin + size] = product_of(high_ref, low_ref, begin, size, table)

    transform(0, LANES, stacked_table(first_high_ref, first_low_ref, 0, LANES))
    for k in range(pairs):
        transform(LANES * (2 * k + 1), 2 * LANES, stacked_table(table_high_ref, table_low_ref, 2 * LANES * k, 2 * LANES))

    for r in range(rows):
        place = slice(levels * r, levels * (r + 1))
        other_ref = row_of(other_refs, r)
        waves = [wave_ref[place, LANES * n : LANES * (n + 1)] for n in range(radix)]
        results = [None] * radix
        results[0] = sum((waves[2 * k - 1] for k in range(1, pairs + 1)), waves[0])
        for n in range(1, pairs + 1):
            even = sum((cosine(k, n) * waves[2 * k - 1] for k in range(1, pairs + 1)), waves[0])
            odd = sine(1, n) * waves[2]
            for k in range(2, pairs + 1):
                odd = odd + sine(k, n) * waves[2 * k]
            results[n], results[radix - n] = even - odd, even + odd
        filtered_row = mask_ref[r] == 1
        turned = [pltpu.roll(result, LANES - shift, 1) for result in results[segments - 1 :]]
        for n in range(segments):
            begin = LANES * n
            size = min(LANES, sector - begin)
            value = jnp.where(filtered_row, results[n], own_ref[r, :, begin : begin + LANES])
            result_ref[:, r, begin : begin + size] = value[:, :size]
            value = jnp.where(lane < LANES - shift, turned[n], turned[min(n + 1, segments - 1)])
            back_ref[r, :, begin : begin + LANES] = jnp.where(filtered_row, value, other_ref[:, begin : begin + LANES])


def finish_kernel(*refs):
    out_hbm, turned_ref, sems = refs[-3:]
    count = turned_ref.shape[0]
    result_refs, received_refs = refs[:count], refs[count : 2 * count]
    rows, levels, width = received_refs[0].shape
    sector = out_hbm.shape[-1]
    piece = levels // PIECES
    copies = []

    def send(source_ref, tracer, slot):
        for part in range(PIECES):
            span = pl.ds(piece * part, piece)
            copies.append(pltpu.make_async_copy(source_ref.at[span], out_hbm.at[tracer, span], sems.at[slot, part]))
            copies[-1].start()

    for i, result_ref in enumerate(result_refs):
        send(result_ref, first_of("keep", 2 * count) + i, i)
    for i in range(count):
        for r in range(rows):
            turned_ref[i, :, r, :] = received_refs[i][r, :, :sector]
        send(turned_ref.at[i], first_of("give", 2 * count) + i, count + i)
    for copy in copies:
        copy.wait()


def on_device(tracers, courant_lat, courant_lon, surface_flux, mixing, decay_rate, owners, polar_mask):
    tracer_count, levels, rows, sector = tracers.shape
    assert rows == 4 and sector % 64 == 0 and lax.axis_size("lon") == 2
    f32 = jnp.float32
    lat_count, lat = lax.axis_size("lat"), lax.axis_index("lat")
    length = 2 * sector
    width = -(-sector // LANES) * LANES
    radix = length // LANES
    downward = [(i + 1, i) for i in range(lat_count - 1)]
    swap = [(0, 1), (1, 0)]

    whole = pl.BlockSpec(memory_space=pltpu.VMEM)
    in_hbm = pl.BlockSpec(memory_space=pltpu.HBM)
    scalars = pl.BlockSpec(memory_space=pltpu.SMEM)
    inside = [pair for i in range(0, lat_count - 1, 2) for pair in ((i, i + 1), (i + 1, i))]
    across = [pair for i in range(1, lat_count - 1, 2) for pair in ((i, i + 1), (i + 1, i))]
    fields = [pltpu.with_memory_space_constraint(array, pltpu.HBM) for array in (tracers, courant_lat, courant_lon)]
    field_buffers = [pltpu.VMEM(array.shape, f32) for array in (tracers, courant_lat, courant_lon)]
    half = tracer_count // 2
    chunk_rows = pltpu.VMEM((levels * 2, length), f32)
    inner = pl.pallas_call(
        functools.partial(pack_kernel, (0, half)),
        in_specs=[in_hbm],
        out_specs=whole,
        out_shape=chunk_rows,
        scratch_shapes=[pltpu.VMEM((2, levels, 2, sector), f32), pltpu.SemaphoreType.DMA((2,))],
        compiler_params=params(),
        cost_estimate=cost(0, 600_000),
        name="pack",
    )(fields[0])
    from_inside = [lax.ppermute(inner, "lat", inside)]
    fields, inner = lax.optimization_barrier((fields, inner))
    fields = [pltpu.with_memory_space_constraint(array, pltpu.HBM) for array in fields]
    *packed, courant_row, sides = pl.pallas_call(
        rest_kernel,
        in_specs=[in_hbm] * 3,
        out_specs=[whole] * (2 * half + 1),
        out_shape=[chunk_rows] * (2 * half - 1)
        + [
            jax.ShapeDtypeStruct((levels // 2, length), f32),
            jax.ShapeDtypeStruct((tracer_count + 1, rows // 2, levels, LANES), f32),
        ],
        scratch_shapes=field_buffers + [pltpu.SemaphoreType.DMA((tracer_count + 2,))],
        compiler_params=params(),
        cost_estimate=cost(0, 0),
        name="rest",
    )(*fields)
    outer, inner = packed[:half], packed[half:]
    from_across = [lax.ppermute(part, "lat", across) for part in outer]
    from_inside += [lax.ppermute(part, "lat", inside) for part in inner]
    top = lax.ppermute(courant_row, "lat", downward)

    sides = lax.ppermute(sides, "lon", swap)
    base, north, lat_courant = pl.pallas_call(
        functools.partial(base_kernel, width),
        in_specs=[in_hbm, in_hbm, in_hbm, whole],
        out_specs=[whole] * 3,
        out_shape=[
            jax.ShapeDtypeStruct((tracer_count, rows, levels, width), f32),
            jax.ShapeDtypeStruct((tracer_count, levels, width), f32),
            jax.ShapeDtypeStruct((rows, levels, width), f32),
        ],
        scratch_shapes=field_buffers + [pltpu.SemaphoreType.DMA((tracer_count + 2,))],
        compiler_params=params(),
        cost_estimate=cost(0, 0),
        name="base",
    )(*fields, sides)

    surface = jnp.pad(surface_flux, ((0, 0), (0, 0), (0, width - sector)))
    decay = decay_rate[:, :, None]
    block_count = rows * sector // BLOCK
    block_of = (np.arange(rows)[:, None] * sector + np.minimum(np.arange(width), sector - 1)[None]) // BLOCK
    owner_of = jnp.repeat(owners.reshape(block_count), BLOCK).reshape(rows, sector)
    owner_of = jnp.pad(owner_of, ((0, 0), (0, width - sector)))
    forward, inverse, numbers, weights = spectral_tables(length)
    row_ids = (lat * rows + jnp.arange(rows)).astype(f32)
    latitude = (-0.5 + (row_ids + 0.5) / (lat_count * rows)) * math.pi
    inverse_sine = np.where(numbers == 0, 1.0, 1.0 / np.where(numbers == 0, 1.0, np.sin(np.pi * numbers / length)))
    ratio = 2.0 * jnp.cos(latitude)[:, None] * jnp.asarray(inverse_sine, f32)[None]
    damping = jnp.where(jnp.asarray(numbers == 0)[None], 1.0, jnp.minimum(1.0, ratio * ratio))
    scale = damping * jnp.asarray(weights, f32)[None]

    base, scale, owner_of, surface, decay = lax.optimization_barrier((base, scale, owner_of, surface, decay))

    circles = jax.ShapeDtypeStruct((half, rows, levels, width), f32)
    result_shape = jax.ShapeDtypeStruct((levels, rows, sector), f32)
    out_shape = jax.ShapeDtypeStruct(tracers.shape, f32)

    def run_physics(chunk, energy, last=False):
        shapes = [jax.ShapeDtypeStruct(circles.shape[1:], f32)] * 2
        shapes.append(jax.ShapeDtypeStruct((1, LANES) if last else energy.shape, f32))
        *results, energy = pl.pallas_call(
            functools.partial(physics_kernel, levels, sector, lat_count if last else 0, chunk, ("give", "keep")),
            in_specs=[whole] * 11,
            out_specs=[whole] * len(shapes),
            out_shape=shapes,
            compiler_params=params(),
            cost_estimate=cost(0, 0),
            name="physics",
        )(base, north, from_inside[chunk], from_across[chunk], top, lat_courant, surface, mixing, decay, owner_of, energy)
        return results, energy

    forward, inverse = ([jnp.asarray(part) for table in tables for part in split_table(table)] for tables in (forward, inverse))
    circle = jax.ShapeDtypeStruct(circles.shape[1:], f32)
    spectra = jax.ShapeDtypeStruct((rows * levels, length), jnp.bfloat16)

    def run_forward(own, other):
        return pl.pallas_call(
            functools.partial(forward_kernel, radix, len(other)),
            in_specs=[whole] * (6 + len(other)),
            out_specs=[whole] * 2,
            out_shape=[spectra] * 2,
            scratch_shapes=[pltpu.VMEM(spectra.shape, jnp.bfloat16)] * 2,
            compiler_params=params(),
            cost_estimate=cost(0, 0),
            name="forward",
        )(own, *other, *forward, scale)

    def run_inverse(own, other, high, low):
        return pl.pallas_call(
            functools.partial(inverse_kernel, radix, len(other)),
            in_specs=[scalars] + [whole] * (7 + len(other)),
            out_specs=[whole] * 2,
            out_shape=[result_shape, circle],
            scratch_shapes=[pltpu.VMEM(spectra.shape, f32)],
            compiler_params=params(),
            cost_estimate=cost(0, 0),
            name="inverse",
        )(polar_mask, own, *other, high, low, *inverse)

    energy = jnp.zeros((rows, 8, width), f32)
    results, received = [], []
    for chunk in range(half - 1):
        (given, own), energy = run_physics(chunk, energy)
        other = [lax.ppermute(given[r : r + 2], "lon", swap) for r in range(0, rows, 2)]
        spectrum = run_forward(own, other)
        result, back = run_inverse(own, other, *spectrum)
        results.append(result)
        received.append(lax.ppermute(back, "lon", swap))
        energy, back = lax.optimization_barrier((energy, back))

    distances = [1 << i for i in range(lat_count.bit_length() - 1)]

    def send_energy(energy):
        distance = distances.pop(0)
        return lax.ppermute(energy, "lat", [(i, i ^ distance) for i in range(lat_count)])

    (given, own), energy = run_physics(half - 1, energy, True)
    other = [lax.ppermute(given, "lon", swap)]

    coming = send_energy(energy)
    high, low = run_forward(own, other)
    coming, high = lax.optimization_barrier((coming, high))
    energy = energy + coming
    energy, high = lax.optimization_barrier((energy, high))

    coming = send_energy(energy)
    result, back = run_inverse(own, other, high, low)
    coming, back = lax.optimization_barrier((coming, back))
    energy = energy + coming
    energy, back = lax.optimization_barrier((energy, back))
    results.append(result)
    received.append(lax.ppermute(back, "lon", swap))

    coming = send_energy(energy)
    out = pl.pallas_call(
        finish_kernel,
        in_specs=[whole] * (2 * half),
        out_specs=in_hbm,
        out_shape=out_shape,
        scratch_shapes=[
            pltpu.VMEM((half,) + result_shape.shape, f32),
            pltpu.SemaphoreType.DMA((2 * half, PIECES)),
        ],
        compiler_params=params(),
        cost_estimate=cost(0, 3_000_000),
        name="finish",
    )(*results, *received)
    coming, out = lax.optimization_barrier((coming, out))
    energy = energy + coming
    while distances:
        energy = energy + send_energy(energy)

    owner_energy = lax.dynamic_slice(energy, (0, lat), (1, 1)) / (block_count * BLOCK)
    return out, owner_energy


def solution(mesh):
    placed = (
        P("group", None, "lat", "lon"),
        P("group", "lat", "lon"),
        P("group", "lat", "lon"),
        P("group", "lat", "lon"),
        P(),
        P(),
        P(("group", "lat"), "lon", None, None),
        P(("group", "lat")),
    )
    return jax.shard_map(
        on_device,
        mesh=mesh,
        in_specs=placed,
        out_specs=(P("group", None, "lat", "lon"), P(("group", "lat"), "lon")),
        check_vma=False,
    )
```

```python
import functools
import math

import jax
import jax.numpy as jnp
import numpy as np
from jax import lax
from jax.experimental import pallas as pl
from jax.experimental.pallas import tpu as pltpu
from jax.sharding import PartitionSpec as P

LANES = 128
BLOCK = 128
VMEM_BYTES = 6 * 1024 * 1024
PIECES = 4
NEAR = 7.0 / 12.0
FAR = 1.0 / 12.0


def params():
    return pltpu.CompilerParams(vmem_limit_bytes=VMEM_BYTES)


def cost(flops, bytes_accessed):
    return pl.CostEstimate(flops=flops, bytes_accessed=bytes_accessed, transcendentals=0)


def split_high_low(value):
    high = value.astype(jnp.bfloat16)
    low = (value - high.astype(jnp.float32)).astype(jnp.bfloat16)
    return high, low


def split_table(table):
    high = table.astype(jnp.bfloat16.dtype)
    return high, (table - high.astype(np.float64)).astype(jnp.bfloat16.dtype)


def spectral_tables(length):
    radix = length // LANES
    pairs = (radix - 1) // 2
    spot = np.arange(LANES)[:, None]
    number = np.arange(LANES)[None, :]
    is_cosine = number <= LANES // 2
    wave = np.where(is_cosine, number, number - LANES // 2)
    angle = 2.0 * np.pi * ((spot * wave) % LANES) / LANES
    first = np.where(is_cosine, np.cos(angle), np.sin(angle))
    others, numbers = [], [radix * wave[0]]
    weights = [np.where((wave[0] == 0) | (wave[0] == LANES // 2), 1.0, 2.0) / length]
    for residue in range(1, pairs + 1):
        whole = residue + radix * number
        angle = 2.0 * np.pi * ((spot * whole) % length) / length
        cosine, sine = np.cos(angle), np.sin(angle)
        others.append(np.block([[cosine, -sine], [sine, cosine]]))
        folded = np.minimum(whole[0], length - whole[0])
        numbers += [folded, folded]
        weights.append(np.full(2 * LANES, 2.0 / length))
    forward = np.concatenate(others), first
    inverse = np.concatenate([table.T for table in others]), first.T
    return forward, inverse, np.concatenate(numbers), np.concatenate(weights)


def is_even():
    return lax.axis_index("lat") % 2 == 0


def first_of(half, tracer_count):
    lon = lax.axis_index("lon")
    return (tracer_count // 2) * (lon if half == "keep" else 1 - lon)


def pack_rows(first, second):
    return jnp.concatenate([first, second], axis=1)


def second_half(packed, sector):
    skip, shift = sector // LANES, sector % LANES
    segments = [packed[:, LANES * i : LANES * (i + 1)] for i in range(packed.shape[1] // LANES)]
    if shift == 0:
        return jnp.concatenate(segments[skip:], axis=1)
    turned = [pltpu.roll(segment, LANES - shift, 1) for segment in segments[skip:]]
    lane = lax.broadcasted_iota(jnp.int32, turned[0].shape, 1)
    parts = [jnp.where(lane < LANES - shift, turned[i], turned[min(i + 1, len(turned) - 1)]) for i in range(len(turned))]
    return jnp.concatenate(parts, axis=1)


def start_copies(pairs, sems):
    copies = [pltpu.make_async_copy(source, target, sems.at[i]) for i, (source, target) in enumerate(pairs)]
    for copy in copies:
        copy.start()
    return copies


def pack_kernel(tracers, tracer_hbm, out_ref, row_ref, sems):
    levels = row_ref.shape[1]
    first_row = pl.multiple_of(jnp.where(is_even(), tracer_hbm.shape[2] - 2, 0), 2)
    sources = [tracer_hbm.at[t, :, pl.ds(first_row, 2), :] for t in tracers]
    copies = start_copies([(source, row_ref.at[i]) for i, source in enumerate(sources)], sems)
    for i, copy in enumerate(copies):
        copy.wait()
        out_ref[levels * i : levels * (i + 1), :] = pack_rows(row_ref[i, :, 0, :], row_ref[i, :, 1, :])


def rest_kernel(tracer_hbm, lat_hbm, lon_hbm, *refs):
    courant_ref, side_ref, tracer_ref, lat_ref, lon_ref, sems = refs[-6:]
    count, levels, rows, sector = tracer_ref.shape
    half = count // 2
    outer_refs, inner_refs = refs[:half], refs[half:-6]
    pairs = [(tracer_hbm.at[t], tracer_ref.at[t]) for t in range(count)] + [(lat_hbm, lat_ref), (lon_hbm, lon_ref)]
    for copy in start_copies(pairs, sems):
        copy.wait()
    shift, whole = sector % LANES, sector // LANES * LANES
    lane = lax.broadcasted_iota(jnp.int32, (levels, LANES), 1)
    even = is_even()

    def side_of(values):
        first = pltpu.roll(values[:, :LANES], shift, 1)
        last = jnp.concatenate([values[:, whole:], values[:, whole:]], axis=1)
        return jnp.where(lane < LANES - 2, first, last)

    def store_sides(i, values):
        for r in range(0, rows, 2):
            side_ref[i, r // 2] = jnp.where(lane < shift, pltpu.roll(side_of(values[r]), shift, 1), side_of(values[r + 1]))

    for t in range(count):
        row = [tracer_ref[t, :, r, :] for r in range(rows)]
        place = slice(levels * (t // half), levels * (t // half + 1))
        top, bottom = pack_rows(row[rows - 2], row[rows - 1]), pack_rows(row[0], row[1])
        outer_refs[t % half][place, :] = jnp.where(even, bottom, top)
        if t % half:
            inner_refs[t % half - 1][place, :] = jnp.where(even, top, bottom)
        store_sides(t, row)
    courant = lat_ref[:, 0, :]
    courant_ref[...] = pack_rows(courant[: levels // 2], courant[levels // 2 :])
    store_sides(count, [lon_ref[:, r, :] for r in range(rows)])


def base_kernel(width, tracer_hbm, lat_hbm, lon_hbm, side_ref, base_ref, north_ref, courant_ref, *scratch):
    tracer_ref, lat_ref, lon_ref, sems = scratch
    tracer_count, levels, rows, sector = tracer_ref.shape
    whole = sector // LANES * LANES
    pairs = [(lat_hbm, lat_ref), (lon_hbm, lon_ref)] + [(tracer_hbm.at[t], tracer_ref.at[t]) for t in range(tracer_count)]
    copies = start_copies(pairs, sems)

    def beside(values, side, part=0):
        begin = (sector - whole) * part
        return jnp.concatenate([values[:, :whole], values[:, whole:], side[:, begin : begin + width - sector]], axis=1)

    copies[0].wait()
    copies[1].wait()
    nothing = jnp.zeros((levels, LANES), jnp.float32)
    for r in range(rows):
        courant = lat_ref[:, r, :] if r else jnp.where(lax.axis_index("lat") > 0, lat_ref[:, r, :], 0.0)
        courant_ref[r] = beside(courant, nothing)
    for t in range(tracer_count):
        copies[t + 2].wait()
        q = [beside(tracer_ref[t, :, r, :], side_ref[t, r // 2], r % 2) for r in range(rows)]
        north_ref[t] = NEAR * q[3] - FAR * q[2]
        own_flux = [
            courant_ref[0] * (NEAR * q[0] - FAR * q[1]),
            courant_ref[1] * (NEAR * (q[1] + q[0]) - FAR * q[2]),
            courant_ref[2] * (NEAR * (q[2] + q[1]) - FAR * (q[3] + q[0])),
            courant_ref[3] * (NEAR * (q[3] + q[2]) - FAR * q[1]),
        ]
        for r in range(rows):
            west, west2, east = pltpu.roll(q[r], 1, 1), pltpu.roll(q[r], 2, 1), pltpu.roll(q[r], width - 1, 1)
            flux = beside(lon_ref[:, r, :], side_ref[tracer_count, r // 2], r % 2) * (NEAR * (q[r] + west) - FAR * (east + west2))
            value = q[r] - (pltpu.roll(flux, width - 1, 1) - flux) + own_flux[r]
            if r + 1 < rows:
                value = value - own_flux[r + 1]
            base_ref[t, r] = value


def physics_kernel(levels, sector, owner_count, chunk, halves, *refs):
    base_ref, north_ref, inner_ref, outer_ref = refs[:4]
    top_ref, courant_ref, surface_ref, mixing_ref, decay_ref, owner_ref, energy_in_ref = refs[4:11]
    physics_refs, energy_ref, scratch = refs[11 : 11 + len(halves)], refs[11 + len(halves)], refs[12 + len(halves) :]
    if scratch:
        for copy in start_copies([(inner_ref, scratch[0]), (outer_ref, scratch[1])], scratch[2]):
            copy.wait()
        inner_ref, outer_ref = scratch[:2]
    rows, width = base_ref.shape[1], base_ref.shape[-1]
    courant = [courant_ref[r] for r in range(rows)]
    even = is_even()
    top = top_ref[...]
    top = jnp.concatenate([top[:, :width], second_half(top, sector)], axis=0)
    mix_high, mix_low = split_high_low(mixing_ref[...])
    mix = jnp.concatenate([mix_high, mix_high, mix_low, mix_low], axis=1)
    level = lax.broadcasted_iota(jnp.int32, (8, width), 0)
    lane = lax.broadcasted_iota(jnp.int32, (8, width), 1)
    energies = [energy_in_ref[r] for r in range(rows)]
    for half, physics_ref in zip(halves, physics_refs):
        first = first_of(half, base_ref.shape[0])
        t = first + chunk
        inner = jnp.where(first == 0, inner_ref[:levels, :], inner_ref[levels:, :])
        outer = jnp.where(first == 0, outer_ref[:levels, :], outer_ref[levels:, :])
        low, high = jnp.where(even, outer, inner), jnp.where(even, inner, outer)
        low_a, low_b = low[:, :width], second_half(low, sector)
        high_a, high_b = high[:, :width], second_half(high, sector)
        south = courant[0] * (NEAR * low_b - FAR * low_a)
        south_in = courant[1] * (FAR * low_b)
        north_in = courant[3] * (FAR * high_a)
        north = top * (NEAR * high_a - FAR * high_b + north_ref[t])
        extra = [south + south_in, -south_in, north_in, -north_in - north]
        for r in range(rows):
            advected = base_ref[t, r] + extra[r]
            part_high, part_low = split_high_low(advected)
            stacked = jnp.concatenate([part_high, part_low, part_high, part_low], axis=0)
            mixed = jnp.dot(mix, stacked, preferred_element_type=jnp.float32)
            surface = jnp.where(level == 7, surface_ref[t, r : r + 1, :], 0.0)
            mixed = jnp.concatenate([mixed[: levels - 8], mixed[levels - 8 :] + surface], axis=0)
            physics = mixed / (1.0 + decay_ref[t] * mixed * mixed)
            physics_ref[r] = physics
            gap = physics - advected
            squared = gap * gap
            for k in range(levels // 8):
                energies[r] = energies[r] + squared[8 * k : 8 * k + 8]
    if not owner_count:
        for r in range(rows):
            energy_ref[r] = energies[r]
        return
    energies = [jnp.where(lane < sector, energy, 0.0) for energy in energies]
    spot = lax.broadcasted_iota(jnp.int32, (1, LANES), 1)
    result = jnp.zeros((1, LANES), jnp.float32)
    for owner in range(owner_count):
        chosen = jnp.zeros((8, LANES), jnp.float32)
        for r in range(rows):
            picked = jnp.where(owner_ref[r : r + 1, :] == owner, energies[r], 0.0)
            for k in range(width // LANES):
                chosen = chosen + picked[:, LANES * k : LANES * (k + 1)]
        total = jnp.sum(jnp.sum(chosen, axis=0, keepdims=True), axis=1, keepdims=True)
        result = jnp.where(spot == owner, total, result)
    energy_ref[...] = result


def waves_of(radix):
    pairs = (radix - 1) // 2
    cosine = lambda k, i: math.cos(2.0 * math.pi * ((k * i) % radix) / radix)
    sine = lambda k, i: math.sin(2.0 * math.pi * ((k * i) % radix) / radix)
    return pairs, cosine, sine


def row_of(piece_refs, r):
    share = piece_refs[0].shape[0]
    return piece_refs[r // share].at[r % share]


def stacked_table(high_ref, low_ref, begin, size):
    high = high_ref[begin : begin + size, :]
    return jnp.concatenate([high, high, low_ref[begin : begin + size, :]], axis=0)


def product_of(high_ref, low_ref, begin, size, table):
    high = high_ref[:, begin : begin + size]
    stacked = jnp.concatenate([high, low_ref[:, begin : begin + size], high], axis=1)
    return jnp.dot(stacked, table, preferred_element_type=jnp.float32)


def forward_kernel(radix, pieces, own_ref, *refs):
    other_refs, refs = refs[:pieces], refs[pieces:]
    table_high_ref, table_low_ref, first_high_ref, first_low_ref, scale_ref, *refs = refs
    out_high_ref, out_low_ref, high_ref, low_ref = refs
    rows, levels, width = own_ref.shape
    pairs, cosine, sine = waves_of(radix)
    segments = width // LANES
    shift = radix * LANES // 2 % LANES
    lane = lax.broadcasted_iota(jnp.int32, (levels, LANES), 1)

    def store(place, column, wave):
        high_ref[place, column : column + LANES], low_ref[place, column : column + LANES] = split_high_low(wave)

    for r in range(rows):
        place = slice(levels * r, levels * (r + 1))
        other_ref = row_of(other_refs, r)
        own = [own_ref[r, :, LANES * n : LANES * (n + 1)] for n in range(segments)]
        turned = [pltpu.roll(other_ref[:, LANES * n : LANES * (n + 1)], shift, 1) for n in range(segments)]
        joined = own[:-1] + [jnp.where(lane < shift, own[-1], turned[0])]
        joined += [jnp.where(lane < shift, turned[n], turned[n + 1]) for n in range(segments - 1)]
        plus = [joined[n] + joined[radix - n] for n in range(1, pairs + 1)]
        minus = [joined[radix - n] - joined[n] for n in range(1, pairs + 1)]
        store(place, 0, sum(plus, joined[0]))
        for k in range(1, pairs + 1):
            real = sum((cosine(k, n) * plus[n - 1] for n in range(1, pairs + 1)), joined[0])
            imaginary = sine(k, 1) * minus[0]
            for n in range(2, pairs + 1):
                imaginary = imaginary + sine(k, n) * minus[n - 1]
            store(place, LANES * (2 * k - 1), real)
            store(place, LANES * 2 * k, imaginary)

    def transform(begin, size, table):
        spectrum = product_of(high_ref, low_ref, begin, size, table)
        for r in range(rows):
            place = slice(levels * r, levels * (r + 1))
            damped = spectrum[place] * scale_ref[r : r + 1, begin : begin + size]
            out_high_ref[place, begin : begin + size], out_low_ref[place, begin : begin + size] = split_high_low(damped)

    transform(0, LANES, stacked_table(first_high_ref, first_low_ref, 0, LANES))
    for k in range(pairs):
        transform(LANES * (2 * k + 1), 2 * LANES, stacked_table(table_high_ref, table_low_ref, 2 * LANES * k, 2 * LANES))


def inverse_kernel(radix, pieces, mask_ref, own_ref, *refs):
    other_refs, refs = refs[:pieces], refs[pieces:]
    high_ref, low_ref, table_high_ref, table_low_ref, first_high_ref, first_low_ref, *refs = refs
    result_ref, back_ref, wave_ref = refs
    rows, levels, width = own_ref.shape
    sector = result_ref.shape[-1]
    pairs, cosine, sine = waves_of(radix)
    segments = width // LANES
    shift = radix * LANES // 2 % LANES
    lane = lax.broadcasted_iota(jnp.int32, (levels, LANES), 1)

    def transform(begin, size, table):
        wave_ref[:, begin : begin + size] = product_of(high_ref, low_ref, begin, size, table)

    transform(0, LANES, stacked_table(first_high_ref, first_low_ref, 0, LANES))
    for k in range(pairs):
        transform(LANES * (2 * k + 1), 2 * LANES, stacked_table(table_high_ref, table_low_ref, 2 * LANES * k, 2 * LANES))

    for r in range(rows):
        place = slice(levels * r, levels * (r + 1))
        other_ref = row_of(other_refs, r)
        waves = [wave_ref[place, LANES * n : LANES * (n + 1)] for n in range(radix)]
        results = [None] * radix
        results[0] = sum((waves[2 * k - 1] for k in range(1, pairs + 1)), waves[0])
        for n in range(1, pairs + 1):
            even = sum((cosine(k, n) * waves[2 * k - 1] for k in range(1, pairs + 1)), waves[0])
            odd = sine(1, n) * waves[2]
            for k in range(2, pairs + 1):
                odd = odd + sine(k, n) * waves[2 * k]
            results[n], results[radix - n] = even - odd, even + odd
        filtered_row = mask_ref[r] == 1
        turned = [pltpu.roll(result, LANES - shift, 1) for result in results[segments - 1 :]]
        for n in range(segments):
            begin = LANES * n
            size = min(LANES, sector - begin)
            value = jnp.where(filtered_row, results[n], own_ref[r, :, begin : begin + LANES])
            result_ref[:, r, begin : begin + size] = value[:, :size]
            value = jnp.where(lane < LANES - shift, turned[n], turned[min(n + 1, segments - 1)])
            back_ref[r, :, begin : begin + LANES] = jnp.where(filtered_row, value, other_ref[:, begin : begin + LANES])


def finish_kernel(*refs):
    out_hbm, turned_ref, sems = refs[-3:]
    count = turned_ref.shape[0]
    result_refs, received_refs = refs[:count], refs[count : 2 * count]
    rows, levels, width = received_refs[0].shape
    sector = out_hbm.shape[-1]
    piece = levels // PIECES
    copies = []

    def send(source_ref, tracer, slot):
        for part in range(PIECES):
            span = pl.ds(piece * part, piece)
            copies.append(pltpu.make_async_copy(source_ref.at[span], out_hbm.at[tracer, span], sems.at[slot, part]))
            copies[-1].start()

    for i, result_ref in enumerate(result_refs):
        send(result_ref, first_of("keep", 2 * count) + i, i)
    for i in range(count):
        for r in range(rows):
            turned_ref[i, :, r, :] = received_refs[i][r, :, :sector]
        send(turned_ref.at[i], first_of("give", 2 * count) + i, count + i)
    for copy in copies:
        copy.wait()


def on_device(tracers, courant_lat, courant_lon, surface_flux, mixing, decay_rate, owners, polar_mask):
    tracer_count, levels, rows, sector = tracers.shape
    assert rows == 4 and sector % 64 == 0 and lax.axis_size("lon") == 2
    f32 = jnp.float32
    lat_count, lat = lax.axis_size("lat"), lax.axis_index("lat")
    length = 2 * sector
    width = -(-sector // LANES) * LANES
    radix = length // LANES
    downward = [(i + 1, i) for i in range(lat_count - 1)]
    swap = [(0, 1), (1, 0)]

    whole = pl.BlockSpec(memory_space=pltpu.VMEM)
    in_hbm = pl.BlockSpec(memory_space=pltpu.HBM)
    scalars = pl.BlockSpec(memory_space=pltpu.SMEM)
    inside = [pair for i in range(0, lat_count - 1, 2) for pair in ((i, i + 1), (i + 1, i))]
    across = [pair for i in range(1, lat_count - 1, 2) for pair in ((i, i + 1), (i + 1, i))]
    fields = [pltpu.with_memory_space_constraint(array, pltpu.HBM) for array in (tracers, courant_lat, courant_lon)]
    field_buffers = [pltpu.VMEM(array.shape, f32) for array in (tracers, courant_lat, courant_lon)]
    half = tracer_count // 2
    chunk_rows = pltpu.VMEM((levels * 2, length), f32)
    inner = pl.pallas_call(
        functools.partial(pack_kernel, (0, half)),
        in_specs=[in_hbm],
        out_specs=whole,
        out_shape=chunk_rows,
        scratch_shapes=[pltpu.VMEM((2, levels, 2, sector), f32), pltpu.SemaphoreType.DMA((2,))],
        compiler_params=params(),
        cost_estimate=cost(0, 600_000),
        name="pack",
    )(fields[0])
    from_inside = [lax.ppermute(inner, "lat", inside)]
    fields, inner = lax.optimization_barrier((fields, inner))
    fields = [pltpu.with_memory_space_constraint(array, pltpu.HBM) for array in fields]
    *packed, courant_row, sides = pl.pallas_call(
        rest_kernel,
        in_specs=[in_hbm] * 3,
        out_specs=[whole] * (2 * half + 1),
        out_shape=[chunk_rows] * (2 * half - 1)
        + [
            jax.ShapeDtypeStruct((levels // 2, length), f32),
            jax.ShapeDtypeStruct((tracer_count + 1, rows // 2, levels, LANES), f32),
        ],
        scratch_shapes=field_buffers + [pltpu.SemaphoreType.DMA((tracer_count + 2,))],
        compiler_params=params(),
        cost_estimate=cost(0, 0),
        name="rest",
    )(*fields)
    outer, inner = packed[:half], packed[half:]
    from_across = [lax.ppermute(part, "lat", across) for part in outer]
    from_inside += [lax.ppermute(part, "lat", inside) for part in inner]
    top = lax.ppermute(courant_row, "lat", downward)

    sides = lax.ppermute(sides, "lon", swap)
    base, north, lat_courant = pl.pallas_call(
        functools.partial(base_kernel, width),
        in_specs=[in_hbm, in_hbm, in_hbm, whole],
        out_specs=[whole] * 3,
        out_shape=[
            jax.ShapeDtypeStruct((tracer_count, rows, levels, width), f32),
            jax.ShapeDtypeStruct((tracer_count, levels, width), f32),
            jax.ShapeDtypeStruct((rows, levels, width), f32),
        ],
        scratch_shapes=field_buffers + [pltpu.SemaphoreType.DMA((tracer_count + 2,))],
        compiler_params=params(),
        cost_estimate=cost(0, 0),
        name="base",
    )(*fields, sides)

    surface = jnp.pad(surface_flux, ((0, 0), (0, 0), (0, width - sector)))
    decay = decay_rate[:, :, None]
    block_count = rows * sector // BLOCK
    block_of = (np.arange(rows)[:, None] * sector + np.minimum(np.arange(width), sector - 1)[None]) // BLOCK
    owner_of = jnp.repeat(owners.reshape(block_count), BLOCK).reshape(rows, sector)
    owner_of = jnp.pad(owner_of, ((0, 0), (0, width - sector)))
    forward, inverse, numbers, weights = spectral_tables(length)
    row_ids = (lat * rows + jnp.arange(rows)).astype(f32)
    latitude = (-0.5 + (row_ids + 0.5) / (lat_count * rows)) * math.pi
    inverse_sine = np.where(numbers == 0, 1.0, 1.0 / np.where(numbers == 0, 1.0, np.sin(np.pi * numbers / length)))
    ratio = 2.0 * jnp.cos(latitude)[:, None] * jnp.asarray(inverse_sine, f32)[None]
    damping = jnp.where(jnp.asarray(numbers == 0)[None], 1.0, jnp.minimum(1.0, ratio * ratio))
    scale = damping * jnp.asarray(weights, f32)[None]

    base, scale, owner_of, surface, decay = lax.optimization_barrier((base, scale, owner_of, surface, decay))

    circles = jax.ShapeDtypeStruct((half, rows, levels, width), f32)
    result_shape = jax.ShapeDtypeStruct((levels, rows, sector), f32)
    out_shape = jax.ShapeDtypeStruct(tracers.shape, f32)

    def rows_of(chunk):
        parts = (from_inside[chunk], from_across[chunk])
        return parts if chunk == half - 1 else [pltpu.with_memory_space_constraint(part, pltpu.HBM) for part in parts]

    def run_physics(chunk, energy, last=False):
        shapes = [jax.ShapeDtypeStruct(circles.shape[1:], f32)] * 2
        shapes.append(jax.ShapeDtypeStruct((1, LANES) if last else energy.shape, f32))
        *results, energy = pl.pallas_call(
            functools.partial(physics_kernel, levels, sector, lat_count if last else 0, chunk, ("give", "keep")),
            in_specs=[whole] * 2 + ([whole] if last else [in_hbm]) * 2 + [whole] * 7,
            out_specs=[whole] * len(shapes),
            scratch_shapes=[] if last else [chunk_rows] * 2 + [pltpu.SemaphoreType.DMA((2,))],
            out_shape=shapes,
            compiler_params=params(),
            cost_estimate=cost(0, 0),
            name="physics",
        )(base, north, *rows_of(chunk), top, lat_courant, surface, mixing, decay, owner_of, energy)
        return results, energy

    forward, inverse = ([jnp.asarray(part) for table in tables for part in split_table(table)] for tables in (forward, inverse))
    circle = jax.ShapeDtypeStruct(circles.shape[1:], f32)
    spectra = jax.ShapeDtypeStruct((rows * levels, length), jnp.bfloat16)

    def run_forward(own, other):
        return pl.pallas_call(
            functools.partial(forward_kernel, radix, len(other)),
            in_specs=[whole] * (6 + len(other)),
            out_specs=[whole] * 2,
            out_shape=[spectra] * 2,
            scratch_shapes=[pltpu.VMEM(spectra.shape, jnp.bfloat16)] * 2,
            compiler_params=params(),
            cost_estimate=cost(0, 0),
            name="forward",
        )(own, *other, *forward, scale)

    def run_inverse(own, other, high, low):
        return pl.pallas_call(
            functools.partial(inverse_kernel, radix, len(other)),
            in_specs=[scalars] + [whole] * (7 + len(other)),
            out_specs=[whole] * 2,
            out_shape=[result_shape, circle],
            scratch_shapes=[pltpu.VMEM(spectra.shape, f32)],
            compiler_params=params(),
            cost_estimate=cost(0, 0),
            name="inverse",
        )(polar_mask, own, *other, high, low, *inverse)

    energy = jnp.zeros((rows, 8, width), f32)
    results, received = [], []
    for chunk in range(half - 1):
        (given, own), energy = run_physics(chunk, energy)
        other = [lax.ppermute(given[r : r + 2], "lon", swap) for r in range(0, rows, 2)]
        spectrum = run_forward(own, other)
        result, back = run_inverse(own, other, *spectrum)
        results.append(result)
        received.append(lax.ppermute(back, "lon", swap))
        energy, back = lax.optimization_barrier((energy, back))

    distances = [1 << i for i in range(lat_count.bit_length() - 1)]

    def send_energy(energy):
        distance = distances.pop(0)
        return lax.ppermute(energy, "lat", [(i, i ^ distance) for i in range(lat_count)])

    (given, own), energy = run_physics(half - 1, energy, True)
    other = [lax.ppermute(given, "lon", swap)]

    coming = send_energy(energy)
    high, low = run_forward(own, other)
    coming, high = lax.optimization_barrier((coming, high))
    energy = energy + coming
    energy, high = lax.optimization_barrier((energy, high))

    coming = send_energy(energy)
    result, back = run_inverse(own, other, high, low)
    coming, back = lax.optimization_barrier((coming, back))
    energy = energy + coming
    energy, back = lax.optimization_barrier((energy, back))
    results.append(result)
    received.append(lax.ppermute(back, "lon", swap))

    coming = send_energy(energy)
    out = pl.pallas_call(
        finish_kernel,
        in_specs=[whole] * (2 * half),
        out_specs=in_hbm,
        out_shape=out_shape,
        scratch_shapes=[
            pltpu.VMEM((half,) + result_shape.shape, f32),
            pltpu.SemaphoreType.DMA((2 * half, PIECES)),
        ],
        compiler_params=params(),
        cost_estimate=cost(0, 3_000_000),
        name="finish",
    )(*results, *received)
    coming, out = lax.optimization_barrier((coming, out))
    energy = energy + coming
    while distances:
        energy = energy + send_energy(energy)

    owner_energy = lax.dynamic_slice(energy, (0, lat), (1, 1)) / (block_count * BLOCK)
    return out, owner_energy


def solution(mesh):
    placed = (
        P("group", None, "lat", "lon"),
        P("group", "lat", "lon"),
        P("group", "lat", "lon"),
        P("group", "lat", "lon"),
        P(),
        P(),
        P(("group", "lat"), "lon", None, None),
        P(("group", "lat")),
    )
    return jax.shard_map(
        on_device,
        mesh=mesh,
        in_specs=placed,
        out_specs=(P("group", None, "lat", "lon"), P(("group", "lat"), "lon")),
        check_vma=False,
    )
```

```python
import functools
import math

import jax
import jax.numpy as jnp
import numpy as np
from jax import lax
from jax.experimental import pallas as pl
from jax.experimental.pallas import tpu as pltpu
from jax.sharding import PartitionSpec as P

LANES = 128
BLOCK = 128
VMEM_BYTES = 6 * 1024 * 1024
PIECES = 4
NEAR = 7.0 / 12.0
FAR = 1.0 / 12.0


def params():
    return pltpu.CompilerParams(vmem_limit_bytes=VMEM_BYTES)


def cost(flops, bytes_accessed):
    return pl.CostEstimate(flops=flops, bytes_accessed=bytes_accessed, transcendentals=0)


def split_high_low(value):
    high = value.astype(jnp.bfloat16)
    low = (value - high.astype(jnp.float32)).astype(jnp.bfloat16)
    return high, low


def split_table(table):
    high = table.astype(jnp.bfloat16.dtype)
    return high, (table - high.astype(np.float64)).astype(jnp.bfloat16.dtype)


def spectral_tables(length):
    radix = length // LANES
    pairs = (radix - 1) // 2
    spot = np.arange(LANES)[:, None]
    number = np.arange(LANES)[None, :]
    is_cosine = number <= LANES // 2
    wave = np.where(is_cosine, number, number - LANES // 2)
    angle = 2.0 * np.pi * ((spot * wave) % LANES) / LANES
    first = np.where(is_cosine, np.cos(angle), np.sin(angle))
    others, numbers = [], [radix * wave[0]]
    weights = [np.where((wave[0] == 0) | (wave[0] == LANES // 2), 1.0, 2.0) / length]
    for residue in range(1, pairs + 1):
        whole = residue + radix * number
        angle = 2.0 * np.pi * ((spot * whole) % length) / length
        cosine, sine = np.cos(angle), np.sin(angle)
        others.append(np.block([[cosine, -sine], [sine, cosine]]))
        folded = np.minimum(whole[0], length - whole[0])
        numbers += [folded, folded]
        weights.append(np.full(2 * LANES, 2.0 / length))
    forward = np.concatenate(others), first
    inverse = np.concatenate([table.T for table in others]), first.T
    return forward, inverse, np.concatenate(numbers), np.concatenate(weights)


def is_even():
    return lax.axis_index("lat") % 2 == 0


def first_of(half, tracer_count):
    lon = lax.axis_index("lon")
    return (tracer_count // 2) * (lon if half == "keep" else 1 - lon)


def pack_rows(first, second):
    return jnp.concatenate([first, second], axis=1)


def second_half(packed, sector):
    skip, shift = sector // LANES, sector % LANES
    segments = [packed[:, LANES * i : LANES * (i + 1)] for i in range(packed.shape[1] // LANES)]
    if shift == 0:
        return jnp.concatenate(segments[skip:], axis=1)
    turned = [pltpu.roll(segment, LANES - shift, 1) for segment in segments[skip:]]
    lane = lax.broadcasted_iota(jnp.int32, turned[0].shape, 1)
    parts = [jnp.where(lane < LANES - shift, turned[i], turned[min(i + 1, len(turned) - 1)]) for i in range(len(turned))]
    return jnp.concatenate(parts, axis=1)


def start_copies(pairs, sems):
    copies = [pltpu.make_async_copy(source, target, sems.at[i]) for i, (source, target) in enumerate(pairs)]
    for copy in copies:
        copy.start()
    return copies


def pack_kernel(tracers, tracer_hbm, out_ref, row_ref, sems):
    levels = row_ref.shape[1]
    first_row = pl.multiple_of(jnp.where(is_even(), tracer_hbm.shape[2] - 2, 0), 2)
    sources = [tracer_hbm.at[t, :, pl.ds(first_row, 2), :] for t in tracers]
    copies = start_copies([(source, row_ref.at[i]) for i, source in enumerate(sources)], sems)
    for i, copy in enumerate(copies):
        copy.wait()
        out_ref[levels * i : levels * (i + 1), :] = pack_rows(row_ref[i, :, 0, :], row_ref[i, :, 1, :])


def rest_kernel(tracer_hbm, lat_hbm, lon_hbm, *refs):
    courant_ref, side_ref, tracer_ref, lat_ref, lon_ref, sems = refs[-6:]
    count, levels, rows, sector = tracer_ref.shape
    half = count // 2
    outer_refs, inner_refs = refs[:half], refs[half:-6]
    pairs = [(tracer_hbm.at[t], tracer_ref.at[t]) for t in range(count)] + [(lat_hbm, lat_ref), (lon_hbm, lon_ref)]
    for copy in start_copies(pairs, sems):
        copy.wait()
    shift, whole = sector % LANES, sector // LANES * LANES
    lane = lax.broadcasted_iota(jnp.int32, (levels, LANES), 1)
    even = is_even()

    def side_of(values):
        first = pltpu.roll(values[:, :LANES], shift, 1)
        last = jnp.concatenate([values[:, whole:], values[:, whole:]], axis=1)
        return jnp.where(lane < LANES - 2, first, last)

    def store_sides(i, values):
        for r in range(0, rows, 2):
            side_ref[i, r // 2] = jnp.where(lane < shift, pltpu.roll(side_of(values[r]), shift, 1), side_of(values[r + 1]))

    for t in range(count):
        row = [tracer_ref[t, :, r, :] for r in range(rows)]
        place = slice(levels * (t // half), levels * (t // half + 1))
        top, bottom = pack_rows(row[rows - 2], row[rows - 1]), pack_rows(row[0], row[1])
        outer_refs[t % half][place, :] = jnp.where(even, bottom, top)
        if t % half:
            inner_refs[t % half - 1][place, :] = jnp.where(even, top, bottom)
        store_sides(t, row)
    courant = lat_ref[:, 0, :]
    courant_ref[...] = pack_rows(courant[: levels // 2], courant[levels // 2 :])
    store_sides(count, [lon_ref[:, r, :] for r in range(rows)])


def base_kernel(width, tracer_hbm, lat_hbm, lon_hbm, side_ref, base_ref, north_ref, courant_ref, *scratch):
    tracer_ref, lat_ref, lon_ref, sems = scratch
    tracer_count, levels, rows, sector = tracer_ref.shape
    whole = sector // LANES * LANES
    pairs = [(lat_hbm, lat_ref), (lon_hbm, lon_ref)] + [(tracer_hbm.at[t], tracer_ref.at[t]) for t in range(tracer_count)]
    copies = start_copies(pairs, sems)

    def beside(values, side, part=0):
        begin = (sector - whole) * part
        return jnp.concatenate([values[:, :whole], values[:, whole:], side[:, begin : begin + width - sector]], axis=1)

    copies[0].wait()
    copies[1].wait()
    nothing = jnp.zeros((levels, LANES), jnp.float32)
    for r in range(rows):
        courant = lat_ref[:, r, :] if r else jnp.where(lax.axis_index("lat") > 0, lat_ref[:, r, :], 0.0)
        courant_ref[r] = beside(courant, nothing)
    for t in range(tracer_count):
        copies[t + 2].wait()
        q = [beside(tracer_ref[t, :, r, :], side_ref[t, r // 2], r % 2) for r in range(rows)]
        north_ref[t] = NEAR * q[3] - FAR * q[2]
        own_flux = [
            courant_ref[0] * (NEAR * q[0] - FAR * q[1]),
            courant_ref[1] * (NEAR * (q[1] + q[0]) - FAR * q[2]),
            courant_ref[2] * (NEAR * (q[2] + q[1]) - FAR * (q[3] + q[0])),
            courant_ref[3] * (NEAR * (q[3] + q[2]) - FAR * q[1]),
        ]
        for r in range(rows):
            west, west2, east = pltpu.roll(q[r], 1, 1), pltpu.roll(q[r], 2, 1), pltpu.roll(q[r], width - 1, 1)
            flux = beside(lon_ref[:, r, :], side_ref[tracer_count, r // 2], r % 2) * (NEAR * (q[r] + west) - FAR * (east + west2))
            value = q[r] - (pltpu.roll(flux, width - 1, 1) - flux) + own_flux[r]
            if r + 1 < rows:
                value = value - own_flux[r + 1]
            base_ref[t, r] = value


def physics_kernel(levels, sector, owner_count, chunk, halves, *refs):
    base_ref, north_ref, inner_ref, outer_ref = refs[:4]
    top_ref, courant_ref, surface_ref, mixing_ref, decay_ref, owner_ref, energy_in_ref = refs[4:11]
    physics_refs, energy_ref, scratch = refs[11 : 11 + len(halves)], refs[11 + len(halves)], refs[12 + len(halves) :]
    if scratch:
        for copy in start_copies([(inner_ref, scratch[0]), (outer_ref, scratch[1])], scratch[2]):
            copy.wait()
        inner_ref, outer_ref = scratch[:2]
    rows, width = base_ref.shape[1], base_ref.shape[-1]
    courant = [courant_ref[r] for r in range(rows)]
    even = is_even()
    top = top_ref[...]
    top = jnp.concatenate([top[:, :width], second_half(top, sector)], axis=0)
    mix_high, mix_low = split_high_low(mixing_ref[...])
    mix = jnp.concatenate([mix_high, mix_high, mix_low, mix_low], axis=1)
    nothing = jnp.zeros_like(mix)
    mix = jnp.concatenate([jnp.concatenate([mix, nothing], axis=1), jnp.concatenate([nothing, mix], axis=1)], axis=0)
    level = lax.broadcasted_iota(jnp.int32, (8, width), 0)
    lane = lax.broadcasted_iota(jnp.int32, (8, width), 1)
    energies = [energy_in_ref[r] for r in range(rows)]
    for half, physics_ref in zip(halves, physics_refs):
        first = first_of(half, base_ref.shape[0])
        t = first + chunk
        inner = jnp.where(first == 0, inner_ref[:levels, :], inner_ref[levels:, :])
        outer = jnp.where(first == 0, outer_ref[:levels, :], outer_ref[levels:, :])
        low, high = jnp.where(even, outer, inner), jnp.where(even, inner, outer)
        low_a, low_b = low[:, :width], second_half(low, sector)
        high_a, high_b = high[:, :width], second_half(high, sector)
        south = courant[0] * (NEAR * low_b - FAR * low_a)
        south_in = courant[1] * (FAR * low_b)
        north_in = courant[3] * (FAR * high_a)
        north = top * (NEAR * high_a - FAR * high_b + north_ref[t])
        extra = [south + south_in, -south_in, north_in, -north_in - north]
        for r in range(rows):
            if r % 2 == 0:
                pair = [base_ref[t, r + i] + extra[r + i] for i in range(2)]
                parts = [split_high_low(row) for row in pair]
                stacked = jnp.concatenate([part for high_low in parts for part in high_low * 2], axis=0)
                both = jnp.dot(mix, stacked, preferred_element_type=jnp.float32)
            advected, mixed = pair[r % 2], both[levels * (r % 2) : levels * (r % 2 + 1)]
            surface = jnp.where(level == 7, surface_ref[t, r : r + 1, :], 0.0)
            mixed = jnp.concatenate([mixed[: levels - 8], mixed[levels - 8 :] + surface], axis=0)
            physics = mixed / (1.0 + decay_ref[t] * mixed * mixed)
            physics_ref[r] = physics
            gap = physics - advected
            squared = gap * gap
            for k in range(levels // 8):
                energies[r] = energies[r] + squared[8 * k : 8 * k + 8]
    if not owner_count:
        for r in range(rows):
            energy_ref[r] = energies[r]
        return
    energies = [jnp.where(lane < sector, energy, 0.0) for energy in energies]
    spot = lax.broadcasted_iota(jnp.int32, (1, LANES), 1)
    result = jnp.zeros((1, LANES), jnp.float32)
    for owner in range(owner_count):
        chosen = jnp.zeros((8, LANES), jnp.float32)
        for r in range(rows):
            picked = jnp.where(owner_ref[r : r + 1, :] == owner, energies[r], 0.0)
            for k in range(width // LANES):
                chosen = chosen + picked[:, LANES * k : LANES * (k + 1)]
        total = jnp.sum(jnp.sum(chosen, axis=0, keepdims=True), axis=1, keepdims=True)
        result = jnp.where(spot == owner, total, result)
    energy_ref[...] = result


def waves_of(radix):
    pairs = (radix - 1) // 2
    cosine = lambda k, i: math.cos(2.0 * math.pi * ((k * i) % radix) / radix)
    sine = lambda k, i: math.sin(2.0 * math.pi * ((k * i) % radix) / radix)
    return pairs, cosine, sine


def row_of(piece_refs, r):
    share = piece_refs[0].shape[0]
    return piece_refs[r // share].at[r % share]


def stacked_table(high_ref, low_ref, begin, size):
    high = high_ref[begin : begin + size, :]
    return jnp.concatenate([high, high, low_ref[begin : begin + size, :]], axis=0)


def product_of(high_ref, low_ref, begin, size, table):
    high = high_ref[:, begin : begin + size]
    stacked = jnp.concatenate([high, low_ref[:, begin : begin + size], high], axis=1)
    return jnp.dot(stacked, table, preferred_element_type=jnp.float32)


def forward_kernel(radix, pieces, own_ref, *refs):
    other_refs, refs = refs[:pieces], refs[pieces:]
    table_high_ref, table_low_ref, first_high_ref, first_low_ref, scale_ref, *refs = refs
    out_high_ref, out_low_ref, high_ref, low_ref = refs
    rows, levels, width = own_ref.shape
    pairs, cosine, sine = waves_of(radix)
    segments = width // LANES
    shift = radix * LANES // 2 % LANES
    lane = lax.broadcasted_iota(jnp.int32, (levels, LANES), 1)

    def store(place, column, wave):
        high_ref[place, column : column + LANES], low_ref[place, column : column + LANES] = split_high_low(wave)

    for r in range(rows):
        place = slice(levels * r, levels * (r + 1))
        other_ref = row_of(other_refs, r)
        own = [own_ref[r, :, LANES * n : LANES * (n + 1)] for n in range(segments)]
        turned = [pltpu.roll(other_ref[:, LANES * n : LANES * (n + 1)], shift, 1) for n in range(segments)]
        joined = own[:-1] + [jnp.where(lane < shift, own[-1], turned[0])]
        joined += [jnp.where(lane < shift, turned[n], turned[n + 1]) for n in range(segments - 1)]
        plus = [joined[n] + joined[radix - n] for n in range(1, pairs + 1)]
        minus = [joined[radix - n] - joined[n] for n in range(1, pairs + 1)]
        store(place, 0, sum(plus, joined[0]))
        for k in range(1, pairs + 1):
            real = sum((cosine(k, n) * plus[n - 1] for n in range(1, pairs + 1)), joined[0])
            imaginary = sine(k, 1) * minus[0]
            for n in range(2, pairs + 1):
                imaginary = imaginary + sine(k, n) * minus[n - 1]
            store(place, LANES * (2 * k - 1), real)
            store(place, LANES * 2 * k, imaginary)

    def transform(begin, size, table):
        spectrum = product_of(high_ref, low_ref, begin, size, table)
        for r in range(rows):
            place = slice(levels * r, levels * (r + 1))
            damped = spectrum[place] * scale_ref[r : r + 1, begin : begin + size]
            out_high_ref[place, begin : begin + size], out_low_ref[place, begin : begin + size] = split_high_low(damped)

    transform(0, LANES, stacked_table(first_high_ref, first_low_ref, 0, LANES))
    for k in range(pairs):
        transform(LANES * (2 * k + 1), 2 * LANES, stacked_table(table_high_ref, table_low_ref, 2 * LANES * k, 2 * LANES))


def inverse_kernel(radix, pieces, mask_ref, own_ref, *refs):
    other_refs, refs = refs[:pieces], refs[pieces:]
    high_ref, low_ref, table_high_ref, table_low_ref, first_high_ref, first_low_ref, *refs = refs
    result_ref, back_ref, wave_ref = refs
    rows, levels, width = own_ref.shape
    sector = result_ref.shape[-1]
    pairs, cosine, sine = waves_of(radix)
    segments = width // LANES
    shift = radix * LANES // 2 % LANES
    lane = lax.broadcasted_iota(jnp.int32, (levels, LANES), 1)

    def transform(begin, size, table):
        wave_ref[:, begin : begin + size] = product_of(high_ref, low_ref, begin, size, table)

    transform(0, LANES, stacked_table(first_high_ref, first_low_ref, 0, LANES))
    for k in range(pairs):
        transform(LANES * (2 * k + 1), 2 * LANES, stacked_table(table_high_ref, table_low_ref, 2 * LANES * k, 2 * LANES))

    for r in range(rows):
        place = slice(levels * r, levels * (r + 1))
        other_ref = row_of(other_refs, r)
        waves = [wave_ref[place, LANES * n : LANES * (n + 1)] for n in range(radix)]
        results = [None] * radix
        results[0] = sum((waves[2 * k - 1] for k in range(1, pairs + 1)), waves[0])
        for n in range(1, pairs + 1):
            even = sum((cosine(k, n) * waves[2 * k - 1] for k in range(1, pairs + 1)), waves[0])
            odd = sine(1, n) * waves[2]
            for k in range(2, pairs + 1):
                odd = odd + sine(k, n) * waves[2 * k]
            results[n], results[radix - n] = even - odd, even + odd
        filtered_row = mask_ref[r] == 1
        turned = [pltpu.roll(result, LANES - shift, 1) for result in results[segments - 1 :]]
        for n in range(segments):
            begin = LANES * n
            size = min(LANES, sector - begin)
            value = jnp.where(filtered_row, results[n], own_ref[r, :, begin : begin + LANES])
            result_ref[:, r, begin : begin + size] = value[:, :size]
            value = jnp.where(lane < LANES - shift, turned[n], turned[min(n + 1, segments - 1)])
            back_ref[r, :, begin : begin + LANES] = jnp.where(filtered_row, value, other_ref[:, begin : begin + LANES])


def finish_kernel(*refs):
    out_hbm, turned_ref, sems = refs[-3:]
    count = turned_ref.shape[0]
    result_refs, received_refs = refs[:count], refs[count : 2 * count]
    rows, levels, width = received_refs[0].shape
    sector = out_hbm.shape[-1]
    piece = levels // PIECES
    copies = []

    def send(source_ref, tracer, slot):
        for part in range(PIECES):
            span = pl.ds(piece * part, piece)
            copies.append(pltpu.make_async_copy(source_ref.at[span], out_hbm.at[tracer, span], sems.at[slot, part]))
            copies[-1].start()

    for i, result_ref in enumerate(result_refs):
        send(result_ref, first_of("keep", 2 * count) + i, i)
    for i in range(count):
        for r in range(rows):
            turned_ref[i, :, r, :] = received_refs[i][r, :, :sector]
        send(turned_ref.at[i], first_of("give", 2 * count) + i, count + i)
    for copy in copies:
        copy.wait()


def on_device(tracers, courant_lat, courant_lon, surface_flux, mixing, decay_rate, owners, polar_mask):
    tracer_count, levels, rows, sector = tracers.shape
    assert rows == 4 and sector % 64 == 0 and lax.axis_size("lon") == 2
    f32 = jnp.float32
    lat_count, lat = lax.axis_size("lat"), lax.axis_index("lat")
    length = 2 * sector
    width = -(-sector // LANES) * LANES
    radix = length // LANES
    downward = [(i + 1, i) for i in range(lat_count - 1)]
    swap = [(0, 1), (1, 0)]

    whole = pl.BlockSpec(memory_space=pltpu.VMEM)
    in_hbm = pl.BlockSpec(memory_space=pltpu.HBM)
    scalars = pl.BlockSpec(memory_space=pltpu.SMEM)
    inside = [pair for i in range(0, lat_count - 1, 2) for pair in ((i, i + 1), (i + 1, i))]
    across = [pair for i in range(1, lat_count - 1, 2) for pair in ((i, i + 1), (i + 1, i))]
    fields = [pltpu.with_memory_space_constraint(array, pltpu.HBM) for array in (tracers, courant_lat, courant_lon)]
    field_buffers = [pltpu.VMEM(array.shape, f32) for array in (tracers, courant_lat, courant_lon)]
    half = tracer_count // 2
    chunk_rows = pltpu.VMEM((levels * 2, length), f32)
    inner = pl.pallas_call(
        functools.partial(pack_kernel, (0, half)),
        in_specs=[in_hbm],
        out_specs=whole,
        out_shape=chunk_rows,
        scratch_shapes=[pltpu.VMEM((2, levels, 2, sector), f32), pltpu.SemaphoreType.DMA((2,))],
        compiler_params=params(),
        cost_estimate=cost(0, 600_000),
        name="pack",
    )(fields[0])
    from_inside = [lax.ppermute(inner, "lat", inside)]
    fields, inner = lax.optimization_barrier((fields, inner))
    fields = [pltpu.with_memory_space_constraint(array, pltpu.HBM) for array in fields]
    *packed, courant_row, sides = pl.pallas_call(
        rest_kernel,
        in_specs=[in_hbm] * 3,
        out_specs=[whole] * (2 * half + 1),
        out_shape=[chunk_rows] * (2 * half - 1)
        + [
            jax.ShapeDtypeStruct((levels // 2, length), f32),
            jax.ShapeDtypeStruct((tracer_count + 1, rows // 2, levels, LANES), f32),
        ],
        scratch_shapes=field_buffers + [pltpu.SemaphoreType.DMA((tracer_count + 2,))],
        compiler_params=params(),
        cost_estimate=cost(0, 0),
        name="rest",
    )(*fields)
    outer, inner = packed[:half], packed[half:]
    from_across = [lax.ppermute(part, "lat", across) for part in outer]
    from_inside += [lax.ppermute(part, "lat", inside) for part in inner]
    top = lax.ppermute(courant_row, "lat", downward)

    sides = lax.ppermute(sides, "lon", swap)
    base, north, lat_courant = pl.pallas_call(
        functools.partial(base_kernel, width),
        in_specs=[in_hbm, in_hbm, in_hbm, whole],
        out_specs=[whole] * 3,
        out_shape=[
            jax.ShapeDtypeStruct((tracer_count, rows, levels, width), f32),
            jax.ShapeDtypeStruct((tracer_count, levels, width), f32),
            jax.ShapeDtypeStruct((rows, levels, width), f32),
        ],
        scratch_shapes=field_buffers + [pltpu.SemaphoreType.DMA((tracer_count + 2,))],
        compiler_params=params(),
        cost_estimate=cost(0, 0),
        name="base",
    )(*fields, sides)

    surface = jnp.pad(surface_flux, ((0, 0), (0, 0), (0, width - sector)))
    decay = decay_rate[:, :, None]
    block_count = rows * sector // BLOCK
    block_of = (np.arange(rows)[:, None] * sector + np.minimum(np.arange(width), sector - 1)[None]) // BLOCK
    owner_of = jnp.repeat(owners.reshape(block_count), BLOCK).reshape(rows, sector)
    owner_of = jnp.pad(owner_of, ((0, 0), (0, width - sector)))
    forward, inverse, numbers, weights = spectral_tables(length)
    row_ids = (lat * rows + jnp.arange(rows)).astype(f32)
    latitude = (-0.5 + (row_ids + 0.5) / (lat_count * rows)) * math.pi
    inverse_sine = np.where(numbers == 0, 1.0, 1.0 / np.where(numbers == 0, 1.0, np.sin(np.pi * numbers / length)))
    ratio = 2.0 * jnp.cos(latitude)[:, None] * jnp.asarray(inverse_sine, f32)[None]
    damping = jnp.where(jnp.asarray(numbers == 0)[None], 1.0, jnp.minimum(1.0, ratio * ratio))
    scale = damping * jnp.asarray(weights, f32)[None]

    base, scale, owner_of, surface, decay = lax.optimization_barrier((base, scale, owner_of, surface, decay))

    circles = jax.ShapeDtypeStruct((half, rows, levels, width), f32)
    result_shape = jax.ShapeDtypeStruct((levels, rows, sector), f32)
    out_shape = jax.ShapeDtypeStruct(tracers.shape, f32)

    def rows_of(chunk):
        parts = (from_inside[chunk], from_across[chunk])
        return parts if chunk == half - 1 else [pltpu.with_memory_space_constraint(part, pltpu.HBM) for part in parts]

    def run_physics(chunk, energy, last=False):
        shapes = [jax.ShapeDtypeStruct(circles.shape[1:], f32)] * 2
        shapes.append(jax.ShapeDtypeStruct((1, LANES) if last else energy.shape, f32))
        *results, energy = pl.pallas_call(
            functools.partial(physics_kernel, levels, sector, lat_count if last else 0, chunk, ("give", "keep")),
            in_specs=[whole] * 2 + ([whole] if last else [in_hbm]) * 2 + [whole] * 7,
            out_specs=[whole] * len(shapes),
            scratch_shapes=[] if last else [chunk_rows] * 2 + [pltpu.SemaphoreType.DMA((2,))],
            out_shape=shapes,
            compiler_params=params(),
            cost_estimate=cost(0, 0),
            name="physics",
        )(base, north, *rows_of(chunk), top, lat_courant, surface, mixing, decay, owner_of, energy)
        return results, energy

    forward, inverse = ([jnp.asarray(part) for table in tables for part in split_table(table)] for tables in (forward, inverse))
    circle = jax.ShapeDtypeStruct(circles.shape[1:], f32)
    spectra = jax.ShapeDtypeStruct((rows * levels, length), jnp.bfloat16)

    def run_forward(own, other):
        return pl.pallas_call(
            functools.partial(forward_kernel, radix, len(other)),
            in_specs=[whole] * (6 + len(other)),
            out_specs=[whole] * 2,
            out_shape=[spectra] * 2,
            scratch_shapes=[pltpu.VMEM(spectra.shape, jnp.bfloat16)] * 2,
            compiler_params=params(),
            cost_estimate=cost(0, 0),
            name="forward",
        )(own, *other, *forward, scale)

    def run_inverse(own, other, high, low):
        return pl.pallas_call(
            functools.partial(inverse_kernel, radix, len(other)),
            in_specs=[scalars] + [whole] * (7 + len(other)),
            out_specs=[whole] * 2,
            out_shape=[result_shape, circle],
            scratch_shapes=[pltpu.VMEM(spectra.shape, f32)],
            compiler_params=params(),
            cost_estimate=cost(0, 0),
            name="inverse",
        )(polar_mask, own, *other, high, low, *inverse)

    energy = jnp.zeros((rows, 8, width), f32)
    results, received = [], []
    for chunk in range(half - 1):
        (given, own), energy = run_physics(chunk, energy)
        other = [lax.ppermute(given[r : r + 2], "lon", swap) for r in range(0, rows, 2)]
        spectrum = run_forward(own, other)
        result, back = run_inverse(own, other, *spectrum)
        results.append(result)
        received.append(lax.ppermute(back, "lon", swap))
        energy, back = lax.optimization_barrier((energy, back))

    distances = [1 << i for i in range(lat_count.bit_length() - 1)]

    def send_energy(energy):
        distance = distances.pop(0)
        return lax.ppermute(energy, "lat", [(i, i ^ distance) for i in range(lat_count)])

    (given, own), energy = run_physics(half - 1, energy, True)
    other = [lax.ppermute(given, "lon", swap)]

    coming = send_energy(energy)
    high, low = run_forward(own, other)
    coming, high = lax.optimization_barrier((coming, high))
    energy = energy + coming
    energy, high = lax.optimization_barrier((energy, high))

    coming = send_energy(energy)
    result, back = run_inverse(own, other, high, low)
    coming, back = lax.optimization_barrier((coming, back))
    energy = energy + coming
    energy, back = lax.optimization_barrier((energy, back))
    results.append(result)
    received.append(lax.ppermute(back, "lon", swap))

    coming = send_energy(energy)
    out = pl.pallas_call(
        finish_kernel,
        in_specs=[whole] * (2 * half),
        out_specs=in_hbm,
        out_shape=out_shape,
        scratch_shapes=[
            pltpu.VMEM((half,) + result_shape.shape, f32),
            pltpu.SemaphoreType.DMA((2 * half, PIECES)),
        ],
        compiler_params=params(),
        cost_estimate=cost(0, 3_000_000),
        name="finish",
    )(*results, *received)
    coming, out = lax.optimization_barrier((coming, out))
    energy = energy + coming
    while distances:
        energy = energy + send_energy(energy)

    owner_energy = lax.dynamic_slice(energy, (0, lat), (1, 1)) / (block_count * BLOCK)
    return out, owner_energy


def solution(mesh):
    placed = (
        P("group", None, "lat", "lon"),
        P("group", "lat", "lon"),
        P("group", "lat", "lon"),
        P("group", "lat", "lon"),
        P(),
        P(),
        P(("group", "lat"), "lon", None, None),
        P(("group", "lat")),
    )
    return jax.shard_map(
        on_device,
        mesh=mesh,
        in_specs=placed,
        out_specs=(P("group", None, "lat", "lon"), P(("group", "lat"), "lon")),
        check_vma=False,
    )
```

```python
import functools
import math

import jax
import jax.numpy as jnp
import numpy as np
from jax import lax
from jax.experimental import pallas as pl
from jax.experimental.pallas import tpu as pltpu
from jax.sharding import PartitionSpec as P

LANES = 128
BLOCK = 128
VMEM_BYTES = 6 * 1024 * 1024
PIECES = 4
NEAR = 7.0 / 12.0
FAR = 1.0 / 12.0


def params():
    return pltpu.CompilerParams(vmem_limit_bytes=VMEM_BYTES)


def cost(flops, bytes_accessed):
    return pl.CostEstimate(flops=flops, bytes_accessed=bytes_accessed, transcendentals=0)


def split_high_low(value):
    high = value.astype(jnp.bfloat16)
    low = (value - high.astype(jnp.float32)).astype(jnp.bfloat16)
    return high, low


def split_table(table):
    high = table.astype(jnp.bfloat16.dtype)
    return high, (table - high.astype(np.float64)).astype(jnp.bfloat16.dtype)


def spectral_tables(length):
    radix = length // LANES
    pairs = (radix - 1) // 2
    spot = np.arange(LANES)[:, None]
    number = np.arange(LANES)[None, :]
    is_cosine = number <= LANES // 2
    wave = np.where(is_cosine, number, number - LANES // 2)
    angle = 2.0 * np.pi * ((spot * wave) % LANES) / LANES
    first = np.where(is_cosine, np.cos(angle), np.sin(angle))
    others, numbers = [], [radix * wave[0]]
    weights = [np.where((wave[0] == 0) | (wave[0] == LANES // 2), 1.0, 2.0) / length]
    for residue in range(1, pairs + 1):
        whole = residue + radix * number
        angle = 2.0 * np.pi * ((spot * whole) % length) / length
        cosine, sine = np.cos(angle), np.sin(angle)
        others.append(np.block([[cosine, -sine], [sine, cosine]]))
        folded = np.minimum(whole[0], length - whole[0])
        numbers += [folded, folded]
        weights.append(np.full(2 * LANES, 2.0 / length))
    forward = np.concatenate(others), first
    inverse = np.concatenate([table.T for table in others]), first.T
    return forward, inverse, np.concatenate(numbers), np.concatenate(weights)


def is_even():
    return lax.axis_index("lat") % 2 == 0


def first_of(half, tracer_count):
    lon = lax.axis_index("lon")
    return (tracer_count // 2) * (lon if half == "keep" else 1 - lon)


def pack_rows(first, second):
    return jnp.concatenate([first, second], axis=1)


def second_half(packed, sector):
    skip, shift = sector // LANES, sector % LANES
    segments = [packed[:, LANES * i : LANES * (i + 1)] for i in range(packed.shape[1] // LANES)]
    if shift == 0:
        return jnp.concatenate(segments[skip:], axis=1)
    turned = [pltpu.roll(segment, LANES - shift, 1) for segment in segments[skip:]]
    lane = lax.broadcasted_iota(jnp.int32, turned[0].shape, 1)
    parts = [jnp.where(lane < LANES - shift, turned[i], turned[min(i + 1, len(turned) - 1)]) for i in range(len(turned))]
    return jnp.concatenate(parts, axis=1)


def start_copies(pairs, sems):
    copies = [pltpu.make_async_copy(source, target, sems.at[i]) for i, (source, target) in enumerate(pairs)]
    for copy in copies:
        copy.start()
    return copies


def pack_kernel(tracers, tracer_hbm, out_ref, row_ref, sems):
    levels = row_ref.shape[1]
    first_row = pl.multiple_of(jnp.where(is_even(), tracer_hbm.shape[2] - 2, 0), 2)
    sources = [tracer_hbm.at[t, :, pl.ds(first_row, 2), :] for t in tracers]
    copies = start_copies([(source, row_ref.at[i]) for i, source in enumerate(sources)], sems)
    for i, copy in enumerate(copies):
        copy.wait()
        out_ref[levels * i : levels * (i + 1), :] = pack_rows(row_ref[i, :, 0, :], row_ref[i, :, 1, :])


def rest_kernel(tracer_hbm, lat_hbm, lon_hbm, *refs):
    courant_ref, side_ref, tracer_ref, lat_ref, lon_ref, sems = refs[-6:]
    count, levels, rows, sector = tracer_ref.shape
    half = count // 2
    outer_refs, inner_refs = refs[:half], refs[half:-6]
    pairs = [(tracer_hbm.at[t], tracer_ref.at[t]) for t in range(count)] + [(lat_hbm, lat_ref), (lon_hbm, lon_ref)]
    for copy in start_copies(pairs, sems):
        copy.wait()
    shift, whole = sector % LANES, sector // LANES * LANES
    lane = lax.broadcasted_iota(jnp.int32, (levels, LANES), 1)
    even = is_even()

    def side_of(values):
        first = pltpu.roll(values[:, :LANES], shift, 1)
        last = jnp.concatenate([values[:, whole:], values[:, whole:]], axis=1)
        return jnp.where(lane < LANES - 2, first, last)

    def store_sides(i, values):
        for r in range(0, rows, 2):
            side_ref[i, r // 2] = jnp.where(lane < shift, pltpu.roll(side_of(values[r]), shift, 1), side_of(values[r + 1]))

    for t in range(count):
        row = [tracer_ref[t, :, r, :] for r in range(rows)]
        place = slice(levels * (t // half), levels * (t // half + 1))
        top, bottom = pack_rows(row[rows - 2], row[rows - 1]), pack_rows(row[0], row[1])
        outer_refs[t % half][place, :] = jnp.where(even, bottom, top)
        if t % half:
            inner_refs[t % half - 1][place, :] = jnp.where(even, top, bottom)
        store_sides(t, row)
    courant = lat_ref[:, 0, :]
    courant_ref[...] = pack_rows(courant[: levels // 2], courant[levels // 2 :])
    store_sides(count, [lon_ref[:, r, :] for r in range(rows)])


def base_kernel(width, tracer_hbm, lat_hbm, lon_hbm, side_ref, base_ref, north_ref, courant_ref, *scratch):
    tracer_ref, lat_ref, lon_ref, sems = scratch
    tracer_count, levels, rows, sector = tracer_ref.shape
    whole = sector // LANES * LANES
    pairs = [(lat_hbm, lat_ref), (lon_hbm, lon_ref)] + [(tracer_hbm.at[t], tracer_ref.at[t]) for t in range(tracer_count)]
    copies = start_copies(pairs, sems)

    def beside(values, side, part=0):
        begin = (sector - whole) * part
        return jnp.concatenate([values[:, :whole], values[:, whole:], side[:, begin : begin + width - sector]], axis=1)

    copies[0].wait()
    copies[1].wait()
    nothing = jnp.zeros((levels, LANES), jnp.float32)
    for r in range(rows):
        courant = lat_ref[:, r, :] if r else jnp.where(lax.axis_index("lat") > 0, lat_ref[:, r, :], 0.0)
        courant_ref[r] = beside(courant, nothing)
    for t in range(tracer_count):
        copies[t + 2].wait()
        q = [beside(tracer_ref[t, :, r, :], side_ref[t, r // 2], r % 2) for r in range(rows)]
        north_ref[t] = NEAR * q[3] - FAR * q[2]
        own_flux = [
            courant_ref[0] * (NEAR * q[0] - FAR * q[1]),
            courant_ref[1] * (NEAR * (q[1] + q[0]) - FAR * q[2]),
            courant_ref[2] * (NEAR * (q[2] + q[1]) - FAR * (q[3] + q[0])),
            courant_ref[3] * (NEAR * (q[3] + q[2]) - FAR * q[1]),
        ]
        for r in range(rows):
            west, west2, east = pltpu.roll(q[r], 1, 1), pltpu.roll(q[r], 2, 1), pltpu.roll(q[r], width - 1, 1)
            flux = beside(lon_ref[:, r, :], side_ref[tracer_count, r // 2], r % 2) * (NEAR * (q[r] + west) - FAR * (east + west2))
            value = q[r] - (pltpu.roll(flux, width - 1, 1) - flux) + own_flux[r]
            if r + 1 < rows:
                value = value - own_flux[r + 1]
            base_ref[t, r] = value


def physics_kernel(levels, sector, owner_count, chunk, halves, *refs):
    base_ref, north_ref, inner_ref, outer_ref = refs[:4]
    top_ref, courant_ref, surface_ref, mixing_ref, decay_ref, owner_ref, energy_in_ref = refs[4:11]
    physics_refs, energy_ref, scratch = refs[11 : 11 + len(halves)], refs[11 + len(halves)], refs[12 + len(halves) :]
    if scratch:
        for copy in start_copies([(inner_ref, scratch[0]), (outer_ref, scratch[1])], scratch[2]):
            copy.wait()
        inner_ref, outer_ref = scratch[:2]
    rows, width = base_ref.shape[1], base_ref.shape[-1]
    courant = [courant_ref[r] for r in range(rows)]
    even = is_even()
    top = top_ref[...]
    top = jnp.concatenate([top[:, :width], second_half(top, sector)], axis=0)
    mix_high, mix_low = split_high_low(mixing_ref[...])
    mix = jnp.concatenate([mix_high, mix_high, mix_low, mix_low], axis=1)
    level = lax.broadcasted_iota(jnp.int32, (8, width), 0)
    lane = lax.broadcasted_iota(jnp.int32, (8, width), 1)
    energies = [energy_in_ref[r] for r in range(rows)]
    for half, physics_ref in zip(halves, physics_refs):
        first = first_of(half, base_ref.shape[0])
        t = first + chunk
        inner = jnp.where(first == 0, inner_ref[:levels, :], inner_ref[levels:, :])
        outer = jnp.where(first == 0, outer_ref[:levels, :], outer_ref[levels:, :])
        low, high = jnp.where(even, outer, inner), jnp.where(even, inner, outer)
        low_a, low_b = low[:, :width], second_half(low, sector)
        high_a, high_b = high[:, :width], second_half(high, sector)
        south = courant[0] * (NEAR * low_b - FAR * low_a)
        south_in = courant[1] * (FAR * low_b)
        north_in = courant[3] * (FAR * high_a)
        north = top * (NEAR * high_a - FAR * high_b + north_ref[t])
        extra = [south + south_in, -south_in, north_in, -north_in - north]
        for r in range(rows):
            advected = base_ref[t, r] + extra[r]
            part_high, part_low = split_high_low(advected)
            stacked = jnp.concatenate([part_high, part_low, part_high, part_low], axis=0)
            mixed = jnp.dot(mix, stacked, preferred_element_type=jnp.float32)
            surface = jnp.where(level == 7, surface_ref[t, r : r + 1, :], 0.0)
            mixed = jnp.concatenate([mixed[: levels - 8], mixed[levels - 8 :] + surface], axis=0)
            physics = mixed / (1.0 + decay_ref[t] * mixed * mixed)
            physics_ref[r] = physics
            gap = physics - advected
            squared = gap * gap
            for k in range(levels // 8):
                energies[r] = energies[r] + squared[8 * k : 8 * k + 8]
    if not owner_count:
        for r in range(rows):
            energy_ref[r] = energies[r]
        return
    energies = [jnp.where(lane < sector, energy, 0.0) for energy in energies]
    sums = []
    for owner in range(owner_count):
        chosen = jnp.zeros((8, LANES), jnp.float32)
        for r in range(rows):
            picked = jnp.where(owner_ref[r : r + 1, :] == owner, energies[r], 0.0)
            for k in range(width // LANES):
                chosen = chosen + picked[:, LANES * k : LANES * (k + 1)]
        sums.append(jnp.sum(chosen, axis=0, keepdims=True))
    totals = jnp.sum(jnp.concatenate(sums, axis=0), axis=1, keepdims=True)
    shape = (owner_count, LANES)
    diagonal = lax.broadcasted_iota(jnp.int32, shape, 0) == lax.broadcasted_iota(jnp.int32, shape, 1)
    energy_ref[...] = jnp.sum(jnp.where(diagonal, totals, 0.0), axis=0, keepdims=True)


def waves_of(radix):
    pairs = (radix - 1) // 2
    cosine = lambda k, i: math.cos(2.0 * math.pi * ((k * i) % radix) / radix)
    sine = lambda k, i: math.sin(2.0 * math.pi * ((k * i) % radix) / radix)
    return pairs, cosine, sine


def row_of(piece_refs, r):
    share = piece_refs[0].shape[0]
    return piece_refs[r // share].at[r % share]


def stacked_table(high_ref, low_ref, begin, size):
    high = high_ref[begin : begin + size, :]
    return jnp.concatenate([high, high, low_ref[begin : begin + size, :]], axis=0)


def product_of(high_ref, low_ref, begin, size, table):
    high = high_ref[:, begin : begin + size]
    stacked = jnp.concatenate([high, low_ref[:, begin : begin + size], high], axis=1)
    return jnp.dot(stacked, table, preferred_element_type=jnp.float32)


def forward_kernel(radix, pieces, own_ref, *refs):
    other_refs, refs = refs[:pieces], refs[pieces:]
    table_high_ref, table_low_ref, first_high_ref, first_low_ref, scale_ref, *refs = refs
    out_high_ref, out_low_ref, high_ref, low_ref = refs
    rows, levels, width = own_ref.shape
    pairs, cosine, sine = waves_of(radix)
    segments = width // LANES
    shift = radix * LANES // 2 % LANES
    lane = lax.broadcasted_iota(jnp.int32, (levels, LANES), 1)

    def store(place, column, wave):
        high_ref[place, column : column + LANES], low_ref[place, column : column + LANES] = split_high_low(wave)

    for r in range(rows):
        place = slice(levels * r, levels * (r + 1))
        other_ref = row_of(other_refs, r)
        own = [own_ref[r, :, LANES * n : LANES * (n + 1)] for n in range(segments)]
        turned = [pltpu.roll(other_ref[:, LANES * n : LANES * (n + 1)], shift, 1) for n in range(segments)]
        joined = own[:-1] + [jnp.where(lane < shift, own[-1], turned[0])]
        joined += [jnp.where(lane < shift, turned[n], turned[n + 1]) for n in range(segments - 1)]
        plus = [joined[n] + joined[radix - n] for n in range(1, pairs + 1)]
        minus = [joined[radix - n] - joined[n] for n in range(1, pairs + 1)]
        store(place, 0, sum(plus, joined[0]))
        for k in range(1, pairs + 1):
            real = sum((cosine(k, n) * plus[n - 1] for n in range(1, pairs + 1)), joined[0])
            imaginary = sine(k, 1) * minus[0]
            for n in range(2, pairs + 1):
                imaginary = imaginary + sine(k, n) * minus[n - 1]
            store(place, LANES * (2 * k - 1), real)
            store(place, LANES * 2 * k, imaginary)

    def transform(begin, size, table):
        spectrum = product_of(high_ref, low_ref, begin, size, table)
        for r in range(rows):
            place = slice(levels * r, levels * (r + 1))
            damped = spectrum[place] * scale_ref[r : r + 1, begin : begin + size]
            out_high_ref[place, begin : begin + size], out_low_ref[place, begin : begin + size] = split_high_low(damped)

    transform(0, LANES, stacked_table(first_high_ref, first_low_ref, 0, LANES))
    for k in range(pairs):
        transform(LANES * (2 * k + 1), 2 * LANES, stacked_table(table_high_ref, table_low_ref, 2 * LANES * k, 2 * LANES))


def inverse_kernel(radix, pieces, mask_ref, own_ref, *refs):
    other_refs, refs = refs[:pieces], refs[pieces:]
    high_ref, low_ref, table_high_ref, table_low_ref, first_high_ref, first_low_ref, *refs = refs
    result_ref, back_ref, wave_ref = refs
    rows, levels, width = own_ref.shape
    sector = result_ref.shape[-1]
    pairs, cosine, sine = waves_of(radix)
    segments = width // LANES
    shift = radix * LANES // 2 % LANES
    lane = lax.broadcasted_iota(jnp.int32, (levels, LANES), 1)

    def transform(begin, size, table):
        wave_ref[:, begin : begin + size] = product_of(high_ref, low_ref, begin, size, table)

    transform(0, LANES, stacked_table(first_high_ref, first_low_ref, 0, LANES))
    for k in range(pairs):
        transform(LANES * (2 * k + 1), 2 * LANES, stacked_table(table_high_ref, table_low_ref, 2 * LANES * k, 2 * LANES))

    for r in range(rows):
        place = slice(levels * r, levels * (r + 1))
        other_ref = row_of(other_refs, r)
        waves = [wave_ref[place, LANES * n : LANES * (n + 1)] for n in range(radix)]
        results = [None] * radix
        results[0] = sum((waves[2 * k - 1] for k in range(1, pairs + 1)), waves[0])
        for n in range(1, pairs + 1):
            even = sum((cosine(k, n) * waves[2 * k - 1] for k in range(1, pairs + 1)), waves[0])
            odd = sine(1, n) * waves[2]
            for k in range(2, pairs + 1):
                odd = odd + sine(k, n) * waves[2 * k]
            results[n], results[radix - n] = even - odd, even + odd
        filtered_row = mask_ref[r] == 1
        turned = [pltpu.roll(result, LANES - shift, 1) for result in results[segments - 1 :]]
        for n in range(segments):
            begin = LANES * n
            size = min(LANES, sector - begin)
            value = jnp.where(filtered_row, results[n], own_ref[r, :, begin : begin + LANES])
            result_ref[:, r, begin : begin + size] = value[:, :size]
            value = jnp.where(lane < LANES - shift, turned[n], turned[min(n + 1, segments - 1)])
            back_ref[r, :, begin : begin + LANES] = jnp.where(filtered_row, value, other_ref[:, begin : begin + LANES])


def finish_kernel(*refs):
    out_hbm, turned_ref, sems = refs[-3:]
    count = turned_ref.shape[0]
    result_refs, received_refs = refs[:count], refs[count : 2 * count]
    rows, levels, width = received_refs[0].shape
    sector = out_hbm.shape[-1]
    piece = levels // PIECES
    copies = []

    def send(source_ref, tracer, slot):
        for part in range(PIECES):
            span = pl.ds(piece * part, piece)
            copies.append(pltpu.make_async_copy(source_ref.at[span], out_hbm.at[tracer, span], sems.at[slot, part]))
            copies[-1].start()

    for i, result_ref in enumerate(result_refs):
        send(result_ref, first_of("keep", 2 * count) + i, i)
    for i in range(count):
        for r in range(rows):
            turned_ref[i, :, r, :] = received_refs[i][r, :, :sector]
        send(turned_ref.at[i], first_of("give", 2 * count) + i, count + i)
    for copy in copies:
        copy.wait()


def on_device(tracers, courant_lat, courant_lon, surface_flux, mixing, decay_rate, owners, polar_mask):
    tracer_count, levels, rows, sector = tracers.shape
    assert rows == 4 and sector % 64 == 0 and lax.axis_size("lon") == 2
    f32 = jnp.float32
    lat_count, lat = lax.axis_size("lat"), lax.axis_index("lat")
    length = 2 * sector
    width = -(-sector // LANES) * LANES
    radix = length // LANES
    downward = [(i + 1, i) for i in range(lat_count - 1)]
    swap = [(0, 1), (1, 0)]

    whole = pl.BlockSpec(memory_space=pltpu.VMEM)
    in_hbm = pl.BlockSpec(memory_space=pltpu.HBM)
    scalars = pl.BlockSpec(memory_space=pltpu.SMEM)
    inside = [pair for i in range(0, lat_count - 1, 2) for pair in ((i, i + 1), (i + 1, i))]
    across = [pair for i in range(1, lat_count - 1, 2) for pair in ((i, i + 1), (i + 1, i))]
    fields = [pltpu.with_memory_space_constraint(array, pltpu.HBM) for array in (tracers, courant_lat, courant_lon)]
    field_buffers = [pltpu.VMEM(array.shape, f32) for array in (tracers, courant_lat, courant_lon)]
    half = tracer_count // 2
    chunk_rows = pltpu.VMEM((levels * 2, length), f32)
    inner = pl.pallas_call(
        functools.partial(pack_kernel, (0, half)),
        in_specs=[in_hbm],
        out_specs=whole,
        out_shape=chunk_rows,
        scratch_shapes=[pltpu.VMEM((2, levels, 2, sector), f32), pltpu.SemaphoreType.DMA((2,))],
        compiler_params=params(),
        cost_estimate=cost(0, 600_000),
        name="pack",
    )(fields[0])
    from_inside = [lax.ppermute(inner, "lat", inside)]
    fields, inner = lax.optimization_barrier((fields, inner))
    fields = [pltpu.with_memory_space_constraint(array, pltpu.HBM) for array in fields]
    *packed, courant_row, sides = pl.pallas_call(
        rest_kernel,
        in_specs=[in_hbm] * 3,
        out_specs=[whole] * (2 * half + 1),
        out_shape=[chunk_rows] * (2 * half - 1)
        + [
            jax.ShapeDtypeStruct((levels // 2, length), f32),
            jax.ShapeDtypeStruct((tracer_count + 1, rows // 2, levels, LANES), f32),
        ],
        scratch_shapes=field_buffers + [pltpu.SemaphoreType.DMA((tracer_count + 2,))],
        compiler_params=params(),
        cost_estimate=cost(0, 0),
        name="rest",
    )(*fields)
    outer, inner = packed[:half], packed[half:]
    from_across = [lax.ppermute(part, "lat", across) for part in outer]
    from_inside += [lax.ppermute(part, "lat", inside) for part in inner]
    top = lax.ppermute(courant_row, "lat", downward)

    sides = lax.ppermute(sides, "lon", swap)
    base, north, lat_courant = pl.pallas_call(
        functools.partial(base_kernel, width),
        in_specs=[in_hbm, in_hbm, in_hbm, whole],
        out_specs=[whole] * 3,
        out_shape=[
            jax.ShapeDtypeStruct((tracer_count, rows, levels, width), f32),
            jax.ShapeDtypeStruct((tracer_count, levels, width), f32),
            jax.ShapeDtypeStruct((rows, levels, width), f32),
        ],
        scratch_shapes=field_buffers + [pltpu.SemaphoreType.DMA((tracer_count + 2,))],
        compiler_params=params(),
        cost_estimate=cost(0, 0),
        name="base",
    )(*fields, sides)

    surface = jnp.pad(surface_flux, ((0, 0), (0, 0), (0, width - sector)))
    decay = decay_rate[:, :, None]
    block_count = rows * sector // BLOCK
    block_of = (np.arange(rows)[:, None] * sector + np.minimum(np.arange(width), sector - 1)[None]) // BLOCK
    owner_of = jnp.repeat(owners.reshape(block_count), BLOCK).reshape(rows, sector)
    owner_of = jnp.pad(owner_of, ((0, 0), (0, width - sector)))
    forward, inverse, numbers, weights = spectral_tables(length)
    row_ids = (lat * rows + jnp.arange(rows)).astype(f32)
    latitude = (-0.5 + (row_ids + 0.5) / (lat_count * rows)) * math.pi
    inverse_sine = np.where(numbers == 0, 1.0, 1.0 / np.where(numbers == 0, 1.0, np.sin(np.pi * numbers / length)))
    ratio = 2.0 * jnp.cos(latitude)[:, None] * jnp.asarray(inverse_sine, f32)[None]
    damping = jnp.where(jnp.asarray(numbers == 0)[None], 1.0, jnp.minimum(1.0, ratio * ratio))
    scale = damping * jnp.asarray(weights, f32)[None]

    base, scale, owner_of, surface, decay = lax.optimization_barrier((base, scale, owner_of, surface, decay))

    circles = jax.ShapeDtypeStruct((half, rows, levels, width), f32)
    result_shape = jax.ShapeDtypeStruct((levels, rows, sector), f32)
    out_shape = jax.ShapeDtypeStruct(tracers.shape, f32)

    def rows_of(chunk):
        parts = (from_inside[chunk], from_across[chunk])
        return parts if chunk == half - 1 else [pltpu.with_memory_space_constraint(part, pltpu.HBM) for part in parts]

    def run_physics(chunk, energy, last=False):
        shapes = [jax.ShapeDtypeStruct(circles.shape[1:], f32)] * 2
        shapes.append(jax.ShapeDtypeStruct((1, LANES) if last else energy.shape, f32))
        *results, energy = pl.pallas_call(
            functools.partial(physics_kernel, levels, sector, lat_count if last else 0, chunk, ("give", "keep")),
            in_specs=[whole] * 2 + ([whole] if last else [in_hbm]) * 2 + [whole] * 7,
            out_specs=[whole] * len(shapes),
            scratch_shapes=[] if last else [chunk_rows] * 2 + [pltpu.SemaphoreType.DMA((2,))],
            out_shape=shapes,
            compiler_params=params(),
            cost_estimate=cost(0, 0),
            name="physics",
        )(base, north, *rows_of(chunk), top, lat_courant, surface, mixing, decay, owner_of, energy)
        return results, energy

    forward, inverse = ([jnp.asarray(part) for table in tables for part in split_table(table)] for tables in (forward, inverse))
    circle = jax.ShapeDtypeStruct(circles.shape[1:], f32)
    spectra = jax.ShapeDtypeStruct((rows * levels, length), jnp.bfloat16)

    def run_forward(own, other):
        return pl.pallas_call(
            functools.partial(forward_kernel, radix, len(other)),
            in_specs=[whole] * (6 + len(other)),
            out_specs=[whole] * 2,
            out_shape=[spectra] * 2,
            scratch_shapes=[pltpu.VMEM(spectra.shape, jnp.bfloat16)] * 2,
            compiler_params=params(),
            cost_estimate=cost(0, 0),
            name="forward",
        )(own, *other, *forward, scale)

    def run_inverse(own, other, high, low):
        return pl.pallas_call(
            functools.partial(inverse_kernel, radix, len(other)),
            in_specs=[scalars] + [whole] * (7 + len(other)),
            out_specs=[whole] * 2,
            out_shape=[result_shape, circle],
            scratch_shapes=[pltpu.VMEM(spectra.shape, f32)],
            compiler_params=params(),
            cost_estimate=cost(0, 0),
            name="inverse",
        )(polar_mask, own, *other, high, low, *inverse)

    energy = jnp.zeros((rows, 8, width), f32)
    results, received = [], []
    for chunk in range(half - 1):
        (given, own), energy = run_physics(chunk, energy)
        other = [lax.ppermute(given[r : r + 2], "lon", swap) for r in range(0, rows, 2)]
        spectrum = run_forward(own, other)
        result, back = run_inverse(own, other, *spectrum)
        results.append(result)
        received.append(lax.ppermute(back, "lon", swap))
        energy, back = lax.optimization_barrier((energy, back))

    distances = [1 << i for i in range(lat_count.bit_length() - 1)]

    def send_energy(energy):
        distance = distances.pop(0)
        return lax.ppermute(energy, "lat", [(i, i ^ distance) for i in range(lat_count)])

    (given, own), energy = run_physics(half - 1, energy, True)
    other = [lax.ppermute(given, "lon", swap)]

    coming = send_energy(energy)
    high, low = run_forward(own, other)
    coming, high = lax.optimization_barrier((coming, high))
    energy = energy + coming
    energy, high = lax.optimization_barrier((energy, high))

    coming = send_energy(energy)
    result, back = run_inverse(own, other, high, low)
    coming, back = lax.optimization_barrier((coming, back))
    energy = energy + coming
    energy, back = lax.optimization_barrier((energy, back))
    results.append(result)
    received.append(lax.ppermute(back, "lon", swap))

    coming = send_energy(energy)
    out = pl.pallas_call(
        finish_kernel,
        in_specs=[whole] * (2 * half),
        out_specs=in_hbm,
        out_shape=out_shape,
        scratch_shapes=[
            pltpu.VMEM((half,) + result_shape.shape, f32),
            pltpu.SemaphoreType.DMA((2 * half, PIECES)),
        ],
        compiler_params=params(),
        cost_estimate=cost(0, 3_000_000),
        name="finish",
    )(*results, *received)
    coming, out = lax.optimization_barrier((coming, out))
    energy = energy + coming
    while distances:
        energy = energy + send_energy(energy)

    owner_energy = lax.dynamic_slice(energy, (0, lat), (1, 1)) / (block_count * BLOCK)
    return out, owner_energy


def solution(mesh):
    placed = (
        P("group", None, "lat", "lon"),
        P("group", "lat", "lon"),
        P("group", "lat", "lon"),
        P("group", "lat", "lon"),
        P(),
        P(),
        P(("group", "lat"), "lon", None, None),
        P(("group", "lat")),
    )
    return jax.shard_map(
        on_device,
        mesh=mesh,
        in_specs=placed,
        out_specs=(P("group", None, "lat", "lon"), P(("group", "lat"), "lon")),
        check_vma=False,
    )
```
